32 devices in a mesh: groups: 2 (over y), gx: 4 (over z), gy: 2 (over x), gz: 2 (over core).
Axes of the slice: x: 2, y: 2, z: 4, core: 2. Of those that a mesh axis runs over, the one named last changes fastest.
Arguments:
- tokens: bfloat16 [64, 16384], P(('groups', 'gx', 'gy', 'gz')), parts along dimension 0, may hold values from -6 to 6
- norm_gain: float32 [16384], replicated, may hold values from 0.25 to 1.75
- query_weight: bfloat16 [16384, 8192], P('gx', ('gy', 'gz')), may hold values from -0.046875 to 0.046875
- key_weight: bfloat16 [16384, 1024], P('gx', ('gy', 'gz')), may hold values from -0.046875 to 0.046875
- value_weight: bfloat16 [16384, 1024], P('gx', ('gy', 'gz')), may hold values from -0.046875 to 0.046875
- out_weight: bfloat16 [8192, 16384], P(('gy', 'gz'), 'gx'), may hold values from -0.0625 to 0.0625
- cache_keys: bfloat16 [64, 256, 1024], P(('groups', 'gx', 'gy', 'gz')), parts along dimension 0, may hold values from -200 to 200
- cache_values: bfloat16 [64, 256, 1024], P(('groups', 'gx', 'gy', 'gz')), parts along dimension 0, may hold values from -18 to 18
- lengths: int32 [64], P(('groups', 'gx', 'gy', 'gz')), parts along dimension 0, may hold values from 1 to 256, as said below
Outputs:
- attention_out: bfloat16 [64, 16384], P(('groups', 'gx', 'gy', 'gz')), parts along dimension 0
The draws below stay inside these ranges and needn't reach their ends.
There are 2 independent parts, one for each index of `groups`. The reference program is written for one: setup_inputs(seed, part) draws one part's arguments, and reference() takes and returns one part's arrays. A program takes and returns all parts, laid end to end along the dimension named above; an argument that names none is the same for every part. Nothing has to cross between parts.
Inputs may be any that keep to these rules, and one draw needn't show every extreme that they name: `lengths`: each row's cache holds from 1 to 256 filled slots; some row holds exactly 256.
All inputs are finite; a program needn't handle non-finite values.
Results may differ from the reference program's by a relative error of at most 0.006.
The reference program's roundings to bfloat16 on the way (of `normed`, `query`, `query_rot`, `probability` and `attended`) count: a program that leaves them out, or rounds other values in their place, can miss the bound.
Values may be sent and summed in bfloat16 or wider, within the bound.
No kernel may reach another device: no remote copies, remote signals or barrier semaphores. Data moves between devices by JAX's collectives and lax.ppermute only.
A program may use at most 128 MiB of HBM per device.

```python
import jax
import jax.numpy as jnp
from jax import lax

D = 16384
H = 64
KVH = 8
HD = 128
CACHE = 256
BATCH = 32


def draw_cache_keys(key, part):
    key = jax.random.fold_in(key, 1)
    base_draw = jax.random.normal(key, (BATCH, CACHE, KVH * HD), jnp.float32)
    return base_draw.astype(jnp.bfloat16)


def draw_lengths(key, part):
    key = jax.random.fold_in(key, 5)
    first_key, second_key = jax.random.split(key)
    filled = jax.random.randint(first_key, (BATCH,), 1, CACHE + 1)
    chosen = jax.random.randint(second_key, (), 0, BATCH)
    return jnp.where(jnp.arange(BATCH) == chosen, CACHE, filled).astype(jnp.int32)


def levels(rng, shape, cuts, least, high):
    level, own = 1.0, jax.random.fold_in(rng, 6)
    for dim, parts in cuts:
        draws = jnp.exp(jax.random.uniform(jax.random.fold_in(own, dim), (parts,), jnp.float32, least / len(cuts), high / len(cuts)))
        level = level * jnp.repeat(draws, shape[dim] // parts).reshape([-1 if axis == dim else 1 for axis in range(len(shape))])
    return level


def gaussian(stream_key, extent, width, most, cuts=(), held_as=jnp.bfloat16):
    loudness = levels(stream_key, extent, cuts, -0.22, 0.18) if cuts else 1.0
    entries = jax.random.normal(stream_key, extent, jnp.float32) * width * loudness
    return jnp.minimum(jnp.maximum(entries, -most), most).astype(held_as)


def setup_inputs(seed: int = 0, part: int = 0) -> dict:
    arg_keys = jax.random.split(jax.random.key(seed), 10)
    part_splits = jax.random.split(jax.random.fold_in(arg_keys[9], part), 10)
    return {
        "tokens": gaussian(part_splits[0], (BATCH, D), 1.0, 6.0, ((0, 16),)),
        "norm_gain": jnp.clip(1.0 + 0.15 * jax.random.normal(arg_keys[1], (D,), jnp.float32), 0.25, 1.75),
        "query_weight": gaussian(arg_keys[2], (D, H * HD), D ** -0.5, 0.046875, ((0, 4), (1, 4))),
        "key_weight": gaussian(arg_keys[3], (D, KVH * HD), D ** -0.5, 0.046875, ((0, 4), (1, 4))),
        "value_weight": gaussian(arg_keys[4], (D, KVH * HD), D ** -0.5, 0.046875, ((0, 4), (1, 4))),
        "out_weight": gaussian(arg_keys[5], (H * HD, D), (H * HD) ** -0.5, 0.0625, ((0, 4), (1, 4))),
        "cache_keys": draw_cache_keys(jax.random.fold_in(jax.random.fold_in(arg_keys[9], part), 71), part),
        "cache_values": gaussian(part_splits[7], (BATCH, CACHE, KVH * HD), 3.0, 18.0, ((0, 16),)),
        "lengths": draw_lengths(jax.random.fold_in(jax.random.fold_in(arg_keys[9], part), 71), part),
    }


def rotate(vector, position):
    half_dim = vector.shape[-1] // 2
    frequency = 500000.0 ** (-jnp.arange(half_dim, dtype=jnp.float32) / half_dim)
    angles = position.astype(jnp.float32)[:, None, None] * frequency
    cosine_part = jnp.cos(angles)
    sine_part = jnp.sin(angles)
    front_half = vector[..., :half_dim]
    back_half = vector[..., half_dim:]
    return jnp.concatenate([front_half * cosine_part - back_half * sine_part, front_half * sine_part + back_half * cosine_part], -1)

def reference(tokens, norm_gain, query_weight, key_weight, value_weight, out_weight, cache_keys, cache_values, lengths):
    float_tokens = tokens.astype(jnp.float32)
    mean_square = lax.optimization_barrier(jnp.mean(float_tokens * float_tokens, -1, keepdims=True))
    normed = (float_tokens * lax.rsqrt(mean_square + 1e-05) * norm_gain).astype(jnp.bfloat16)
    query = jnp.dot(normed, query_weight, preferred_element_type=jnp.float32).astype(jnp.bfloat16)
    key_new = jnp.dot(normed, key_weight, preferred_element_type=jnp.float32).astype(jnp.bfloat16)
    value_new = jnp.dot(normed, value_weight, preferred_element_type=jnp.float32).astype(jnp.bfloat16)
    row_count = tokens.shape[0]
    group_size = H // KVH
    query_rot = rotate(query.astype(jnp.float32).reshape(row_count, H, HD), lengths).astype(jnp.bfloat16)
    key_rot = rotate(key_new.astype(jnp.float32).reshape(row_count, KVH, HD), lengths).astype(jnp.bfloat16)
    query_group = query_rot.reshape(row_count, KVH, group_size, HD).astype(jnp.float32)
    key_cache = cache_keys.reshape(row_count, CACHE, KVH, HD).astype(jnp.float32)
    value_cache = cache_values.reshape(row_count, CACHE, KVH, HD).astype(jnp.float32)
    scale = 1.0 / HD ** 0.5
    scores = jnp.einsum('rkgd,rskd->rkgs', query_group, key_cache) * scale
    valid_mask = (jnp.arange(CACHE, dtype=jnp.int32)[None, :] < lengths[:, None])[:, None, None, :]
    scores = jnp.where(valid_mask, scores, -1e+30)
    fresh_score = jnp.einsum('rkgd,rkd->rkg', query_group, key_rot.astype(jnp.float32)) * scale
    top_score = jnp.maximum(lax.optimization_barrier(jnp.max(scores, -1)), fresh_score)
    weights = jnp.exp(scores - top_score[..., None])
    own_weight = jnp.exp(fresh_score - top_score)
    denominator = lax.optimization_barrier(jnp.sum(weights, -1)) + own_weight
    probability = (weights / denominator[..., None]).astype(jnp.bfloat16)
    own_prob = (own_weight / denominator).astype(jnp.bfloat16)
    mixed_heads = jnp.einsum('rkgs,rskd->rkgd', probability.astype(jnp.float32), value_cache)
    mixed_heads = mixed_heads + own_prob.astype(jnp.float32)[..., None] * value_new.reshape(row_count, KVH, 1, HD).astype(jnp.float32)
    attended = mixed_heads.reshape(row_count, H * HD).astype(jnp.bfloat16)
    return jnp.dot(attended, out_weight, preferred_element_type=jnp.float32).astype(jnp.bfloat16)
```

```python
import functools

import jax
import jax.numpy as jnp
import numpy as np
from jax import lax
from jax.experimental import pallas as pl
from jax.experimental.pallas import tpu as pltpu
from jax.sharding import PartitionSpec as P

HD = 128
ROW_AXES = ("gx", "gy", "gz")
PLANE = ("gy", "gz")
MIB = 1024 * 1024
IN_VMEM = pl.BlockSpec(memory_space=pltpu.VMEM)
IN_HBM = pl.BlockSpec(memory_space=pl.ANY)
IN_SMEM = pl.BlockSpec(memory_space=pltpu.SMEM)


def norm_kernel(wide, plane, tokens_ref, gain_ref, blocks_ref):
    tokens = tokens_ref[...].astype(jnp.float32)
    mean_square = jnp.mean(tokens * tokens, -1, keepdims=True)
    normed = (tokens * lax.rsqrt(mean_square + 1e-05) * gain_ref[...]).astype(jnp.bfloat16)
    width = normed.shape[1] // wide
    for i in range(wide):
        for j in range(plane):
            blocks_ref[i * plane + j] = normed[:, i * width : (i + 1) * width]


def stream_kernel(count, chunk, rows_ref, *refs):
    weights, sums_ref = refs[:count], refs[count]
    held, sems = refs[count + 1 : 2 * count + 1], refs[2 * count + 1]
    steps = weights[0].shape[0] // chunk

    def copies(s):
        return [
            pltpu.make_async_copy(
                weights[w].at[pl.ds(s * chunk, chunk)],
                held[w].at[pl.ds(s * chunk, chunk)],
                sems.at[w, s],
            )
            for w in range(count)
        ]

    for s in range(steps):
        for copy in copies(s):
            copy.start()
    for s in range(steps):
        part = rows_ref[:, s * chunk : (s + 1) * chunk]
        at = 0
        for w, copy in enumerate(copies(s)):
            copy.wait()
            cols = weights[w].shape[1]
            term = jnp.dot(
                part, held[w][s * chunk : (s + 1) * chunk, :], preferred_element_type=jnp.float32
            )
            if s == 0:
                sums_ref[:, at : at + cols] = term
            else:
                sums_ref[:, at : at + cols] += term
            at += cols


def stream_matmul(rows, weights, chunk):
    depth = rows.shape[1]
    cols = sum(w.shape[1] for w in weights)
    count = len(weights)
    return pl.pallas_call(
        functools.partial(stream_kernel, count, chunk),
        out_shape=jax.ShapeDtypeStruct((rows.shape[0], cols), jnp.float32),
        in_specs=[IN_VMEM] + [IN_HBM] * count,
        out_specs=IN_VMEM,
        scratch_shapes=[pltpu.VMEM(w.shape, w.dtype) for w in weights]
        + [pltpu.SemaphoreType.DMA((count, depth // chunk))],
        compiler_params=pltpu.CompilerParams(vmem_limit_bytes=40 * MIB),
        cost_estimate=pl.CostEstimate(
            flops=2 * rows.shape[0] * depth * cols,
            bytes_accessed=2 * depth * cols,
            transcendentals=0,
        ),
    )(rows, *weights)


def attend_kernel(
    wide, plane, rows, query_cols, kv_cols,
    lengths_ref, partial_ref, frequency_ref, keys_hbm, values_hbm,
    blocks_ref, keys_ref, values_ref, sems,
):
    key_copy = pltpu.make_async_copy(keys_hbm, keys_ref, sems.at[0])
    value_copy = pltpu.make_async_copy(values_hbm, values_ref, sems.at[1])
    key_copy.start()
    value_copy.start()
    slots = keys_ref.shape[1]
    kv_heads = kv_cols // HD
    group = query_cols // kv_cols
    pairs = plane * rows
    scale = 1.0 / HD**0.5
    total = partial_ref[0]
    for i in range(1, wide):
        total = total + partial_ref[i]
    heads = total.astype(jnp.bfloat16).astype(jnp.float32)

    row_of = lax.broadcasted_iota(jnp.int32, (pairs, 1), 0) % rows
    position = jnp.zeros((pairs, 1), jnp.int32)
    for r in range(rows):
        position = jnp.where(row_of == r, lengths_ref[r], position)
    angles = position.astype(jnp.float32) * frequency_ref[...]
    cosine, sine = jnp.cos(angles), jnp.sin(angles)
    front = lax.broadcasted_iota(jnp.int32, (1, HD), 1) < HD // 2
    sine = jnp.where(front, -sine, sine)

    def rotate(vector):
        turned = vector * cosine + pltpu.roll(vector, HD // 2, 1) * sine
        return turned.astype(jnp.bfloat16).astype(jnp.float32)

    query, fresh, value_new = [], [], []
    for h in range(kv_heads):
        turned = jnp.stack(
            [
                rotate(heads[:, (h * group + g) * HD : (h * group + g + 1) * HD])
                for g in range(group)
            ],
            0,
        )
        turned = jnp.swapaxes(turned, 0, 1)
        at = query_cols + h * HD
        key_rot = rotate(heads[:, at : at + HD])
        fresh.append(jnp.sum(turned * key_rot[:, None, :], -1, keepdims=True) * scale)
        query.append(turned.astype(jnp.bfloat16))
        at = query_cols + kv_cols + h * HD
        value_new.append(heads[:, at : at + HD])
    key_copy.wait()
    value_copy.wait()
    slot = lax.broadcasted_iota(jnp.int32, (1, slots), 1)
    attended = []
    for h in range(kv_heads):
        mixed = []
        for p in range(pairs):
            j, r = p // rows, p % rows
            at = (j * kv_heads + h) * HD
            scores = (
                lax.dot_general(
                    query[h][p],
                    keys_ref[r, :, at : at + HD],
                    (((1,), (1,)), ((), ())),
                    preferred_element_type=jnp.float32,
                )
                * scale
            )
            scores = jnp.where(slot < lengths_ref[r], scores, -1e30)
            own = fresh[h][p]
            top = jnp.maximum(jnp.max(scores, -1, keepdims=True), own)
            weights = jnp.exp(scores - top)
            own_weight = jnp.exp(own - top)
            denominator = jnp.sum(weights, -1, keepdims=True) + own_weight
            probability = (weights / denominator).astype(jnp.bfloat16)
            own_prob = (own_weight / denominator).astype(jnp.bfloat16).astype(jnp.float32)
            mix = jnp.dot(
                probability, values_ref[r, :, at : at + HD], preferred_element_type=jnp.float32
            )
            mixed.append(mix + own_prob * value_new[h][p : p + 1])
        by_head = jnp.swapaxes(jnp.stack(mixed, 0), 0, 1)
        attended += [by_head[g] for g in range(group)]
    attended = jnp.concatenate(attended, 1)
    for j in range(plane):
        block = attended[j * rows : (j + 1) * rows].astype(jnp.bfloat16)
        for i in range(wide):
            blocks_ref[i * plane + j] = block


def sum_kernel(terms_ref, sum_ref):
    total = terms_ref[0]
    for j in range(1, terms_ref.shape[0]):
        total = total + terms_ref[j]
    sum_ref[...] = total.astype(sum_ref.dtype)


def swap_blocks(blocks, axes):
    return lax.all_to_all(blocks, axes, split_axis=0, concat_axis=0, tiled=True)


def shards(
    tokens,
    norm_gain,
    query_weight,
    key_weight,
    value_weight,
    out_weight,
    cache_keys,
    cache_values,
    lengths,
):
    rows = tokens.shape[0]
    wide = lax.axis_size("gx")
    plane = lax.axis_size(PLANE)
    owners = wide * plane
    width, query_cols = query_weight.shape
    kv_cols = key_weight.shape[1]
    depth, out_cols = out_weight.shape

    normed = pl.pallas_call(
        functools.partial(norm_kernel, wide, plane),
        out_shape=jax.ShapeDtypeStruct((owners, rows, width), jnp.bfloat16),
        in_specs=[IN_VMEM, IN_VMEM],
        out_specs=IN_VMEM,
    )(tokens, norm_gain.reshape(1, -1))
    all_rows = swap_blocks(normed, ROW_AXES).reshape(owners * rows, width)
    partial = stream_matmul(all_rows, (query_weight, key_weight, value_weight), 256)
    partial = swap_blocks(partial.reshape(owners, rows, -1), ROW_AXES)
    partial = partial.reshape(wide, plane * rows, -1)

    half_dim = HD // 2
    frequency = 500000.0 ** (-np.arange(half_dim, dtype=np.float64) / half_dim)
    frequency = np.tile(frequency.astype(np.float32), 2).reshape(1, HD)
    attended = pl.pallas_call(
        functools.partial(attend_kernel, wide, plane, rows, query_cols, kv_cols),
        out_shape=jax.ShapeDtypeStruct((owners, rows, query_cols), jnp.bfloat16),
        in_specs=[IN_SMEM, IN_VMEM, IN_VMEM, IN_HBM, IN_HBM],
        out_specs=IN_VMEM,
        scratch_shapes=[
            pltpu.VMEM(cache_keys.shape, cache_keys.dtype),
            pltpu.VMEM(cache_values.shape, cache_values.dtype),
            pltpu.SemaphoreType.DMA((2,)),
        ],
        compiler_params=pltpu.CompilerParams(vmem_limit_bytes=16 * MIB),
    )(lengths, partial, jnp.asarray(frequency), cache_keys, cache_values)
    head_rows = swap_blocks(attended, ROW_AXES)
    head_rows = head_rows.reshape(wide, plane, rows, depth).swapaxes(0, 1)
    head_rows = head_rows.reshape(owners * rows, depth)
    out_partial = stream_matmul(head_rows, (out_weight,), 256)
    out_partial = swap_blocks(out_partial.reshape(plane, wide * rows, out_cols), PLANE)
    out_own = pl.pallas_call(
        sum_kernel,
        out_shape=jax.ShapeDtypeStruct((wide * rows, out_cols), jnp.bfloat16),
        in_specs=[IN_VMEM],
        out_specs=IN_VMEM,
    )(out_partial)
    result = swap_blocks(out_own.reshape(wide, rows, out_cols), "gx")
    return result.swapaxes(0, 1).reshape(rows, wide * out_cols)


def solution(mesh):
    placed = (
        P(("groups", "gx", "gy", "gz"), None),
        P(),
        P("gx", ("gy", "gz")),
        P("gx", ("gy", "gz")),
        P("gx", ("gy", "gz")),
        P(("gy", "gz"), "gx"),
        P(("groups", "gx", "gy", "gz"), None, None),
        P(("groups", "gx", "gy", "gz"), None, None),
        P(("groups", "gx", "gy", "gz")),
    )
    return jax.shard_map(
        shards,
        mesh=mesh,
        in_specs=placed,
        out_specs=P(("groups", "gx", "gy", "gz"), None),
        check_vma=False,
    )
```

```python
import functools

import jax
import jax.numpy as jnp
import numpy as np
from jax import lax
from jax.experimental import pallas as pl
from jax.experimental.pallas import tpu as pltpu
from jax.sharding import PartitionSpec as P

HD = 128
ROW_AXES = ("gx", "gy", "gz")
CHIPS = ("gx", "gy")
PLANE = ("gy", "gz")
MIB = 1024 * 1024
IN_VMEM = pl.BlockSpec(memory_space=pltpu.VMEM)
IN_HBM = pl.BlockSpec(memory_space=pltpu.HBM)
IN_SMEM = pl.BlockSpec(memory_space=pltpu.SMEM)


def norm_kernel(wide, plane, tokens_ref, gain_ref, blocks_ref):
    tokens = tokens_ref[...].astype(jnp.float32)
    mean_square = jnp.mean(tokens * tokens, -1, keepdims=True)
    normed = (tokens * lax.rsqrt(mean_square + 1e-05) * gain_ref[...]).astype(jnp.bfloat16)
    width = normed.shape[1] // wide
    for i in range(wide):
        for j in range(plane):
            blocks_ref[i * plane + j] = normed[:, i * width : (i + 1) * width]


def project_kernel(rows_ref, query_ref, key_ref, value_ref, sums_ref):
    owners, rows, width = rows_ref.shape
    normed = rows_ref[...].reshape(owners * rows, width)
    at = 0
    for weight in (query_ref, key_ref, value_ref):
        cols = weight.shape[1]
        step = min(cols, 256)
        for c in range(0, cols, step):
            part = jnp.dot(normed, weight[:, c : c + step], preferred_element_type=jnp.float32)
            sums_ref[:, :, at : at + step] = part.reshape(owners, rows, step)
            at += step


def attend_kernel(
    wide, plane, rows, query_cols, kv_cols,
    lengths_ref, partial_ref, frequency_ref, keys_ref, values_ref, blocks_ref,
):
    slots = keys_ref.shape[1]
    kv_heads = kv_cols // HD
    all_kv = kv_heads * plane
    group = query_cols // kv_cols
    pairs = plane * rows
    scale = 1.0 / HD**0.5
    total = partial_ref[:plane]
    for i in range(1, wide):
        total = total + partial_ref[i * plane : (i + 1) * plane]
    total = total.reshape(pairs, total.shape[-1])
    heads = total.astype(jnp.bfloat16).astype(jnp.float32)

    row_of = lax.broadcasted_iota(jnp.int32, (pairs, 1), 0) % rows
    position = jnp.zeros((pairs, 1), jnp.int32)
    for r in range(rows):
        position = jnp.where(row_of == r, lengths_ref[r], position)
    angles = position.astype(jnp.float32) * frequency_ref[...]
    cosine, sine = jnp.cos(angles), jnp.sin(angles)
    front = lax.broadcasted_iota(jnp.int32, (1, HD), 1) < HD // 2
    sine = jnp.where(front, -sine, sine)

    def rotate(vector):
        return vector * cosine + pltpu.roll(vector, HD // 2, 1) * sine

    query, key_new, value_new = [], [], []
    for h in range(kv_heads):
        turned = jnp.stack(
            [
                rotate(heads[:, (h * group + g) * HD : (h * group + g + 1) * HD])
                for g in range(group)
            ],
            0,
        )
        query.append(jnp.swapaxes(turned, 0, 1))
        at = query_cols + h * HD
        key_new.append(rotate(heads[:, at : at + HD]))
        at = query_cols + kv_cols + h * HD
        value_new.append(heads[:, at : at + HD])

    def row_vector(parts, r):
        return jnp.concatenate(
            [
                parts[h][j * rows + r : j * rows + r + 1]
                for j in range(plane)
                for h in range(kv_heads)
            ],
            1,
        )

    first = lax.broadcasted_iota(jnp.int32, (16, 1), 0) == 0
    slot = lax.broadcasted_iota(jnp.int32, (slots, 1), 0)
    mixed = [[None] * pairs for h in range(kv_heads)]
    for r in range(rows):
        wide_query = []
        for kv in range(all_kv):
            j, h = kv // kv_heads, kv % kv_heads
            parts = [query[h][j * rows + r]]
            if kv:
                parts.insert(0, jnp.zeros((group, kv * HD), jnp.float32))
            if kv < all_kv - 1:
                parts.append(jnp.zeros((group, (all_kv - 1 - kv) * HD), jnp.float32))
            wide_query.append(jnp.concatenate(parts, 1))
        wide_query = jnp.concatenate(wide_query, 0).astype(jnp.bfloat16)
        contract_lanes = (((1,), (1,)), ((), ()))
        contract_rows = (((0,), (0,)), ((), ()))
        own_key = jnp.where(first, row_vector(key_new, r), 0.0).astype(jnp.bfloat16)
        own_value = jnp.where(first, row_vector(value_new, r), 0.0).astype(jnp.bfloat16)
        scores = scale * lax.dot_general(
            keys_ref[r], wide_query, contract_lanes, preferred_element_type=jnp.float32
        )
        own = scale * lax.dot_general(
            own_key, wide_query, contract_lanes, preferred_element_type=jnp.float32
        )
        scores = jnp.where(slot < lengths_ref[r], scores, -1e30)
        own = own[:1]
        top = jnp.maximum(jnp.max(scores, 0, keepdims=True), own)
        weights = jnp.exp(scores - top)
        own_weight = jnp.exp(own - top)
        denominator = jnp.sum(weights, 0, keepdims=True) + own_weight
        probability = (weights / denominator).astype(jnp.bfloat16)
        own_prob = jnp.where(first, own_weight / denominator, 0.0).astype(jnp.bfloat16)
        mix = lax.dot_general(
            probability, values_ref[r], contract_rows, preferred_element_type=jnp.float32
        )
        mix = mix + lax.dot_general(
            own_prob, own_value, contract_rows, preferred_element_type=jnp.float32
        )
        for kv in range(all_kv):
            mixed[kv % kv_heads][kv // kv_heads * rows + r] = mix[
                kv * group : (kv + 1) * group, kv * HD : (kv + 1) * HD
            ]
    attended = []
    for h in range(kv_heads):
        by_head = jnp.swapaxes(jnp.stack(mixed[h], 0), 0, 1)
        attended += [by_head[g] for g in range(group)]
    attended = jnp.concatenate(attended, 1)
    for j in range(plane):
        block = attended[j * rows : (j + 1) * rows].astype(jnp.bfloat16)
        for i in range(wide):
            blocks_ref[i * plane + j] = block


def output_kernel(core_ref, rows_ref, weight_ref, keep_ref, give_ref):
    owners, rows, depth = rows_ref.shape
    attended = rows_ref[...].reshape(owners * rows, depth)
    mine = core_ref[0] == 0
    cols = weight_ref.shape[1]
    step = min(cols, 512)
    for c in range(0, cols, step):
        part = jnp.dot(attended, weight_ref[:, c : c + step], preferred_element_type=jnp.float32)
        part = part.reshape(owners // 2, 2 * rows, step)
        even, odd = part[:, :rows], part[:, rows:]
        keep_ref[:, :, c : c + step] = jnp.where(mine, even, odd)
        give_ref[:, :, c : c + step] = jnp.where(mine, odd, even)


def add_kernel(a_ref, b_ref, sum_ref):
    sum_ref[...] = a_ref[...] + b_ref[...]


def finish_kernel(wide, terms_ref, result_ref):
    chips, _, cols = terms_ref.shape
    count = chips // wide
    for i in range(wide):
        total = terms_ref[i * count]
        for j in range(1, count):
            total = total + terms_ref[i * count + j]
        result_ref[:, i * cols : (i + 1) * cols] = total.astype(result_ref.dtype)


def swap_blocks(blocks, axes):
    return lax.all_to_all(blocks, axes, split_axis=0, concat_axis=0, tiled=True)


def shards(
    tokens,
    norm_gain,
    query_weight,
    key_weight,
    value_weight,
    out_weight,
    cache_keys,
    cache_values,
    lengths,
):
    rows = tokens.shape[0]
    wide = lax.axis_size("gx")
    plane = lax.axis_size(PLANE)
    owners = wide * plane
    width, query_cols = query_weight.shape
    kv_cols = key_weight.shape[1]
    depth, out_cols = out_weight.shape
    cols = query_cols + 2 * kv_cols

    def params(mib):
        return pltpu.CompilerParams(vmem_limit_bytes=mib * MIB)

    def cost(flops, size):
        return pl.CostEstimate(flops=flops, bytes_accessed=size, transcendentals=0)

    normed = pl.pallas_call(
        functools.partial(norm_kernel, wide, plane),
        out_shape=jax.ShapeDtypeStruct((owners, rows, width), jnp.bfloat16),
        in_specs=[IN_VMEM, IN_VMEM],
        out_specs=IN_VMEM,
        compiler_params=params(8),
        cost_estimate=cost(40 * 10**9, MIB),
    )(tokens, norm_gain.reshape(1, -1))
    all_rows = swap_blocks(normed, ROW_AXES)
    partial = pl.pallas_call(
        project_kernel,
        out_shape=jax.ShapeDtypeStruct((owners, rows, cols), jnp.float32),
        in_specs=[IN_VMEM] * 4,
        out_specs=IN_VMEM,
        compiler_params=params(8),
        cost_estimate=cost(2 * owners * rows * width * cols, 2 * width * cols),
    )(all_rows, query_weight, key_weight, value_weight)
    partial = swap_blocks(partial, ROW_AXES)

    half_dim = HD // 2
    frequency = 500000.0 ** (-np.arange(half_dim, dtype=np.float64) / half_dim)
    frequency = np.tile(frequency.astype(np.float32), 2).reshape(1, HD)
    attended = pl.pallas_call(
        functools.partial(attend_kernel, wide, plane, rows, query_cols, kv_cols),
        out_shape=jax.ShapeDtypeStruct((owners, rows, query_cols), jnp.bfloat16),
        in_specs=[IN_SMEM] + [IN_VMEM] * 4,
        out_specs=IN_VMEM,
        compiler_params=params(8),
        cost_estimate=cost(10**9, 4 * MIB),
    )(lengths, partial, jnp.asarray(frequency), cache_keys, cache_values)
    head_rows = swap_blocks(attended, ROW_AXES)
    half = jax.ShapeDtypeStruct((owners // 2, rows, out_cols), jnp.float32)
    keep, give = pl.pallas_call(
        output_kernel,
        out_shape=(half, half),
        in_specs=[IN_SMEM, IN_VMEM, IN_VMEM],
        out_specs=(IN_VMEM, IN_VMEM),
        compiler_params=params(8),
        cost_estimate=cost(2 * owners * rows * depth * out_cols, 2 * depth * out_cols),
    )(lax.axis_index("gz").reshape(1), head_rows, out_weight)
    given = lax.ppermute(give, "gz", [(0, 1), (1, 0)])
    by_core = pl.pallas_call(
        add_kernel, out_shape=half, in_specs=[IN_VMEM, IN_VMEM], out_specs=IN_VMEM
    )(keep, given)
    terms = swap_blocks(by_core, CHIPS)
    return pl.pallas_call(
        functools.partial(finish_kernel, wide),
        out_shape=jax.ShapeDtypeStruct((rows, wide * out_cols), jnp.bfloat16),
        in_specs=[IN_VMEM],
        out_specs=IN_VMEM,
    )(terms)


def solution(mesh):
    placed = (
        P(("groups", "gx", "gy", "gz"), None),
        P(),
        P("gx", ("gy", "gz")),
        P("gx", ("gy", "gz")),
        P("gx", ("gy", "gz")),
        P(("gy", "gz"), "gx"),
        P(("groups", "gx", "gy", "gz"), None, None),
        P(("groups", "gx", "gy", "gz"), None, None),
        P(("groups", "gx", "gy", "gz")),
    )
    return jax.shard_map(
        shards,
        mesh=mesh,
        in_specs=placed,
        out_specs=P(("groups", "gx", "gy", "gz"), None),
        check_vma=False,
    )
```

```python
import functools

import jax
import jax.numpy as jnp
import numpy as np
from jax import lax
from jax.experimental import pallas as pl
from jax.experimental.pallas import tpu as pltpu
from jax.sharding import PartitionSpec as P

HD = 128
ROW_AXES = ("gx", "gy", "gz")
CHIPS = ("gx", "gy")
PLANE = ("gy", "gz")
MIB = 1024 * 1024
IN_VMEM = pl.BlockSpec(memory_space=pltpu.VMEM)
IN_SMEM = pl.BlockSpec(memory_space=pltpu.SMEM)


def norm_kernel(wide, plane, tokens_ref, gain_ref, blocks_ref):
    tokens = tokens_ref[...].astype(jnp.float32)
    mean_square = jnp.mean(tokens * tokens, -1, keepdims=True)
    normed = (tokens * lax.rsqrt(mean_square + 1e-05) * gain_ref[...]).astype(jnp.bfloat16)
    half = normed.shape[1] // wide // 2
    for i in range(wide):
        for j in range(plane):
            at = (2 * i + j % 2) * half
            blocks_ref[i * plane + j] = normed[:, at : at + half]


def project_kernel(own, rows_ref, query_ref, key_ref, value_ref, *refs):
    sums_ref = refs[-1]
    owners, rows, half = rows_ref.shape
    core = lax.axis_index("gz")
    at_row = pl.multiple_of((core if own else 1 - core) * half, half)
    normed = rows_ref[...].reshape(owners * rows, half)
    at = 0
    for weight in (query_ref, key_ref, value_ref):
        cols = weight.shape[1]
        step = min(cols, 256)
        for c in range(0, cols, step):
            part = jnp.dot(
                normed,
                weight[pl.ds(at_row, half), c : c + step],
                preferred_element_type=jnp.float32,
            )
            if own:
                sums_ref[:, at : at + step] = part
            else:
                part = part + refs[0][:, at : at + step]
                sums_ref[:, :, at : at + step] = part.reshape(owners, rows, step)
            at += step


def attend_kernel(
    wide, plane, rows, query_cols, kv_cols,
    lengths_ref, partial_ref, frequency_ref, keys_ref, values_ref, blocks_ref,
):
    slots = keys_ref.shape[1]
    kv_heads = kv_cols // HD
    all_kv = kv_heads * plane
    group = query_cols // kv_cols
    pairs = plane * rows
    scale = 1.0 / HD**0.5
    total = partial_ref[:plane]
    for i in range(1, wide):
        total = total + partial_ref[i * plane : (i + 1) * plane]
    total = total.reshape(pairs, total.shape[-1])
    heads = total.astype(jnp.bfloat16).astype(jnp.float32)

    row_of = lax.broadcasted_iota(jnp.int32, (pairs, 1), 0) % rows
    position = jnp.zeros((pairs, 1), jnp.int32)
    for r in range(rows):
        position = jnp.where(row_of == r, lengths_ref[r], position)
    angles = position.astype(jnp.float32) * frequency_ref[...]
    cosine, sine = jnp.cos(angles), jnp.sin(angles)
    front = lax.broadcasted_iota(jnp.int32, (1, HD), 1) < HD // 2
    sine = jnp.where(front, -sine, sine)

    def rotate(vector):
        return vector * cosine + pltpu.roll(vector, HD // 2, 1) * sine

    query, key_new, value_new = [], [], []
    for h in range(kv_heads):
        turned = jnp.stack(
            [
                rotate(heads[:, (h * group + g) * HD : (h * group + g + 1) * HD])
                for g in range(group)
            ],
            0,
        )
        query.append(jnp.swapaxes(turned, 0, 1))
        at = query_cols + h * HD
        key_new.append(rotate(heads[:, at : at + HD]))
        at = query_cols + kv_cols + h * HD
        value_new.append(heads[:, at : at + HD])

    def row_vector(parts, r):
        return jnp.concatenate(
            [
                parts[h][j * rows + r : j * rows + r + 1]
                for j in range(plane)
                for h in range(kv_heads)
            ],
            1,
        )

    first = lax.broadcasted_iota(jnp.int32, (16, 1), 0) == 0
    slot = lax.broadcasted_iota(jnp.int32, (slots, 1), 0)
    mixed = [[None] * pairs for h in range(kv_heads)]
    for r in range(rows):
        wide_query = []
        for kv in range(all_kv):
            j, h = kv // kv_heads, kv % kv_heads
            parts = [query[h][j * rows + r]]
            if kv:
                parts.insert(0, jnp.zeros((group, kv * HD), jnp.float32))
            if kv < all_kv - 1:
                parts.append(jnp.zeros((group, (all_kv - 1 - kv) * HD), jnp.float32))
            wide_query.append(jnp.concatenate(parts, 1))
        wide_query = jnp.concatenate(wide_query, 0).astype(jnp.bfloat16)
        contract_lanes = (((1,), (1,)), ((), ()))
        contract_rows = (((0,), (0,)), ((), ()))
        own_key = jnp.where(first, row_vector(key_new, r), 0.0).astype(jnp.bfloat16)
        own_value = jnp.where(first, row_vector(value_new, r), 0.0).astype(jnp.bfloat16)
        scores = scale * lax.dot_general(
            keys_ref[r], wide_query, contract_lanes, preferred_element_type=jnp.float32
        )
        own = scale * lax.dot_general(
            own_key, wide_query, contract_lanes, preferred_element_type=jnp.float32
        )
        scores = jnp.where(slot < lengths_ref[r], scores, -1e30)
        own = own[:1]
        top = jnp.maximum(jnp.max(scores, 0, keepdims=True), own)
        weights = jnp.exp(scores - top)
        own_weight = jnp.exp(own - top)
        denominator = jnp.sum(weights, 0, keepdims=True) + own_weight
        probability = (weights / denominator).astype(jnp.bfloat16)
        own_prob = jnp.where(first, own_weight / denominator, 0.0).astype(jnp.bfloat16)
        mix = lax.dot_general(
            probability, values_ref[r], contract_rows, preferred_element_type=jnp.float32
        )
        mix = mix + lax.dot_general(
            own_prob, own_value, contract_rows, preferred_element_type=jnp.float32
        )
        for kv in range(all_kv):
            mixed[kv % kv_heads][kv // kv_heads * rows + r] = mix[
                kv * group : (kv + 1) * group, kv * HD : (kv + 1) * HD
            ]
    attended = []
    for h in range(kv_heads):
        by_head = jnp.swapaxes(jnp.stack(mixed[h], 0), 0, 1)
        attended += [by_head[g] for g in range(group)]
    attended = jnp.concatenate(attended, 1)
    for j in range(plane):
        block = attended[j * rows : (j + 1) * rows].astype(jnp.bfloat16)
        for i in range(wide):
            blocks_ref[i * plane + j] = block


def output_kernel(rows_ref, weight_ref, keep_ref, give_ref):
    owners, rows, depth = rows_ref.shape
    attended = rows_ref[...].reshape(owners * rows, depth)
    mine = lax.axis_index("gz") == 0
    cols = weight_ref.shape[1]
    step = min(cols, 512)
    for c in range(0, cols, step):
        part = jnp.dot(attended, weight_ref[:, c : c + step], preferred_element_type=jnp.float32)
        part = part.reshape(owners // 2, 2 * rows, step)
        even, odd = part[:, :rows], part[:, rows:]
        keep_ref[:, :, c : c + step] = jnp.where(mine, even, odd)
        give_ref[:, :, c : c + step] = jnp.where(mine, odd, even)


def add_kernel(a_ref, b_ref, sum_ref):
    sum_ref[...] = a_ref[...] + b_ref[...]


def finish_kernel(wide, terms_ref, result_ref):
    chips, _, cols = terms_ref.shape
    count = chips // wide
    for i in range(wide):
        total = terms_ref[i * count]
        for j in range(1, count):
            total = total + terms_ref[i * count + j]
        result_ref[:, i * cols : (i + 1) * cols] = total.astype(result_ref.dtype)


def swap_blocks(blocks, axes):
    return lax.all_to_all(blocks, axes, split_axis=0, concat_axis=0, tiled=True)


def swap_cores(value):
    return lax.ppermute(value, "gz", [(0, 1), (1, 0)])


def shards(
    tokens,
    norm_gain,
    query_weight,
    key_weight,
    value_weight,
    out_weight,
    cache_keys,
    cache_values,
    lengths,
):
    rows = tokens.shape[0]
    wide = lax.axis_size("gx")
    plane = lax.axis_size(PLANE)
    owners = wide * plane
    width, query_cols = query_weight.shape
    kv_cols = key_weight.shape[1]
    depth, out_cols = out_weight.shape
    cols = query_cols + 2 * kv_cols

    def params(mib):
        return pltpu.CompilerParams(vmem_limit_bytes=mib * MIB)

    def cost(flops, size):
        return pl.CostEstimate(flops=flops, bytes_accessed=size, transcendentals=0)

    half = width // 2
    normed = pl.pallas_call(
        functools.partial(norm_kernel, wide, plane),
        out_shape=jax.ShapeDtypeStruct((owners, rows, half), jnp.bfloat16),
        in_specs=[IN_VMEM, IN_VMEM],
        out_specs=IN_VMEM,
        compiler_params=params(8),
        cost_estimate=cost(40 * 10**9, MIB),
    )(tokens, norm_gain.reshape(1, -1))
    own_half = swap_blocks(normed, ROW_AXES)
    other_half = swap_cores(own_half)
    weights = (query_weight, key_weight, value_weight)
    half_cost = cost(owners * rows * width * cols, width * cols)
    partial = pl.pallas_call(
        functools.partial(project_kernel, True),
        out_shape=jax.ShapeDtypeStruct((owners * rows, cols), jnp.float32),
        in_specs=[IN_VMEM] * 4,
        out_specs=IN_VMEM,
        compiler_params=params(8),
        cost_estimate=half_cost,
    )(own_half, *weights)
    partial = pl.pallas_call(
        functools.partial(project_kernel, False),
        out_shape=jax.ShapeDtypeStruct((owners, rows, cols), jnp.float32),
        in_specs=[IN_VMEM] * 5,
        out_specs=IN_VMEM,
        compiler_params=params(8),
        cost_estimate=half_cost,
    )(other_half, *weights, partial)
    partial = swap_blocks(partial, ROW_AXES)

    half_dim = HD // 2
    frequency = 500000.0 ** (-np.arange(half_dim, dtype=np.float64) / half_dim)
    frequency = np.tile(frequency.astype(np.float32), 2).reshape(1, HD)
    attended = pl.pallas_call(
        functools.partial(attend_kernel, wide, plane, rows, query_cols, kv_cols),
        out_shape=jax.ShapeDtypeStruct((owners, rows, query_cols), jnp.bfloat16),
        in_specs=[IN_SMEM] + [IN_VMEM] * 4,
        out_specs=IN_VMEM,
        compiler_params=params(8),
        cost_estimate=cost(10**9, 4 * MIB),
    )(lengths, partial, jnp.asarray(frequency), cache_keys, cache_values)
    head_rows = swap_blocks(attended, ROW_AXES)
    by_chip = jax.ShapeDtypeStruct((owners // 2, rows, out_cols), jnp.float32)
    keep, give = pl.pallas_call(
        output_kernel,
        out_shape=(by_chip, by_chip),
        in_specs=[IN_VMEM, IN_VMEM],
        out_specs=(IN_VMEM, IN_VMEM),
        compiler_params=params(8),
        cost_estimate=cost(2 * owners * rows * depth * out_cols, 2 * depth * out_cols),
    )(head_rows, out_weight)
    given = swap_cores(give)
    by_core = pl.pallas_call(
        add_kernel,
        out_shape=by_chip,
        in_specs=[IN_VMEM, IN_VMEM],
        out_specs=IN_VMEM,
        compiler_params=params(8),
    )(keep, given)
    terms = swap_blocks(by_core, CHIPS)
    return pl.pallas_call(
        functools.partial(finish_kernel, wide),
        out_shape=jax.ShapeDtypeStruct((rows, wide * out_cols), jnp.bfloat16),
        in_specs=[IN_VMEM],
        out_specs=IN_VMEM,
        compiler_params=params(8),
    )(terms)


def solution(mesh):
    placed = (
        P(("groups", "gx", "gy", "gz"), None),
        P(),
        P("gx", ("gy", "gz")),
        P("gx", ("gy", "gz")),
        P("gx", ("gy", "gz")),
        P(("gy", "gz"), "gx"),
        P(("groups", "gx", "gy", "gz"), None, None),
        P(("groups", "gx", "gy", "gz"), None, None),
        P(("groups", "gx", "gy", "gz")),
    )
    return jax.shard_map(
        shards,
        mesh=mesh,
        in_specs=placed,
        out_specs=P(("groups", "gx", "gy", "gz"), None),
        check_vma=False,
    )
```

```python
import functools

import jax
import jax.numpy as jnp
import numpy as np
from jax import lax
from jax.experimental import pallas as pl
from jax.experimental.pallas import tpu as pltpu
from jax.sharding import PartitionSpec as P

HD = 128
ROW_AXES = ("gx", "gy", "gz")
PLANE = ("gy", "gz")
MIB = 1024 * 1024
IN_VMEM = pl.BlockSpec(memory_space=pltpu.VMEM)
IN_SMEM = pl.BlockSpec(memory_space=pltpu.SMEM)


def scale_kernel(tokens_ref, scaled_ref):
    tokens = tokens_ref[...].astype(jnp.float32)
    mean_square = jnp.mean(tokens * tokens, -1, keepdims=True)
    scaled_ref[...] = tokens * lax.rsqrt(mean_square + 1e-05)


def gain_kernel(wide, plane, scaled_ref, gain_ref, blocks_ref):
    normed = (scaled_ref[...] * gain_ref[...]).astype(jnp.bfloat16)
    half = normed.shape[1] // wide // 2
    for i in range(wide):
        for j in range(plane):
            at = (2 * i + j % 2) * half
            blocks_ref[i * plane + j] = normed[:, at : at + half]


def project_kernel(own, rows_ref, query_ref, key_ref, value_ref, *refs):
    sums_ref = refs[-1]
    owners, rows, half = rows_ref.shape
    core = lax.axis_index("gz")
    at_row = pl.multiple_of((core if own else 1 - core) * half, half)
    normed = rows_ref[...].reshape(owners * rows, half)
    at = 0
    for weight in (query_ref, key_ref, value_ref):
        cols = weight.shape[1]
        step = min(cols, 256)
        for c in range(0, cols, step):
            part = jnp.dot(
                normed,
                weight[pl.ds(at_row, half), c : c + step],
                preferred_element_type=jnp.float32,
            )
            if own:
                sums_ref[:, at : at + step] = part
            else:
                part = part + refs[0][:, at : at + step]
                sums_ref[:, :, at : at + step] = part.reshape(owners, rows, step)
            at += step


def attend_kernel(
    wide, plane, rows, query_cols, kv_cols,
    lengths_ref, partial_ref, frequency_ref, keys_ref, values_ref, blocks_ref,
):
    slots = keys_ref.shape[1]
    kv_heads = kv_cols // HD
    all_kv = kv_heads * plane
    group = query_cols // kv_cols
    pairs = plane * rows
    scale = 1.0 / HD**0.5
    total = partial_ref[:plane]
    for i in range(1, wide):
        total = total + partial_ref[i * plane : (i + 1) * plane]
    total = total.reshape(pairs, total.shape[-1])
    heads = total.astype(jnp.bfloat16).astype(jnp.float32)

    row_of = lax.broadcasted_iota(jnp.int32, (pairs, 1), 0) % rows
    position = jnp.zeros((pairs, 1), jnp.int32)
    for r in range(rows):
        position = jnp.where(row_of == r, lengths_ref[r], position)
    angles = position.astype(jnp.float32) * frequency_ref[...]
    cosine, sine = jnp.cos(angles), jnp.sin(angles)
    front = lax.broadcasted_iota(jnp.int32, (1, HD), 1) < HD // 2
    sine = jnp.where(front, -sine, sine)

    def rotate(vector):
        return vector * cosine + pltpu.roll(vector, HD // 2, 1) * sine

    query, key_new, value_new = [], [], []
    for h in range(kv_heads):
        turned = jnp.stack(
            [
                rotate(heads[:, (h * group + g) * HD : (h * group + g + 1) * HD])
                for g in range(group)
            ],
            0,
        )
        query.append(jnp.swapaxes(turned, 0, 1))
        at = query_cols + h * HD
        key_new.append(rotate(heads[:, at : at + HD]))
        at = query_cols + kv_cols + h * HD
        value_new.append(heads[:, at : at + HD])

    def row_vector(parts, r):
        return jnp.concatenate(
            [
                parts[h][j * rows + r : j * rows + r + 1]
                for j in range(plane)
                for h in range(kv_heads)
            ],
            1,
        )

    first = lax.broadcasted_iota(jnp.int32, (16, 1), 0) == 0
    slot = lax.broadcasted_iota(jnp.int32, (slots, 1), 0)
    mixed = [[None] * pairs for h in range(kv_heads)]
    for r in range(rows):
        wide_query = []
        for kv in range(all_kv):
            j, h = kv // kv_heads, kv % kv_heads
            parts = [query[h][j * rows + r]]
            if kv:
                parts.insert(0, jnp.zeros((group, kv * HD), jnp.float32))
            if kv < all_kv - 1:
                parts.append(jnp.zeros((group, (all_kv - 1 - kv) * HD), jnp.float32))
            wide_query.append(jnp.concatenate(parts, 1))
        wide_query = jnp.concatenate(wide_query, 0).astype(jnp.bfloat16)
        contract_lanes = (((1,), (1,)), ((), ()))
        contract_rows = (((0,), (0,)), ((), ()))
        own_key = jnp.where(first, row_vector(key_new, r), 0.0).astype(jnp.bfloat16)
        own_value = jnp.where(first, row_vector(value_new, r), 0.0).astype(jnp.bfloat16)
        scores = scale * lax.dot_general(
            keys_ref[r], wide_query, contract_lanes, preferred_element_type=jnp.float32
        )
        own = scale * lax.dot_general(
            own_key, wide_query, contract_lanes, preferred_element_type=jnp.float32
        )
        scores = jnp.where(slot < lengths_ref[r], scores, -1e30)
        own = own[:1]
        top = jnp.maximum(jnp.max(scores, 0, keepdims=True), own)
        weights = jnp.exp(scores - top)
        own_weight = jnp.exp(own - top)
        denominator = jnp.sum(weights, 0, keepdims=True) + own_weight
        probability = (weights / denominator).astype(jnp.bfloat16)
        own_prob = jnp.where(first, own_weight / denominator, 0.0).astype(jnp.bfloat16)
        mix = lax.dot_general(
            probability, values_ref[r], contract_rows, preferred_element_type=jnp.float32
        )
        mix = mix + lax.dot_general(
            own_prob, own_value, contract_rows, preferred_element_type=jnp.float32
        )
        for kv in range(all_kv):
            mixed[kv % kv_heads][kv // kv_heads * rows + r] = mix[
                kv * group : (kv + 1) * group, kv * HD : (kv + 1) * HD
            ]
    attended = []
    for h in range(kv_heads):
        by_head = jnp.swapaxes(jnp.stack(mixed[h], 0), 0, 1)
        attended += [by_head[g] for g in range(group)]
    attended = jnp.concatenate(attended, 1)
    for j in range(plane):
        block = attended[j * rows : (j + 1) * rows].astype(jnp.bfloat16)
        for i in range(wide):
            blocks_ref[i * plane + j] = block


def output_kernel(at, cols, rows_ref, weight_ref, keep_ref, give_ref):
    owners, rows, depth = rows_ref.shape
    attended = rows_ref[...].reshape(owners * rows, depth)
    mine = lax.axis_index("gz") == 0
    step = min(cols, 512)
    for c in range(0, cols, step):
        part = jnp.dot(
            attended, weight_ref[:, at + c : at + c + step], preferred_element_type=jnp.float32
        )
        part = part.reshape(owners // 2, 2 * rows, step)
        even, odd = part[:, :rows], part[:, rows:]
        keep_ref[:, :, c : c + step] = jnp.where(mine, even, odd)
        give_ref[:, :, c : c + step] = jnp.where(mine, odd, even)


def halve_kernel(a_ref, b_ref, keep_ref, give_ref):
    half = a_ref.shape[1] // 2
    mine = lax.axis_index("gy") // half % 2 == 0
    low = a_ref[:, :half] + b_ref[:, :half]
    high = a_ref[:, half:] + b_ref[:, half:]
    keep_ref[...] = jnp.where(mine, low, high)
    give_ref[...] = jnp.where(mine, high, low)


def total_kernel(parts, wide, *refs):
    sums, outs, held = refs[: 2 * parts], refs[2 * parts : -1], refs[-1]
    cols = sums[0].shape[-1]
    for p in range(parts):
        total = sums[2 * p][...] + sums[2 * p + 1][...]
        held[:, :, p * cols : (p + 1) * cols] = total.reshape(
            wide, total.shape[-2], cols
        ).astype(jnp.bfloat16)
    if len(outs) == 1:
        outs[0][...] = held[...]
    else:
        own = lax.axis_index("gx")
        for k in range(wide):
            outs[k][...] = held[own ^ k]


def finish_kernel(*refs):
    blocks, result_ref = refs[:-1], refs[-1]
    own = lax.axis_index("gx")
    cols = blocks[0].shape[-1]
    for k, block in enumerate(blocks):
        at = pl.multiple_of((own ^ k) * cols, cols)
        result_ref[:, pl.ds(at, cols)] = block[...]


def lay_kernel(blocks_ref, result_ref):
    wide, _, cols = blocks_ref.shape
    for i in range(wide):
        result_ref[:, i * cols : (i + 1) * cols] = blocks_ref[i]


def swap_blocks(blocks, axes):
    return lax.all_to_all(blocks, axes, split_axis=0, concat_axis=0, tiled=True)


def swap_pairs(value, axis, step):
    return lax.ppermute(value, axis, [(i, i ^ step) for i in range(lax.axis_size(axis))])


def shards(
    tokens,
    norm_gain,
    query_weight,
    key_weight,
    value_weight,
    out_weight,
    cache_keys,
    cache_values,
    lengths,
):
    rows = tokens.shape[0]
    wide = lax.axis_size("gx")
    plane = lax.axis_size(PLANE)
    owners = wide * plane
    width, query_cols = query_weight.shape
    kv_cols = key_weight.shape[1]
    depth, out_cols = out_weight.shape
    cols = query_cols + 2 * kv_cols

    def params(mib):
        return pltpu.CompilerParams(vmem_limit_bytes=mib * MIB)

    def cost(flops, size):
        return pl.CostEstimate(flops=flops, bytes_accessed=size, transcendentals=0)

    half = width // 2
    scaled = pl.pallas_call(
        scale_kernel,
        out_shape=jax.ShapeDtypeStruct(tokens.shape, jnp.float32),
        in_specs=[IN_VMEM],
        out_specs=IN_VMEM,
        compiler_params=params(8),
        cost_estimate=cost(40 * 10**9, MIB),
    )(tokens)
    normed = pl.pallas_call(
        functools.partial(gain_kernel, wide, plane),
        out_shape=jax.ShapeDtypeStruct((owners, rows, half), jnp.bfloat16),
        in_specs=[IN_VMEM, IN_VMEM],
        out_specs=IN_VMEM,
        compiler_params=params(8),
    )(scaled, norm_gain.reshape(1, -1))
    own_half = swap_blocks(normed, ROW_AXES)
    other_half = swap_pairs(own_half, "gz", 1)
    weights = (query_weight, key_weight, value_weight)
    half_cost = cost(owners * rows * width * cols, width * cols)
    partial = pl.pallas_call(
        functools.partial(project_kernel, True),
        out_shape=jax.ShapeDtypeStruct((owners * rows, cols), jnp.float32),
        in_specs=[IN_VMEM] * 4,
        out_specs=IN_VMEM,
        compiler_params=params(8),
        cost_estimate=half_cost,
    )(own_half, *weights)
    partial = pl.pallas_call(
        functools.partial(project_kernel, False),
        out_shape=jax.ShapeDtypeStruct((owners, rows, cols), jnp.float32),
        in_specs=[IN_VMEM] * 5,
        out_specs=IN_VMEM,
        compiler_params=params(8),
        cost_estimate=half_cost,
    )(other_half, *weights, partial)
    partial = swap_blocks(partial, ROW_AXES)

    half_dim = HD // 2
    frequency = 500000.0 ** (-np.arange(half_dim, dtype=np.float64) / half_dim)
    frequency = np.tile(frequency.astype(np.float32), 2).reshape(1, HD)
    attended = pl.pallas_call(
        functools.partial(attend_kernel, wide, plane, rows, query_cols, kv_cols),
        out_shape=jax.ShapeDtypeStruct((owners, rows, query_cols), jnp.bfloat16),
        in_specs=[IN_SMEM] + [IN_VMEM] * 4,
        out_specs=IN_VMEM,
        compiler_params=params(8),
        cost_estimate=cost(10**9, 4 * MIB),
    )(lengths, partial, jnp.asarray(frequency), cache_keys, cache_values)
    head_rows = swap_blocks(attended, ROW_AXES)
    parts, chips = 2, owners // 2
    part_cols = out_cols // parts
    sums = []
    for p in range(parts):
        shape = jax.ShapeDtypeStruct((chips, rows, part_cols), jnp.float32)
        keep, give = pl.pallas_call(
            functools.partial(output_kernel, p * part_cols, part_cols),
            out_shape=(shape, shape),
            in_specs=[IN_VMEM, IN_VMEM],
            out_specs=(IN_VMEM, IN_VMEM),
            compiler_params=params(8),
            cost_estimate=cost(2 * owners * rows * depth * part_cols, 2 * depth * part_cols),
        )(head_rows, out_weight)
        count = chips // wide
        keep = keep.reshape(wide, count, rows, part_cols)
        give = swap_pairs(give, "gz", 1).reshape(keep.shape)
        while count > 1:
            count //= 2
            shape = jax.ShapeDtypeStruct((wide, count, rows, part_cols), jnp.float32)
            keep, give = pl.pallas_call(
                halve_kernel,
                out_shape=(shape, shape),
                in_specs=[IN_VMEM, IN_VMEM],
                out_specs=(IN_VMEM, IN_VMEM),
                compiler_params=params(8),
            )(keep, give)
            give = swap_pairs(give, "gy", count)
        sums += [keep, give]
    result = jax.ShapeDtypeStruct((rows, wide * out_cols), jnp.bfloat16)
    by_pairs = wide <= 4
    if by_pairs:
        shapes = [jax.ShapeDtypeStruct((rows, out_cols), jnp.bfloat16)] * wide
    else:
        shapes = [jax.ShapeDtypeStruct((wide, rows, out_cols), jnp.bfloat16)]
    blocks = pl.pallas_call(
        functools.partial(total_kernel, parts, wide),
        out_shape=shapes,
        in_specs=[IN_VMEM] * len(sums),
        out_specs=[IN_VMEM] * len(shapes),
        scratch_shapes=[pltpu.VMEM((wide, rows, out_cols), jnp.bfloat16)],
        compiler_params=params(8),
    )(*sums)
    if by_pairs:
        moved = [swap_pairs(blocks[k], "gx", k) for k in range(wide - 1, 0, -1)]
        blocks = [blocks[0]] + moved[::-1]
    else:
        blocks = [swap_blocks(blocks[0], "gx")]
    return pl.pallas_call(
        finish_kernel if by_pairs else lay_kernel,
        out_shape=result,
        in_specs=[IN_VMEM] * len(blocks),
        out_specs=IN_VMEM,
        compiler_params=params(8),
    )(*blocks)


def solution(mesh):
    placed = (
        P(("groups", "gx", "gy", "gz"), None),
        P(),
        P("gx", ("gy", "gz")),
        P("gx", ("gy", "gz")),
        P("gx", ("gy", "gz")),
        P(("gy", "gz"), "gx"),
        P(("groups", "gx", "gy", "gz"), None, None),
        P(("groups", "gx", "gy", "gz"), None, None),
        P(("groups", "gx", "gy", "gz")),
    )
    return jax.shard_map(
        shards,
        mesh=mesh,
        in_specs=placed,
        out_specs=P(("groups", "gx", "gy", "gz"), None),
        check_vma=False,
    )
```

```python
import functools

import jax
import jax.numpy as jnp
import numpy as np
from jax import lax
from jax.experimental import pallas as pl
from jax.experimental.pallas import tpu as pltpu
from jax.sharding import PartitionSpec as P

HD = 128
ROW_AXES = ("gx", "gy", "gz")
PLANE = ("gy", "gz")
MIB = 1024 * 1024
IN_VMEM = pl.BlockSpec(memory_space=pltpu.VMEM)
IN_SMEM = pl.BlockSpec(memory_space=pltpu.SMEM)


def scale_kernel(tokens_ref, scaled_ref):
    tokens = tokens_ref[...].astype(jnp.float32)
    mean_square = jnp.mean(tokens * tokens, -1, keepdims=True)
    scaled_ref[...] = tokens * lax.rsqrt(mean_square + 1e-05)


def gain_kernel(wide, plane, scaled_ref, gain_ref, blocks_ref):
    normed = (scaled_ref[...] * gain_ref[...]).astype(jnp.bfloat16)
    half = normed.shape[1] // wide // 2
    for i in range(wide):
        for j in range(plane):
            at = (2 * i + j % 2) * half
            blocks_ref[i * plane + j] = normed[:, at : at + half]


def project_kernel(own, rows_ref, query_ref, key_ref, value_ref, *refs):
    sums_ref = refs[-1]
    owners, rows, half = rows_ref.shape
    core = lax.axis_index("gz")
    at_row = pl.multiple_of((core if own else 1 - core) * half, half)
    normed = rows_ref[...].reshape(owners * rows, half)
    at = 0
    for weight in (query_ref, key_ref, value_ref):
        cols = weight.shape[1]
        step = min(cols, 256)
        for c in range(0, cols, step):
            part = jnp.dot(
                normed,
                weight[pl.ds(at_row, half), c : c + step],
                preferred_element_type=jnp.float32,
            )
            if own:
                sums_ref[:, at : at + step] = part
            else:
                part = part + refs[0][:, at : at + step]
                sums_ref[:, :, at : at + step] = part.reshape(owners, rows, step)
            at += step


def attend_kernel(
    wide, plane, rows, query_cols, kv_cols,
    lengths_ref, partial_ref, frequency_ref, keys_ref, values_ref, blocks_ref,
):
    slots = keys_ref.shape[1]
    kv_heads = kv_cols // HD
    all_kv = kv_heads * plane
    group = query_cols // kv_cols
    pairs = plane * rows
    scale = 1.0 / HD**0.5
    total = partial_ref[:plane]
    for i in range(1, wide):
        total = total + partial_ref[i * plane : (i + 1) * plane]
    total = total.reshape(pairs, total.shape[-1])
    heads = total.astype(jnp.bfloat16).astype(jnp.float32)

    row_of = lax.broadcasted_iota(jnp.int32, (pairs, 1), 0) % rows
    position = jnp.zeros((pairs, 1), jnp.int32)
    for r in range(rows):
        position = jnp.where(row_of == r, lengths_ref[r], position)
    angles = position.astype(jnp.float32) * frequency_ref[...]
    cosine, sine = jnp.cos(angles), jnp.sin(angles)
    front = lax.broadcasted_iota(jnp.int32, (1, HD), 1) < HD // 2
    sine = jnp.where(front, -sine, sine)

    def rotate(vector):
        return vector * cosine + pltpu.roll(vector, HD // 2, 1) * sine

    query, key_new, value_new = [], [], []
    for h in range(kv_heads):
        turned = jnp.stack(
            [
                rotate(heads[:, (h * group + g) * HD : (h * group + g + 1) * HD])
                for g in range(group)
            ],
            0,
        )
        query.append(jnp.swapaxes(turned, 0, 1))
        at = query_cols + h * HD
        key_new.append(rotate(heads[:, at : at + HD]))
        at = query_cols + kv_cols + h * HD
        value_new.append(heads[:, at : at + HD])

    def row_vector(parts, r):
        return jnp.concatenate(
            [
                parts[h][j * rows + r : j * rows + r + 1]
                for j in range(plane)
                for h in range(kv_heads)
            ],
            1,
        )

    first = lax.broadcasted_iota(jnp.int32, (16, 1), 0) == 0
    slot = lax.broadcasted_iota(jnp.int32, (slots, 1), 0)
    mixed = [[None] * pairs for h in range(kv_heads)]
    for r in range(rows):
        wide_query = []
        for kv in range(all_kv):
            j, h = kv // kv_heads, kv % kv_heads
            parts = [query[h][j * rows + r]]
            if kv:
                parts.insert(0, jnp.zeros((group, kv * HD), jnp.float32))
            if kv < all_kv - 1:
                parts.append(jnp.zeros((group, (all_kv - 1 - kv) * HD), jnp.float32))
            wide_query.append(jnp.concatenate(parts, 1))
        wide_query = jnp.concatenate(wide_query, 0).astype(jnp.bfloat16)
        contract_lanes = (((1,), (1,)), ((), ()))
        contract_rows = (((0,), (0,)), ((), ()))
        own_key = jnp.where(first, row_vector(key_new, r), 0.0).astype(jnp.bfloat16)
        own_value = jnp.where(first, row_vector(value_new, r), 0.0).astype(jnp.bfloat16)
        scores = scale * lax.dot_general(
            keys_ref[r], wide_query, contract_lanes, preferred_element_type=jnp.float32
        )
        own = scale * lax.dot_general(
            own_key, wide_query, contract_lanes, preferred_element_type=jnp.float32
        )
        scores = jnp.where(slot < lengths_ref[r], scores, -1e30)
        own = own[:1]
        top = jnp.maximum(jnp.max(scores, 0, keepdims=True), own)
        weights = jnp.exp(scores - top)
        own_weight = jnp.exp(own - top)
        denominator = jnp.sum(weights, 0, keepdims=True) + own_weight
        probability = (weights / denominator).astype(jnp.bfloat16)
        own_prob = jnp.where(first, own_weight / denominator, 0.0).astype(jnp.bfloat16)
        mix = lax.dot_general(
            probability, values_ref[r], contract_rows, preferred_element_type=jnp.float32
        )
        mix = mix + lax.dot_general(
            own_prob, own_value, contract_rows, preferred_element_type=jnp.float32
        )
        for kv in range(all_kv):
            mixed[kv % kv_heads][kv // kv_heads * rows + r] = mix[
                kv * group : (kv + 1) * group, kv * HD : (kv + 1) * HD
            ]
    attended = []
    for h in range(kv_heads):
        by_head = jnp.swapaxes(jnp.stack(mixed[h], 0), 0, 1)
        attended += [by_head[g] for g in range(group)]
    attended = jnp.concatenate(attended, 1)
    for j in range(plane):
        block = attended[j * rows : (j + 1) * rows].astype(jnp.bfloat16)
        for i in range(wide):
            blocks_ref[i * plane + j] = block


def output_kernel(at, cols, rows_ref, weight_ref, keep_ref, give_ref):
    owners, rows, depth = rows_ref.shape
    attended = rows_ref[...].reshape(owners * rows, depth)
    mine = lax.axis_index("gz") == 0
    step = min(cols, 512)
    for c in range(0, cols, step):
        part = jnp.dot(
            attended, weight_ref[:, at + c : at + c + step], preferred_element_type=jnp.float32
        )
        part = part.reshape(owners // 2, 2 * rows, step)
        even, odd = part[:, :rows], part[:, rows:]
        keep_ref[:, :, c : c + step] = jnp.where(mine, even, odd)
        give_ref[:, :, c : c + step] = jnp.where(mine, odd, even)


def halve_kernel(a_ref, b_ref, keep_ref, give_ref):
    half = a_ref.shape[1] // 2
    mine = lax.axis_index("gy") // half % 2 == 0
    low = a_ref[:, :half] + b_ref[:, :half]
    high = a_ref[:, half:] + b_ref[:, half:]
    keep_ref[...] = jnp.where(mine, low, high)
    give_ref[...] = jnp.where(mine, high, low)


def total_kernel(parts, wide, *refs):
    sums, outs, held = refs[: 2 * parts], refs[2 * parts : -1], refs[-1]
    cols = sums[0].shape[-1]
    for p in range(parts):
        total = sums[2 * p][...] + sums[2 * p + 1][...]
        held[:, :, p * cols : (p + 1) * cols] = total.reshape(
            wide, total.shape[-2], cols
        ).astype(jnp.bfloat16)
    if len(outs) == 1:
        outs[0][...] = held[...]
    else:
        own = lax.axis_index("gx")
        for k in range(wide):
            outs[k][...] = held[own ^ k]


def finish_kernel(*refs):
    blocks, result_ref = refs[-2::-1], refs[-1]
    own = lax.axis_index("gx")
    cols = blocks[0].shape[-1]
    for k, block in enumerate(blocks):
        at = pl.multiple_of((own ^ k) * cols, cols)
        result_ref[:, pl.ds(at, cols)] = block[...]


def lay_kernel(blocks_ref, result_ref):
    wide, _, cols = blocks_ref.shape
    for i in range(wide):
        result_ref[:, i * cols : (i + 1) * cols] = blocks_ref[i]


def swap_blocks(blocks, axes):
    return lax.all_to_all(blocks, axes, split_axis=0, concat_axis=0, tiled=True)


def swap_pairs(value, axis, step):
    return lax.ppermute(value, axis, [(i, i ^ step) for i in range(lax.axis_size(axis))])


def shards(
    tokens,
    norm_gain,
    query_weight,
    key_weight,
    value_weight,
    out_weight,
    cache_keys,
    cache_values,
    lengths,
):
    rows = tokens.shape[0]
    wide = lax.axis_size("gx")
    plane = lax.axis_size(PLANE)
    owners = wide * plane
    width, query_cols = query_weight.shape
    kv_cols = key_weight.shape[1]
    depth, out_cols = out_weight.shape
    cols = query_cols + 2 * kv_cols

    def params(mib):
        return pltpu.CompilerParams(vmem_limit_bytes=mib * MIB)

    def cost(flops, size):
        return pl.CostEstimate(flops=flops, bytes_accessed=size, transcendentals=0)

    half = width // 2
    scaled = pl.pallas_call(
        scale_kernel,
        out_shape=jax.ShapeDtypeStruct(tokens.shape, jnp.float32),
        in_specs=[IN_VMEM],
        out_specs=IN_VMEM,
        compiler_params=params(8),
        cost_estimate=cost(40 * 10**9, MIB),
    )(tokens)
    normed = pl.pallas_call(
        functools.partial(gain_kernel, wide, plane),
        out_shape=jax.ShapeDtypeStruct((owners, rows, half), jnp.bfloat16),
        in_specs=[IN_VMEM, IN_VMEM],
        out_specs=IN_VMEM,
        compiler_params=params(8),
    )(scaled, norm_gain.reshape(1, -1))
    own_half = swap_blocks(normed, ROW_AXES)
    other_half = swap_pairs(own_half, "gz", 1)
    weights = (query_weight, key_weight, value_weight)
    half_cost = cost(owners * rows * width * cols, width * cols)
    partial = pl.pallas_call(
        functools.partial(project_kernel, True),
        out_shape=jax.ShapeDtypeStruct((owners * rows, cols), jnp.float32),
        in_specs=[IN_VMEM] * 4,
        out_specs=IN_VMEM,
        compiler_params=params(8),
        cost_estimate=half_cost,
    )(own_half, *weights)
    partial = pl.pallas_call(
        functools.partial(project_kernel, False),
        out_shape=jax.ShapeDtypeStruct((owners, rows, cols), jnp.float32),
        in_specs=[IN_VMEM] * 5,
        out_specs=IN_VMEM,
        compiler_params=params(8),
        cost_estimate=half_cost,
    )(other_half, *weights, partial)
    partial = swap_blocks(partial, ROW_AXES)

    half_dim = HD // 2
    frequency = 500000.0 ** (-np.arange(half_dim, dtype=np.float64) / half_dim)
    frequency = np.tile(frequency.astype(np.float32), 2).reshape(1, HD)
    attended = pl.pallas_call(
        functools.partial(attend_kernel, wide, plane, rows, query_cols, kv_cols),
        out_shape=jax.ShapeDtypeStruct((owners, rows, query_cols), jnp.bfloat16),
        in_specs=[IN_SMEM] + [IN_VMEM] * 4,
        out_specs=IN_VMEM,
        compiler_params=params(8),
        cost_estimate=cost(10**9, 4 * MIB),
    )(lengths, partial, jnp.asarray(frequency), cache_keys, cache_values)
    head_rows = swap_blocks(attended, ROW_AXES)
    parts, chips = 2, owners // 2
    part_cols = out_cols // parts
    sums = []
    for p in range(parts):
        shape = jax.ShapeDtypeStruct((chips, rows, part_cols), jnp.float32)
        keep, give = pl.pallas_call(
            functools.partial(output_kernel, p * part_cols, part_cols),
            out_shape=(shape, shape),
            in_specs=[IN_VMEM, IN_VMEM],
            out_specs=(IN_VMEM, IN_VMEM),
            compiler_params=params(8),
            cost_estimate=cost(2 * owners * rows * depth * part_cols, 2 * depth * part_cols),
        )(head_rows, out_weight)
        count = chips // wide
        keep = keep.reshape(wide, count, rows, part_cols)
        give = swap_pairs(give, "gz", 1).reshape(keep.shape)
        while count > 1:
            count //= 2
            shape = jax.ShapeDtypeStruct((wide, count, rows, part_cols), jnp.float32)
            keep, give = pl.pallas_call(
                halve_kernel,
                out_shape=(shape, shape),
                in_specs=[IN_VMEM, IN_VMEM],
                out_specs=(IN_VMEM, IN_VMEM),
                compiler_params=params(8),
            )(keep, give)
            give = swap_pairs(give, "gy", count)
        sums += [keep, give]
    result = jax.ShapeDtypeStruct((rows, wide * out_cols), jnp.bfloat16)
    by_pairs = wide <= 4
    if by_pairs:
        shapes = [jax.ShapeDtypeStruct((rows, out_cols), jnp.bfloat16)] * wide
    else:
        shapes = [jax.ShapeDtypeStruct((wide, rows, out_cols), jnp.bfloat16)]
    blocks = pl.pallas_call(
        functools.partial(total_kernel, parts, wide),
        out_shape=shapes,
        in_specs=[IN_VMEM] * len(sums),
        out_specs=[IN_VMEM] * len(shapes),
        scratch_shapes=[pltpu.VMEM((wide, rows, out_cols), jnp.bfloat16)],
        compiler_params=params(8),
    )(*sums)
    if by_pairs:
        blocks = [swap_pairs(blocks[k], "gx", k) for k in range(wide - 1, 0, -1)] + [blocks[0]]
    else:
        blocks = [swap_blocks(blocks[0], "gx")]
    return pl.pallas_call(
        finish_kernel if by_pairs else lay_kernel,
        out_shape=result,
        in_specs=[IN_VMEM] * len(blocks),
        out_specs=IN_VMEM,
        compiler_params=params(8),
    )(*blocks)


def solution(mesh):
    placed = (
        P(("groups", "gx", "gy", "gz"), None),
        P(),
        P("gx", ("gy", "gz")),
        P("gx", ("gy", "gz")),
        P("gx", ("gy", "gz")),
        P(("gy", "gz"), "gx"),
        P(("groups", "gx", "gy", "gz"), None, None),
        P(("groups", "gx", "gy", "gz"), None, None),
        P(("groups", "gx", "gy", "gz")),
    )
    return jax.shard_map(
        shards,
        mesh=mesh,
        in_specs=placed,
        out_specs=P(("groups", "gx", "gy", "gz"), None),
        check_vma=False,
    )
```

```python
import functools

import jax
import jax.numpy as jnp
import numpy as np
from jax import lax
from jax.experimental import pallas as pl
from jax.experimental.pallas import tpu as pltpu
from jax.sharding import PartitionSpec as P

HD = 128
ROW_AXES = ("gx", "gy", "gz")
PLANE = ("gy", "gz")
MIB = 1024 * 1024
IN_VMEM = pl.BlockSpec(memory_space=pltpu.VMEM)
IN_SMEM = pl.BlockSpec(memory_space=pltpu.SMEM)


def scale_kernel(tokens_ref, scaled_ref):
    tokens = tokens_ref[...].astype(jnp.float32)
    mean_square = jnp.mean(tokens * tokens, -1, keepdims=True)
    scaled_ref[...] = tokens * lax.rsqrt(mean_square + 1e-05)


def gain_kernel(wide, plane, scaled_ref, gain_ref, blocks_ref):
    normed = (scaled_ref[...] * gain_ref[...]).astype(jnp.bfloat16)
    half = normed.shape[1] // wide // 2
    for i in range(wide):
        for j in range(plane):
            at = (2 * i + j % 2) * half
            blocks_ref[i * plane + j] = normed[:, at : at + half]


def project_kernel(own, wide, plane, rows_ref, query_ref, key_ref, value_ref, _, *refs):
    owners, rows, half = rows_ref.shape
    core = lax.axis_index("gz")
    at_row = pl.multiple_of((core if own else 1 - core) * half, half)
    normed = rows_ref[...].reshape(owners * rows, half)
    sums_ref = refs[-1]
    at = 0
    for weight in (query_ref, key_ref, value_ref):
        cols = weight.shape[1]
        step = min(cols, 256)
        for c in range(0, cols, step):
            part = jnp.dot(
                normed,
                weight[pl.ds(at_row, half), c : c + step],
                preferred_element_type=jnp.float32,
            )
            if own:
                sums_ref[:, at : at + step] = part
            else:
                part = part + refs[0][:, at : at + step]
                sums_ref[:, :, at : at + step] = part.reshape(owners, rows, step)
            at += step
    if not own:
        own_wide = lax.axis_index("gx")
        own_plane = 2 * lax.axis_index("gy") + core
        for k in range(wide):
            for l in range(plane):
                refs[1 + k][l] = sums_ref[(own_wide ^ k) * plane + (own_plane ^ l)]


def share_kernel(plane, lengths_ref, keys_ref, values_ref, _, *blocks):
    rows, slots, _ = keys_ref.shape
    cols = blocks[0].shape[1]
    own_plane = 2 * lax.axis_index("gy") + lax.axis_index("gz")
    at_row = lax.broadcasted_iota(jnp.int32, (16, cols), 0)
    filled = jnp.zeros((16, cols), jnp.float32)
    for r in range(rows):
        filled = jnp.where(at_row == r, lengths_ref[r].astype(jnp.float32), filled)
    for l in range(plane):
        at = pl.multiple_of((own_plane ^ l) * cols, cols)
        for c, cache in enumerate((keys_ref, values_ref)):
            for r in range(rows):
                to = (c * rows + r) * slots
                blocks[l][to : to + slots] = cache[r, :, pl.ds(at, cols)]
        blocks[l][2 * rows * slots :] = filled.astype(jnp.bfloat16)


def attend_kernel(wide, plane, query_cols, frequency_ref, *refs):
    partials, shared, attended_ref = refs[wide - 1 :: -1], refs[wide:-1], refs[-1]
    rows, cols = partials[0].shape[1:]
    kv_cols = (cols - query_cols) // 2
    kv_heads, group = kv_cols // HD, query_cols // kv_cols
    slots = (shared[0].shape[0] - 16) // (2 * rows)
    pairs = plane * rows
    count = pairs * kv_heads
    heads = count * group
    scale = 1.0 / HD**0.5
    total = partials[0][...]
    for k in range(1, wide):
        total = total + partials[k][...]
    total = total.reshape(pairs, cols).astype(jnp.bfloat16).astype(jnp.float32)

    filled = [
        shared[p // rows][2 * rows * slots : 2 * rows * slots + 16, :HD]
        .astype(jnp.float32)[p % rows : p % rows + 1]
        for p in range(pairs)
    ]
    angles = jnp.concatenate(filled, 0) * frequency_ref[...]
    cosine, sine = jnp.cos(angles), jnp.sin(angles)
    front = lax.broadcasted_iota(jnp.int32, (1, HD), 1) < HD // 2
    sine = jnp.where(front, -sine, sine)

    def rotate(vector):
        return vector * cosine + pltpu.roll(vector, HD // 2, 1) * sine

    query, key_new, value_new = [], [], []
    for h in range(kv_heads):
        turned = [
            rotate(total[:, (h * group + g) * HD : (h * group + g + 1) * HD]) for g in range(group)
        ]
        query.append(jnp.swapaxes(jnp.stack(turned, 0), 0, 1))
        at = query_cols + h * HD
        key_new.append(rotate(total[:, at : at + HD]))
        value_new.append(total[:, at + kv_cols : at + kv_cols + HD])
    query = jnp.stack(query, 1).reshape(heads, HD)
    turned_query = query.T.astype(jnp.bfloat16)
    key_new = jnp.stack(key_new, 1).reshape(count, HD).astype(jnp.bfloat16)
    value_new = jnp.stack(value_new, 1).reshape(count, HD)

    def cached(c):
        return jnp.concatenate(
            [
                shared[p // rows][(c * rows + p % rows) * slots : (c * rows + p % rows + 1) * slots]
                for p in range(pairs)
            ],
            1,
        )

    head_pair = lax.broadcasted_iota(jnp.int32, (1, heads), 1) // group
    by_pair = jnp.concatenate(
        [jnp.where(head_pair == b, turned_query, jnp.zeros_like(turned_query)) for b in range(count)],
        0,
    )
    scores = scale * jnp.dot(cached(0), by_pair, preferred_element_type=jnp.float32)
    own = scale * jnp.dot(key_new, turned_query, preferred_element_type=jnp.float32)
    of_pair = lax.broadcasted_iota(jnp.int32, (count, 1), 0) == head_pair
    own = jnp.sum(jnp.where(of_pair, own, 0.0), 0, keepdims=True)
    length = jnp.zeros((1, heads), jnp.float32)
    for p in range(pairs):
        length = jnp.where(head_pair // kv_heads == p, filled[p][:, :1], length)
    slot = lax.broadcasted_iota(jnp.int32, (slots, 1), 0).astype(jnp.float32)
    scores = jnp.where(slot < length, scores, -1e30)
    top = jnp.maximum(jnp.max(scores, 0, keepdims=True), own)
    weights = jnp.exp(scores - top)
    own_weight = jnp.exp(own - top)
    denominator = jnp.sum(weights, 0, keepdims=True) + own_weight
    probability = (weights / denominator).astype(jnp.bfloat16)
    own_prob = (own_weight / denominator).astype(jnp.bfloat16)
    contract_rows = (((0,), (0,)), ((), ()))
    mixed = lax.dot_general(
        probability, cached(1), contract_rows, preferred_element_type=jnp.float32
    )
    own_prob = jnp.where(of_pair, own_prob.astype(jnp.float32), 0.0).astype(jnp.bfloat16)
    fresh = lax.dot_general(
        own_prob, value_new.astype(jnp.bfloat16), contract_rows, preferred_element_type=jnp.float32
    )
    mixed = [
        mixed[b * group : (b + 1) * group, b * HD : (b + 1) * HD]
        + fresh[b * group : (b + 1) * group]
        for b in range(count)
    ]
    attended = []
    for h in range(kv_heads):
        by_head = jnp.swapaxes(jnp.stack(mixed[h::kv_heads], 0), 0, 1)
        attended += [by_head[g] for g in range(group)]
    attended = jnp.concatenate(attended, 1)
    attended_ref[...] = attended.reshape(plane, rows, query_cols).astype(jnp.bfloat16)


def output_kernel(at, cols, weight_ref, *refs):
    blocks, keep_ref, give_ref = refs[:-2], refs[-2], refs[-1]
    wide = len(blocks)
    plane, rows, depth = blocks[0].shape
    attended = jnp.concatenate(
        [block[...].reshape(plane * rows, depth) for block in blocks], 0
    )
    step = min(cols, 512)
    for c in range(0, cols, step):
        part = jnp.dot(
            attended, weight_ref[:, at + c : at + c + step], preferred_element_type=jnp.float32
        )
        part = part.reshape(wide * plane // 2, 2 * rows, step)
        keep_ref[:, :, c : c + step] = part[:, :rows]
        give_ref[:, :, c : c + step] = part[:, rows:]


def halve_kernel(a_ref, b_ref, keep_ref, give_ref):
    for n in range(keep_ref.shape[0]):
        keep_ref[n] = a_ref[2 * n] + b_ref[2 * n]
        give_ref[n] = a_ref[2 * n + 1] + b_ref[2 * n + 1]


def total_kernel(parts, *refs):
    sums, blocks = refs[: 2 * parts], refs[2 * parts :]
    cols = sums[0].shape[-1]
    for p in range(parts):
        for k, block in enumerate(blocks):
            total = sums[2 * p][k] + sums[2 * p + 1][k]
            block[:, p * cols : (p + 1) * cols] = total.astype(jnp.bfloat16)


def finish_kernel(*refs):
    blocks, result_ref = refs[-2::-1], refs[-1]
    own = lax.axis_index("gx")
    cols = blocks[0].shape[-1]
    for k, block in enumerate(blocks):
        at = pl.multiple_of((own ^ k) * cols, cols)
        result_ref[:, pl.ds(at, cols)] = block[...]


def swap_blocks(blocks, axes):
    return lax.all_to_all(blocks, axes, split_axis=0, concat_axis=0, tiled=True)


def swap_pairs(value, axis, step):
    return lax.ppermute(value, axis, [(i, i ^ step) for i in range(lax.axis_size(axis))])


def swap_plane(value, step):
    return lax.ppermute(value, PLANE, [(i, i ^ step) for i in range(lax.axis_size(PLANE))])


def swap_wide(blocks):
    moved = [swap_pairs(blocks[k], "gx", k) for k in range(len(blocks) - 1, 0, -1)]
    return [blocks[0]] + moved[::-1]


def shards(
    tokens,
    norm_gain,
    query_weight,
    key_weight,
    value_weight,
    out_weight,
    cache_keys,
    cache_values,
    lengths,
):
    rows = tokens.shape[0]
    wide = lax.axis_size("gx")
    plane = lax.axis_size(PLANE)
    owners = wide * plane
    width, query_cols = query_weight.shape
    kv_cols = key_weight.shape[1]
    depth, out_cols = out_weight.shape
    cols = query_cols + 2 * kv_cols

    def params(mib):
        return pltpu.CompilerParams(vmem_limit_bytes=mib * MIB)

    def cost(flops, size):
        return pl.CostEstimate(flops=flops, bytes_accessed=size, transcendentals=0)

    half = width // 2
    scaled = pl.pallas_call(
        scale_kernel,
        out_shape=jax.ShapeDtypeStruct(tokens.shape, jnp.float32),
        in_specs=[IN_VMEM],
        out_specs=IN_VMEM,
        compiler_params=params(8),
        cost_estimate=cost(40 * 10**9, MIB),
    )(tokens)
    normed = pl.pallas_call(
        functools.partial(gain_kernel, wide, plane),
        out_shape=jax.ShapeDtypeStruct((owners, rows, half), jnp.bfloat16),
        in_specs=[IN_VMEM, IN_VMEM],
        out_specs=IN_VMEM,
        compiler_params=params(8),
    )(scaled, norm_gain.reshape(1, -1))
    shared_rows = 2 * rows * cache_keys.shape[1] + 16
    shared = pl.pallas_call(
        functools.partial(share_kernel, plane),
        out_shape=[jax.ShapeDtypeStruct((shared_rows, kv_cols), jnp.bfloat16)] * plane,
        in_specs=[IN_SMEM] + [IN_VMEM] * 3,
        out_specs=[IN_VMEM] * plane,
        compiler_params=params(8),
    )(lengths, cache_keys, cache_values, normed)
    shared = [shared[0]] + [swap_plane(shared[l], l) for l in range(1, plane)]
    own_half = swap_blocks(normed, ROW_AXES)
    other_half = swap_pairs(own_half, "gz", 1)
    weights = (query_weight, key_weight, value_weight)
    half_cost = cost(owners * rows * width * cols, width * cols)
    partial = pl.pallas_call(
        functools.partial(project_kernel, True, wide, plane),
        out_shape=jax.ShapeDtypeStruct((owners * rows, cols), jnp.float32),
        in_specs=[IN_VMEM] * 5,
        out_specs=IN_VMEM,
        compiler_params=params(8),
        cost_estimate=half_cost,
    )(own_half, *weights, shared[1])
    partial = pl.pallas_call(
        functools.partial(project_kernel, False, wide, plane),
        out_shape=[jax.ShapeDtypeStruct((plane, rows, cols), jnp.float32)] * wide,
        in_specs=[IN_VMEM] * 6,
        out_specs=[IN_VMEM] * wide,
        scratch_shapes=[pltpu.VMEM((owners, rows, cols), jnp.float32)],
        compiler_params=params(8),
        cost_estimate=half_cost,
    )(other_half, *weights, shared[1], partial)
    partial = swap_wide(partial)

    half_dim = HD // 2
    frequency = 500000.0 ** (-np.arange(half_dim, dtype=np.float64) / half_dim)
    frequency = np.tile(frequency.astype(np.float32), 2).reshape(1, HD)
    attended = pl.pallas_call(
        functools.partial(attend_kernel, wide, plane, query_cols),
        out_shape=jax.ShapeDtypeStruct((plane, rows, query_cols), jnp.bfloat16),
        in_specs=[IN_VMEM] * (1 + wide + plane),
        out_specs=IN_VMEM,
        compiler_params=params(8),
        cost_estimate=cost(10**9, 4 * MIB),
    )(jnp.asarray(frequency), *partial[::-1], *shared)
    head_rows = swap_wide([attended] * wide)
    parts = 2
    part_cols = out_cols // parts
    sums = []
    for p in range(parts):
        count = owners // 2
        shape = jax.ShapeDtypeStruct((count, rows, part_cols), jnp.float32)
        keep, give = pl.pallas_call(
            functools.partial(output_kernel, p * part_cols, part_cols),
            out_shape=(shape, shape),
            in_specs=[IN_VMEM] * (1 + wide),
            out_specs=(IN_VMEM, IN_VMEM),
            compiler_params=params(8),
            cost_estimate=cost(2 * owners * rows * depth * part_cols, 2 * depth * part_cols),
        )(out_weight, *head_rows)
        give = swap_plane(give, 1)
        step = 2
        while step < plane:
            count //= 2
            shape = jax.ShapeDtypeStruct((count, rows, part_cols), jnp.float32)
            keep, give = pl.pallas_call(
                halve_kernel,
                out_shape=(shape, shape),
                in_specs=[IN_VMEM, IN_VMEM],
                out_specs=(IN_VMEM, IN_VMEM),
                compiler_params=params(8),
            )(keep, give)
            give = swap_plane(give, step)
            step *= 2
        sums += [keep, give]
    blocks = pl.pallas_call(
        functools.partial(total_kernel, parts),
        out_shape=[jax.ShapeDtypeStruct((rows, out_cols), jnp.bfloat16)] * wide,
        in_specs=[IN_VMEM] * len(sums),
        out_specs=[IN_VMEM] * wide,
        compiler_params=params(8),
    )(*sums)
    blocks = swap_wide(blocks)
    return pl.pallas_call(
        finish_kernel,
        out_shape=jax.ShapeDtypeStruct((rows, wide * out_cols), jnp.bfloat16),
        in_specs=[IN_VMEM] * wide,
        out_specs=IN_VMEM,
        compiler_params=params(8),
    )(*blocks[::-1])


def solution(mesh):
    placed = (
        P(("groups", "gx", "gy", "gz"), None),
        P(),
        P("gx", ("gy", "gz")),
        P("gx", ("gy", "gz")),
        P("gx", ("gy", "gz")),
        P(("gy", "gz"), "gx"),
        P(("groups", "gx", "gy", "gz"), None, None),
        P(("groups", "gx", "gy", "gz"), None, None),
        P(("groups", "gx", "gy", "gz")),
    )
    return jax.shard_map(
        shards,
        mesh=mesh,
        in_specs=placed,
        out_specs=P(("groups", "gx", "gy", "gz"), None),
        check_vma=False,
    )
```

```python
import functools

import jax
import jax.numpy as jnp
import numpy as np
from jax import lax
from jax.experimental import pallas as pl
from jax.experimental.pallas import tpu as pltpu
from jax.sharding import PartitionSpec as P

HD = 128
ROW_AXES = ("gx", "gy", "gz")
PLANE = ("gy", "gz")
MIB = 1024 * 1024
IN_VMEM = pl.BlockSpec(memory_space=pltpu.VMEM)
IN_SMEM = pl.BlockSpec(memory_space=pltpu.SMEM)


def scale_kernel(tokens_ref, scaled_ref):
    tokens = tokens_ref[...].astype(jnp.float32)
    mean_square = jnp.mean(tokens * tokens, -1, keepdims=True)
    scaled_ref[...] = tokens * lax.rsqrt(mean_square + 1e-05)


def gain_kernel(wide, plane, scaled_ref, gain_ref, blocks_ref):
    normed = (scaled_ref[...] * gain_ref[...]).astype(jnp.bfloat16)
    half = normed.shape[1] // wide // 2
    for i in range(wide):
        for j in range(plane):
            at = (2 * i + j % 2) * half
            blocks_ref[i * plane + j] = normed[:, at : at + half]


def project_kernel(own, rows_ref, query_ref, key_ref, value_ref, *refs):
    sums_ref = refs[-1]
    owners, rows, half = rows_ref.shape
    core = lax.axis_index("gz")
    at_row = pl.multiple_of((core if own else 1 - core) * half, half)
    normed = rows_ref[...].reshape(owners * rows, half)
    at = 0
    for weight in (query_ref, key_ref, value_ref):
        cols = weight.shape[1]
        step = min(cols, 2048)
        for c in range(0, cols, step):
            part = jnp.dot(
                normed,
                weight[pl.ds(at_row, half), c : c + step],
                preferred_element_type=jnp.float32,
            )
            if own:
                sums_ref[:, at : at + step] = part
            else:
                part = part + refs[0][:, at : at + step]
                sums_ref[:, :, at : at + step] = part.reshape(owners, rows, step)
            at += step


def attend_kernel(
    wide, plane, query_cols, lengths_ref, partial_ref, frequency_ref, keys_ref, values_ref, blocks_ref
):
    rows, slots, _ = keys_ref.shape
    cols = partial_ref.shape[-1]
    kv_cols = (cols - query_cols) // 2
    kv_heads, group = kv_cols // HD, query_cols // kv_cols
    pairs = plane * rows
    count = pairs * kv_heads
    heads = count * group
    scale = 1.0 / HD**0.5
    total = partial_ref[:plane]
    for i in range(1, wide):
        total = total + partial_ref[i * plane : (i + 1) * plane]
    total = total.reshape(pairs, cols).astype(jnp.bfloat16).astype(jnp.float32)

    def by_row(index):
        spread = jnp.zeros(index.shape, jnp.float32)
        for r in range(rows):
            spread = jnp.where(index == r, lengths_ref[r].astype(jnp.float32), spread)
        return spread

    angles = by_row(lax.broadcasted_iota(jnp.int32, (pairs, 1), 0) % rows) * frequency_ref[...]
    cosine, sine = jnp.cos(angles), jnp.sin(angles)
    front = lax.broadcasted_iota(jnp.int32, (1, HD), 1) < HD // 2
    sine = jnp.where(front, -sine, sine)

    def rotate(vector):
        return vector * cosine + pltpu.roll(vector, HD // 2, 1) * sine

    query, key_new, value_new = [], [], []
    for h in range(kv_heads):
        turned = [
            rotate(total[:, (h * group + g) * HD : (h * group + g + 1) * HD]) for g in range(group)
        ]
        query.append(jnp.swapaxes(jnp.stack(turned, 0), 0, 1))
        at = query_cols + h * HD
        key_new.append(rotate(total[:, at : at + HD]))
        value_new.append(total[:, at + kv_cols : at + kv_cols + HD])
    query = jnp.stack(query, 1).reshape(heads, HD)
    turned_query = query.T.astype(jnp.bfloat16)
    key_new = jnp.stack(key_new, 1).reshape(count, HD).astype(jnp.bfloat16)
    value_new = jnp.stack(value_new, 1).reshape(count, HD)

    def cached(cache_ref):
        return jnp.concatenate(
            [
                cache_ref[p % rows, :, p // rows * kv_cols : (p // rows + 1) * kv_cols]
                for p in range(pairs)
            ],
            1,
        )

    head_pair = lax.broadcasted_iota(jnp.int32, (1, heads), 1) // group
    by_pair = jnp.concatenate(
        [jnp.where(head_pair == b, turned_query, jnp.zeros_like(turned_query)) for b in range(count)],
        0,
    )
    scores = scale * jnp.dot(cached(keys_ref), by_pair, preferred_element_type=jnp.float32)
    own = scale * jnp.dot(key_new, turned_query, preferred_element_type=jnp.float32)
    of_pair = lax.broadcasted_iota(jnp.int32, (count, 1), 0) == head_pair
    own = jnp.sum(jnp.where(of_pair, own, 0.0), 0, keepdims=True)
    length = by_row(head_pair // kv_heads % rows)
    slot = lax.broadcasted_iota(jnp.int32, (slots, 1), 0).astype(jnp.float32)
    scores = jnp.where(slot < length, scores, -1e30)
    top = jnp.maximum(jnp.max(scores, 0, keepdims=True), own)
    weights = jnp.exp(scores - top)
    own_weight = jnp.exp(own - top)
    denominator = jnp.sum(weights, 0, keepdims=True) + own_weight
    probability = (weights / denominator).astype(jnp.bfloat16)
    own_prob = (own_weight / denominator).astype(jnp.bfloat16)
    contract_rows = (((0,), (0,)), ((), ()))
    mixed = lax.dot_general(
        probability, cached(values_ref), contract_rows, preferred_element_type=jnp.float32
    )
    own_prob = jnp.where(of_pair, own_prob.astype(jnp.float32), 0.0).astype(jnp.bfloat16)
    fresh = lax.dot_general(
        own_prob, value_new.astype(jnp.bfloat16), contract_rows, preferred_element_type=jnp.float32
    )
    mixed = [
        mixed[b * group : (b + 1) * group, b * HD : (b + 1) * HD]
        + fresh[b * group : (b + 1) * group]
        for b in range(count)
    ]
    attended = []
    for h in range(kv_heads):
        by_head = jnp.swapaxes(jnp.stack(mixed[h::kv_heads], 0), 0, 1)
        attended += [by_head[g] for g in range(group)]
    attended = jnp.concatenate(attended, 1)
    for j in range(plane):
        block = attended[j * rows : (j + 1) * rows].astype(jnp.bfloat16)
        for i in range(wide):
            blocks_ref[i * plane + j] = block


def output_kernel(at, cols, rows_ref, weight_ref, keep_ref, give_ref):
    owners, rows, depth = rows_ref.shape
    attended = rows_ref[...].reshape(owners * rows, depth)
    mine = lax.axis_index("gz") == 0
    step = min(cols, 2048)
    for c in range(0, cols, step):
        part = jnp.dot(
            attended, weight_ref[:, at + c : at + c + step], preferred_element_type=jnp.float32
        )
        part = part.reshape(owners // 2, 2 * rows, step)
        even, odd = part[:, :rows], part[:, rows:]
        keep_ref[:, :, c : c + step] = jnp.where(mine, even, odd)
        give_ref[:, :, c : c + step] = jnp.where(mine, odd, even)


def halve_kernel(a_ref, b_ref, keep_ref, give_ref):
    half = a_ref.shape[1] // 2
    mine = lax.axis_index("gy") // half % 2 == 0
    low = a_ref[:, :half] + b_ref[:, :half]
    high = a_ref[:, half:] + b_ref[:, half:]
    keep_ref[...] = jnp.where(mine, low, high)
    give_ref[...] = jnp.where(mine, high, low)


def total_kernel(parts, wide, *refs):
    sums, outs, held = refs[: 2 * parts], refs[2 * parts : -1], refs[-1]
    cols = sums[0].shape[-1]
    for p in range(parts):
        total = sums[2 * p][...] + sums[2 * p + 1][...]
        held[:, :, p * cols : (p + 1) * cols] = total.reshape(
            wide, total.shape[-2], cols
        ).astype(jnp.bfloat16)
    if len(outs) == 1:
        outs[0][...] = held[...]
    else:
        own = lax.axis_index("gx")
        for k in range(wide):
            outs[k][...] = held[own ^ k]


def finish_kernel(*refs):
    blocks, result_ref = refs[-2::-1], refs[-1]
    own = lax.axis_index("gx")
    cols = blocks[0].shape[-1]
    for k, block in enumerate(blocks):
        at = pl.multiple_of((own ^ k) * cols, cols)
        result_ref[:, pl.ds(at, cols)] = block[...]


def lay_kernel(blocks_ref, result_ref):
    wide, _, cols = blocks_ref.shape
    for i in range(wide):
        result_ref[:, i * cols : (i + 1) * cols] = blocks_ref[i]


def swap_blocks(blocks, axes):
    return lax.all_to_all(blocks, axes, split_axis=0, concat_axis=0, tiled=True)


def swap_pairs(value, axis, step):
    return lax.ppermute(value, axis, [(i, i ^ step) for i in range(lax.axis_size(axis))])


def shards(
    tokens,
    norm_gain,
    query_weight,
    key_weight,
    value_weight,
    out_weight,
    cache_keys,
    cache_values,
    lengths,
):
    rows = tokens.shape[0]
    wide = lax.axis_size("gx")
    plane = lax.axis_size(PLANE)
    owners = wide * plane
    width, query_cols = query_weight.shape
    kv_cols = key_weight.shape[1]
    depth, out_cols = out_weight.shape
    cols = query_cols + 2 * kv_cols

    def params(mib):
        return pltpu.CompilerParams(vmem_limit_bytes=mib * MIB)

    def cost(flops, size):
        return pl.CostEstimate(flops=flops, bytes_accessed=size, transcendentals=0)

    half = width // 2
    scaled = pl.pallas_call(
        scale_kernel,
        out_shape=jax.ShapeDtypeStruct(tokens.shape, jnp.float32),
        in_specs=[IN_VMEM],
        out_specs=IN_VMEM,
        compiler_params=params(8),
        cost_estimate=cost(40 * 10**9, MIB),
    )(tokens)
    normed = pl.pallas_call(
        functools.partial(gain_kernel, wide, plane),
        out_shape=jax.ShapeDtypeStruct((owners, rows, half), jnp.bfloat16),
        in_specs=[IN_VMEM, IN_VMEM],
        out_specs=IN_VMEM,
        compiler_params=params(8),
    )(scaled, norm_gain.reshape(1, -1))
    own_half = swap_blocks(normed, ROW_AXES)
    other_half = swap_pairs(own_half, "gz", 1)
    weights = (query_weight, key_weight, value_weight)
    half_cost = cost(owners * rows * width * cols, width * cols)
    partial = pl.pallas_call(
        functools.partial(project_kernel, True),
        out_shape=jax.ShapeDtypeStruct((owners * rows, cols), jnp.float32),
        in_specs=[IN_VMEM] * 4,
        out_specs=IN_VMEM,
        compiler_params=params(8),
        cost_estimate=half_cost,
    )(own_half, *weights)
    partial = pl.pallas_call(
        functools.partial(project_kernel, False),
        out_shape=jax.ShapeDtypeStruct((owners, rows, cols), jnp.float32),
        in_specs=[IN_VMEM] * 5,
        out_specs=IN_VMEM,
        compiler_params=params(8),
        cost_estimate=half_cost,
    )(other_half, *weights, partial)
    partial = swap_blocks(partial, ROW_AXES)

    half_dim = HD // 2
    frequency = 500000.0 ** (-np.arange(half_dim, dtype=np.float64) / half_dim)
    frequency = np.tile(frequency.astype(np.float32), 2).reshape(1, HD)
    attended = pl.pallas_call(
        functools.partial(attend_kernel, wide, plane, query_cols),
        out_shape=jax.ShapeDtypeStruct((owners, rows, query_cols), jnp.bfloat16),
        in_specs=[IN_SMEM] + [IN_VMEM] * 4,
        out_specs=IN_VMEM,
        compiler_params=params(8),
        cost_estimate=cost(10**9, 4 * MIB),
    )(lengths, partial, jnp.asarray(frequency), cache_keys, cache_values)
    head_rows = swap_blocks(attended, ROW_AXES)
    parts, chips = 2, owners // 2
    part_cols = out_cols // parts
    sums = []
    for p in range(parts):
        shape = jax.ShapeDtypeStruct((chips, rows, part_cols), jnp.float32)
        keep, give = pl.pallas_call(
            functools.partial(output_kernel, p * part_cols, part_cols),
            out_shape=(shape, shape),
            in_specs=[IN_VMEM, IN_VMEM],
            out_specs=(IN_VMEM, IN_VMEM),
            compiler_params=params(8),
            cost_estimate=cost(2 * owners * rows * depth * part_cols, 2 * depth * part_cols),
        )(head_rows, out_weight)
        count = chips // wide
        keep = keep.reshape(wide, count, rows, part_cols)
        give = swap_pairs(give, "gz", 1).reshape(keep.shape)
        while count > 1:
            count //= 2
            shape = jax.ShapeDtypeStruct((wide, count, rows, part_cols), jnp.float32)
            keep, give = pl.pallas_call(
                halve_kernel,
                out_shape=(shape, shape),
                in_specs=[IN_VMEM, IN_VMEM],
                out_specs=(IN_VMEM, IN_VMEM),
                compiler_params=params(8),
            )(keep, give)
            give = swap_pairs(give, "gy", count)
        sums += [keep, give]
    result = jax.ShapeDtypeStruct((rows, wide * out_cols), jnp.bfloat16)
    by_pairs = wide <= 4
    if by_pairs:
        shapes = [jax.ShapeDtypeStruct((rows, out_cols), jnp.bfloat16)] * wide
    else:
        shapes = [jax.ShapeDtypeStruct((wide, rows, out_cols), jnp.bfloat16)]
    blocks = pl.pallas_call(
        functools.partial(total_kernel, parts, wide),
        out_shape=shapes,
        in_specs=[IN_VMEM] * len(sums),
        out_specs=[IN_VMEM] * len(shapes),
        scratch_shapes=[pltpu.VMEM((wide, rows, out_cols), jnp.bfloat16)],
        compiler_params=params(8),
    )(*sums)
    if by_pairs:
        blocks = [swap_pairs(blocks[k], "gx", k) for k in range(wide - 1, 0, -1)] + [blocks[0]]
    else:
        blocks = [swap_blocks(blocks[0], "gx")]
    return pl.pallas_call(
        finish_kernel if by_pairs else lay_kernel,
        out_shape=result,
        in_specs=[IN_VMEM] * len(blocks),
        out_specs=IN_VMEM,
        compiler_params=params(8),
    )(*blocks)


def solution(mesh):
    placed = (
        P(("groups", "gx", "gy", "gz"), None),
        P(),
        P("gx", ("gy", "gz")),
        P("gx", ("gy", "gz")),
        P("gx", ("gy", "gz")),
        P(("gy", "gz"), "gx"),
        P(("groups", "gx", "gy", "gz"), None, None),
        P(("groups", "gx", "gy", "gz"), None, None),
        P(("groups", "gx", "gy", "gz")),
    )
    return jax.shard_map(
        shards,
        mesh=mesh,
        in_specs=placed,
        out_specs=P(("groups", "gx", "gy", "gz"), None),
        check_vma=False,
    )
```

```python
import functools

import jax
import jax.numpy as jnp
import numpy as np
from jax import lax
from jax.experimental import pallas as pl
from jax.experimental.pallas import tpu as pltpu
from jax.sharding import PartitionSpec as P

HD = 128
ROW_AXES = ("gx", "gy", "gz")
PLANE = ("gy", "gz")
MIB = 1024 * 1024
IN_VMEM = pl.BlockSpec(memory_space=pltpu.VMEM)
IN_SMEM = pl.BlockSpec(memory_space=pltpu.SMEM)


def scale_kernel(tokens_ref, scaled_ref):
    tokens = tokens_ref[...].astype(jnp.float32)
    mean_square = jnp.mean(tokens * tokens, -1, keepdims=True)
    scaled_ref[...] = tokens * lax.rsqrt(mean_square + 1e-05)


def gain_kernel(wide, plane, scaled_ref, gain_ref, blocks_ref):
    normed = (scaled_ref[...] * gain_ref[...]).astype(jnp.bfloat16)
    half = normed.shape[1] // wide // 2
    for i in range(wide):
        for j in range(plane):
            at = (2 * i + j % 2) * half
            blocks_ref[i * plane + j] = normed[:, at : at + half]


def project_kernel(own, wide, plane, rows_ref, query_ref, key_ref, value_ref, *refs):
    owners, rows, half = rows_ref.shape
    core = lax.axis_index("gz")
    at_row = pl.multiple_of((core if own else 1 - core) * half, half)
    normed = rows_ref[...].reshape(owners * rows, half)
    sums_ref = refs[-1]
    at = 0
    for weight in (query_ref, key_ref, value_ref):
        cols = weight.shape[1]
        step = min(cols, 256)
        for c in range(0, cols, step):
            part = jnp.dot(
                normed,
                weight[pl.ds(at_row, half), c : c + step],
                preferred_element_type=jnp.float32,
            )
            if own:
                sums_ref[:, at : at + step] = part
            else:
                part = part + refs[1][:, at : at + step]
                sums_ref[:, :, at : at + step] = part.reshape(owners, rows, step)
            at += step
    if not own:
        own_wide = lax.axis_index("gx")
        own_plane = 2 * lax.axis_index("gy") + core
        for k in range(wide):
            for l in range(plane):
                refs[2 + k][l] = sums_ref[(own_wide ^ k) * plane + (own_plane ^ l)]


def own_place():
    return 2 * lax.axis_index("gy") + lax.axis_index("gz")


def write_heads(cache_ref, block_ref, start, owner):
    rows, slots, _ = cache_ref.shape
    cols = block_ref.shape[1]
    at = pl.multiple_of(owner * cols, cols)
    for r in range(rows):
        block_ref[start + r * slots : start + (r + 1) * slots] = cache_ref[r, :, pl.ds(at, cols)]


def write_lengths(rows, lengths_ref, block_ref):
    at_row = lax.broadcasted_iota(jnp.int32, (16, block_ref.shape[1]), 0)
    filled = jnp.zeros(at_row.shape, jnp.float32)
    for r in range(rows):
        filled = jnp.where(at_row == r, lengths_ref[r].astype(jnp.float32), filled)
    block_ref[block_ref.shape[0] - 16 :] = filled.astype(jnp.bfloat16)


def first_kernel(lengths_ref, keys_ref, _, *blocks):
    for s, block in enumerate(blocks):
        write_heads(keys_ref, block, 0, own_place() ^ (2 * s + 2))
        write_lengths(keys_ref.shape[0], lengths_ref, block)


def rest_kernel(even, lengths_ref, keys_ref, values_ref, _, *refs):
    rows, slots, _ = keys_ref.shape
    blocks, count = refs[even:], even
    for s, block in enumerate(blocks[:count]):
        write_heads(values_ref, block, 0, own_place() ^ (2 * s + 2))
    for s, block in enumerate(blocks[count:]):
        write_heads(keys_ref, block, 0, own_place() ^ (2 * s + 1))
        write_heads(values_ref, block, rows * slots, own_place() ^ (2 * s + 1))
        write_lengths(rows, lengths_ref, block)


def attend_kernel(
    wide, plane, query_cols, lengths_ref, keys_ref, values_ref, frequency_ref, *refs
):
    partials, held, attended_ref = refs[wide - 1 :: -1], refs[wide:-1], refs[-1]
    even = plane // 2 - 1
    even_keys, even_values, odd = held[:even], held[even : 2 * even], held[2 * even :]
    rows, slots, _ = keys_ref.shape
    cols = partials[0].shape[-1]
    kv_cols = (cols - query_cols) // 2
    kv_heads, group = kv_cols // HD, query_cols // kv_cols
    pairs = plane * rows
    count = pairs * kv_heads
    heads = count * group
    scale = 1.0 / HD**0.5
    total = partials[0][...]
    for k in range(1, wide):
        total = total + partials[k][...]
    total = total.reshape(pairs, cols).astype(jnp.bfloat16).astype(jnp.float32)
    own_at = pl.multiple_of(own_place() * kv_cols, kv_cols)

    def cached(cache_ref, even_blocks, start):
        parts = []
        for p in range(pairs):
            l, r = p // rows, p % rows
            if l == 0:
                parts.append(cache_ref[r, :, pl.ds(own_at, kv_cols)])
            elif l % 2:
                at = start + r * slots
                parts.append(odd[l // 2][at : at + slots])
            else:
                parts.append(even_blocks[l // 2 - 1][r * slots : (r + 1) * slots])
        return jnp.concatenate(parts, 1)

    filled = [jnp.full((1, HD), lengths_ref[r].astype(jnp.float32)) for r in range(rows)]
    for l in range(1, plane):
        block = odd[l // 2] if l % 2 else even_keys[l // 2 - 1]
        last = block[block.shape[0] - 16 :, :HD].astype(jnp.float32)
        filled += [last[r : r + 1] for r in range(rows)]
    angles = jnp.concatenate(filled, 0) * frequency_ref[...]
    cosine, sine = jnp.cos(angles), jnp.sin(angles)
    front = lax.broadcasted_iota(jnp.int32, (1, HD), 1) < HD // 2
    sine = jnp.where(front, -sine, sine)

    def rotate(vector):
        return vector * cosine + pltpu.roll(vector, HD // 2, 1) * sine

    query, key_new, value_new = [], [], []
    for h in range(kv_heads):
        turned = [
            rotate(total[:, (h * group + g) * HD : (h * group + g + 1) * HD]) for g in range(group)
        ]
        query.append(jnp.swapaxes(jnp.stack(turned, 0), 0, 1))
        at = query_cols + h * HD
        key_new.append(rotate(total[:, at : at + HD]))
        value_new.append(total[:, at + kv_cols : at + kv_cols + HD])
    query = jnp.stack(query, 1).reshape(heads, HD)
    turned_query = query.T.astype(jnp.bfloat16)
    key_new = jnp.stack(key_new, 1).reshape(count, HD).astype(jnp.bfloat16)
    value_new = jnp.stack(value_new, 1).reshape(count, HD)

    head_pair = lax.broadcasted_iota(jnp.int32, (1, heads), 1) // group
    by_pair = jnp.concatenate(
        [jnp.where(head_pair == b, turned_query, jnp.zeros_like(turned_query)) for b in range(count)],
        0,
    )
    scores = scale * jnp.dot(cached(keys_ref, even_keys, 0), by_pair, preferred_element_type=jnp.float32)
    own = scale * jnp.dot(key_new, turned_query, preferred_element_type=jnp.float32)
    of_pair = lax.broadcasted_iota(jnp.int32, (count, 1), 0) == head_pair
    own = jnp.sum(jnp.where(of_pair, own, 0.0), 0, keepdims=True)
    length = jnp.zeros((1, heads), jnp.float32)
    for p in range(pairs):
        length = jnp.where(head_pair // kv_heads == p, filled[p][:, :1], length)
    slot = lax.broadcasted_iota(jnp.int32, (slots, 1), 0).astype(jnp.float32)
    scores = jnp.where(slot < length, scores, -1e30)
    top = jnp.maximum(jnp.max(scores, 0, keepdims=True), own)
    weights = jnp.exp(scores - top)
    own_weight = jnp.exp(own - top)
    denominator = jnp.sum(weights, 0, keepdims=True) + own_weight
    probability = (weights / denominator).astype(jnp.bfloat16)
    own_prob = (own_weight / denominator).astype(jnp.bfloat16)
    contract_rows = (((0,), (0,)), ((), ()))
    mixed = lax.dot_general(
        probability, cached(values_ref, even_values, rows * slots), contract_rows, preferred_element_type=jnp.float32
    )
    own_prob = jnp.where(of_pair, own_prob.astype(jnp.float32), 0.0).astype(jnp.bfloat16)
    fresh = lax.dot_general(
        own_prob, value_new.astype(jnp.bfloat16), contract_rows, preferred_element_type=jnp.float32
    )
    mixed = [
        mixed[b * group : (b + 1) * group, b * HD : (b + 1) * HD]
        + fresh[b * group : (b + 1) * group]
        for b in range(count)
    ]
    attended = []
    for h in range(kv_heads):
        by_head = jnp.swapaxes(jnp.stack(mixed[h::kv_heads], 0), 0, 1)
        attended += [by_head[g] for g in range(group)]
    attended = jnp.concatenate(attended, 1)
    attended_ref[...] = attended.reshape(plane, rows, query_cols).astype(jnp.bfloat16)


def output_kernel(at, cols, weight_ref, *refs):
    blocks, keep_ref, give_ref = refs[-3::-1], refs[-2], refs[-1]
    wide = len(blocks)
    plane, rows, depth = blocks[0].shape
    attended = jnp.concatenate(
        [block[...].reshape(plane * rows, depth) for block in blocks], 0
    )
    step = min(cols, 512)
    for c in range(0, cols, step):
        part = jnp.dot(
            attended, weight_ref[:, at + c : at + c + step], preferred_element_type=jnp.float32
        )
        part = part.reshape(wide * plane // 2, 2 * rows, step)
        keep_ref[:, :, c : c + step] = part[:, :rows]
        give_ref[:, :, c : c + step] = part[:, rows:]


def halve_kernel(a_ref, b_ref, keep_ref, give_ref):
    for n in range(keep_ref.shape[0]):
        keep_ref[n] = a_ref[2 * n] + b_ref[2 * n]
        give_ref[n] = a_ref[2 * n + 1] + b_ref[2 * n + 1]


def total_kernel(parts, *refs):
    sums, blocks = refs[: 2 * parts], refs[2 * parts :]
    cols = sums[0].shape[-1]
    for p in range(parts):
        for k, block in enumerate(blocks):
            total = sums[2 * p][k] + sums[2 * p + 1][k]
            block[:, p * cols : (p + 1) * cols] = total.astype(jnp.bfloat16)


def finish_kernel(*refs):
    blocks, result_ref = refs[-2::-1], refs[-1]
    own = lax.axis_index("gx")
    cols = blocks[0].shape[-1]
    for k, block in enumerate(blocks):
        at = pl.multiple_of((own ^ k) * cols, cols)
        result_ref[:, pl.ds(at, cols)] = block[...]


def swap_blocks(blocks, axes):
    return lax.all_to_all(blocks, axes, split_axis=0, concat_axis=0, tiled=True)


def swap_pairs(value, axis, step):
    return lax.ppermute(value, axis, [(i, i ^ step) for i in range(lax.axis_size(axis))])


def swap_plane(value, step):
    return lax.ppermute(value, PLANE, [(i, i ^ step) for i in range(lax.axis_size(PLANE))])


def swap_wide(blocks):
    moved = [swap_pairs(blocks[k], "gx", k) for k in range(len(blocks) - 1, 0, -1)]
    return [blocks[0]] + moved[::-1]


def shards(
    tokens,
    norm_gain,
    query_weight,
    key_weight,
    value_weight,
    out_weight,
    cache_keys,
    cache_values,
    lengths,
):
    rows = tokens.shape[0]
    wide = lax.axis_size("gx")
    plane = lax.axis_size(PLANE)
    owners = wide * plane
    width, query_cols = query_weight.shape
    kv_cols = key_weight.shape[1]
    depth, out_cols = out_weight.shape
    cols = query_cols + 2 * kv_cols

    def params(mib):
        return pltpu.CompilerParams(vmem_limit_bytes=mib * MIB)

    def cost(flops, size):
        return pl.CostEstimate(flops=flops, bytes_accessed=size, transcendentals=0)

    half = width // 2
    scaled = pl.pallas_call(
        scale_kernel,
        out_shape=jax.ShapeDtypeStruct(tokens.shape, jnp.float32),
        in_specs=[IN_VMEM],
        out_specs=IN_VMEM,
        compiler_params=params(8),
        cost_estimate=cost(40 * 10**9, MIB),
    )(tokens)
    normed = pl.pallas_call(
        functools.partial(gain_kernel, wide, plane),
        out_shape=jax.ShapeDtypeStruct((owners, rows, half), jnp.bfloat16),
        in_specs=[IN_VMEM, IN_VMEM],
        out_specs=IN_VMEM,
        compiler_params=params(8),
    )(scaled, norm_gain.reshape(1, -1))
    block_rows = rows * cache_keys.shape[1]
    even = plane // 2 - 1

    def block_of(count):
        return jax.ShapeDtypeStruct((count, kv_cols), jnp.bfloat16)

    keys = pl.pallas_call(
        first_kernel,
        out_shape=[block_of(block_rows + 16)] * even,
        in_specs=[IN_SMEM] + [IN_VMEM] * 2,
        out_specs=[IN_VMEM] * even,
        compiler_params=params(8),
    )(lengths, cache_keys, normed)
    keys = [swap_plane(keys[s], 2 * s + 2) for s in range(even)]
    own_half = swap_blocks(normed, ROW_AXES)
    other_half = swap_pairs(own_half, "gz", 1)
    rest = pl.pallas_call(
        functools.partial(rest_kernel, even),
        out_shape=[block_of(block_rows)] * even + [block_of(2 * block_rows + 16)] * (even + 1),
        in_specs=[IN_SMEM] + [IN_VMEM] * (3 + even),
        out_specs=[IN_VMEM] * (2 * even + 1),
        compiler_params=params(8),
    )(lengths, cache_keys, cache_values, own_half, *keys)
    values = [swap_plane(rest[s], 2 * s + 2) for s in range(even)]
    odd = [swap_plane(rest[even + s], 2 * s + 1) for s in range(even + 1)]
    held = [*keys, *values, *odd]
    weights = (query_weight, key_weight, value_weight)
    half_cost = cost(owners * rows * width * cols, width * cols)
    partial = pl.pallas_call(
        functools.partial(project_kernel, True, wide, plane),
        out_shape=jax.ShapeDtypeStruct((owners * rows, cols), jnp.float32),
        in_specs=[IN_VMEM] * 4,
        out_specs=IN_VMEM,
        compiler_params=params(8),
        cost_estimate=half_cost,
    )(own_half, *weights)
    partial = pl.pallas_call(
        functools.partial(project_kernel, False, wide, plane),
        out_shape=[jax.ShapeDtypeStruct((plane, rows, cols), jnp.float32)] * wide,
        in_specs=[IN_VMEM] * 6,
        out_specs=[IN_VMEM] * wide,
        scratch_shapes=[pltpu.VMEM((owners, rows, cols), jnp.float32)],
        compiler_params=params(8),
        cost_estimate=half_cost,
    )(other_half, *weights, odd[0], partial)
    partial = swap_wide(partial)

    half_dim = HD // 2
    frequency = 500000.0 ** (-np.arange(half_dim, dtype=np.float64) / half_dim)
    frequency = np.tile(frequency.astype(np.float32), 2).reshape(1, HD)
    attended = pl.pallas_call(
        functools.partial(attend_kernel, wide, plane, query_cols),
        out_shape=jax.ShapeDtypeStruct((plane, rows, query_cols), jnp.bfloat16),
        in_specs=[IN_SMEM] + [IN_VMEM] * (3 + wide + len(held)),
        out_specs=IN_VMEM,
        compiler_params=params(8),
        cost_estimate=cost(10**9, 4 * MIB),
    )(lengths, cache_keys, cache_values, jnp.asarray(frequency), *partial[::-1], *held)
    head_rows = swap_wide([attended] * wide)
    parts = 2
    part_cols = out_cols // parts
    sums = []
    for p in range(parts):
        count = owners // 2
        shape = jax.ShapeDtypeStruct((count, rows, part_cols), jnp.float32)
        keep, give = pl.pallas_call(
            functools.partial(output_kernel, p * part_cols, part_cols),
            out_shape=(shape, shape),
            in_specs=[IN_VMEM] * (1 + wide),
            out_specs=(IN_VMEM, IN_VMEM),
            compiler_params=params(8),
            cost_estimate=cost(2 * owners * rows * depth * part_cols, 2 * depth * part_cols),
        )(out_weight, *head_rows[::-1])
        give = swap_plane(give, 1)
        step = 2
        while step < plane:
            count //= 2
            shape = jax.ShapeDtypeStruct((count, rows, part_cols), jnp.float32)
            keep, give = pl.pallas_call(
                halve_kernel,
                out_shape=(shape, shape),
                in_specs=[IN_VMEM, IN_VMEM],
                out_specs=(IN_VMEM, IN_VMEM),
                compiler_params=params(8),
            )(keep, give)
            give = swap_plane(give, step)
            step *= 2
        sums += [keep, give]
    blocks = pl.pallas_call(
        functools.partial(total_kernel, parts),
        out_shape=[jax.ShapeDtypeStruct((rows, out_cols), jnp.bfloat16)] * wide,
        in_specs=[IN_VMEM] * len(sums),
        out_specs=[IN_VMEM] * wide,
        compiler_params=params(8),
    )(*sums)
    blocks = swap_wide(blocks)
    return pl.pallas_call(
        finish_kernel,
        out_shape=jax.ShapeDtypeStruct((rows, wide * out_cols), jnp.bfloat16),
        in_specs=[IN_VMEM] * wide,
        out_specs=IN_VMEM,
        compiler_params=params(8),
    )(*blocks[::-1])


def solution(mesh):
    placed = (
        P(("groups", "gx", "gy", "gz"), None),
        P(),
        P("gx", ("gy", "gz")),
        P("gx", ("gy", "gz")),
        P("gx", ("gy", "gz")),
        P(("gy", "gz"), "gx"),
        P(("groups", "gx", "gy", "gz"), None, None),
        P(("groups", "gx", "gy", "gz"), None, None),
        P(("groups", "gx", "gy", "gz")),
    )
    return jax.shard_map(
        shards,
        mesh=mesh,
        in_specs=placed,
        out_specs=P(("groups", "gx", "gy", "gz"), None),
        check_vma=False,
    )
```

```python
import functools

import jax
import jax.numpy as jnp
import numpy as np
from jax import lax
from jax.experimental import pallas as pl
from jax.experimental.pallas import tpu as pltpu
from jax.sharding import PartitionSpec as P

HD = 128
ROW_AXES = ("gx", "gy", "gz")
PLANE = ("gy", "gz")
MIB = 1024 * 1024
IN_VMEM = pl.BlockSpec(memory_space=pltpu.VMEM)
IN_SMEM = pl.BlockSpec(memory_space=pltpu.SMEM)


def scale_kernel(tokens_ref, scaled_ref):
    tokens = tokens_ref[...].astype(jnp.float32)
    mean_square = jnp.mean(tokens * tokens, -1, keepdims=True)
    scaled_ref[...] = tokens * lax.rsqrt(mean_square + 1e-05)


def gain_kernel(wide, plane, scaled_ref, gain_ref, blocks_ref):
    normed = (scaled_ref[...] * gain_ref[...]).astype(jnp.bfloat16)
    half = normed.shape[1] // wide // 2
    for i in range(wide):
        for j in range(plane):
            at = (2 * i + j % 2) * half
            blocks_ref[i * plane + j] = normed[:, at : at + half]


def project_kernel(own, wide, plane, rows_ref, query_ref, key_ref, value_ref, *refs):
    owners, rows, half = rows_ref.shape
    core = lax.axis_index("gz")
    at_row = pl.multiple_of((core if own else 1 - core) * half, half)
    normed = rows_ref[...].reshape(owners * rows, half)
    sums_ref = refs[-1]
    at = 0
    for weight in (query_ref, key_ref, value_ref):
        cols = weight.shape[1]
        step = min(cols, 256)
        for c in range(0, cols, step):
            part = jnp.dot(
                normed,
                weight[pl.ds(at_row, half), c : c + step],
                preferred_element_type=jnp.float32,
            )
            if own:
                sums_ref[:, at : at + step] = part
            else:
                part = part + refs[0][:, at : at + step]
                sums_ref[:, :, at : at + step] = part.reshape(owners, rows, step)
            at += step
    if not own:
        own_wide = lax.axis_index("gx")
        own_plane = 2 * lax.axis_index("gy") + core
        for k in range(wide):
            for l in range(plane):
                refs[1 + k][l] = sums_ref[(own_wide ^ k) * plane + (own_plane ^ l)]


def own_place():
    return 2 * lax.axis_index("gy") + lax.axis_index("gz")


def write_heads(cache_ref, block_ref, start, owner):
    rows, slots, _ = cache_ref.shape
    cols = block_ref.shape[1]
    at = pl.multiple_of(owner * cols, cols)
    for r in range(rows):
        block_ref[start + r * slots : start + (r + 1) * slots] = cache_ref[r, :, pl.ds(at, cols)]


def write_lengths(rows, lengths_ref, block_ref):
    at_row = lax.broadcasted_iota(jnp.int32, (16, block_ref.shape[1]), 0)
    filled = jnp.zeros(at_row.shape, jnp.float32)
    for r in range(rows):
        filled = jnp.where(at_row == r, lengths_ref[r].astype(jnp.float32), filled)
    block_ref[block_ref.shape[0] - 16 :] = filled.astype(jnp.bfloat16)


def cut_kernel(side, lengths_ref, keys_ref, values_ref, _, *blocks):
    rows, slots, _ = keys_ref.shape
    for s, block in enumerate(blocks):
        write_heads(keys_ref, block, 0, own_place() ^ (2 * s + side))
        write_heads(values_ref, block, rows * slots, own_place() ^ (2 * s + side))
        write_lengths(rows, lengths_ref, block)


def round_kernel(wide, *refs):
    partials, outs = refs[wide - 1 :: -1], refs[wide:]
    for s, out in enumerate(outs):
        total = partials[0][2 * s : 2 * s + 2]
        for k in range(1, wide):
            total = total + partials[k][2 * s : 2 * s + 2]
        out[...] = total.astype(jnp.bfloat16)


def pair_kernel(*refs):
    for s, block in enumerate(refs[:-1]):
        refs[-1][2 * s : 2 * s + 2] = block[...]


def attend_kernel(
    query_cols, frequency_ref, heads_ref, mine_ref, mate_ref, attended_ref
):
    chip, rows, cols = heads_ref.shape
    kv_cols = (cols - query_cols) // 2
    kv_heads, group = kv_cols // HD, query_cols // kv_cols
    slots = (mine_ref.shape[0] - 16) // (2 * rows)
    pairs = chip * rows
    count = pairs * kv_heads
    heads = count * group
    scale = 1.0 / HD**0.5
    total = heads_ref[...].reshape(pairs, cols).astype(jnp.float32)

    def cached(start):
        return jnp.concatenate(
            [
                ref[start + r * slots : start + (r + 1) * slots]
                for ref in (mine_ref, mate_ref)
                for r in range(rows)
            ],
            1,
        )

    filled = []
    for ref in (mine_ref, mate_ref):
        last = ref[ref.shape[0] - 16 :, :HD].astype(jnp.float32)
        filled += [last[r : r + 1] for r in range(rows)]
    angles = jnp.concatenate(filled, 0) * frequency_ref[...]
    cosine, sine = jnp.cos(angles), jnp.sin(angles)
    front = lax.broadcasted_iota(jnp.int32, (1, HD), 1) < HD // 2
    sine = jnp.where(front, -sine, sine)

    def rotate(vector):
        return vector * cosine + pltpu.roll(vector, HD // 2, 1) * sine

    query, key_new, value_new = [], [], []
    for h in range(kv_heads):
        turned = [
            rotate(total[:, (h * group + g) * HD : (h * group + g + 1) * HD]) for g in range(group)
        ]
        query.append(jnp.swapaxes(jnp.stack(turned, 0), 0, 1))
        at = query_cols + h * HD
        key_new.append(rotate(total[:, at : at + HD]))
        value_new.append(total[:, at + kv_cols : at + kv_cols + HD])
    query = jnp.stack(query, 1).reshape(heads, HD)
    turned_query = query.T.astype(jnp.bfloat16)
    key_new = jnp.stack(key_new, 1).reshape(count, HD).astype(jnp.bfloat16)
    value_new = jnp.stack(value_new, 1).reshape(count, HD)

    head_pair = lax.broadcasted_iota(jnp.int32, (1, heads), 1) // group
    by_pair = jnp.concatenate(
        [jnp.where(head_pair == b, turned_query, jnp.zeros_like(turned_query)) for b in range(count)],
        0,
    )
    scores = scale * jnp.dot(cached(0), by_pair, preferred_element_type=jnp.float32)
    own = scale * jnp.dot(key_new, turned_query, preferred_element_type=jnp.float32)
    of_pair = lax.broadcasted_iota(jnp.int32, (count, 1), 0) == head_pair
    own = jnp.sum(jnp.where(of_pair, own, 0.0), 0, keepdims=True)
    length = jnp.zeros((1, heads), jnp.float32)
    for p in range(pairs):
        length = jnp.where(head_pair // kv_heads == p, filled[p][:, :1], length)
    slot = lax.broadcasted_iota(jnp.int32, (slots, 1), 0).astype(jnp.float32)
    scores = jnp.where(slot < length, scores, -1e30)
    top = jnp.maximum(jnp.max(scores, 0, keepdims=True), own)
    weights = jnp.exp(scores - top)
    own_weight = jnp.exp(own - top)
    denominator = jnp.sum(weights, 0, keepdims=True) + own_weight
    probability = (weights / denominator).astype(jnp.bfloat16)
    own_prob = (own_weight / denominator).astype(jnp.bfloat16)
    contract_rows = (((0,), (0,)), ((), ()))
    mixed = lax.dot_general(
        probability, cached(rows * slots), contract_rows, preferred_element_type=jnp.float32
    )
    own_prob = jnp.where(of_pair, own_prob.astype(jnp.float32), 0.0).astype(jnp.bfloat16)
    fresh = lax.dot_general(
        own_prob, value_new.astype(jnp.bfloat16), contract_rows, preferred_element_type=jnp.float32
    )
    mixed = [
        mixed[b * group : (b + 1) * group, b * HD : (b + 1) * HD]
        + fresh[b * group : (b + 1) * group]
        for b in range(count)
    ]
    attended = []
    for h in range(kv_heads):
        by_head = jnp.swapaxes(jnp.stack(mixed[h::kv_heads], 0), 0, 1)
        attended += [by_head[g] for g in range(group)]
    attended = jnp.concatenate(attended, 1)
    attended_ref[...] = attended.reshape(chip, rows, query_cols).astype(jnp.bfloat16)


def output_kernel(at, cols, weight_ref, *refs):
    blocks, keep_ref, give_ref = refs[:-2], refs[-2], refs[-1]
    wide = len(blocks)
    plane, rows, depth = blocks[0].shape
    attended = jnp.concatenate(
        [block[...].reshape(plane * rows, depth) for block in blocks], 0
    )
    step = min(cols, 512)
    for c in range(0, cols, step):
        part = jnp.dot(
            attended, weight_ref[:, at + c : at + c + step], preferred_element_type=jnp.float32
        )
        part = part.reshape(wide * plane // 2, 2 * rows, step)
        keep_ref[:, :, c : c + step] = part[:, :rows]
        give_ref[:, :, c : c + step] = part[:, rows:]


def halve_kernel(a_ref, b_ref, keep_ref, give_ref):
    for n in range(keep_ref.shape[0]):
        keep_ref[n] = a_ref[2 * n] + b_ref[2 * n]
        give_ref[n] = a_ref[2 * n + 1] + b_ref[2 * n + 1]


def total_kernel(parts, *refs):
    sums, blocks = refs[: 2 * parts], refs[2 * parts :]
    cols = sums[0].shape[-1]
    for p in range(parts):
        for k, block in enumerate(blocks):
            total = sums[2 * p][k] + sums[2 * p + 1][k]
            block[:, p * cols : (p + 1) * cols] = total.astype(jnp.bfloat16)


def finish_kernel(*refs):
    blocks, result_ref = refs[-2::-1], refs[-1]
    own = lax.axis_index("gx")
    cols = blocks[0].shape[-1]
    for k, block in enumerate(blocks):
        at = pl.multiple_of((own ^ k) * cols, cols)
        result_ref[:, pl.ds(at, cols)] = block[...]


def swap_blocks(blocks, axes):
    return lax.all_to_all(blocks, axes, split_axis=0, concat_axis=0, tiled=True)


def swap_pairs(value, axis, step):
    return lax.ppermute(value, axis, [(i, i ^ step) for i in range(lax.axis_size(axis))])


def swap_plane(value, step):
    return lax.ppermute(value, PLANE, [(i, i ^ step) for i in range(lax.axis_size(PLANE))])


def swap_wide(blocks):
    moved = [swap_pairs(blocks[k], "gx", k) for k in range(len(blocks) - 1, 0, -1)]
    return [blocks[0]] + moved[::-1]


def shards(
    tokens,
    norm_gain,
    query_weight,
    key_weight,
    value_weight,
    out_weight,
    cache_keys,
    cache_values,
    lengths,
):
    rows = tokens.shape[0]
    wide = lax.axis_size("gx")
    plane = lax.axis_size(PLANE)
    owners = wide * plane
    width, query_cols = query_weight.shape
    kv_cols = key_weight.shape[1]
    depth, out_cols = out_weight.shape
    cols = query_cols + 2 * kv_cols

    def params(mib):
        return pltpu.CompilerParams(vmem_limit_bytes=mib * MIB)

    def cost(flops, size):
        return pl.CostEstimate(flops=flops, bytes_accessed=size, transcendentals=0)

    half = width // 2
    scaled = pl.pallas_call(
        scale_kernel,
        out_shape=jax.ShapeDtypeStruct(tokens.shape, jnp.float32),
        in_specs=[IN_VMEM],
        out_specs=IN_VMEM,
        compiler_params=params(8),
        cost_estimate=cost(40 * 10**9, MIB),
    )(tokens)
    normed = pl.pallas_call(
        functools.partial(gain_kernel, wide, plane),
        out_shape=jax.ShapeDtypeStruct((owners, rows, half), jnp.bfloat16),
        in_specs=[IN_VMEM, IN_VMEM],
        out_specs=IN_VMEM,
        compiler_params=params(8),
    )(scaled, norm_gain.reshape(1, -1))
    own_half = swap_blocks(normed, ROW_AXES)
    other_half = swap_pairs(own_half, "gz", 1)
    chips = plane // 2
    block = jax.ShapeDtypeStruct(
        (2 * rows * cache_keys.shape[1] + 16, kv_cols), cache_keys.dtype
    )

    def cut(side, after):
        return pl.pallas_call(
            functools.partial(cut_kernel, side),
            out_shape=[block] * chips,
            in_specs=[IN_SMEM] + [IN_VMEM] * 3,
            out_specs=[IN_VMEM] * chips,
            compiler_params=params(8),
        )(lengths, cache_keys, cache_values, after)

    mates = [swap_plane(value, 1) for value in cut(1, normed)]
    mine = cut(0, own_half)
    weights = (query_weight, key_weight, value_weight)
    half_cost = cost(owners * rows * width * cols, width * cols)
    partial = pl.pallas_call(
        functools.partial(project_kernel, True, wide, plane),
        out_shape=jax.ShapeDtypeStruct((owners * rows, cols), jnp.float32),
        in_specs=[IN_VMEM] * 4,
        out_specs=IN_VMEM,
        compiler_params=params(8),
        cost_estimate=half_cost,
    )(own_half, *weights)
    partial = pl.pallas_call(
        functools.partial(project_kernel, False, wide, plane),
        out_shape=[jax.ShapeDtypeStruct((plane, rows, cols), jnp.float32)] * wide,
        in_specs=[IN_VMEM] * 5,
        out_specs=[IN_VMEM] * wide,
        scratch_shapes=[pltpu.VMEM((owners, rows, cols), jnp.float32)],
        compiler_params=params(8),
        cost_estimate=half_cost,
    )(other_half, *weights, partial)
    partial = swap_wide(partial)

    half_dim = HD // 2
    frequency = 500000.0 ** (-np.arange(half_dim, dtype=np.float64) / half_dim)
    frequency = np.tile(frequency.astype(np.float32), 2).reshape(1, HD)
    heads = pl.pallas_call(
        functools.partial(round_kernel, wide),
        out_shape=[jax.ShapeDtypeStruct((2, rows, cols), jnp.bfloat16)] * chips,
        in_specs=[IN_VMEM] * wide,
        out_specs=[IN_VMEM] * chips,
        compiler_params=params(8),
    )(*partial[::-1])
    attended = []
    for s in range(chips):
        chip_rows = pl.pallas_call(
            functools.partial(attend_kernel, query_cols),
            out_shape=jax.ShapeDtypeStruct((2, rows, query_cols), jnp.bfloat16),
            in_specs=[IN_VMEM] * 4,
            out_specs=IN_VMEM,
            compiler_params=params(8),
            cost_estimate=cost(10**9, 2 * MIB),
        )(
            jnp.asarray(frequency),
            swap_plane(heads[s], 2 * s) if s else heads[s],
            mine[s],
            mates[s],
        )
        attended.append(swap_plane(chip_rows, 2 * s) if s else chip_rows)
    attended = pl.pallas_call(
        pair_kernel,
        out_shape=jax.ShapeDtypeStruct((plane, rows, query_cols), jnp.bfloat16),
        in_specs=[IN_VMEM] * chips,
        out_specs=IN_VMEM,
        compiler_params=params(8),
    )(*attended)
    head_rows = swap_wide([attended] * wide)
    parts = 2
    part_cols = out_cols // parts
    sums = []
    for p in range(parts):
        count = owners // 2
        shape = jax.ShapeDtypeStruct((count, rows, part_cols), jnp.float32)
        keep, give = pl.pallas_call(
            functools.partial(output_kernel, p * part_cols, part_cols),
            out_shape=(shape, shape),
            in_specs=[IN_VMEM] * (1 + wide),
            out_specs=(IN_VMEM, IN_VMEM),
            compiler_params=params(8),
            cost_estimate=cost(2 * owners * rows * depth * part_cols, 2 * depth * part_cols),
        )(out_weight, *head_rows)
        give = swap_plane(give, 1)
        step = 2
        while step < plane:
            count //= 2
            shape = jax.ShapeDtypeStruct((count, rows, part_cols), jnp.float32)
            keep, give = pl.pallas_call(
                halve_kernel,
                out_shape=(shape, shape),
                in_specs=[IN_VMEM, IN_VMEM],
                out_specs=(IN_VMEM, IN_VMEM),
                compiler_params=params(8),
            )(keep, give)
            give = swap_plane(give, step)
            step *= 2
        sums += [keep, give]
    blocks = pl.pallas_call(
        functools.partial(total_kernel, parts),
        out_shape=[jax.ShapeDtypeStruct((rows, out_cols), jnp.bfloat16)] * wide,
        in_specs=[IN_VMEM] * len(sums),
        out_specs=[IN_VMEM] * wide,
        compiler_params=params(8),
    )(*sums)
    blocks = swap_wide(blocks)
    return pl.pallas_call(
        finish_kernel,
        out_shape=jax.ShapeDtypeStruct((rows, wide * out_cols), jnp.bfloat16),
        in_specs=[IN_VMEM] * wide,
        out_specs=IN_VMEM,
        compiler_params=params(8),
    )(*blocks[::-1])


def solution(mesh):
    placed = (
        P(("groups", "gx", "gy", "gz"), None),
        P(),
        P("gx", ("gy", "gz")),
        P("gx", ("gy", "gz")),
        P("gx", ("gy", "gz")),
        P(("gy", "gz"), "gx"),
        P(("groups", "gx", "gy", "gz"), None, None),
        P(("groups", "gx", "gy", "gz"), None, None),
        P(("groups", "gx", "gy", "gz")),
    )
    return jax.shard_map(
        shards,
        mesh=mesh,
        in_specs=placed,
        out_specs=P(("groups", "gx", "gy", "gz"), None),
        check_vma=False,
    )
```

```python
import functools

import jax
import jax.numpy as jnp
import numpy as np
from jax import lax
from jax.experimental import pallas as pl
from jax.experimental.pallas import tpu as pltpu
from jax.sharding import PartitionSpec as P

HD = 128
ROW_AXES = ("gx", "gy", "gz")
PLANE = ("gy", "gz")
MIB = 1024 * 1024
IN_VMEM = pl.BlockSpec(memory_space=pltpu.VMEM)
IN_SMEM = pl.BlockSpec(memory_space=pltpu.SMEM)


def scale_kernel(tokens_ref, scaled_ref):
    tokens = tokens_ref[...].astype(jnp.float32)
    mean_square = jnp.mean(tokens * tokens, -1, keepdims=True)
    scaled_ref[...] = tokens * lax.rsqrt(mean_square + 1e-05)


def gain_kernel(wide, plane, scaled_ref, gain_ref, blocks_ref):
    normed = (scaled_ref[...] * gain_ref[...]).astype(jnp.bfloat16)
    half = normed.shape[1] // wide // 2
    for i in range(wide):
        for j in range(plane):
            at = (2 * i + j % 2) * half
            blocks_ref[i * plane + j] = normed[:, at : at + half]


def project_kernel(own, wide, plane, rows_ref, query_ref, key_ref, value_ref, *refs):
    owners, rows, half = rows_ref.shape
    core = lax.axis_index("gz")
    at_row = pl.multiple_of((core if own else 1 - core) * half, half)
    normed = rows_ref[...].reshape(owners * rows, half)
    sums_ref = refs[-1]
    at = 0
    for weight in (query_ref, key_ref, value_ref):
        cols = weight.shape[1]
        step = min(cols, 256)
        for c in range(0, cols, step):
            part = jnp.dot(
                normed,
                weight[pl.ds(at_row, half), c : c + step],
                preferred_element_type=jnp.float32,
            )
            if own:
                sums_ref[:, at : at + step] = part
            else:
                part = part + refs[0][:, at : at + step]
                sums_ref[:, :, at : at + step] = part.reshape(owners, rows, step)
            at += step
    if not own:
        own_wide = lax.axis_index("gx")
        own_plane = 2 * lax.axis_index("gy") + core
        for k in range(wide):
            for l in range(plane):
                refs[1 + k][l] = sums_ref[(own_wide ^ k) * plane + (own_plane ^ l)]


def own_place():
    return 2 * lax.axis_index("gy") + lax.axis_index("gz")


def write_heads(cache_ref, block_ref, start, owner):
    rows, slots, _ = cache_ref.shape
    cols = block_ref.shape[1]
    at = pl.multiple_of(owner * cols, cols)
    for r in range(rows):
        block_ref[start + r * slots : start + (r + 1) * slots] = cache_ref[r, :, pl.ds(at, cols)]


def write_lengths(rows, lengths_ref, block_ref, end):
    at_row = lax.broadcasted_iota(jnp.int32, (16, block_ref.shape[1]), 0)
    filled = jnp.zeros(at_row.shape, jnp.float32)
    for r in range(rows):
        filled = jnp.where(at_row == r, lengths_ref[r].astype(jnp.float32), filled)
    block_ref[end - 16 : end] = filled.astype(jnp.bfloat16)


def cut_kernel(side, lengths_ref, keys_ref, values_ref, _, block_ref):
    rows, slots, _ = keys_ref.shape
    size = 2 * rows * slots + 16
    for s in range(block_ref.shape[0] // size):
        write_heads(keys_ref, block_ref, s * size, own_place() ^ (2 * s + side))
        write_heads(values_ref, block_ref, s * size + rows * slots, own_place() ^ (2 * s + side))
        write_lengths(rows, lengths_ref, block_ref, (s + 1) * size)


def round_kernel(wide, *refs):
    partials, outs = refs[wide - 1 :: -1], refs[wide:]
    for s, out in enumerate(outs):
        total = partials[0][2 * s : 2 * s + 2]
        for k in range(1, wide):
            total = total + partials[k][2 * s : 2 * s + 2]
        out[...] = total.astype(jnp.bfloat16)


def pair_kernel(*refs):
    for s, block in enumerate(refs[:-1]):
        refs[-1][2 * s : 2 * s + 2] = block[...]


def attend_kernel(
    query_cols, block, size, frequency_ref, heads_ref, mine_ref, mate_ref, attended_ref
):
    chip, rows, cols = heads_ref.shape
    kv_cols = (cols - query_cols) // 2
    kv_heads, group = kv_cols // HD, query_cols // kv_cols
    slots = (size - 16) // (2 * rows)
    pairs = chip * rows
    count = pairs * kv_heads
    heads = count * group
    scale = 1.0 / HD**0.5
    total = heads_ref[...].reshape(pairs, cols).astype(jnp.float32)

    def cached(start):
        at = block * size + start
        return jnp.concatenate(
            [
                ref[at + r * slots : at + (r + 1) * slots]
                for ref in (mine_ref, mate_ref)
                for r in range(rows)
            ],
            1,
        )

    filled = []
    for ref in (mine_ref, mate_ref):
        last = ref[(block + 1) * size - 16 : (block + 1) * size, :HD].astype(jnp.float32)
        filled += [last[r : r + 1] for r in range(rows)]
    angles = jnp.concatenate(filled, 0) * frequency_ref[...]
    cosine, sine = jnp.cos(angles), jnp.sin(angles)
    front = lax.broadcasted_iota(jnp.int32, (1, HD), 1) < HD // 2
    sine = jnp.where(front, -sine, sine)

    def rotate(vector):
        return vector * cosine + pltpu.roll(vector, HD // 2, 1) * sine

    query, key_new, value_new = [], [], []
    for h in range(kv_heads):
        turned = [
            rotate(total[:, (h * group + g) * HD : (h * group + g + 1) * HD]) for g in range(group)
        ]
        query.append(jnp.swapaxes(jnp.stack(turned, 0), 0, 1))
        at = query_cols + h * HD
        key_new.append(rotate(total[:, at : at + HD]))
        value_new.append(total[:, at + kv_cols : at + kv_cols + HD])
    query = jnp.stack(query, 1).reshape(heads, HD)
    turned_query = query.T.astype(jnp.bfloat16)
    key_new = jnp.stack(key_new, 1).reshape(count, HD).astype(jnp.bfloat16)
    value_new = jnp.stack(value_new, 1).reshape(count, HD)

    head_pair = lax.broadcasted_iota(jnp.int32, (1, heads), 1) // group
    by_pair = jnp.concatenate(
        [jnp.where(head_pair == b, turned_query, jnp.zeros_like(turned_query)) for b in range(count)],
        0,
    )
    scores = scale * jnp.dot(cached(0), by_pair, preferred_element_type=jnp.float32)
    own = scale * jnp.dot(key_new, turned_query, preferred_element_type=jnp.float32)
    of_pair = lax.broadcasted_iota(jnp.int32, (count, 1), 0) == head_pair
    own = jnp.sum(jnp.where(of_pair, own, 0.0), 0, keepdims=True)
    length = jnp.zeros((1, heads), jnp.float32)
    for p in range(pairs):
        length = jnp.where(head_pair // kv_heads == p, filled[p][:, :1], length)
    slot = lax.broadcasted_iota(jnp.int32, (slots, 1), 0).astype(jnp.float32)
    scores = jnp.where(slot < length, scores, -1e30)
    top = jnp.maximum(jnp.max(scores, 0, keepdims=True), own)
    weights = jnp.exp(scores - top)
    own_weight = jnp.exp(own - top)
    denominator = jnp.sum(weights, 0, keepdims=True) + own_weight
    probability = (weights / denominator).astype(jnp.bfloat16)
    own_prob = (own_weight / denominator).astype(jnp.bfloat16)
    contract_rows = (((0,), (0,)), ((), ()))
    mixed = lax.dot_general(
        probability, cached(rows * slots), contract_rows, preferred_element_type=jnp.float32
    )
    own_prob = jnp.where(of_pair, own_prob.astype(jnp.float32), 0.0).astype(jnp.bfloat16)
    fresh = lax.dot_general(
        own_prob, value_new.astype(jnp.bfloat16), contract_rows, preferred_element_type=jnp.float32
    )
    mixed = [
        mixed[b * group : (b + 1) * group, b * HD : (b + 1) * HD]
        + fresh[b * group : (b + 1) * group]
        for b in range(count)
    ]
    attended = []
    for h in range(kv_heads):
        by_head = jnp.swapaxes(jnp.stack(mixed[h::kv_heads], 0), 0, 1)
        attended += [by_head[g] for g in range(group)]
    attended = jnp.concatenate(attended, 1)
    attended_ref[...] = attended.reshape(chip, rows, query_cols).astype(jnp.bfloat16)


def output_kernel(at, cols, weight_ref, *refs):
    blocks, keep_ref, give_ref = refs[:-2], refs[-2], refs[-1]
    wide = len(blocks)
    plane, rows, depth = blocks[0].shape
    attended = jnp.concatenate(
        [block[...].reshape(plane * rows, depth) for block in blocks], 0
    )
    step = min(cols, 512)
    for c in range(0, cols, step):
        part = jnp.dot(
            attended, weight_ref[:, at + c : at + c + step], preferred_element_type=jnp.float32
        )
        part = part.reshape(wide * plane // 2, 2 * rows, step)
        keep_ref[:, :, c : c + step] = part[:, :rows]
        give_ref[:, :, c : c + step] = part[:, rows:]


def halve_kernel(a_ref, b_ref, keep_ref, give_ref):
    for n in range(keep_ref.shape[0]):
        keep_ref[n] = a_ref[2 * n] + b_ref[2 * n]
        give_ref[n] = a_ref[2 * n + 1] + b_ref[2 * n + 1]


def total_kernel(parts, *refs):
    sums, blocks = refs[: 2 * parts], refs[2 * parts :]
    cols = sums[0].shape[-1]
    for p in range(parts):
        for k, block in enumerate(blocks):
            total = sums[2 * p][k] + sums[2 * p + 1][k]
            block[:, p * cols : (p + 1) * cols] = total.astype(jnp.bfloat16)


def finish_kernel(*refs):
    blocks, result_ref = refs[-2::-1], refs[-1]
    own = lax.axis_index("gx")
    cols = blocks[0].shape[-1]
    for k, block in enumerate(blocks):
        at = pl.multiple_of((own ^ k) * cols, cols)
        result_ref[:, pl.ds(at, cols)] = block[...]


def swap_blocks(blocks, axes):
    return lax.all_to_all(blocks, axes, split_axis=0, concat_axis=0, tiled=True)


def swap_pairs(value, axis, step):
    return lax.ppermute(value, axis, [(i, i ^ step) for i in range(lax.axis_size(axis))])


def swap_plane(value, step):
    return lax.ppermute(value, PLANE, [(i, i ^ step) for i in range(lax.axis_size(PLANE))])


def swap_wide(blocks):
    moved = [swap_pairs(blocks[k], "gx", k) for k in range(len(blocks) - 1, 0, -1)]
    return [blocks[0]] + moved[::-1]


def shards(
    tokens,
    norm_gain,
    query_weight,
    key_weight,
    value_weight,
    out_weight,
    cache_keys,
    cache_values,
    lengths,
):
    rows = tokens.shape[0]
    wide = lax.axis_size("gx")
    plane = lax.axis_size(PLANE)
    owners = wide * plane
    width, query_cols = query_weight.shape
    kv_cols = key_weight.shape[1]
    depth, out_cols = out_weight.shape
    cols = query_cols + 2 * kv_cols

    def params(mib):
        return pltpu.CompilerParams(vmem_limit_bytes=mib * MIB)

    def cost(flops, size):
        return pl.CostEstimate(flops=flops, bytes_accessed=size, transcendentals=0)

    half = width // 2
    scaled = pl.pallas_call(
        scale_kernel,
        out_shape=jax.ShapeDtypeStruct(tokens.shape, jnp.float32),
        in_specs=[IN_VMEM],
        out_specs=IN_VMEM,
        compiler_params=params(8),
        cost_estimate=cost(40 * 10**9, MIB),
    )(tokens)
    normed = pl.pallas_call(
        functools.partial(gain_kernel, wide, plane),
        out_shape=jax.ShapeDtypeStruct((owners, rows, half), jnp.bfloat16),
        in_specs=[IN_VMEM, IN_VMEM],
        out_specs=IN_VMEM,
        compiler_params=params(8),
    )(scaled, norm_gain.reshape(1, -1))
    own_half = swap_blocks(normed, ROW_AXES)
    other_half = swap_pairs(own_half, "gz", 1)
    chips = plane // 2
    size = 2 * rows * cache_keys.shape[1] + 16

    def cut(side, after):
        return pl.pallas_call(
            functools.partial(cut_kernel, side),
            out_shape=jax.ShapeDtypeStruct((chips * size, kv_cols), cache_keys.dtype),
            in_specs=[IN_SMEM] + [IN_VMEM] * 3,
            out_specs=IN_VMEM,
            compiler_params=params(8),
        )(lengths, cache_keys, cache_values, after)

    mates = swap_plane(cut(1, normed), 1)
    mine = cut(0, own_half)
    weights = (query_weight, key_weight, value_weight)
    half_cost = cost(owners * rows * width * cols, width * cols)
    partial = pl.pallas_call(
        functools.partial(project_kernel, True, wide, plane),
        out_shape=jax.ShapeDtypeStruct((owners * rows, cols), jnp.float32),
        in_specs=[IN_VMEM] * 4,
        out_specs=IN_VMEM,
        compiler_params=params(8),
        cost_estimate=half_cost,
    )(own_half, *weights)
    partial = pl.pallas_call(
        functools.partial(project_kernel, False, wide, plane),
        out_shape=[jax.ShapeDtypeStruct((plane, rows, cols), jnp.float32)] * wide,
        in_specs=[IN_VMEM] * 5,
        out_specs=[IN_VMEM] * wide,
        scratch_shapes=[pltpu.VMEM((owners, rows, cols), jnp.float32)],
        compiler_params=params(8),
        cost_estimate=half_cost,
    )(other_half, *weights, partial)
    partial = swap_wide(partial)

    half_dim = HD // 2
    frequency = 500000.0 ** (-np.arange(half_dim, dtype=np.float64) / half_dim)
    frequency = np.tile(frequency.astype(np.float32), 2).reshape(1, HD)
    heads = pl.pallas_call(
        functools.partial(round_kernel, wide),
        out_shape=[jax.ShapeDtypeStruct((2, rows, cols), jnp.bfloat16)] * chips,
        in_specs=[IN_VMEM] * wide,
        out_specs=[IN_VMEM] * chips,
        compiler_params=params(8),
    )(*partial[::-1])
    attended = []
    for s in range(chips):
        chip_rows = pl.pallas_call(
            functools.partial(attend_kernel, query_cols, s, size),
            out_shape=jax.ShapeDtypeStruct((2, rows, query_cols), jnp.bfloat16),
            in_specs=[IN_VMEM] * 4,
            out_specs=IN_VMEM,
            compiler_params=params(8),
            cost_estimate=cost(10**9, 2 * MIB),
        )(
            jnp.asarray(frequency),
            swap_plane(heads[s], 2 * s) if s else heads[s],
            mine,
            mates,
        )
        attended.append(swap_plane(chip_rows, 2 * s) if s else chip_rows)
    attended = pl.pallas_call(
        pair_kernel,
        out_shape=jax.ShapeDtypeStruct((plane, rows, query_cols), jnp.bfloat16),
        in_specs=[IN_VMEM] * chips,
        out_specs=IN_VMEM,
        compiler_params=params(8),
    )(*attended)
    head_rows = swap_wide([attended] * wide)
    parts = 2
    part_cols = out_cols // parts
    sums = []
    for p in range(parts):
        count = owners // 2
        shape = jax.ShapeDtypeStruct((count, rows, part_cols), jnp.float32)
        keep, give = pl.pallas_call(
            functools.partial(output_kernel, p * part_cols, part_cols),
            out_shape=(shape, shape),
            in_specs=[IN_VMEM] * (1 + wide),
            out_specs=(IN_VMEM, IN_VMEM),
            compiler_params=params(8),
            cost_estimate=cost(2 * owners * rows * depth * part_cols, 2 * depth * part_cols),
        )(out_weight, *head_rows)
        give = swap_plane(give, 1)
        step = 2
        while step < plane:
            count //= 2
            shape = jax.ShapeDtypeStruct((count, rows, part_cols), jnp.float32)
            keep, give = pl.pallas_call(
                halve_kernel,
                out_shape=(shape, shape),
                in_specs=[IN_VMEM, IN_VMEM],
                out_specs=(IN_VMEM, IN_VMEM),
                compiler_params=params(8),
            )(keep, give)
            give = swap_plane(give, step)
            step *= 2
        sums += [keep, give]
    blocks = pl.pallas_call(
        functools.partial(total_kernel, parts),
        out_shape=[jax.ShapeDtypeStruct((rows, out_cols), jnp.bfloat16)] * wide,
        in_specs=[IN_VMEM] * len(sums),
        out_specs=[IN_VMEM] * wide,
        compiler_params=params(8),
    )(*sums)
    blocks = swap_wide(blocks)
    return pl.pallas_call(
        finish_kernel,
        out_shape=jax.ShapeDtypeStruct((rows, wide * out_cols), jnp.bfloat16),
        in_specs=[IN_VMEM] * wide,
        out_specs=IN_VMEM,
        compiler_params=params(8),
    )(*blocks[::-1])


def solution(mesh):
    placed = (
        P(("groups", "gx", "gy", "gz"), None),
        P(),
        P("gx", ("gy", "gz")),
        P("gx", ("gy", "gz")),
        P("gx", ("gy", "gz")),
        P(("gy", "gz"), "gx"),
        P(("groups", "gx", "gy", "gz"), None, None),
        P(("groups", "gx", "gy", "gz"), None, None),
        P(("groups", "gx", "gy", "gz")),
    )
    return jax.shard_map(
        shards,
        mesh=mesh,
        in_specs=placed,
        out_specs=P(("groups", "gx", "gy", "gz"), None),
        check_vma=False,
    )
```

```python
import functools

import jax
import jax.numpy as jnp
import numpy as np
from jax import lax
from jax.experimental import pallas as pl
from jax.experimental.pallas import tpu as pltpu
from jax.sharding import PartitionSpec as P

HD = 128
ROW_AXES = ("gx", "gy", "gz")
PLANE = ("gy", "gz")
MIB = 1024 * 1024
IN_VMEM = pl.BlockSpec(memory_space=pltpu.VMEM)
ANYWHERE = pl.BlockSpec(memory_space=pl.ANY)


def scale_kernel(tokens_ref, scaled_ref):
    tokens = tokens_ref[...].astype(jnp.float32)
    mean_square = jnp.mean(tokens * tokens, -1, keepdims=True)
    scaled_ref[...] = tokens * lax.rsqrt(mean_square + 1e-05)


def gain_kernel(wide, plane, scaled_ref, gain_ref, blocks_ref):
    normed = (scaled_ref[...] * gain_ref[...]).astype(jnp.bfloat16)
    half = normed.shape[1] // wide // 2
    for i in range(wide):
        for j in range(plane):
            at = (2 * i + j % 2) * half
            blocks_ref[i * plane + j] = normed[:, at : at + half]


def project_kernel(own, wide, plane, rows_ref, query_ref, key_ref, value_ref, *refs):
    owners, rows, half = rows_ref.shape
    core = lax.axis_index("gz")
    at_row = pl.multiple_of((core if own else 1 - core) * half, half)
    normed = rows_ref[...].reshape(owners * rows, half)
    sums_ref = refs[-1]
    at = 0
    for weight in (query_ref, key_ref, value_ref):
        cols = weight.shape[1]
        step = min(cols, 256)
        for c in range(0, cols, step):
            part = jnp.dot(
                normed,
                weight[pl.ds(at_row, half), c : c + step],
                preferred_element_type=jnp.float32,
            )
            if own:
                sums_ref[:, at : at + step] = part
            else:
                part = part + refs[1][:, at : at + step]
                sums_ref[:, :, at : at + step] = part.reshape(owners, rows, step)
            at += step
    if not own:
        own_wide = lax.axis_index("gx")
        own_plane = 2 * lax.axis_index("gy") + core
        for k in range(wide):
            for l in range(plane):
                refs[2 + k][l] = sums_ref[(own_wide ^ k) * plane + (own_plane ^ l)]


def own_place():
    return 2 * lax.axis_index("gy") + lax.axis_index("gz")


def write_heads(cache_ref, block_ref, start, owner):
    rows, slots, _ = cache_ref.shape
    cols = block_ref.shape[1]
    at = pl.multiple_of(owner * cols, cols)
    for r in range(rows):
        block_ref[start + r * slots : start + (r + 1) * slots] = cache_ref[r, :, pl.ds(at, cols)]


def write_lengths(rows, lengths_ref, block_ref):
    at_row = lax.broadcasted_iota(jnp.int32, (16, block_ref.shape[1]), 0)
    filled = jnp.zeros(at_row.shape, jnp.float32)
    for r in range(rows):
        filled = jnp.where(at_row == r, lengths_ref[:, r : r + 1].astype(jnp.float32), filled)
    block_ref[block_ref.shape[0] - 16 :] = filled.astype(jnp.bfloat16)


def cut_kernel(plan, lengths_ref, keys_ref, values_ref, _, *blocks):
    rows, slots, _ = keys_ref.shape
    for (slot, parts), block in zip(plan, blocks):
        start = 0
        for part, cache in (("k", keys_ref), ("v", values_ref)):
            if part in parts:
                write_heads(cache, block, start, own_place() ^ slot)
                start += rows * slots
        if "n" in parts:
            write_lengths(rows, lengths_ref, block)


def pass_kernel(*refs):
    pass


def attend_kernel(wide, plane, rows, query_cols, frequency_ref, *refs):
    partials, held, attended_ref = refs[wide - 1 :: -1], refs[wide:-1], refs[-1]
    even = plane // 2 - 1
    split_keys, split_values, whole = held[:even], held[even : 2 * even], held[2 * even :]
    slots = (whole[0].shape[0] - 16) // (2 * rows)
    cols = partials[0].shape[-1]
    kv_cols = (cols - query_cols) // 2
    kv_heads, group = kv_cols // HD, query_cols // kv_cols
    pairs = plane * rows
    count = pairs * kv_heads
    heads = count * group
    scale = 1.0 / HD**0.5
    total = partials[0][...]
    for k in range(1, wide):
        total = total + partials[k][...]
    total = total.reshape(pairs, cols).astype(jnp.bfloat16).astype(jnp.float32)

    def cached(split, start):
        parts = []
        for p in range(pairs):
            l, r = p // rows, p % rows
            if l % 2 == 0 and l:
                parts.append(split[l // 2 - 1][r * slots : (r + 1) * slots])
            else:
                at = start + r * slots
                parts.append(whole[(l + 1) // 2][at : at + slots])
        return jnp.concatenate(parts, 1)

    filled = []
    for l in range(plane):
        block = split_values[l // 2 - 1] if l % 2 == 0 and l else whole[(l + 1) // 2]
        last = block[block.shape[0] - 16 :, :HD].astype(jnp.float32)
        filled += [last[r : r + 1] for r in range(rows)]
    angles = jnp.concatenate(filled, 0) * frequency_ref[...]
    cosine, sine = jnp.cos(angles), jnp.sin(angles)
    front = lax.broadcasted_iota(jnp.int32, (1, HD), 1) < HD // 2
    sine = jnp.where(front, -sine, sine)

    def rotate(vector):
        return vector * cosine + pltpu.roll(vector, HD // 2, 1) * sine

    query, key_new, value_new = [], [], []
    for h in range(kv_heads):
        turned = [
            rotate(total[:, (h * group + g) * HD : (h * group + g + 1) * HD]) for g in range(group)
        ]
        query.append(jnp.swapaxes(jnp.stack(turned, 0), 0, 1))
        at = query_cols + h * HD
        key_new.append(rotate(total[:, at : at + HD]))
        value_new.append(total[:, at + kv_cols : at + kv_cols + HD])
    query = jnp.stack(query, 1).reshape(heads, HD)
    turned_query = query.T.astype(jnp.bfloat16)
    key_new = jnp.stack(key_new, 1).reshape(count, HD).astype(jnp.bfloat16)
    value_new = jnp.stack(value_new, 1).reshape(count, HD)

    head_pair = lax.broadcasted_iota(jnp.int32, (1, heads), 1) // group
    by_pair = jnp.concatenate(
        [jnp.where(head_pair == b, turned_query, jnp.zeros_like(turned_query)) for b in range(count)],
        0,
    )
    scores = scale * jnp.dot(cached(split_keys, 0), by_pair, preferred_element_type=jnp.float32)
    own = scale * jnp.dot(key_new, turned_query, preferred_element_type=jnp.float32)
    of_pair = lax.broadcasted_iota(jnp.int32, (count, 1), 0) == head_pair
    own = jnp.sum(jnp.where(of_pair, own, 0.0), 0, keepdims=True)
    length = jnp.zeros((1, heads), jnp.float32)
    for p in range(pairs):
        length = jnp.where(head_pair // kv_heads == p, filled[p][:, :1], length)
    slot = lax.broadcasted_iota(jnp.int32, (slots, 1), 0).astype(jnp.float32)
    scores = jnp.where(slot < length, scores, -1e30)
    top = jnp.maximum(jnp.max(scores, 0, keepdims=True), own)
    weights = jnp.exp(scores - top)
    own_weight = jnp.exp(own - top)
    denominator = jnp.sum(weights, 0, keepdims=True) + own_weight
    probability = (weights / denominator).astype(jnp.bfloat16)
    own_prob = (own_weight / denominator).astype(jnp.bfloat16)
    contract_rows = (((0,), (0,)), ((), ()))
    mixed = lax.dot_general(
        probability, cached(split_values, rows * slots), contract_rows, preferred_element_type=jnp.float32
    )
    own_prob = jnp.where(of_pair, own_prob.astype(jnp.float32), 0.0).astype(jnp.bfloat16)
    fresh = lax.dot_general(
        own_prob, value_new.astype(jnp.bfloat16), contract_rows, preferred_element_type=jnp.float32
    )
    mixed = [
        mixed[b * group : (b + 1) * group, b * HD : (b + 1) * HD]
        + fresh[b * group : (b + 1) * group]
        for b in range(count)
    ]
    attended = []
    for h in range(kv_heads):
        by_head = jnp.swapaxes(jnp.stack(mixed[h::kv_heads], 0), 0, 1)
        attended += [by_head[g] for g in range(group)]
    attended = jnp.concatenate(attended, 1)
    attended_ref[...] = attended.reshape(plane, rows, query_cols).astype(jnp.bfloat16)


def output_kernel(at, cols, order, weight_ref, *refs):
    blocks, keep_ref, give_ref = [refs[n] for n in order], refs[-2], refs[-1]
    wide = len(blocks)
    plane, rows, depth = blocks[0].shape
    attended = jnp.concatenate(
        [block[...].reshape(plane * rows, depth) for block in blocks], 0
    )
    step = min(cols, 512)
    for c in range(0, cols, step):
        part = jnp.dot(
            attended, weight_ref[:, at + c : at + c + step], preferred_element_type=jnp.float32
        )
        part = part.reshape(wide * plane // 2, 2 * rows, step)
        keep_ref[:, :, c : c + step] = part[:, :rows]
        give_ref[:, :, c : c + step] = part[:, rows:]


def halve_kernel(a_ref, b_ref, keep_ref, give_ref):
    for n in range(keep_ref.shape[0]):
        keep_ref[n] = a_ref[2 * n] + b_ref[2 * n]
        give_ref[n] = a_ref[2 * n + 1] + b_ref[2 * n + 1]


def total_kernel(parts, *refs):
    sums, blocks = refs[: 2 * parts], refs[2 * parts :]
    cols = sums[0].shape[-1]
    for p in range(parts):
        for k, block in enumerate(blocks):
            total = sums[2 * p][k] + sums[2 * p + 1][k]
            block[:, p * cols : (p + 1) * cols] = total.astype(jnp.bfloat16)


def finish_kernel(*refs):
    blocks, result_ref = refs[-2::-1], refs[-1]
    own = lax.axis_index("gx")
    cols = blocks[0].shape[-1]
    for k, block in enumerate(blocks):
        at = pl.multiple_of((own ^ k) * cols, cols)
        result_ref[:, pl.ds(at, cols)] = block[...]


def swap_blocks(blocks, axes):
    return lax.all_to_all(blocks, axes, split_axis=0, concat_axis=0, tiled=True)


def swap_pairs(value, axis, step):
    return lax.ppermute(value, axis, [(i, i ^ step) for i in range(lax.axis_size(axis))])


def swap_plane(value, step):
    return lax.ppermute(value, PLANE, [(i, i ^ step) for i in range(lax.axis_size(PLANE))])


def swap_wide(blocks):
    moved = [swap_pairs(blocks[k], "gx", k) for k in range(len(blocks) - 1, 0, -1)]
    return [blocks[0]] + moved[::-1]


def shards(
    tokens,
    norm_gain,
    query_weight,
    key_weight,
    value_weight,
    out_weight,
    cache_keys,
    cache_values,
    lengths,
):
    rows = tokens.shape[0]
    wide = lax.axis_size("gx")
    plane = lax.axis_size(PLANE)
    owners = wide * plane
    width, query_cols = query_weight.shape
    kv_cols = key_weight.shape[1]
    depth, out_cols = out_weight.shape
    cols = query_cols + 2 * kv_cols

    def params(mib):
        return pltpu.CompilerParams(vmem_limit_bytes=mib * MIB)

    def cost(flops, size):
        return pl.CostEstimate(flops=flops, bytes_accessed=size, transcendentals=0)

    half = width // 2
    scaled = pl.pallas_call(
        scale_kernel,
        out_shape=jax.ShapeDtypeStruct(tokens.shape, jnp.float32),
        in_specs=[IN_VMEM],
        out_specs=IN_VMEM,
        compiler_params=params(8),
        cost_estimate=cost(40 * 10**9, MIB),
    )(tokens)
    normed = pl.pallas_call(
        functools.partial(gain_kernel, wide, plane),
        out_shape=jax.ShapeDtypeStruct((owners, rows, half), jnp.bfloat16),
        in_specs=[IN_VMEM, IN_VMEM],
        out_specs=IN_VMEM,
        compiler_params=params(8),
    )(scaled, norm_gain.reshape(1, -1))
    block_rows = rows * cache_keys.shape[1]
    even = plane // 2 - 1

    def cut(plan, after):
        return pl.pallas_call(
            functools.partial(cut_kernel, plan),
            out_shape=[
                jax.ShapeDtypeStruct(
                    (("k" in parts) * block_rows + ("v" in parts) * block_rows + ("n" in parts) * 16, kv_cols),
                    cache_keys.dtype,
                )
                for _, parts in plan
            ],
            in_specs=[IN_VMEM] * 4,
            out_specs=[IN_VMEM] * len(plan),
            compiler_params=params(8),
        )(lengths.reshape(1, -1), cache_keys, cache_values, after)

    plan = [(l, "k") for l in range(2, plane, 2)] + [(l, "vn") for l in range(2, plane, 2)]
    plan += [(l, "kvn") for l in range(1, plane, 2)]
    blocks = cut(plan, normed)
    keys, rest = blocks[:even], blocks[even:]
    keys = [swap_plane(keys[s], 2 * s + 2) for s in range(even)]
    own_half = swap_blocks(normed, ROW_AXES)
    other_half = swap_pairs(own_half, "gz", 1)
    rest = pl.pallas_call(
        pass_kernel,
        out_shape=[jax.ShapeDtypeStruct(value.shape, value.dtype) for value in rest],
        in_specs=[ANYWHERE] * (len(rest) + even + 1),
        out_specs=[ANYWHERE] * len(rest),
        input_output_aliases={n: n for n in range(len(rest))},
    )(*rest, own_half, *keys)
    values = [swap_plane(rest[s], 2 * s + 2) for s in range(even)]
    odd = [swap_plane(rest[even + s], 2 * s + 1) for s in range(even + 1)]
    (mine,) = cut([(0, "kvn")], own_half)
    held = [*keys, *values, mine, *odd]
    weights = (query_weight, key_weight, value_weight)
    half_cost = cost(owners * rows * width * cols, width * cols)
    partial = pl.pallas_call(
        functools.partial(project_kernel, True, wide, plane),
        out_shape=jax.ShapeDtypeStruct((owners * rows, cols), jnp.float32),
        in_specs=[IN_VMEM] * 4,
        out_specs=IN_VMEM,
        compiler_params=params(8),
        cost_estimate=half_cost,
    )(own_half, *weights)
    partial = pl.pallas_call(
        functools.partial(project_kernel, False, wide, plane),
        out_shape=[jax.ShapeDtypeStruct((plane, rows, cols), jnp.float32)] * wide,
        in_specs=[IN_VMEM] * 6,
        out_specs=[IN_VMEM] * wide,
        scratch_shapes=[pltpu.VMEM((owners, rows, cols), jnp.float32)],
        compiler_params=params(8),
        cost_estimate=half_cost,
    )(other_half, *weights, odd[0], partial)
    partial = swap_wide(partial)

    half_dim = HD // 2
    frequency = 500000.0 ** (-np.arange(half_dim, dtype=np.float64) / half_dim)
    frequency = np.tile(frequency.astype(np.float32), 2).reshape(1, HD)
    attended = pl.pallas_call(
        functools.partial(attend_kernel, wide, plane, rows, query_cols),
        out_shape=jax.ShapeDtypeStruct((plane, rows, query_cols), jnp.bfloat16),
        in_specs=[IN_VMEM] * (1 + wide + len(held)),
        out_specs=IN_VMEM,
        compiler_params=params(8),
        cost_estimate=cost(10**10, 4 * MIB),
    )(jnp.asarray(frequency), *partial[::-1], *held)
    head_rows = swap_wide([attended] * wide)
    parts = 2
    order = [0, *range(wide - 2, 0, -1), wide - 1]
    part_cols = out_cols // parts
    sums = []
    for p in range(parts):
        count = owners // 2
        shape = jax.ShapeDtypeStruct((count, rows, part_cols), jnp.float32)
        keep, give = pl.pallas_call(
            functools.partial(output_kernel, p * part_cols, part_cols, order),
            out_shape=(shape, shape),
            in_specs=[IN_VMEM] * (1 + wide),
            out_specs=(IN_VMEM, IN_VMEM),
            compiler_params=params(8),
            cost_estimate=cost(2 * owners * rows * depth * part_cols, 2 * depth * part_cols),
        )(out_weight, *[head_rows[k] for k in order])
        give = swap_plane(give, 1)
        step = 2
        while step < plane:
            count //= 2
            shape = jax.ShapeDtypeStruct((count, rows, part_cols), jnp.float32)
            keep, give = pl.pallas_call(
                halve_kernel,
                out_shape=(shape, shape),
                in_specs=[IN_VMEM, IN_VMEM],
                out_specs=(IN_VMEM, IN_VMEM),
                compiler_params=params(8),
            )(keep, give)
            give = swap_plane(give, step)
            step *= 2
        sums += [keep, give]
    blocks = pl.pallas_call(
        functools.partial(total_kernel, parts),
        out_shape=[jax.ShapeDtypeStruct((rows, out_cols), jnp.bfloat16)] * wide,
        in_specs=[IN_VMEM] * len(sums),
        out_specs=[IN_VMEM] * wide,
        compiler_params=params(8),
    )(*sums)
    blocks = swap_wide(blocks)
    return pl.pallas_call(
        finish_kernel,
        out_shape=jax.ShapeDtypeStruct((rows, wide * out_cols), jnp.bfloat16),
        in_specs=[IN_VMEM] * wide,
        out_specs=IN_VMEM,
        compiler_params=params(8),
    )(*blocks[::-1])


def solution(mesh):
    placed = (
        P(("groups", "gx", "gy", "gz"), None),
        P(),
        P("gx", ("gy", "gz")),
        P("gx", ("gy", "gz")),
        P("gx", ("gy", "gz")),
        P(("gy", "gz"), "gx"),
        P(("groups", "gx", "gy", "gz"), None, None),
        P(("groups", "gx", "gy", "gz"), None, None),
        P(("groups", "gx", "gy", "gz")),
    )
    return jax.shard_map(
        shards,
        mesh=mesh,
        in_specs=placed,
        out_specs=P(("groups", "gx", "gy", "gz"), None),
        check_vma=False,
    )
```

```python
import functools

import jax
import jax.numpy as jnp
import numpy as np
from jax import lax
from jax.experimental import pallas as pl
from jax.experimental.pallas import tpu as pltpu
from jax.sharding import PartitionSpec as P

HD = 128
ROW_AXES = ("gx", "gy", "gz")
PLANE = ("gy", "gz")
MIB = 1024 * 1024
IN_VMEM = pl.BlockSpec(memory_space=pltpu.VMEM)
ANYWHERE = pl.BlockSpec(memory_space=pl.ANY)


def scale_kernel(tokens_ref, scaled_ref):
    tokens = tokens_ref[...].astype(jnp.float32)
    mean_square = jnp.mean(tokens * tokens, -1, keepdims=True)
    scaled_ref[...] = tokens * lax.rsqrt(mean_square + 1e-05)


def gain_kernel(wide, plane, scaled_ref, gain_ref, blocks_ref):
    normed = (scaled_ref[...] * gain_ref[...]).astype(jnp.bfloat16)
    half = normed.shape[1] // wide // 2
    for i in range(wide):
        for j in range(plane):
            at = (2 * i + j % 2) * half
            blocks_ref[i * plane + j] = normed[:, at : at + half]


def project_kernel(own, wide, plane, rows_ref, query_ref, key_ref, value_ref, *refs):
    owners, rows, half = rows_ref.shape
    core = lax.axis_index("gz")
    at_row = pl.multiple_of((core if own else 1 - core) * half, half)
    normed = rows_ref[...].reshape(owners * rows, half)
    sums_ref = refs[-1]
    at = 0
    for weight in (query_ref, key_ref, value_ref):
        cols = weight.shape[1]
        step = min(cols, 256)
        for c in range(0, cols, step):
            part = jnp.dot(
                normed,
                weight[pl.ds(at_row, half), c : c + step],
                preferred_element_type=jnp.float32,
            )
            if own:
                sums_ref[:, at : at + step] = part
            else:
                part = part + refs[1][:, at : at + step]
                sums_ref[:, :, at : at + step] = part.reshape(owners, rows, step)
            at += step
    if not own:
        own_wide = lax.axis_index("gx")
        own_plane = 2 * lax.axis_index("gy") + core
        for k in range(wide):
            for l in range(plane):
                refs[2 + k][l] = sums_ref[(own_wide ^ k) * plane + (own_plane ^ l)]


def own_place():
    return 2 * lax.axis_index("gy") + lax.axis_index("gz")


def write_heads(cache_ref, block_ref, start, owner):
    rows, slots, _ = cache_ref.shape
    cols = block_ref.shape[1]
    at = pl.multiple_of(owner * cols, cols)
    for r in range(rows):
        block_ref[start + r * slots : start + (r + 1) * slots] = cache_ref[r, :, pl.ds(at, cols)]


def write_lengths(rows, lengths_ref, block_ref):
    at_row = lax.broadcasted_iota(jnp.int32, (16, block_ref.shape[1]), 0)
    filled = jnp.zeros(at_row.shape, jnp.float32)
    for r in range(rows):
        filled = jnp.where(at_row == r, lengths_ref[:, r : r + 1].astype(jnp.float32), filled)
    block_ref[block_ref.shape[0] - 16 :] = filled.astype(jnp.bfloat16)


def cut_kernel(plan, lengths_ref, keys_ref, values_ref, _, *blocks):
    rows, slots, _ = keys_ref.shape
    for (slot, parts), block in zip(plan, blocks):
        start = 0
        for part, cache in (("k", keys_ref), ("v", values_ref)):
            if part in parts:
                write_heads(cache, block, start, own_place() ^ slot)
                start += rows * slots
        if "n" in parts:
            write_lengths(rows, lengths_ref, block)


def pass_kernel(*refs):
    pass


def attend_kernel(wide, plane, rows, query_cols, frequency_ref, *refs):
    partials, held, attended_ref = refs[wide - 1 :: -1], refs[wide:-1], refs[-1]
    even = plane // 2 - 1
    split_keys, split_values, whole = held[:even], held[even : 2 * even], held[2 * even :]
    slots = (whole[0].shape[0] - 16) // (2 * rows)
    cols = partials[0].shape[-1]
    kv_cols = (cols - query_cols) // 2
    kv_heads, group = kv_cols // HD, query_cols // kv_cols
    pairs = plane * rows
    count = pairs * kv_heads
    heads = count * group
    scale = 1.0 / HD**0.5
    total = partials[0][...]
    for k in range(1, wide):
        total = total + partials[k][...]
    total = total.reshape(pairs, cols).astype(jnp.bfloat16).astype(jnp.float32)

    def cached(split, start):
        parts = []
        for p in range(pairs):
            l, r = p // rows, p % rows
            if l % 2 == 0 and l:
                parts.append(split[l // 2 - 1][r * slots : (r + 1) * slots])
            else:
                at = start + r * slots
                parts.append(whole[(l + 1) // 2][at : at + slots])
        return jnp.concatenate(parts, 1)

    filled = []
    for l in range(plane):
        block = split_values[l // 2 - 1] if l % 2 == 0 and l else whole[(l + 1) // 2]
        last = block[block.shape[0] - 16 :, :HD].astype(jnp.float32)
        filled += [last[r : r + 1] for r in range(rows)]
    angles = jnp.concatenate(filled, 0) * frequency_ref[...]
    cosine, sine = jnp.cos(angles), jnp.sin(angles)
    front = lax.broadcasted_iota(jnp.int32, (1, HD), 1) < HD // 2
    sine = jnp.where(front, -sine, sine)

    def rotate(vector):
        return vector * cosine + pltpu.roll(vector, HD // 2, 1) * sine

    query, key_new, value_new = [], [], []
    for h in range(kv_heads):
        turned = [
            rotate(total[:, (h * group + g) * HD : (h * group + g + 1) * HD]) for g in range(group)
        ]
        query.append(jnp.swapaxes(jnp.stack(turned, 0), 0, 1))
        at = query_cols + h * HD
        key_new.append(rotate(total[:, at : at + HD]))
        value_new.append(total[:, at + kv_cols : at + kv_cols + HD])
    query = jnp.stack(query, 1).reshape(heads, HD)
    turned_query = query.T.astype(jnp.bfloat16)
    key_new = jnp.stack(key_new, 1).reshape(count, HD).astype(jnp.bfloat16)
    value_new = jnp.stack(value_new, 1).reshape(count, HD)

    head_pair = lax.broadcasted_iota(jnp.int32, (1, heads), 1) // group
    by_pair = jnp.concatenate(
        [jnp.where(head_pair == b, turned_query, jnp.zeros_like(turned_query)) for b in range(count)],
        0,
    )
    scores = scale * jnp.dot(cached(split_keys, 0), by_pair, preferred_element_type=jnp.float32)
    own = scale * jnp.dot(key_new, turned_query, preferred_element_type=jnp.float32)
    of_pair = lax.broadcasted_iota(jnp.int32, (count, 1), 0) == head_pair
    own = jnp.sum(jnp.where(of_pair, own, 0.0), 0, keepdims=True)
    length = jnp.zeros((1, heads), jnp.float32)
    for p in range(pairs):
        length = jnp.where(head_pair // kv_heads == p, filled[p][:, :1], length)
    slot = lax.broadcasted_iota(jnp.int32, (slots, 1), 0).astype(jnp.float32)
    scores = jnp.where(slot < length, scores, -1e30)
    top = jnp.maximum(jnp.max(scores, 0, keepdims=True), own)
    weights = jnp.exp(scores - top)
    own_weight = jnp.exp(own - top)
    denominator = jnp.sum(weights, 0, keepdims=True) + own_weight
    probability = (weights / denominator).astype(jnp.bfloat16)
    own_prob = (own_weight / denominator).astype(jnp.bfloat16)
    contract_rows = (((0,), (0,)), ((), ()))
    mixed = lax.dot_general(
        probability, cached(split_values, rows * slots), contract_rows, preferred_element_type=jnp.float32
    )
    own_prob = jnp.where(of_pair, own_prob.astype(jnp.float32), 0.0).astype(jnp.bfloat16)
    fresh = lax.dot_general(
        own_prob, value_new.astype(jnp.bfloat16), contract_rows, preferred_element_type=jnp.float32
    )
    mixed = [
        mixed[b * group : (b + 1) * group, b * HD : (b + 1) * HD]
        + fresh[b * group : (b + 1) * group]
        for b in range(count)
    ]
    attended = []
    for h in range(kv_heads):
        by_head = jnp.swapaxes(jnp.stack(mixed[h::kv_heads], 0), 0, 1)
        attended += [by_head[g] for g in range(group)]
    attended = jnp.concatenate(attended, 1)
    attended_ref[...] = attended.reshape(plane, rows, query_cols).astype(jnp.bfloat16)


def output_kernel(at, cols, order, weight_ref, *refs):
    blocks, keep_ref, give_ref = [refs[n] for n in order], refs[-2], refs[-1]
    wide = len(blocks)
    plane, rows, depth = blocks[0].shape
    attended = jnp.concatenate(
        [block[...].reshape(plane * rows, depth) for block in blocks], 0
    )
    step = min(cols, 512)
    for c in range(0, cols, step):
        part = jnp.dot(
            attended, weight_ref[:, at + c : at + c + step], preferred_element_type=jnp.float32
        )
        part = part.reshape(wide * plane // 2, 2 * rows, step)
        keep_ref[:, :, c : c + step] = part[:, :rows]
        give_ref[:, :, c : c + step] = part[:, rows:]


def halve_kernel(a_ref, b_ref, keep_ref, give_ref):
    for n in range(keep_ref.shape[0]):
        keep_ref[n] = a_ref[2 * n] + b_ref[2 * n]
        give_ref[n] = a_ref[2 * n + 1] + b_ref[2 * n + 1]


def total_kernel(parts, *refs):
    sums, blocks = refs[: 2 * parts], refs[2 * parts :]
    cols = sums[0].shape[-1]
    for p in range(parts):
        for k, block in enumerate(blocks):
            total = sums[2 * p][k] + sums[2 * p + 1][k]
            block[:, p * cols : (p + 1) * cols] = total.astype(jnp.bfloat16)


def finish_kernel(*refs):
    blocks, result_ref = refs[-2::-1], refs[-1]
    own = lax.axis_index("gx")
    cols = blocks[0].shape[-1]
    for k, block in enumerate(blocks):
        at = pl.multiple_of((own ^ k) * cols, cols)
        result_ref[:, pl.ds(at, cols)] = block[...]


def swap_blocks(blocks, axes):
    return lax.all_to_all(blocks, axes, split_axis=0, concat_axis=0, tiled=True)


def swap_pairs(value, axis, step):
    return lax.ppermute(value, axis, [(i, i ^ step) for i in range(lax.axis_size(axis))])


def swap_plane(value, step):
    return lax.ppermute(value, PLANE, [(i, i ^ step) for i in range(lax.axis_size(PLANE))])


def swap_wide(blocks):
    moved = [swap_pairs(blocks[k], "gx", k) for k in range(len(blocks) - 1, 0, -1)]
    return [blocks[0]] + moved[::-1]


def shards(
    tokens,
    norm_gain,
    query_weight,
    key_weight,
    value_weight,
    out_weight,
    cache_keys,
    cache_values,
    lengths,
):
    rows = tokens.shape[0]
    wide = lax.axis_size("gx")
    plane = lax.axis_size(PLANE)
    owners = wide * plane
    width, query_cols = query_weight.shape
    kv_cols = key_weight.shape[1]
    depth, out_cols = out_weight.shape
    cols = query_cols + 2 * kv_cols

    def params(mib):
        return pltpu.CompilerParams(vmem_limit_bytes=mib * MIB)

    def cost(flops, size):
        return pl.CostEstimate(flops=flops, bytes_accessed=size, transcendentals=0)

    half = width // 2
    scaled = pl.pallas_call(
        scale_kernel,
        out_shape=jax.ShapeDtypeStruct(tokens.shape, jnp.float32),
        in_specs=[IN_VMEM],
        out_specs=IN_VMEM,
        compiler_params=params(8),
        cost_estimate=cost(40 * 10**9, MIB),
    )(tokens)
    normed = pl.pallas_call(
        functools.partial(gain_kernel, wide, plane),
        out_shape=jax.ShapeDtypeStruct((owners, rows, half), jnp.bfloat16),
        in_specs=[IN_VMEM, IN_VMEM],
        out_specs=IN_VMEM,
        compiler_params=params(8),
    )(scaled, norm_gain.reshape(1, -1))
    block_rows = rows * cache_keys.shape[1]
    even = plane // 2 - 1

    def cut(plan, after):
        return pl.pallas_call(
            functools.partial(cut_kernel, plan),
            out_shape=[
                jax.ShapeDtypeStruct(
                    (("k" in parts) * block_rows + ("v" in parts) * block_rows + ("n" in parts) * 16, kv_cols),
                    cache_keys.dtype,
                )
                for _, parts in plan
            ],
            in_specs=[IN_VMEM] * 4,
            out_specs=[IN_VMEM] * len(plan),
            compiler_params=params(8),
        )(lengths.reshape(1, -1), cache_keys, cache_values, after)

    plan = [(l, "k") for l in range(2, plane, 2)] + [(l, "vn") for l in range(2, plane, 2)]
    plan += [(l, "kvn") for l in range(1, plane, 2)]
    blocks = cut(plan, normed)
    keys, rest = blocks[:even], blocks[even:]
    keys = [swap_plane(keys[s], 2 * s + 2) for s in range(even)]
    own_half = swap_blocks(normed, ROW_AXES)
    other_half = swap_pairs(own_half, "gz", 1)
    rest = pl.pallas_call(
        pass_kernel,
        out_shape=[jax.ShapeDtypeStruct(value.shape, value.dtype) for value in rest],
        in_specs=[ANYWHERE] * (len(rest) + even + 1),
        out_specs=[ANYWHERE] * len(rest),
        input_output_aliases={n: n for n in range(len(rest))},
        compiler_params=params(1),
    )(*rest, own_half, *keys)
    values = [swap_plane(rest[s], 2 * s + 2) for s in range(even)]
    odd = [swap_plane(rest[even + s], 2 * s + 1) for s in range(even + 1)]
    (mine,) = cut([(0, "kvn")], own_half)
    held = [*keys, *values, mine, *odd]
    weights = (query_weight, key_weight, value_weight)
    half_cost = cost(owners * rows * width * cols, width * cols)
    partial = pl.pallas_call(
        functools.partial(project_kernel, True, wide, plane),
        out_shape=jax.ShapeDtypeStruct((owners * rows, cols), jnp.float32),
        in_specs=[IN_VMEM] * 4,
        out_specs=IN_VMEM,
        compiler_params=params(8),
        cost_estimate=half_cost,
    )(own_half, *weights)
    partial = pl.pallas_call(
        functools.partial(project_kernel, False, wide, plane),
        out_shape=[jax.ShapeDtypeStruct((plane, rows, cols), jnp.float32)] * wide,
        in_specs=[IN_VMEM] * 6,
        out_specs=[IN_VMEM] * wide,
        scratch_shapes=[pltpu.VMEM((owners, rows, cols), jnp.float32)],
        compiler_params=params(8),
        cost_estimate=half_cost,
    )(other_half, *weights, odd[0], partial)
    partial = swap_wide(partial)

    half_dim = HD // 2
    frequency = 500000.0 ** (-np.arange(half_dim, dtype=np.float64) / half_dim)
    frequency = np.tile(frequency.astype(np.float32), 2).reshape(1, HD)
    attended = pl.pallas_call(
        functools.partial(attend_kernel, wide, plane, rows, query_cols),
        out_shape=jax.ShapeDtypeStruct((plane, rows, query_cols), jnp.bfloat16),
        in_specs=[IN_VMEM] * (1 + wide + len(held)),
        out_specs=IN_VMEM,
        compiler_params=params(8),
        cost_estimate=cost(10**10, 4 * MIB),
    )(jnp.asarray(frequency), *partial[::-1], *held)
    head_rows = swap_wide([attended] * wide)
    parts = 2
    order = [0, *range(wide - 2, 0, -1), wide - 1]
    part_cols = out_cols // parts
    sums = []
    for p in range(parts):
        count = owners // 2
        shape = jax.ShapeDtypeStruct((count, rows, part_cols), jnp.float32)
        keep, give = pl.pallas_call(
            functools.partial(output_kernel, p * part_cols, part_cols, order),
            out_shape=(shape, shape),
            in_specs=[IN_VMEM] * (1 + wide),
            out_specs=(IN_VMEM, IN_VMEM),
            compiler_params=params(8),
            cost_estimate=cost(2 * owners * rows * depth * part_cols, 2 * depth * part_cols),
        )(out_weight, *[head_rows[k] for k in order])
        give = swap_plane(give, 1)
        step = 2
        while step < plane:
            count //= 2
            shape = jax.ShapeDtypeStruct((count, rows, part_cols), jnp.float32)
            keep, give = pl.pallas_call(
                halve_kernel,
                out_shape=(shape, shape),
                in_specs=[IN_VMEM, IN_VMEM],
                out_specs=(IN_VMEM, IN_VMEM),
                compiler_params=params(8),
            )(keep, give)
            give = swap_plane(give, step)
            step *= 2
        sums += [keep, give]
    blocks = pl.pallas_call(
        functools.partial(total_kernel, parts),
        out_shape=[jax.ShapeDtypeStruct((rows, out_cols), jnp.bfloat16)] * wide,
        in_specs=[IN_VMEM] * len(sums),
        out_specs=[IN_VMEM] * wide,
        compiler_params=params(8),
    )(*sums)
    blocks = swap_wide(blocks)
    return pl.pallas_call(
        finish_kernel,
        out_shape=jax.ShapeDtypeStruct((rows, wide * out_cols), jnp.bfloat16),
        in_specs=[IN_VMEM] * wide,
        out_specs=IN_VMEM,
        compiler_params=params(8),
    )(*blocks[::-1])


def solution(mesh):
    placed = (
        P(("groups", "gx", "gy", "gz"), None),
        P(),
        P("gx", ("gy", "gz")),
        P("gx", ("gy", "gz")),
        P("gx", ("gy", "gz")),
        P(("gy", "gz"), "gx"),
        P(("groups", "gx", "gy", "gz"), None, None),
        P(("groups", "gx", "gy", "gz"), None, None),
        P(("groups", "gx", "gy", "gz")),
    )
    return jax.shard_map(
        shards,
        mesh=mesh,
        in_specs=placed,
        out_specs=P(("groups", "gx", "gy", "gz"), None),
        check_vma=False,
    )
```

```python
import functools

import jax
import jax.numpy as jnp
import numpy as np
from jax import lax
from jax.experimental import pallas as pl
from jax.experimental.pallas import tpu as pltpu
from jax.sharding import PartitionSpec as P

HD = 128
ROW_AXES = ("gx", "gy", "gz")
PLANE = ("gy", "gz")
MIB = 1024 * 1024
IN_VMEM = pl.BlockSpec(memory_space=pltpu.VMEM)
ANYWHERE = pl.BlockSpec(memory_space=pl.ANY)


def scale_kernel(tokens_ref, scaled_ref):
    tokens = tokens_ref[...].astype(jnp.float32)
    mean_square = jnp.mean(tokens * tokens, -1, keepdims=True)
    scaled_ref[...] = tokens * lax.rsqrt(mean_square + 1e-05)


def gain_kernel(wide, plane, scaled_ref, gain_ref, blocks_ref):
    normed = (scaled_ref[...] * gain_ref[...]).astype(jnp.bfloat16)
    half = normed.shape[1] // wide // 2
    for i in range(wide):
        for j in range(plane):
            at = (2 * i + j % 2) * half
            blocks_ref[i * plane + j] = normed[:, at : at + half]


def project_kernel(own, wide, plane, rows_ref, query_ref, key_ref, value_ref, *refs):
    owners, rows, half = rows_ref.shape
    core = lax.axis_index("gz")
    at_row = pl.multiple_of((core if own else 1 - core) * half, half)
    normed = rows_ref[...].reshape(owners * rows, half)
    sums_ref = refs[-1]
    at = 0
    for weight in (query_ref, key_ref, value_ref):
        cols = weight.shape[1]
        step = min(cols, 256)
        for c in range(0, cols, step):
            part = jnp.dot(
                normed,
                weight[pl.ds(at_row, half), c : c + step],
                preferred_element_type=jnp.float32,
            )
            if own:
                sums_ref[:, at : at + step] = part
            else:
                part = part + refs[1][:, at : at + step]
                sums_ref[:, :, at : at + step] = part.reshape(owners, rows, step)
            at += step
    if not own:
        own_wide = lax.axis_index("gx")
        own_plane = 2 * lax.axis_index("gy") + core
        for k in range(wide):
            for l in range(plane):
                refs[2 + k][l] = sums_ref[(own_wide ^ k) * plane + (own_plane ^ l)]


def own_place():
    return 2 * lax.axis_index("gy") + lax.axis_index("gz")


def write_lengths(rows, lengths_ref, block_ref):
    at_row = lax.broadcasted_iota(jnp.int32, (16, block_ref.shape[1]), 0)
    filled = jnp.zeros(at_row.shape, jnp.float32)
    for r in range(rows):
        filled = jnp.where(at_row == r, lengths_ref[:, r : r + 1].astype(jnp.float32), filled)
    block_ref[block_ref.shape[0] - 16 :] = filled.astype(jnp.bfloat16)


def cut_kernel(plan, lengths_ref, keys_ref, values_ref, _, *blocks):
    rows, slots, _ = keys_ref.shape
    cols = blocks[0].shape[1]
    for (slot, key_rows, value_rows, with_lengths), block in zip(plan, blocks):
        at = pl.multiple_of((own_place() ^ slot) * cols, cols)
        start = 0
        for cache_ref, wanted in ((keys_ref, key_rows), (values_ref, value_rows)):
            for r in wanted:
                block[start : start + slots] = cache_ref[r, :, pl.ds(at, cols)]
                start += slots
        if with_lengths:
            write_lengths(rows, lengths_ref, block)


def pass_kernel(*refs):
    pass


def attend_kernel(wide, plane, rows, early, query_cols, frequency_ref, *refs):
    partials, held, attended_ref = refs[wide - 1 :: -1], refs[wide:-1], refs[-1]
    even = plane // 2 - 1
    firsts, lasts, whole = held[:even], held[even : 2 * even], held[2 * even :]
    slots = (whole[0].shape[0] - 16) // (2 * rows)
    cols = partials[0].shape[-1]
    kv_cols = (cols - query_cols) // 2
    kv_heads, group = kv_cols // HD, query_cols // kv_cols
    pairs = plane * rows
    count = pairs * kv_heads
    heads = count * group
    scale = 1.0 / HD**0.5
    total = partials[0][...]
    for k in range(1, wide):
        total = total + partials[k][...]
    total = total.reshape(pairs, cols).astype(jnp.bfloat16).astype(jnp.float32)

    def cached(values):
        parts = []
        for p in range(pairs):
            l, r = p // rows, p % rows
            ref, at = whole[(l + 1) // 2], values * rows + r
            if l % 2 == 0 and l:
                ref = firsts[l // 2 - 1]
                if at >= rows + early:
                    ref, at = lasts[l // 2 - 1], at - rows - early
            parts.append(ref[at * slots : (at + 1) * slots])
        return jnp.concatenate(parts, 1)

    filled = []
    for l in range(plane):
        block = lasts[l // 2 - 1] if l % 2 == 0 and l else whole[(l + 1) // 2]
        last = block[block.shape[0] - 16 :, :HD].astype(jnp.float32)
        filled += [last[r : r + 1] for r in range(rows)]
    angles = jnp.concatenate(filled, 0) * frequency_ref[...]
    cosine, sine = jnp.cos(angles), jnp.sin(angles)
    front = lax.broadcasted_iota(jnp.int32, (1, HD), 1) < HD // 2
    sine = jnp.where(front, -sine, sine)

    def rotate(vector):
        return vector * cosine + pltpu.roll(vector, HD // 2, 1) * sine

    query, key_new, value_new = [], [], []
    for h in range(kv_heads):
        turned = [
            rotate(total[:, (h * group + g) * HD : (h * group + g + 1) * HD]) for g in range(group)
        ]
        query.append(jnp.swapaxes(jnp.stack(turned, 0), 0, 1))
        at = query_cols + h * HD
        key_new.append(rotate(total[:, at : at + HD]))
        value_new.append(total[:, at + kv_cols : at + kv_cols + HD])
    query = jnp.stack(query, 1).reshape(heads, HD)
    turned_query = query.T.astype(jnp.bfloat16)
    key_new = jnp.stack(key_new, 1).reshape(count, HD).astype(jnp.bfloat16)
    value_new = jnp.stack(value_new, 1).reshape(count, HD)

    head_pair = lax.broadcasted_iota(jnp.int32, (1, heads), 1) // group
    by_pair = jnp.concatenate(
        [jnp.where(head_pair == b, turned_query, jnp.zeros_like(turned_query)) for b in range(count)],
        0,
    )
    scores = scale * jnp.dot(cached(0), by_pair, preferred_element_type=jnp.float32)
    own = scale * jnp.dot(key_new, turned_query, preferred_element_type=jnp.float32)
    of_pair = lax.broadcasted_iota(jnp.int32, (count, 1), 0) == head_pair
    own = jnp.sum(jnp.where(of_pair, own, 0.0), 0, keepdims=True)
    length = jnp.zeros((1, heads), jnp.float32)
    for p in range(pairs):
        length = jnp.where(head_pair // kv_heads == p, filled[p][:, :1], length)
    slot = lax.broadcasted_iota(jnp.int32, (slots, 1), 0).astype(jnp.float32)
    scores = jnp.where(slot < length, scores, -1e30)
    top = jnp.maximum(jnp.max(scores, 0, keepdims=True), own)
    weights = jnp.exp(scores - top)
    own_weight = jnp.exp(own - top)
    denominator = jnp.sum(weights, 0, keepdims=True) + own_weight
    probability = (weights / denominator).astype(jnp.bfloat16)
    own_prob = (own_weight / denominator).astype(jnp.bfloat16)
    contract_rows = (((0,), (0,)), ((), ()))
    mixed = lax.dot_general(
        probability, cached(1), contract_rows, preferred_element_type=jnp.float32
    )
    own_prob = jnp.where(of_pair, own_prob.astype(jnp.float32), 0.0).astype(jnp.bfloat16)
    fresh = lax.dot_general(
        own_prob, value_new.astype(jnp.bfloat16), contract_rows, preferred_element_type=jnp.float32
    )
    mixed = [
        mixed[b * group : (b + 1) * group, b * HD : (b + 1) * HD]
        + fresh[b * group : (b + 1) * group]
        for b in range(count)
    ]
    attended = []
    for h in range(kv_heads):
        by_head = jnp.swapaxes(jnp.stack(mixed[h::kv_heads], 0), 0, 1)
        attended += [by_head[g] for g in range(group)]
    attended = jnp.concatenate(attended, 1)
    attended_ref[...] = attended.reshape(plane, rows, query_cols).astype(jnp.bfloat16)


def output_kernel(at, cols, order, weight_ref, *refs):
    blocks, keep_ref, give_ref = [refs[n] for n in order], refs[-2], refs[-1]
    wide = len(blocks)
    plane, rows, depth = blocks[0].shape
    attended = jnp.concatenate(
        [block[...].reshape(plane * rows, depth) for block in blocks], 0
    )
    step = min(cols, 512)
    for c in range(0, cols, step):
        part = jnp.dot(
            attended, weight_ref[:, at + c : at + c + step], preferred_element_type=jnp.float32
        )
        part = part.reshape(wide * plane // 2, 2 * rows, step)
        keep_ref[:, :, c : c + step] = part[:, :rows]
        give_ref[:, :, c : c + step] = part[:, rows:]


def halve_kernel(a_ref, b_ref, keep_ref, give_ref):
    for n in range(keep_ref.shape[0]):
        keep_ref[n] = a_ref[2 * n] + b_ref[2 * n]
        give_ref[n] = a_ref[2 * n + 1] + b_ref[2 * n + 1]


def total_kernel(parts, *refs):
    sums, blocks = refs[: 2 * parts], refs[2 * parts :]
    cols = sums[0].shape[-1]
    for p in range(parts):
        for k, block in enumerate(blocks):
            total = sums[2 * p][k] + sums[2 * p + 1][k]
            block[:, p * cols : (p + 1) * cols] = total.astype(jnp.bfloat16)


def finish_kernel(*refs):
    blocks, result_ref = refs[-2::-1], refs[-1]
    own = lax.axis_index("gx")
    cols = blocks[0].shape[-1]
    for k, block in enumerate(blocks):
        at = pl.multiple_of((own ^ k) * cols, cols)
        result_ref[:, pl.ds(at, cols)] = block[...]


def swap_blocks(blocks, axes):
    return lax.all_to_all(blocks, axes, split_axis=0, concat_axis=0, tiled=True)


def swap_pairs(value, axis, step):
    return lax.ppermute(value, axis, [(i, i ^ step) for i in range(lax.axis_size(axis))])


def swap_plane(value, step):
    return lax.ppermute(value, PLANE, [(i, i ^ step) for i in range(lax.axis_size(PLANE))])


def swap_wide(blocks):
    moved = [swap_pairs(blocks[k], "gx", k) for k in range(len(blocks) - 1, 0, -1)]
    return [blocks[0]] + moved[::-1]


def shards(
    tokens,
    norm_gain,
    query_weight,
    key_weight,
    value_weight,
    out_weight,
    cache_keys,
    cache_values,
    lengths,
):
    rows = tokens.shape[0]
    wide = lax.axis_size("gx")
    plane = lax.axis_size(PLANE)
    owners = wide * plane
    width, query_cols = query_weight.shape
    kv_cols = key_weight.shape[1]
    depth, out_cols = out_weight.shape
    cols = query_cols + 2 * kv_cols

    def params(mib):
        return pltpu.CompilerParams(vmem_limit_bytes=mib * MIB)

    def cost(flops, size):
        return pl.CostEstimate(flops=flops, bytes_accessed=size, transcendentals=0)

    half = width // 2
    scaled = pl.pallas_call(
        scale_kernel,
        out_shape=jax.ShapeDtypeStruct(tokens.shape, jnp.float32),
        in_specs=[IN_VMEM],
        out_specs=IN_VMEM,
        compiler_params=params(8),
        cost_estimate=cost(40 * 10**9, MIB),
    )(tokens)
    normed = pl.pallas_call(
        functools.partial(gain_kernel, wide, plane),
        out_shape=jax.ShapeDtypeStruct((owners, rows, half), jnp.bfloat16),
        in_specs=[IN_VMEM, IN_VMEM],
        out_specs=IN_VMEM,
        compiler_params=params(8),
    )(scaled, norm_gain.reshape(1, -1))
    slots = cache_keys.shape[1]
    even = plane // 2 - 1
    early = rows // 2
    every = range(rows)

    def cut(plan, after):
        return pl.pallas_call(
            functools.partial(cut_kernel, plan),
            out_shape=[
                jax.ShapeDtypeStruct(
                    ((len(key_rows) + len(value_rows)) * slots + 16 * with_lengths, kv_cols),
                    cache_keys.dtype,
                )
                for _, key_rows, value_rows, with_lengths in plan
            ],
            in_specs=[IN_VMEM] * 4,
            out_specs=[IN_VMEM] * len(plan),
            compiler_params=params(8),
        )(lengths.reshape(1, -1), cache_keys, cache_values, after)

    plan = [(l, every, every[:early], False) for l in range(2, plane, 2)]
    plan += [(l, (), every[early:], True) for l in range(2, plane, 2)]
    plan += [(l, every, every, True) for l in range(1, plane, 2)]
    blocks = cut(plan, normed)
    firsts, rest = blocks[:even], blocks[even:]
    firsts = [swap_plane(firsts[s], 2 * s + 2) for s in range(even)]
    own_half = swap_blocks(normed, ROW_AXES)
    other_half = swap_pairs(own_half, "gz", 1)
    rest = pl.pallas_call(
        pass_kernel,
        out_shape=[jax.ShapeDtypeStruct(value.shape, value.dtype) for value in rest],
        in_specs=[ANYWHERE] * (len(rest) + even + 1),
        out_specs=[ANYWHERE] * len(rest),
        input_output_aliases={n: n for n in range(len(rest))},
        compiler_params=params(1),
    )(*rest, own_half, *firsts)
    lasts = [swap_plane(rest[s], 2 * s + 2) for s in range(even)]
    odd = [swap_plane(rest[even + s], 2 * s + 1) for s in range(even + 1)]
    (mine,) = cut([(0, every, every, True)], own_half)
    held = [*firsts, *lasts, mine, *odd]
    weights = (query_weight, key_weight, value_weight)
    half_cost = cost(owners * rows * width * cols, width * cols)
    partial = pl.pallas_call(
        functools.partial(project_kernel, True, wide, plane),
        out_shape=jax.ShapeDtypeStruct((owners * rows, cols), jnp.float32),
        in_specs=[IN_VMEM] * 4,
        out_specs=IN_VMEM,
        compiler_params=params(8),
        cost_estimate=half_cost,
    )(own_half, *weights)
    partial = pl.pallas_call(
        functools.partial(project_kernel, False, wide, plane),
        out_shape=[jax.ShapeDtypeStruct((plane, rows, cols), jnp.float32)] * wide,
        in_specs=[IN_VMEM] * 6,
        out_specs=[IN_VMEM] * wide,
        scratch_shapes=[pltpu.VMEM((owners, rows, cols), jnp.float32)],
        compiler_params=params(8),
        cost_estimate=half_cost,
    )(other_half, *weights, odd[0], partial)
    partial = swap_wide(partial)

    half_dim = HD // 2
    frequency = 500000.0 ** (-np.arange(half_dim, dtype=np.float64) / half_dim)
    frequency = np.tile(frequency.astype(np.float32), 2).reshape(1, HD)
    attended = pl.pallas_call(
        functools.partial(attend_kernel, wide, plane, rows, early, query_cols),
        out_shape=jax.ShapeDtypeStruct((plane, rows, query_cols), jnp.bfloat16),
        in_specs=[IN_VMEM] * (1 + wide + len(held)),
        out_specs=IN_VMEM,
        compiler_params=params(8),
        cost_estimate=cost(10**10, 4 * MIB),
    )(jnp.asarray(frequency), *partial[::-1], *held)
    head_rows = swap_wide([attended] * wide)
    parts = 2
    order = [0, *range(wide - 2, 0, -1), wide - 1]
    part_cols = out_cols // parts
    sums = []
    for p in range(parts):
        count = owners // 2
        shape = jax.ShapeDtypeStruct((count, rows, part_cols), jnp.float32)
        keep, give = pl.pallas_call(
            functools.partial(output_kernel, p * part_cols, part_cols, order),
            out_shape=(shape, shape),
            in_specs=[IN_VMEM] * (1 + wide),
            out_specs=(IN_VMEM, IN_VMEM),
            compiler_params=params(8),
            cost_estimate=cost(2 * owners * rows * depth * part_cols, 2 * depth * part_cols),
        )(out_weight, *[head_rows[k] for k in order])
        give = swap_plane(give, 1)
        step = 2
        while step < plane:
            count //= 2
            shape = jax.ShapeDtypeStruct((count, rows, part_cols), jnp.float32)
            keep, give = pl.pallas_call(
                halve_kernel,
                out_shape=(shape, shape),
                in_specs=[IN_VMEM, IN_VMEM],
                out_specs=(IN_VMEM, IN_VMEM),
                compiler_params=params(8),
            )(keep, give)
            give = swap_plane(give, step)
            step *= 2
        sums += [keep, give]
    blocks = pl.pallas_call(
        functools.partial(total_kernel, parts),
        out_shape=[jax.ShapeDtypeStruct((rows, out_cols), jnp.bfloat16)] * wide,
        in_specs=[IN_VMEM] * len(sums),
        out_specs=[IN_VMEM] * wide,
        compiler_params=params(8),
    )(*sums)
    blocks = swap_wide(blocks)
    return pl.pallas_call(
        finish_kernel,
        out_shape=jax.ShapeDtypeStruct((rows, wide * out_cols), jnp.bfloat16),
        in_specs=[IN_VMEM] * wide,
        out_specs=IN_VMEM,
        compiler_params=params(8),
    )(*blocks[::-1])


def solution(mesh):
    placed = (
        P(("groups", "gx", "gy", "gz"), None),
        P(),
        P("gx", ("gy", "gz")),
        P("gx", ("gy", "gz")),
        P("gx", ("gy", "gz")),
        P(("gy", "gz"), "gx"),
        P(("groups", "gx", "gy", "gz"), None, None),
        P(("groups", "gx", "gy", "gz"), None, None),
        P(("groups", "gx", "gy", "gz")),
    )
    return jax.shard_map(
        shards,
        mesh=mesh,
        in_specs=placed,
        out_specs=P(("groups", "gx", "gy", "gz"), None),
        check_vma=False,
    )
```

```python
import functools

import jax
import jax.numpy as jnp
import numpy as np
from jax import lax
from jax.experimental import pallas as pl
from jax.experimental.pallas import tpu as pltpu
from jax.sharding import PartitionSpec as P

HD = 128
ROW_AXES = ("gx", "gy", "gz")
PLANE = ("gy", "gz")
MIB = 1024 * 1024
IN_VMEM = pl.BlockSpec(memory_space=pltpu.VMEM)
ANYWHERE = pl.BlockSpec(memory_space=pl.ANY)


def scale_kernel(tokens_ref, scaled_ref):
    tokens = tokens_ref[...].astype(jnp.float32)
    mean_square = jnp.mean(tokens * tokens, -1, keepdims=True)
    scaled_ref[...] = tokens * lax.rsqrt(mean_square + 1e-05)


def gain_kernel(wide, plane, scaled_ref, gain_ref, blocks_ref):
    normed = (scaled_ref[...] * gain_ref[...]).astype(jnp.bfloat16)
    half = normed.shape[1] // wide // 2
    for i in range(wide):
        for j in range(plane):
            at = (2 * i + j % 2) * half
            blocks_ref[i * plane + j] = normed[:, at : at + half]


def project_kernel(own, wide, plane, rows_ref, query_ref, key_ref, value_ref, *refs):
    owners, rows, half = rows_ref.shape
    core = lax.axis_index("gz")
    at_row = pl.multiple_of((core if own else 1 - core) * half, half)
    normed = rows_ref[...].reshape(owners * rows, half)
    sums_ref = refs[-1]
    at = 0
    for weight in (query_ref, key_ref, value_ref):
        cols = weight.shape[1]
        step = min(cols, 256)
        for c in range(0, cols, step):
            part = jnp.dot(
                normed,
                weight[pl.ds(at_row, half), c : c + step],
                preferred_element_type=jnp.float32,
            )
            if own:
                sums_ref[:, at : at + step] = part
            else:
                part = part + refs[1][:, at : at + step]
                sums_ref[:, :, at : at + step] = part.reshape(owners, rows, step)
            at += step
    if not own:
        own_wide = lax.axis_index("gx")
        own_plane = 2 * lax.axis_index("gy") + core
        for k in range(wide):
            for l in range(plane):
                refs[2 + k][l] = sums_ref[(own_wide ^ k) * plane + (own_plane ^ l)]


def own_place():
    return 2 * lax.axis_index("gy") + lax.axis_index("gz")


def write_lengths(rows, lengths_ref, block_ref):
    at_row = lax.broadcasted_iota(jnp.int32, (16, block_ref.shape[1]), 0)
    filled = jnp.zeros(at_row.shape, jnp.float32)
    for r in range(rows):
        filled = jnp.where(at_row == r, lengths_ref[:, r : r + 1].astype(jnp.float32), filled)
    block_ref[block_ref.shape[0] - 16 :] = filled.astype(jnp.bfloat16)


def cut_kernel(plan, lengths_ref, keys_ref, values_ref, _, *blocks):
    rows, slots, _ = keys_ref.shape
    cols = blocks[0].shape[1]
    for (slot, key_rows, value_rows, with_lengths), block in zip(plan, blocks):
        at = pl.multiple_of((own_place() ^ slot) * cols, cols)
        start = 0
        for cache_ref, wanted in ((keys_ref, key_rows), (values_ref, value_rows)):
            for r in wanted:
                block[start : start + slots] = cache_ref[r, :, pl.ds(at, cols)]
                start += slots
        if with_lengths:
            write_lengths(rows, lengths_ref, block)


def early_kernel(early, keys_hbm, values_hbm, *refs):
    blocks, sems = refs[:-1], refs[-1]
    rows, slots, _ = keys_hbm.shape
    cols = blocks[0].shape[1]
    copies = []
    for s, block in enumerate(blocks):
        at = pl.multiple_of((own_place() ^ (2 * s + 2)) * cols, cols)
        wanted = [(keys_hbm, r) for r in range(rows)] + [(values_hbm, r) for r in range(early)]
        for n, (cache, r) in enumerate(wanted):
            copies.append(
                pltpu.make_async_copy(
                    cache.at[r, :, pl.ds(at, cols)],
                    block.at[pl.ds(n * slots, slots)],
                    sems.at[s, n],
                )
            )
    for copy in copies:
        copy.start()
    for copy in copies:
        copy.wait()


def pass_kernel(*refs):
    pass


def attend_kernel(wide, plane, rows, early, query_cols, frequency_ref, *refs):
    partials, held, attended_ref = refs[wide - 1 :: -1], refs[wide:-1], refs[-1]
    even = plane // 2 - 1
    firsts, lasts, whole = held[:even], held[even : 2 * even], held[2 * even :]
    slots = (whole[0].shape[0] - 16) // (2 * rows)
    cols = partials[0].shape[-1]
    kv_cols = (cols - query_cols) // 2
    kv_heads, group = kv_cols // HD, query_cols // kv_cols
    pairs = plane * rows
    count = pairs * kv_heads
    heads = count * group
    scale = 1.0 / HD**0.5
    total = partials[0][...]
    for k in range(1, wide):
        total = total + partials[k][...]
    total = total.reshape(pairs, cols).astype(jnp.bfloat16).astype(jnp.float32)

    def cached(values):
        parts = []
        for p in range(pairs):
            l, r = p // rows, p % rows
            ref, at = whole[(l + 1) // 2], values * rows + r
            if l % 2 == 0 and l:
                ref = firsts[l // 2 - 1]
                if at >= rows + early:
                    ref, at = lasts[l // 2 - 1], at - rows - early
            parts.append(ref[at * slots : (at + 1) * slots])
        return jnp.concatenate(parts, 1)

    filled = []
    for l in range(plane):
        block = lasts[l // 2 - 1] if l % 2 == 0 and l else whole[(l + 1) // 2]
        last = block[block.shape[0] - 16 :, :HD].astype(jnp.float32)
        filled += [last[r : r + 1] for r in range(rows)]
    angles = jnp.concatenate(filled, 0) * frequency_ref[...]
    cosine, sine = jnp.cos(angles), jnp.sin(angles)
    front = lax.broadcasted_iota(jnp.int32, (1, HD), 1) < HD // 2
    sine = jnp.where(front, -sine, sine)

    def rotate(vector):
        return vector * cosine + pltpu.roll(vector, HD // 2, 1) * sine

    query, key_new, value_new = [], [], []
    for h in range(kv_heads):
        turned = [
            rotate(total[:, (h * group + g) * HD : (h * group + g + 1) * HD]) for g in range(group)
        ]
        query.append(jnp.swapaxes(jnp.stack(turned, 0), 0, 1))
        at = query_cols + h * HD
        key_new.append(rotate(total[:, at : at + HD]))
        value_new.append(total[:, at + kv_cols : at + kv_cols + HD])
    query = jnp.stack(query, 1).reshape(heads, HD)
    turned_query = query.T.astype(jnp.bfloat16)
    key_new = jnp.stack(key_new, 1).reshape(count, HD).astype(jnp.bfloat16)
    value_new = jnp.stack(value_new, 1).reshape(count, HD)

    head_pair = lax.broadcasted_iota(jnp.int32, (1, heads), 1) // group
    by_pair = jnp.concatenate(
        [jnp.where(head_pair == b, turned_query, jnp.zeros_like(turned_query)) for b in range(count)],
        0,
    )
    scores = scale * jnp.dot(cached(0), by_pair, preferred_element_type=jnp.float32)
    own = scale * jnp.dot(key_new, turned_query, preferred_element_type=jnp.float32)
    of_pair = lax.broadcasted_iota(jnp.int32, (count, 1), 0) == head_pair
    own = jnp.sum(jnp.where(of_pair, own, 0.0), 0, keepdims=True)
    length = jnp.zeros((1, heads), jnp.float32)
    for p in range(pairs):
        length = jnp.where(head_pair // kv_heads == p, filled[p][:, :1], length)
    slot = lax.broadcasted_iota(jnp.int32, (slots, 1), 0).astype(jnp.float32)
    scores = jnp.where(slot < length, scores, -1e30)
    top = jnp.maximum(jnp.max(scores, 0, keepdims=True), own)
    weights = jnp.exp(scores - top)
    own_weight = jnp.exp(own - top)
    denominator = jnp.sum(weights, 0, keepdims=True) + own_weight
    probability = (weights / denominator).astype(jnp.bfloat16)
    own_prob = (own_weight / denominator).astype(jnp.bfloat16)
    contract_rows = (((0,), (0,)), ((), ()))
    mixed = lax.dot_general(
        probability, cached(1), contract_rows, preferred_element_type=jnp.float32
    )
    own_prob = jnp.where(of_pair, own_prob.astype(jnp.float32), 0.0).astype(jnp.bfloat16)
    fresh = lax.dot_general(
        own_prob, value_new.astype(jnp.bfloat16), contract_rows, preferred_element_type=jnp.float32
    )
    mixed = [
        mixed[b * group : (b + 1) * group, b * HD : (b + 1) * HD]
        + fresh[b * group : (b + 1) * group]
        for b in range(count)
    ]
    attended = []
    for h in range(kv_heads):
        by_head = jnp.swapaxes(jnp.stack(mixed[h::kv_heads], 0), 0, 1)
        attended += [by_head[g] for g in range(group)]
    attended = jnp.concatenate(attended, 1)
    attended_ref[...] = attended.reshape(plane, rows, query_cols).astype(jnp.bfloat16)


def output_kernel(at, cols, order, weight_ref, *refs):
    blocks, keep_ref, give_ref = [refs[n] for n in order], refs[-2], refs[-1]
    wide = len(blocks)
    plane, rows, depth = blocks[0].shape
    attended = jnp.concatenate(
        [block[...].reshape(plane * rows, depth) for block in blocks], 0
    )
    step = min(cols, 512)
    for c in range(0, cols, step):
        part = jnp.dot(
            attended, weight_ref[:, at + c : at + c + step], preferred_element_type=jnp.float32
        )
        part = part.reshape(wide * plane // 2, 2 * rows, step)
        keep_ref[:, :, c : c + step] = part[:, :rows]
        give_ref[:, :, c : c + step] = part[:, rows:]


def halve_kernel(a_ref, b_ref, keep_ref, give_ref):
    for n in range(keep_ref.shape[0]):
        keep_ref[n] = a_ref[2 * n] + b_ref[2 * n]
        give_ref[n] = a_ref[2 * n + 1] + b_ref[2 * n + 1]


def total_kernel(parts, *refs):
    sums, blocks = refs[: 2 * parts], refs[2 * parts :]
    cols = sums[0].shape[-1]
    for p in range(parts):
        for k, block in enumerate(blocks):
            total = sums[2 * p][k] + sums[2 * p + 1][k]
            block[:, p * cols : (p + 1) * cols] = total.astype(jnp.bfloat16)


def finish_kernel(*refs):
    blocks, result_ref = refs[-2::-1], refs[-1]
    own = lax.axis_index("gx")
    cols = blocks[0].shape[-1]
    for k, block in enumerate(blocks):
        at = pl.multiple_of((own ^ k) * cols, cols)
        result_ref[:, pl.ds(at, cols)] = block[...]


def swap_blocks(blocks, axes):
    return lax.all_to_all(blocks, axes, split_axis=0, concat_axis=0, tiled=True)


def swap_pairs(value, axis, step):
    return lax.ppermute(value, axis, [(i, i ^ step) for i in range(lax.axis_size(axis))])


def swap_plane(value, step):
    return lax.ppermute(value, PLANE, [(i, i ^ step) for i in range(lax.axis_size(PLANE))])


def swap_wide(blocks):
    moved = [swap_pairs(blocks[k], "gx", k) for k in range(len(blocks) - 1, 0, -1)]
    return [blocks[0]] + moved[::-1]


def shards(
    tokens,
    norm_gain,
    query_weight,
    key_weight,
    value_weight,
    out_weight,
    cache_keys,
    cache_values,
    lengths,
):
    rows = tokens.shape[0]
    wide = lax.axis_size("gx")
    plane = lax.axis_size(PLANE)
    owners = wide * plane
    width, query_cols = query_weight.shape
    kv_cols = key_weight.shape[1]
    depth, out_cols = out_weight.shape
    cols = query_cols + 2 * kv_cols

    def params(mib):
        return pltpu.CompilerParams(vmem_limit_bytes=mib * MIB)

    def cost(flops, size):
        return pl.CostEstimate(flops=flops, bytes_accessed=size, transcendentals=0)

    half = width // 2
    slots = cache_keys.shape[1]
    even = plane // 2 - 1
    early = rows // 2
    every = range(rows)

    firsts = pl.pallas_call(
        functools.partial(early_kernel, early),
        out_shape=[
            jax.ShapeDtypeStruct(((rows + early) * slots, kv_cols), cache_keys.dtype)
        ] * even,
        in_specs=[ANYWHERE] * 2,
        out_specs=[ANYWHERE] * even,
        scratch_shapes=[pltpu.SemaphoreType.DMA((even, rows + early))],
        compiler_params=params(62),
        cost_estimate=cost(40 * 10**9, MIB),
    )(cache_keys, cache_values)
    firsts = [swap_plane(firsts[s], 2 * s + 2) for s in range(even)]
    scaled = pl.pallas_call(
        scale_kernel,
        out_shape=jax.ShapeDtypeStruct(tokens.shape, jnp.float32),
        in_specs=[IN_VMEM],
        out_specs=IN_VMEM,
        compiler_params=params(8),
        cost_estimate=cost(40 * 10**9, MIB),
    )(tokens)
    normed = pl.pallas_call(
        functools.partial(gain_kernel, wide, plane),
        out_shape=jax.ShapeDtypeStruct((owners, rows, half), jnp.bfloat16),
        in_specs=[IN_VMEM, IN_VMEM],
        out_specs=IN_VMEM,
        compiler_params=params(8),
    )(scaled, norm_gain.reshape(1, -1))
    def cut(plan, after):
        return pl.pallas_call(
            functools.partial(cut_kernel, plan),
            out_shape=[
                jax.ShapeDtypeStruct(
                    ((len(key_rows) + len(value_rows)) * slots + 16 * with_lengths, kv_cols),
                    cache_keys.dtype,
                )
                for _, key_rows, value_rows, with_lengths in plan
            ],
            in_specs=[IN_VMEM] * 4,
            out_specs=[IN_VMEM] * len(plan),
            compiler_params=params(8),
        )(lengths.reshape(1, -1), cache_keys, cache_values, after)

    plan = [(l, (), every[early:], True) for l in range(2, plane, 2)]
    plan += [(l, every, every, True) for l in range(1, plane, 2)]
    rest = cut(plan, normed)
    own_half = swap_blocks(normed, ROW_AXES)
    other_half = swap_pairs(own_half, "gz", 1)
    rest = pl.pallas_call(
        pass_kernel,
        out_shape=[jax.ShapeDtypeStruct(value.shape, value.dtype) for value in rest],
        in_specs=[ANYWHERE] * (len(rest) + even + 1),
        out_specs=[ANYWHERE] * len(rest),
        input_output_aliases={n: n for n in range(len(rest))},
        compiler_params=params(1),
    )(*rest, own_half, *firsts)
    lasts = [swap_plane(rest[s], 2 * s + 2) for s in range(even)]
    odd = [swap_plane(rest[even + s], 2 * s + 1) for s in range(even + 1)]
    (mine,) = cut([(0, every, every, True)], own_half)
    held = [*firsts, *lasts, mine, *odd]
    weights = (query_weight, key_weight, value_weight)
    half_cost = cost(owners * rows * width * cols, width * cols)
    partial = pl.pallas_call(
        functools.partial(project_kernel, True, wide, plane),
        out_shape=jax.ShapeDtypeStruct((owners * rows, cols), jnp.float32),
        in_specs=[IN_VMEM] * 4,
        out_specs=IN_VMEM,
        compiler_params=params(8),
        cost_estimate=half_cost,
    )(own_half, *weights)
    partial = pl.pallas_call(
        functools.partial(project_kernel, False, wide, plane),
        out_shape=[jax.ShapeDtypeStruct((plane, rows, cols), jnp.float32)] * wide,
        in_specs=[IN_VMEM] * 6,
        out_specs=[IN_VMEM] * wide,
        scratch_shapes=[pltpu.VMEM((owners, rows, cols), jnp.float32)],
        compiler_params=params(8),
        cost_estimate=half_cost,
    )(other_half, *weights, odd[0], partial)
    partial = swap_wide(partial)

    half_dim = HD // 2
    frequency = 500000.0 ** (-np.arange(half_dim, dtype=np.float64) / half_dim)
    frequency = np.tile(frequency.astype(np.float32), 2).reshape(1, HD)
    attended = pl.pallas_call(
        functools.partial(attend_kernel, wide, plane, rows, early, query_cols),
        out_shape=jax.ShapeDtypeStruct((plane, rows, query_cols), jnp.bfloat16),
        in_specs=[IN_VMEM] * (1 + wide + len(held)),
        out_specs=IN_VMEM,
        compiler_params=params(8),
        cost_estimate=cost(10**10, 4 * MIB),
    )(jnp.asarray(frequency), *partial[::-1], *held)
    head_rows = swap_wide([attended] * wide)
    parts = 2
    order = [0, *range(wide - 2, 0, -1), wide - 1]
    part_cols = out_cols // parts
    sums = []
    for p in range(parts):
        count = owners // 2
        shape = jax.ShapeDtypeStruct((count, rows, part_cols), jnp.float32)
        keep, give = pl.pallas_call(
            functools.partial(output_kernel, p * part_cols, part_cols, order),
            out_shape=(shape, shape),
            in_specs=[IN_VMEM] * (1 + wide),
            out_specs=(IN_VMEM, IN_VMEM),
            compiler_params=params(8),
            cost_estimate=cost(2 * owners * rows * depth * part_cols, 2 * depth * part_cols),
        )(out_weight, *[head_rows[k] for k in order])
        give = swap_plane(give, 1)
        step = 2
        while step < plane:
            count //= 2
            shape = jax.ShapeDtypeStruct((count, rows, part_cols), jnp.float32)
            keep, give = pl.pallas_call(
                halve_kernel,
                out_shape=(shape, shape),
                in_specs=[IN_VMEM, IN_VMEM],
                out_specs=(IN_VMEM, IN_VMEM),
                compiler_params=params(8),
            )(keep, give)
            give = swap_plane(give, step)
            step *= 2
        sums += [keep, give]
    blocks = pl.pallas_call(
        functools.partial(total_kernel, parts),
        out_shape=[jax.ShapeDtypeStruct((rows, out_cols), jnp.bfloat16)] * wide,
        in_specs=[IN_VMEM] * len(sums),
        out_specs=[IN_VMEM] * wide,
        compiler_params=params(8),
    )(*sums)
    blocks = swap_wide(blocks)
    return pl.pallas_call(
        finish_kernel,
        out_shape=jax.ShapeDtypeStruct((rows, wide * out_cols), jnp.bfloat16),
        in_specs=[IN_VMEM] * wide,
        out_specs=IN_VMEM,
        compiler_params=params(8),
    )(*blocks[::-1])


def solution(mesh):
    placed = (
        P(("groups", "gx", "gy", "gz"), None),
        P(),
        P("gx", ("gy", "gz")),
        P("gx", ("gy", "gz")),
        P("gx", ("gy", "gz")),
        P(("gy", "gz"), "gx"),
        P(("groups", "gx", "gy", "gz"), None, None),
        P(("groups", "gx", "gy", "gz"), None, None),
        P(("groups", "gx", "gy", "gz")),
    )
    return jax.shard_map(
        shards,
        mesh=mesh,
        in_specs=placed,
        out_specs=P(("groups", "gx", "gy", "gz"), None),
        check_vma=False,
    )
```

```python
import functools

import jax
import jax.numpy as jnp
import numpy as np
from jax import lax
from jax.experimental import pallas as pl
from jax.experimental.pallas import tpu as pltpu
from jax.sharding import PartitionSpec as P

HD = 128
ROW_AXES = ("gx", "gy", "gz")
PLANE = ("gy", "gz")
MIB = 1024 * 1024
IN_VMEM = pl.BlockSpec(memory_space=pltpu.VMEM)
ANYWHERE = pl.BlockSpec(memory_space=pl.ANY)


def scale_kernel(tokens_ref, scaled_ref):
    tokens = tokens_ref[...].astype(jnp.float32)
    mean_square = jnp.mean(tokens * tokens, -1, keepdims=True)
    scaled_ref[...] = tokens * lax.rsqrt(mean_square + 1e-05)


def gain_kernel(wide, plane, scaled_ref, gain_ref, _, blocks_ref):
    normed = (scaled_ref[...] * gain_ref[...]).astype(jnp.bfloat16)
    half = normed.shape[1] // wide // 2
    for i in range(wide):
        for j in range(plane):
            at = (2 * i + j % 2) * half
            blocks_ref[i * plane + j] = normed[:, at : at + half]


def project_kernel(own, wide, plane, rows_ref, query_ref, key_ref, value_ref, *refs):
    owners, rows, half = rows_ref.shape
    core = lax.axis_index("gz")
    at_row = pl.multiple_of((core if own else 1 - core) * half, half)
    normed = rows_ref[...].reshape(owners * rows, half)
    sums_ref = refs[-1]
    at = 0
    for weight in (query_ref, key_ref, value_ref):
        cols = weight.shape[1]
        step = min(cols, 256)
        for c in range(0, cols, step):
            part = jnp.dot(
                normed,
                weight[pl.ds(at_row, half), c : c + step],
                preferred_element_type=jnp.float32,
            )
            if own:
                sums_ref[:, at : at + step] = part
            else:
                part = part + refs[1][:, at : at + step]
                sums_ref[:, :, at : at + step] = part.reshape(owners, rows, step)
            at += step
    if not own:
        own_wide = lax.axis_index("gx")
        own_plane = 2 * lax.axis_index("gy") + core
        for k in range(wide):
            for l in range(plane):
                refs[2 + k][l] = sums_ref[(own_wide ^ k) * plane + (own_plane ^ l)]


def own_place():
    return 2 * lax.axis_index("gy") + lax.axis_index("gz")


def write_lengths(rows, lengths_ref, block_ref):
    at_row = lax.broadcasted_iota(jnp.int32, (16, block_ref.shape[1]), 0)
    filled = jnp.zeros(at_row.shape, jnp.float32)
    for r in range(rows):
        filled = jnp.where(at_row == r, lengths_ref[:, r : r + 1].astype(jnp.float32), filled)
    block_ref[block_ref.shape[0] - 16 :] = filled.astype(jnp.bfloat16)


def cut_kernel(plan, lengths_ref, keys_ref, values_ref, _, *blocks):
    rows, slots, _ = keys_ref.shape
    cols = blocks[0].shape[1]
    for (slot, key_rows, value_rows, with_lengths), block in zip(plan, blocks):
        at = pl.multiple_of((own_place() ^ slot) * cols, cols)
        start = 0
        for cache_ref, wanted in ((keys_ref, key_rows), (values_ref, value_rows)):
            for r in wanted:
                block[start : start + slots] = cache_ref[r, :, pl.ds(at, cols)]
                start += slots
        if with_lengths:
            write_lengths(rows, lengths_ref, block)


def early_kernel(early, keys_ref, *blocks):
    rows, slots, _ = keys_ref.shape
    cols = blocks[0].shape[1]
    for s, block in enumerate(blocks):
        wanted = [(2 * s + 2, r) for r in range(rows)] + [(2 * s + 3, r) for r in range(early)]
        for n, (slot, r) in enumerate(wanted):
            at = pl.multiple_of((own_place() ^ slot) * cols, cols)
            block[n * slots : (n + 1) * slots] = keys_ref[r, :, pl.ds(at, cols)]


def near_kernel(early, lengths_ref, keys_ref, values_ref, _, *refs):
    firsts, near_ref = refs[:-1], refs[-1]
    rows, slots, _ = keys_ref.shape
    cols = near_ref.shape[1]
    at = pl.multiple_of((own_place() ^ 1) * cols, cols)
    n = 0
    for cache_ref in (keys_ref, values_ref):
        for r in range(rows):
            near_ref[n * slots : (n + 1) * slots] = cache_ref[r, :, pl.ds(at, cols)]
            n += 1
    for first in firsts:
        near_ref[n * slots : (n + early) * slots] = first[rows * slots :]
        n += early
    write_lengths(rows, lengths_ref, near_ref)


def pass_kernel(*refs):
    pass


def attend_kernel(wide, plane, rows, early, query_cols, frequency_ref, *refs):
    partials, held, attended_ref = refs[wide - 1 :: -1], refs[wide:-1], refs[-1]
    even = plane // 2 - 1
    mine, near = held[:2]
    firsts, lasts, odds = held[2 : 2 + even], held[2 + even : 2 + 2 * even], held[2 + 2 * even :]
    slots = (mine.shape[0] - 16) // (2 * rows)

    def place(l, values, r):
        s = l // 2 - 1
        if l < 2:
            return (mine, near)[l], values * rows + r
        if l % 2 == 0:
            return (lasts if values else firsts)[s], r
        if values:
            return odds[s], rows - early + r
        return (near, 2 * rows + s * early + r) if r < early else (odds[s], r - early)

    cols = partials[0].shape[-1]
    kv_cols = (cols - query_cols) // 2
    kv_heads, group = kv_cols // HD, query_cols // kv_cols
    pairs = plane * rows
    count = pairs * kv_heads
    heads = count * group
    scale = 1.0 / HD**0.5
    total = partials[0][...]
    for k in range(1, wide):
        total = total + partials[k][...]
    total = total.reshape(pairs, cols).astype(jnp.bfloat16).astype(jnp.float32)

    def cached(values):
        parts = []
        for p in range(pairs):
            ref, at = place(p // rows, values, p % rows)
            parts.append(ref[at * slots : (at + 1) * slots])
        return jnp.concatenate(parts, 1)

    filled = []
    for l in range(plane):
        block = place(l, 1, 0)[0]
        last = block[block.shape[0] - 16 :, :HD].astype(jnp.float32)
        filled += [last[r : r + 1] for r in range(rows)]
    angles = jnp.concatenate(filled, 0) * frequency_ref[...]
    cosine, sine = jnp.cos(angles), jnp.sin(angles)
    front = lax.broadcasted_iota(jnp.int32, (1, HD), 1) < HD // 2
    sine = jnp.where(front, -sine, sine)

    def rotate(vector):
        return vector * cosine + pltpu.roll(vector, HD // 2, 1) * sine

    query, key_new, value_new = [], [], []
    for h in range(kv_heads):
        turned = [
            rotate(total[:, (h * group + g) * HD : (h * group + g + 1) * HD]) for g in range(group)
        ]
        query.append(jnp.swapaxes(jnp.stack(turned, 0), 0, 1))
        at = query_cols + h * HD
        key_new.append(rotate(total[:, at : at + HD]))
        value_new.append(total[:, at + kv_cols : at + kv_cols + HD])
    query = jnp.stack(query, 1).reshape(heads, HD)
    turned_query = query.T.astype(jnp.bfloat16)
    key_new = jnp.stack(key_new, 1).reshape(count, HD).astype(jnp.bfloat16)
    value_new = jnp.stack(value_new, 1).reshape(count, HD)

    head_pair = lax.broadcasted_iota(jnp.int32, (1, heads), 1) // group
    by_pair = jnp.concatenate(
        [jnp.where(head_pair == b, turned_query, jnp.zeros_like(turned_query)) for b in range(count)],
        0,
    )
    scores = scale * jnp.dot(cached(0), by_pair, preferred_element_type=jnp.float32)
    own = scale * jnp.dot(key_new, turned_query, preferred_element_type=jnp.float32)
    of_pair = lax.broadcasted_iota(jnp.int32, (count, 1), 0) == head_pair
    own = jnp.sum(jnp.where(of_pair, own, 0.0), 0, keepdims=True)
    length = jnp.zeros((1, heads), jnp.float32)
    for p in range(pairs):
        length = jnp.where(head_pair // kv_heads == p, filled[p][:, :1], length)
    slot = lax.broadcasted_iota(jnp.int32, (slots, 1), 0).astype(jnp.float32)
    scores = jnp.where(slot < length, scores, -1e30)
    top = jnp.maximum(jnp.max(scores, 0, keepdims=True), own)
    weights = jnp.exp(scores - top)
    own_weight = jnp.exp(own - top)
    denominator = jnp.sum(weights, 0, keepdims=True) + own_weight
    probability = (weights / denominator).astype(jnp.bfloat16)
    own_prob = (own_weight / denominator).astype(jnp.bfloat16)
    contract_rows = (((0,), (0,)), ((), ()))
    mixed = lax.dot_general(
        probability, cached(1), contract_rows, preferred_element_type=jnp.float32
    )
    own_prob = jnp.where(of_pair, own_prob.astype(jnp.float32), 0.0).astype(jnp.bfloat16)
    fresh = lax.dot_general(
        own_prob, value_new.astype(jnp.bfloat16), contract_rows, preferred_element_type=jnp.float32
    )
    mixed = [
        mixed[b * group : (b + 1) * group, b * HD : (b + 1) * HD]
        + fresh[b * group : (b + 1) * group]
        for b in range(count)
    ]
    attended = []
    for h in range(kv_heads):
        by_head = jnp.swapaxes(jnp.stack(mixed[h::kv_heads], 0), 0, 1)
        attended += [by_head[g] for g in range(group)]
    attended = jnp.concatenate(attended, 1)
    attended_ref[...] = attended.reshape(plane, rows, query_cols).astype(jnp.bfloat16)


def output_kernel(at, cols, order, weight_ref, *refs):
    blocks, keep_ref, give_ref = [refs[n] for n in order], refs[-2], refs[-1]
    wide = len(blocks)
    plane, rows, depth = blocks[0].shape
    attended = jnp.concatenate(
        [block[...].reshape(plane * rows, depth) for block in blocks], 0
    )
    step = min(cols, 512)
    for c in range(0, cols, step):
        part = jnp.dot(
            attended, weight_ref[:, at + c : at + c + step], preferred_element_type=jnp.float32
        )
        part = part.reshape(wide * plane // 2, 2 * rows, step)
        keep_ref[:, :, c : c + step] = part[:, :rows]
        give_ref[:, :, c : c + step] = part[:, rows:]


def halve_kernel(a_ref, b_ref, keep_ref, give_ref):
    for n in range(keep_ref.shape[0]):
        keep_ref[n] = a_ref[2 * n] + b_ref[2 * n]
        give_ref[n] = a_ref[2 * n + 1] + b_ref[2 * n + 1]


def total_kernel(parts, *refs):
    sums, blocks = refs[: 2 * parts], refs[2 * parts :]
    cols = sums[0].shape[-1]
    for p in range(parts):
        for k, block in enumerate(blocks):
            total = sums[2 * p][k] + sums[2 * p + 1][k]
            block[:, p * cols : (p + 1) * cols] = total.astype(jnp.bfloat16)


def finish_kernel(*refs):
    blocks, result_ref = refs[-2::-1], refs[-1]
    own = lax.axis_index("gx")
    cols = blocks[0].shape[-1]
    for k, block in enumerate(blocks):
        at = pl.multiple_of((own ^ k) * cols, cols)
        result_ref[:, pl.ds(at, cols)] = block[...]


def swap_blocks(blocks, axes):
    return lax.all_to_all(blocks, axes, split_axis=0, concat_axis=0, tiled=True)


def swap_pairs(value, axis, step):
    return lax.ppermute(value, axis, [(i, i ^ step) for i in range(lax.axis_size(axis))])


def swap_plane(value, step):
    return lax.ppermute(value, PLANE, [(i, i ^ step) for i in range(lax.axis_size(PLANE))])


def swap_wide(blocks):
    moved = [swap_pairs(blocks[k], "gx", k) for k in range(len(blocks) - 1, 0, -1)]
    return [blocks[0]] + moved[::-1]


def shards(
    tokens,
    norm_gain,
    query_weight,
    key_weight,
    value_weight,
    out_weight,
    cache_keys,
    cache_values,
    lengths,
):
    rows = tokens.shape[0]
    wide = lax.axis_size("gx")
    plane = lax.axis_size(PLANE)
    owners = wide * plane
    width, query_cols = query_weight.shape
    kv_cols = key_weight.shape[1]
    depth, out_cols = out_weight.shape
    cols = query_cols + 2 * kv_cols

    def params(mib):
        return pltpu.CompilerParams(vmem_limit_bytes=mib * MIB)

    def cost(flops, size):
        return pl.CostEstimate(flops=flops, bytes_accessed=size, transcendentals=0)

    half = width // 2
    slots = cache_keys.shape[1]
    even = plane // 2 - 1
    early = rows // 2
    every = range(rows)

    firsts = pl.pallas_call(
        functools.partial(early_kernel, early),
        out_shape=[
            jax.ShapeDtypeStruct(((rows + early) * slots, kv_cols), cache_keys.dtype)
        ] * even,
        in_specs=[IN_VMEM],
        out_specs=[IN_VMEM] * even,
        compiler_params=params(8),
        cost_estimate=cost(40 * 10**9, MIB),
    )(cache_keys)
    firsts = [swap_plane(firsts[s], 2 * s + 2) for s in range(even)]
    scaled = pl.pallas_call(
        scale_kernel,
        out_shape=jax.ShapeDtypeStruct(tokens.shape, jnp.float32),
        in_specs=[IN_VMEM],
        out_specs=IN_VMEM,
        compiler_params=params(8),
        cost_estimate=cost(40 * 10**9, MIB),
    )(tokens)
    def cut(plan, after):
        return pl.pallas_call(
            functools.partial(cut_kernel, plan),
            out_shape=[
                jax.ShapeDtypeStruct(
                    ((len(key_rows) + len(value_rows)) * slots + 16 * with_lengths, kv_cols),
                    cache_keys.dtype,
                )
                for _, key_rows, value_rows, with_lengths in plan
            ],
            in_specs=[IN_VMEM] * 4,
            out_specs=[IN_VMEM] * len(plan),
            compiler_params=params(8),
        )(lengths.reshape(1, -1), cache_keys, cache_values, after)

    plan = [(l, (), every, True) for l in range(2, plane, 2)]
    plan += [(l, every[early:], every, True) for l in range(3, plane, 2)]
    rest = cut(plan, scaled)
    normed = pl.pallas_call(
        functools.partial(gain_kernel, wide, plane),
        out_shape=jax.ShapeDtypeStruct((owners, rows, half), jnp.bfloat16),
        in_specs=[IN_VMEM] * 3,
        out_specs=IN_VMEM,
        compiler_params=params(8),
    )(scaled, norm_gain.reshape(1, -1), rest[0])
    own_half = swap_blocks(normed, ROW_AXES)
    other_half = swap_pairs(own_half, "gz", 1)
    rest = pl.pallas_call(
        pass_kernel,
        out_shape=[jax.ShapeDtypeStruct(value.shape, value.dtype) for value in rest],
        in_specs=[ANYWHERE] * (len(rest) + even + 1),
        out_specs=[ANYWHERE] * len(rest),
        input_output_aliases={n: n for n in range(len(rest))},
        compiler_params=params(1),
    )(*rest, own_half, *firsts)
    lasts = [swap_plane(rest[s], 2 * s + 2) for s in range(even)]
    odds = [swap_plane(rest[even + s], 2 * s + 3) for s in range(even)]
    near = pl.pallas_call(
        functools.partial(near_kernel, early),
        out_shape=jax.ShapeDtypeStruct(
            ((2 * rows + even * early) * slots + 16, kv_cols), cache_keys.dtype
        ),
        in_specs=[IN_VMEM] * (4 + even),
        out_specs=IN_VMEM,
        compiler_params=params(8),
    )(lengths.reshape(1, -1), cache_keys, cache_values, rest[0], *firsts)
    near = swap_plane(near, 1)
    (mine,) = cut([(0, every, every, True)], own_half)
    held = [mine, near, *firsts, *lasts, *odds]
    weights = (query_weight, key_weight, value_weight)
    half_cost = cost(owners * rows * width * cols, width * cols)
    partial = pl.pallas_call(
        functools.partial(project_kernel, True, wide, plane),
        out_shape=jax.ShapeDtypeStruct((owners * rows, cols), jnp.float32),
        in_specs=[IN_VMEM] * 4,
        out_specs=IN_VMEM,
        compiler_params=params(8),
        cost_estimate=half_cost,
    )(own_half, *weights)
    partial = pl.pallas_call(
        functools.partial(project_kernel, False, wide, plane),
        out_shape=[jax.ShapeDtypeStruct((plane, rows, cols), jnp.float32)] * wide,
        in_specs=[IN_VMEM] * 6,
        out_specs=[IN_VMEM] * wide,
        scratch_shapes=[pltpu.VMEM((owners, rows, cols), jnp.float32)],
        compiler_params=params(8),
        cost_estimate=half_cost,
    )(other_half, *weights, near, partial)
    partial = swap_wide(partial)

    half_dim = HD // 2
    frequency = 500000.0 ** (-np.arange(half_dim, dtype=np.float64) / half_dim)
    frequency = np.tile(frequency.astype(np.float32), 2).reshape(1, HD)
    attended = pl.pallas_call(
        functools.partial(attend_kernel, wide, plane, rows, early, query_cols),
        out_shape=jax.ShapeDtypeStruct((plane, rows, query_cols), jnp.bfloat16),
        in_specs=[IN_VMEM] * (1 + wide + len(held)),
        out_specs=IN_VMEM,
        compiler_params=params(8),
        cost_estimate=cost(10**10, 4 * MIB),
    )(jnp.asarray(frequency), *partial[::-1], *held)
    head_rows = swap_wide([attended] * wide)
    parts = 2
    order = [0, *range(wide - 2, 0, -1), wide - 1]
    part_cols = out_cols // parts
    sums = []
    for p in range(parts):
        count = owners // 2
        shape = jax.ShapeDtypeStruct((count, rows, part_cols), jnp.float32)
        keep, give = pl.pallas_call(
            functools.partial(output_kernel, p * part_cols, part_cols, order),
            out_shape=(shape, shape),
            in_specs=[IN_VMEM] * (1 + wide),
            out_specs=(IN_VMEM, IN_VMEM),
            compiler_params=params(8),
            cost_estimate=cost(2 * owners * rows * depth * part_cols, 2 * depth * part_cols),
        )(out_weight, *[head_rows[k] for k in order])
        give = swap_plane(give, 1)
        step = 2
        while step < plane:
            count //= 2
            shape = jax.ShapeDtypeStruct((count, rows, part_cols), jnp.float32)
            keep, give = pl.pallas_call(
                halve_kernel,
                out_shape=(shape, shape),
                in_specs=[IN_VMEM, IN_VMEM],
                out_specs=(IN_VMEM, IN_VMEM),
                compiler_params=params(8),
            )(keep, give)
            give = swap_plane(give, step)
            step *= 2
        sums += [keep, give]
    blocks = pl.pallas_call(
        functools.partial(total_kernel, parts),
        out_shape=[jax.ShapeDtypeStruct((rows, out_cols), jnp.bfloat16)] * wide,
        in_specs=[IN_VMEM] * len(sums),
        out_specs=[IN_VMEM] * wide,
        compiler_params=params(8),
    )(*sums)
    blocks = swap_wide(blocks)
    return pl.pallas_call(
        finish_kernel,
        out_shape=jax.ShapeDtypeStruct((rows, wide * out_cols), jnp.bfloat16),
        in_specs=[IN_VMEM] * wide,
        out_specs=IN_VMEM,
        compiler_params=params(8),
    )(*blocks[::-1])


def solution(mesh):
    placed = (
        P(("groups", "gx", "gy", "gz"), None),
        P(),
        P("gx", ("gy", "gz")),
        P("gx", ("gy", "gz")),
        P("gx", ("gy", "gz")),
        P(("gy", "gz"), "gx"),
        P(("groups", "gx", "gy", "gz"), None, None),
        P(("groups", "gx", "gy", "gz"), None, None),
        P(("groups", "gx", "gy", "gz")),
    )
    return jax.shard_map(
        shards,
        mesh=mesh,
        in_specs=placed,
        out_specs=P(("groups", "gx", "gy", "gz"), None),
        check_vma=False,
    )
```

```python
import functools

import jax
import jax.numpy as jnp
import numpy as np
from jax import lax
from jax.experimental import pallas as pl
from jax.experimental.pallas import tpu as pltpu
from jax.sharding import PartitionSpec as P

HD = 128
ROW_AXES = ("gx", "gy", "gz")
PLANE = ("gy", "gz")
MIB = 1024 * 1024
IN_VMEM = pl.BlockSpec(memory_space=pltpu.VMEM)
ANYWHERE = pl.BlockSpec(memory_space=pl.ANY)


def scale_kernel(tokens_ref, scaled_ref):
    tokens = tokens_ref[...].astype(jnp.float32)
    mean_square = jnp.mean(tokens * tokens, -1, keepdims=True)
    scaled_ref[...] = tokens * lax.rsqrt(mean_square + 1e-05)


def gain_kernel(wide, plane, scaled_ref, gain_ref, blocks_ref):
    normed = (scaled_ref[...] * gain_ref[...]).astype(jnp.bfloat16)
    half = normed.shape[1] // wide // 2
    for i in range(wide):
        for j in range(plane):
            at = (2 * i + j % 2) * half
            blocks_ref[i * plane + j] = normed[:, at : at + half]


def project_kernel(own, wide, plane, rows_ref, query_ref, key_ref, value_ref, *refs):
    owners, rows, half = rows_ref.shape
    core = lax.axis_index("gz")
    at_row = pl.multiple_of((core if own else 1 - core) * half, half)
    normed = rows_ref[...].reshape(owners * rows, half)
    sums_ref = refs[-1]
    at = 0
    for weight in (query_ref, key_ref, value_ref):
        cols = weight.shape[1]
        step = min(cols, 256)
        for c in range(0, cols, step):
            part = jnp.dot(
                normed,
                weight[pl.ds(at_row, half), c : c + step],
                preferred_element_type=jnp.float32,
            )
            if own:
                sums_ref[:, at : at + step] = part
            else:
                part = part + refs[1][:, at : at + step]
                sums_ref[:, :, at : at + step] = part.reshape(owners, rows, step)
            at += step
    if not own:
        own_wide = lax.axis_index("gx")
        own_plane = 2 * lax.axis_index("gy") + core
        for k in range(wide):
            for l in range(plane):
                refs[2 + k][l] = sums_ref[(own_wide ^ k) * plane + (own_plane ^ l)]


def own_place():
    return 2 * lax.axis_index("gy") + lax.axis_index("gz")


def write_lengths(rows, lengths_ref, block_ref):
    at_row = lax.broadcasted_iota(jnp.int32, (16, block_ref.shape[1]), 0)
    filled = jnp.zeros(at_row.shape, jnp.float32)
    for r in range(rows):
        filled = jnp.where(at_row == r, lengths_ref[:, r : r + 1].astype(jnp.float32), filled)
    block_ref[block_ref.shape[0] - 16 :] = filled.astype(jnp.bfloat16)


def cut_kernel(plan, lengths_ref, keys_ref, values_ref, _, *blocks):
    rows, slots, _ = keys_ref.shape
    cols = blocks[0].shape[1]
    for (slot, key_rows, value_rows, with_lengths), block in zip(plan, blocks):
        at = pl.multiple_of((own_place() ^ slot) * cols, cols)
        start = 0
        for cache_ref, wanted in ((keys_ref, key_rows), (values_ref, value_rows)):
            for r in wanted:
                block[start : start + slots] = cache_ref[r, :, pl.ds(at, cols)]
                start += slots
        if with_lengths:
            write_lengths(rows, lengths_ref, block)


def pass_kernel(*refs):
    pass


def attend_kernel(wide, plane, rows, early, query_cols, frequency_ref, *refs):
    partials, held, attended_ref = refs[wide - 1 :: -1], refs[wide:-1], refs[-1]
    even = plane // 2 - 1
    firsts, lasts, whole = held[:even], held[even : 2 * even], held[2 * even :]
    slots = (whole[0].shape[0] - 16) // (2 * rows)
    cols = partials[0].shape[-1]
    kv_cols = (cols - query_cols) // 2
    kv_heads, group = kv_cols // HD, query_cols // kv_cols
    pairs = plane * rows
    count = pairs * kv_heads
    heads = count * group
    scale = 1.0 / HD**0.5
    total = partials[0][...]
    for k in range(1, wide):
        total = total + partials[k][...]
    total = total.reshape(pairs, cols).astype(jnp.bfloat16).astype(jnp.float32)

    def cached(values):
        parts = []
        for p in range(pairs):
            l, r = p // rows, p % rows
            ref, at = whole[(l + 1) // 2], values * rows + r
            if l % 2 == 0 and l:
                ref = firsts[l // 2 - 1]
                if at >= rows + early:
                    ref, at = lasts[l // 2 - 1], at - rows - early
            parts.append(ref[at * slots : (at + 1) * slots])
        return jnp.concatenate(parts, 1)

    filled = []
    for l in range(plane):
        block = lasts[l // 2 - 1] if l % 2 == 0 and l else whole[(l + 1) // 2]
        last = block[block.shape[0] - 16 :, :HD].astype(jnp.float32)
        filled += [last[r : r + 1] for r in range(rows)]
    angles = jnp.concatenate(filled, 0) * frequency_ref[...]
    cosine, sine = jnp.cos(angles), jnp.sin(angles)
    front = lax.broadcasted_iota(jnp.int32, (1, HD), 1) < HD // 2
    sine = jnp.where(front, -sine, sine)

    def rotate(vector):
        return vector * cosine + pltpu.roll(vector, HD // 2, 1) * sine

    query, key_new, value_new = [], [], []
    for h in range(kv_heads):
        turned = [
            rotate(total[:, (h * group + g) * HD : (h * group + g + 1) * HD]) for g in range(group)
        ]
        query.append(jnp.swapaxes(jnp.stack(turned, 0), 0, 1))
        at = query_cols + h * HD
        key_new.append(rotate(total[:, at : at + HD]))
        value_new.append(total[:, at + kv_cols : at + kv_cols + HD])
    query = jnp.stack(query, 1).reshape(heads, HD)
    turned_query = query.T.astype(jnp.bfloat16)
    key_new = jnp.stack(key_new, 1).reshape(count, HD).astype(jnp.bfloat16)
    value_new = jnp.stack(value_new, 1).reshape(count, HD)

    head_pair = lax.broadcasted_iota(jnp.int32, (1, heads), 1) // group
    by_pair = jnp.concatenate(
        [jnp.where(head_pair == b, turned_query, jnp.zeros_like(turned_query)) for b in range(count)],
        0,
    )
    scores = scale * jnp.dot(cached(0), by_pair, preferred_element_type=jnp.float32)
    own = scale * jnp.dot(key_new, turned_query, preferred_element_type=jnp.float32)
    of_pair = lax.broadcasted_iota(jnp.int32, (count, 1), 0) == head_pair
    own = jnp.sum(jnp.where(of_pair, own, 0.0), 0, keepdims=True)
    length = jnp.zeros((1, heads), jnp.float32)
    for p in range(pairs):
        length = jnp.where(head_pair // kv_heads == p, filled[p][:, :1], length)
    slot = lax.broadcasted_iota(jnp.int32, (slots, 1), 0).astype(jnp.float32)
    scores = jnp.where(slot < length, scores, -1e30)
    top = jnp.maximum(jnp.max(scores, 0, keepdims=True), own)
    weights = jnp.exp(scores - top)
    own_weight = jnp.exp(own - top)
    denominator = jnp.sum(weights, 0, keepdims=True) + own_weight
    probability = (weights / denominator).astype(jnp.bfloat16)
    own_prob = (own_weight / denominator).astype(jnp.bfloat16)
    contract_rows = (((0,), (0,)), ((), ()))
    mixed = lax.dot_general(
        probability, cached(1), contract_rows, preferred_element_type=jnp.float32
    )
    own_prob = jnp.where(of_pair, own_prob.astype(jnp.float32), 0.0).astype(jnp.bfloat16)
    fresh = lax.dot_general(
        own_prob, value_new.astype(jnp.bfloat16), contract_rows, preferred_element_type=jnp.float32
    )
    mixed = [
        mixed[b * group : (b + 1) * group, b * HD : (b + 1) * HD]
        + fresh[b * group : (b + 1) * group]
        for b in range(count)
    ]
    attended = []
    for h in range(kv_heads):
        by_head = jnp.swapaxes(jnp.stack(mixed[h::kv_heads], 0), 0, 1)
        attended += [by_head[g] for g in range(group)]
    attended = jnp.concatenate(attended, 1)
    attended_ref[...] = attended.reshape(plane, rows, query_cols).astype(jnp.bfloat16)


def output_kernel(at, cols, order, weight_ref, *refs):
    blocks, keep_ref, give_ref = [refs[n] for n in order], refs[-2], refs[-1]
    wide = len(blocks)
    plane, rows, depth = blocks[0].shape
    attended = jnp.concatenate(
        [block[...].reshape(plane * rows, depth) for block in blocks], 0
    )
    step = min(cols, 512)
    for c in range(0, cols, step):
        part = jnp.dot(
            attended, weight_ref[:, at + c : at + c + step], preferred_element_type=jnp.float32
        )
        part = part.reshape(wide * plane // 2, 2 * rows, step)
        keep_ref[:, :, c : c + step] = part[:, :rows]
        give_ref[:, :, c : c + step] = part[:, rows:]


def halve_kernel(a_ref, b_ref, keep_ref, give_ref):
    for n in range(keep_ref.shape[0]):
        keep_ref[n] = a_ref[2 * n] + b_ref[2 * n]
        give_ref[n] = a_ref[2 * n + 1] + b_ref[2 * n + 1]


def total_kernel(parts, *refs):
    sums, blocks = refs[: 2 * parts], refs[2 * parts :]
    cols = sums[0].shape[-1]
    for p in range(parts):
        for k, block in enumerate(blocks):
            total = sums[2 * p][k] + sums[2 * p + 1][k]
            block[:, p * cols : (p + 1) * cols] = total.astype(jnp.bfloat16)


def finish_kernel(*refs):
    blocks, result_ref = refs[-2::-1], refs[-1]
    own = lax.axis_index("gx")
    cols = blocks[0].shape[-1]
    for k, block in enumerate(blocks):
        at = pl.multiple_of((own ^ k) * cols, cols)
        result_ref[:, pl.ds(at, cols)] = block[...]


def swap_blocks(blocks, axes):
    return lax.all_to_all(blocks, axes, split_axis=0, concat_axis=0, tiled=True)


def swap_pairs(value, axis, step):
    return lax.ppermute(value, axis, [(i, i ^ step) for i in range(lax.axis_size(axis))])


def swap_plane(value, step):
    return lax.ppermute(value, PLANE, [(i, i ^ step) for i in range(lax.axis_size(PLANE))])


def swap_wide(blocks):
    moved = [swap_pairs(blocks[k], "gx", k) for k in range(len(blocks) - 1, 0, -1)]
    return [blocks[0]] + moved[::-1]


def shards(
    tokens,
    norm_gain,
    query_weight,
    key_weight,
    value_weight,
    out_weight,
    cache_keys,
    cache_values,
    lengths,
):
    rows = tokens.shape[0]
    wide = lax.axis_size("gx")
    plane = lax.axis_size(PLANE)
    owners = wide * plane
    width, query_cols = query_weight.shape
    kv_cols = key_weight.shape[1]
    depth, out_cols = out_weight.shape
    cols = query_cols + 2 * kv_cols

    def params(mib):
        return pltpu.CompilerParams(vmem_limit_bytes=mib * MIB)

    def cost(flops, size):
        return pl.CostEstimate(flops=flops, bytes_accessed=size, transcendentals=0)

    half = width // 2
    scaled = pl.pallas_call(
        scale_kernel,
        out_shape=jax.ShapeDtypeStruct(tokens.shape, jnp.float32),
        in_specs=[IN_VMEM],
        out_specs=IN_VMEM,
        compiler_params=params(8),
        cost_estimate=cost(40 * 10**9, MIB),
    )(tokens)
    normed = pl.pallas_call(
        functools.partial(gain_kernel, wide, plane),
        out_shape=jax.ShapeDtypeStruct((owners, rows, half), jnp.bfloat16),
        in_specs=[IN_VMEM, IN_VMEM],
        out_specs=IN_VMEM,
        compiler_params=params(8),
    )(scaled, norm_gain.reshape(1, -1))
    slots = cache_keys.shape[1]
    even = plane // 2 - 1
    early = rows // 2
    every = range(rows)

    def cut(plan, after):
        return pl.pallas_call(
            functools.partial(cut_kernel, plan),
            out_shape=[
                jax.ShapeDtypeStruct(
                    ((len(key_rows) + len(value_rows)) * slots + 16 * with_lengths, kv_cols),
                    cache_keys.dtype,
                )
                for _, key_rows, value_rows, with_lengths in plan
            ],
            in_specs=[IN_VMEM] * 4,
            out_specs=[IN_VMEM] * len(plan),
            compiler_params=params(8),
        )(lengths.reshape(1, -1), cache_keys, cache_values, after)

    plan = [(l, every, every[:early], False) for l in range(2, plane, 2)]
    plan += [(l, (), every[early:], True) for l in range(2, plane, 2)]
    plan += [(l, every, every, True) for l in range(1, plane, 2)]
    blocks = cut(plan, normed)
    firsts, rest = blocks[:even], blocks[even:]
    firsts = [swap_plane(firsts[s], 2 * s + 2) for s in range(even)]
    near = swap_plane(rest[even], 1)
    rest = [*rest[:even], *rest[even + 1 :]]
    own_half = swap_blocks(normed, ROW_AXES)
    other_half = swap_pairs(own_half, "gz", 1)
    rest = pl.pallas_call(
        pass_kernel,
        out_shape=[jax.ShapeDtypeStruct(value.shape, value.dtype) for value in rest],
        in_specs=[ANYWHERE] * (len(rest) + even + 1),
        out_specs=[ANYWHERE] * len(rest),
        input_output_aliases={n: n for n in range(len(rest))},
        compiler_params=params(1),
    )(*rest, own_half, *firsts)
    lasts = [swap_plane(rest[s], 2 * s + 2) for s in range(even)]
    odd = [near, *[swap_plane(rest[even + s], 2 * s + 3) for s in range(even)]]
    (mine,) = cut([(0, every, every, True)], own_half)
    held = [*firsts, *lasts, mine, *odd]
    weights = (query_weight, key_weight, value_weight)
    half_cost = cost(owners * rows * width * cols, width * cols)
    partial = pl.pallas_call(
        functools.partial(project_kernel, True, wide, plane),
        out_shape=jax.ShapeDtypeStruct((owners * rows, cols), jnp.float32),
        in_specs=[IN_VMEM] * 4,
        out_specs=IN_VMEM,
        compiler_params=params(8),
        cost_estimate=half_cost,
    )(own_half, *weights)
    partial = pl.pallas_call(
        functools.partial(project_kernel, False, wide, plane),
        out_shape=[jax.ShapeDtypeStruct((plane, rows, cols), jnp.float32)] * wide,
        in_specs=[IN_VMEM] * 6,
        out_specs=[IN_VMEM] * wide,
        scratch_shapes=[pltpu.VMEM((owners, rows, cols), jnp.float32)],
        compiler_params=params(8),
        cost_estimate=half_cost,
    )(other_half, *weights, odd[0], partial)
    partial = swap_wide(partial)

    half_dim = HD // 2
    frequency = 500000.0 ** (-np.arange(half_dim, dtype=np.float64) / half_dim)
    frequency = np.tile(frequency.astype(np.float32), 2).reshape(1, HD)
    attended = pl.pallas_call(
        functools.partial(attend_kernel, wide, plane, rows, early, query_cols),
        out_shape=jax.ShapeDtypeStruct((plane, rows, query_cols), jnp.bfloat16),
        in_specs=[IN_VMEM] * (1 + wide + len(held)),
        out_specs=IN_VMEM,
        compiler_params=params(8),
        cost_estimate=cost(10**10, 4 * MIB),
    )(jnp.asarray(frequency), *partial[::-1], *held)
    head_rows = swap_wide([attended] * wide)
    parts = 2
    order = [0, *range(wide - 2, 0, -1), wide - 1]
    part_cols = out_cols // parts
    sums = []
    for p in range(parts):
        count = owners // 2
        shape = jax.ShapeDtypeStruct((count, rows, part_cols), jnp.float32)
        keep, give = pl.pallas_call(
            functools.partial(output_kernel, p * part_cols, part_cols, order),
            out_shape=(shape, shape),
            in_specs=[IN_VMEM] * (1 + wide),
            out_specs=(IN_VMEM, IN_VMEM),
            compiler_params=params(8),
            cost_estimate=cost(2 * owners * rows * depth * part_cols, 2 * depth * part_cols),
        )(out_weight, *[head_rows[k] for k in order])
        give = swap_plane(give, 1)
        step = 2
        while step < plane:
            count //= 2
            shape = jax.ShapeDtypeStruct((count, rows, part_cols), jnp.float32)
            keep, give = pl.pallas_call(
                halve_kernel,
                out_shape=(shape, shape),
                in_specs=[IN_VMEM, IN_VMEM],
                out_specs=(IN_VMEM, IN_VMEM),
                compiler_params=params(8),
            )(keep, give)
            give = swap_plane(give, step)
            step *= 2
        sums += [keep, give]
    blocks = pl.pallas_call(
        functools.partial(total_kernel, parts),
        out_shape=[jax.ShapeDtypeStruct((rows, out_cols), jnp.bfloat16)] * wide,
        in_specs=[IN_VMEM] * len(sums),
        out_specs=[IN_VMEM] * wide,
        compiler_params=params(8),
    )(*sums)
    blocks = swap_wide(blocks)
    return pl.pallas_call(
        finish_kernel,
        out_shape=jax.ShapeDtypeStruct((rows, wide * out_cols), jnp.bfloat16),
        in_specs=[IN_VMEM] * wide,
        out_specs=IN_VMEM,
        compiler_params=params(8),
    )(*blocks[::-1])


def solution(mesh):
    placed = (
        P(("groups", "gx", "gy", "gz"), None),
        P(),
        P("gx", ("gy", "gz")),
        P("gx", ("gy", "gz")),
        P("gx", ("gy", "gz")),
        P(("gy", "gz"), "gx"),
        P(("groups", "gx", "gy", "gz"), None, None),
        P(("groups", "gx", "gy", "gz"), None, None),
        P(("groups", "gx", "gy", "gz")),
    )
    return jax.shard_map(
        shards,
        mesh=mesh,
        in_specs=placed,
        out_specs=P(("groups", "gx", "gy", "gz"), None),
        check_vma=False,
    )
```

```python
import functools

import jax
import jax.numpy as jnp
import numpy as np
from jax import lax
from jax.experimental import pallas as pl
from jax.experimental.pallas import tpu as pltpu
from jax.sharding import PartitionSpec as P

HD = 128
ROW_AXES = ("gx", "gy", "gz")
PLANE = ("gy", "gz")
MIB = 1024 * 1024
IN_VMEM = pl.BlockSpec(memory_space=pltpu.VMEM)
ANYWHERE = pl.BlockSpec(memory_space=pl.ANY)


def scale_kernel(tokens_ref, scaled_ref):
    tokens = tokens_ref[...].astype(jnp.float32)
    mean_square = jnp.mean(tokens * tokens, -1, keepdims=True)
    scaled_ref[...] = tokens * lax.rsqrt(mean_square + 1e-05)


def gain_kernel(wide, plane, scaled_ref, gain_ref, blocks_ref):
    normed = (scaled_ref[...] * gain_ref[...]).astype(jnp.bfloat16)
    half = normed.shape[1] // wide // 2
    for i in range(wide):
        for j in range(plane):
            at = (2 * i + j % 2) * half
            blocks_ref[i * plane + j] = normed[:, at : at + half]


def project_kernel(own, wide, plane, rows_ref, query_ref, key_ref, value_ref, *refs):
    owners, rows, half = rows_ref.shape
    core = lax.axis_index("gz")
    at_row = pl.multiple_of((core if own else 1 - core) * half, half)
    normed = rows_ref[...].reshape(owners * rows, half)
    sums_ref = refs[-1]
    at = 0
    for weight in (query_ref, key_ref, value_ref):
        cols = weight.shape[1]
        step = min(cols, 256)
        for c in range(0, cols, step):
            part = jnp.dot(
                normed,
                weight[pl.ds(at_row, half), c : c + step],
                preferred_element_type=jnp.float32,
            )
            if own:
                sums_ref[:, at : at + step] = part
            else:
                part = part + refs[1][:, at : at + step]
                sums_ref[:, :, at : at + step] = part.reshape(owners, rows, step)
            at += step
    if not own:
        own_wide = lax.axis_index("gx")
        own_plane = 2 * lax.axis_index("gy") + core
        for k in range(wide):
            for l in range(plane):
                refs[2 + k][l] = sums_ref[(own_wide ^ k) * plane + (own_plane ^ l)]


def own_place():
    return 2 * lax.axis_index("gy") + lax.axis_index("gz")


def write_lengths(rows, lengths_ref, block_ref):
    at_row = lax.broadcasted_iota(jnp.int32, (16, block_ref.shape[1]), 0)
    filled = jnp.zeros(at_row.shape, jnp.float32)
    for r in range(rows):
        filled = jnp.where(at_row == r, lengths_ref[:, r : r + 1].astype(jnp.float32), filled)
    block_ref[block_ref.shape[0] - 16 :] = filled.astype(jnp.bfloat16)


def cut_kernel(plan, lengths_ref, keys_ref, values_ref, _, *blocks):
    rows, slots, _ = keys_ref.shape
    cols = blocks[0].shape[1]
    for (slot, key_rows, value_rows, with_lengths), block in zip(plan, blocks):
        at = pl.multiple_of((own_place() ^ slot) * cols, cols)
        start = 0
        for cache_ref, wanted in ((keys_ref, key_rows), (values_ref, value_rows)):
            for r in wanted:
                block[start : start + slots] = cache_ref[r, :, pl.ds(at, cols)]
                start += slots
        if with_lengths:
            write_lengths(rows, lengths_ref, block)


def pass_kernel(*refs):
    pass


def attend_kernel(wide, plane, members, rows, early, query_cols, frequency_ref, *refs):
    partials, held, attended_ref = refs[wide - 1 :: -1], refs[wide:-1], refs[-1]
    even = plane // 2 - 1 if members[0] else 0
    firsts, lasts, whole = held[:even], held[even : 2 * even], held[2 * even :]
    slots = (whole[0].shape[0] - 16) // (2 * rows)
    cols = partials[0].shape[-1]
    kv_cols = (cols - query_cols) // 2
    kv_heads, group = kv_cols // HD, query_cols // kv_cols
    pairs = len(members) * rows
    count = pairs * kv_heads
    heads = count * group
    scale = 1.0 / HD**0.5
    own = slice(members[0], members[-1] + 1)
    total = partials[0][own]
    for k in range(1, wide):
        total = total + partials[k][own]
    total = total.reshape(pairs, cols).astype(jnp.bfloat16).astype(jnp.float32)

    def cached(values):
        parts = []
        for p in range(pairs):
            l, r = members[p // rows], p % rows
            ref, at = whole[(l + 1) // 2], values * rows + r
            if l % 2 == 0 and l:
                ref = firsts[l // 2 - 1]
                if at >= rows + early:
                    ref, at = lasts[l // 2 - 1], at - rows - early
            parts.append(ref[at * slots : (at + 1) * slots])
        return jnp.concatenate(parts, 1)

    filled = []
    for l in members:
        block = lasts[l // 2 - 1] if l % 2 == 0 and l else whole[(l + 1) // 2]
        last = block[block.shape[0] - 16 :, :HD].astype(jnp.float32)
        filled += [last[r : r + 1] for r in range(rows)]
    angles = jnp.concatenate(filled, 0) * frequency_ref[...]
    cosine, sine = jnp.cos(angles), jnp.sin(angles)
    front = lax.broadcasted_iota(jnp.int32, (1, HD), 1) < HD // 2
    sine = jnp.where(front, -sine, sine)

    def rotate(vector):
        return vector * cosine + pltpu.roll(vector, HD // 2, 1) * sine

    query, key_new, value_new = [], [], []
    for h in range(kv_heads):
        turned = [
            rotate(total[:, (h * group + g) * HD : (h * group + g + 1) * HD]) for g in range(group)
        ]
        query.append(jnp.swapaxes(jnp.stack(turned, 0), 0, 1))
        at = query_cols + h * HD
        key_new.append(rotate(total[:, at : at + HD]))
        value_new.append(total[:, at + kv_cols : at + kv_cols + HD])
    query = jnp.stack(query, 1).reshape(heads, HD)
    turned_query = query.T.astype(jnp.bfloat16)
    key_new = jnp.stack(key_new, 1).reshape(count, HD).astype(jnp.bfloat16)
    value_new = jnp.stack(value_new, 1).reshape(count, HD)

    head_pair = lax.broadcasted_iota(jnp.int32, (1, heads), 1) // group
    by_pair = jnp.concatenate(
        [jnp.where(head_pair == b, turned_query, jnp.zeros_like(turned_query)) for b in range(count)],
        0,
    )
    scores = scale * jnp.dot(cached(0), by_pair, preferred_element_type=jnp.float32)
    own = scale * jnp.dot(key_new, turned_query, preferred_element_type=jnp.float32)
    of_pair = lax.broadcasted_iota(jnp.int32, (count, 1), 0) == head_pair
    own = jnp.sum(jnp.where(of_pair, own, 0.0), 0, keepdims=True)
    length = jnp.zeros((1, heads), jnp.float32)
    for p in range(pairs):
        length = jnp.where(head_pair // kv_heads == p, filled[p][:, :1], length)
    slot = lax.broadcasted_iota(jnp.int32, (slots, 1), 0).astype(jnp.float32)
    scores = jnp.where(slot < length, scores, -1e30)
    top = jnp.maximum(jnp.max(scores, 0, keepdims=True), own)
    weights = jnp.exp(scores - top)
    own_weight = jnp.exp(own - top)
    denominator = jnp.sum(weights, 0, keepdims=True) + own_weight
    probability = (weights / denominator).astype(jnp.bfloat16)
    own_prob = (own_weight / denominator).astype(jnp.bfloat16)
    contract_rows = (((0,), (0,)), ((), ()))
    mixed = lax.dot_general(
        probability, cached(1), contract_rows, preferred_element_type=jnp.float32
    )
    own_prob = jnp.where(of_pair, own_prob.astype(jnp.float32), 0.0).astype(jnp.bfloat16)
    fresh = lax.dot_general(
        own_prob, value_new.astype(jnp.bfloat16), contract_rows, preferred_element_type=jnp.float32
    )
    mixed = [
        mixed[b * group : (b + 1) * group, b * HD : (b + 1) * HD]
        + fresh[b * group : (b + 1) * group]
        for b in range(count)
    ]
    attended = []
    for h in range(kv_heads):
        by_head = jnp.swapaxes(jnp.stack(mixed[h::kv_heads], 0), 0, 1)
        attended += [by_head[g] for g in range(group)]
    attended = jnp.concatenate(attended, 1)
    attended_ref[...] = attended.reshape(len(members), rows, query_cols).astype(jnp.bfloat16)


def join_kernel(*refs):
    at = 0
    for block in refs[:-1]:
        refs[-1][at : at + block.shape[0]] = block[...]
        at += block.shape[0]


def output_kernel(at, cols, order, weight_ref, *refs):
    blocks, keep_ref, give_ref = [refs[n] for n in order], refs[-2], refs[-1]
    wide = len(blocks)
    plane, rows, depth = blocks[0].shape
    attended = jnp.concatenate(
        [block[...].reshape(plane * rows, depth) for block in blocks], 0
    )
    step = min(cols, 512)
    for c in range(0, cols, step):
        part = jnp.dot(
            attended, weight_ref[:, at + c : at + c + step], preferred_element_type=jnp.float32
        )
        part = part.reshape(wide * plane // 2, 2 * rows, step)
        keep_ref[:, :, c : c + step] = part[:, :rows]
        give_ref[:, :, c : c + step] = part[:, rows:]


def halve_kernel(a_ref, b_ref, keep_ref, give_ref):
    for n in range(keep_ref.shape[0]):
        keep_ref[n] = a_ref[2 * n] + b_ref[2 * n]
        give_ref[n] = a_ref[2 * n + 1] + b_ref[2 * n + 1]


def total_kernel(parts, *refs):
    sums, blocks = refs[: 2 * parts], refs[2 * parts :]
    cols = sums[0].shape[-1]
    for p in range(parts):
        for k, block in enumerate(blocks):
            total = sums[2 * p][k] + sums[2 * p + 1][k]
            block[:, p * cols : (p + 1) * cols] = total.astype(jnp.bfloat16)


def finish_kernel(*refs):
    blocks, result_ref = refs[-2::-1], refs[-1]
    own = lax.axis_index("gx")
    cols = blocks[0].shape[-1]
    for k, block in enumerate(blocks):
        at = pl.multiple_of((own ^ k) * cols, cols)
        result_ref[:, pl.ds(at, cols)] = block[...]


def swap_blocks(blocks, axes):
    return lax.all_to_all(blocks, axes, split_axis=0, concat_axis=0, tiled=True)


def swap_pairs(value, axis, step):
    return lax.ppermute(value, axis, [(i, i ^ step) for i in range(lax.axis_size(axis))])


def swap_plane(value, step):
    return lax.ppermute(value, PLANE, [(i, i ^ step) for i in range(lax.axis_size(PLANE))])


def swap_wide(blocks):
    moved = [swap_pairs(blocks[k], "gx", k) for k in range(len(blocks) - 1, 0, -1)]
    return [blocks[0]] + moved[::-1]


def shards(
    tokens,
    norm_gain,
    query_weight,
    key_weight,
    value_weight,
    out_weight,
    cache_keys,
    cache_values,
    lengths,
):
    rows = tokens.shape[0]
    wide = lax.axis_size("gx")
    plane = lax.axis_size(PLANE)
    owners = wide * plane
    width, query_cols = query_weight.shape
    kv_cols = key_weight.shape[1]
    depth, out_cols = out_weight.shape
    cols = query_cols + 2 * kv_cols

    def params(mib):
        return pltpu.CompilerParams(vmem_limit_bytes=mib * MIB)

    def cost(flops, size):
        return pl.CostEstimate(flops=flops, bytes_accessed=size, transcendentals=0)

    half = width // 2
    scaled = pl.pallas_call(
        scale_kernel,
        out_shape=jax.ShapeDtypeStruct(tokens.shape, jnp.float32),
        in_specs=[IN_VMEM],
        out_specs=IN_VMEM,
        compiler_params=params(8),
        cost_estimate=cost(40 * 10**9, MIB),
    )(tokens)
    normed = pl.pallas_call(
        functools.partial(gain_kernel, wide, plane),
        out_shape=jax.ShapeDtypeStruct((owners, rows, half), jnp.bfloat16),
        in_specs=[IN_VMEM, IN_VMEM],
        out_specs=IN_VMEM,
        compiler_params=params(8),
    )(scaled, norm_gain.reshape(1, -1))
    slots = cache_keys.shape[1]
    even = plane // 2 - 1
    early = rows // 2
    every = range(rows)

    def cut(plan, after):
        return pl.pallas_call(
            functools.partial(cut_kernel, plan),
            out_shape=[
                jax.ShapeDtypeStruct(
                    ((len(key_rows) + len(value_rows)) * slots + 16 * with_lengths, kv_cols),
                    cache_keys.dtype,
                )
                for _, key_rows, value_rows, with_lengths in plan
            ],
            in_specs=[IN_VMEM] * 4,
            out_specs=[IN_VMEM] * len(plan),
            compiler_params=params(8),
        )(lengths.reshape(1, -1), cache_keys, cache_values, after)

    plan = [(l, every, every[:early], False) for l in range(2, plane, 2)]
    plan += [(l, (), every[early:], True) for l in range(2, plane, 2)]
    plan += [(l, every, every, True) for l in range(1, plane, 2)]
    blocks = cut(plan, normed)
    firsts, rest = blocks[:even], blocks[even:]
    firsts = [swap_plane(firsts[s], 2 * s + 2) for s in range(even)]
    own_half = swap_blocks(normed, ROW_AXES)
    other_half = swap_pairs(own_half, "gz", 1)
    rest = pl.pallas_call(
        pass_kernel,
        out_shape=[jax.ShapeDtypeStruct(value.shape, value.dtype) for value in rest],
        in_specs=[ANYWHERE] * (len(rest) + even + 1),
        out_specs=[ANYWHERE] * len(rest),
        input_output_aliases={n: n for n in range(len(rest))},
        compiler_params=params(1),
    )(*rest, own_half, *firsts)
    lasts = [swap_plane(rest[s], 2 * s + 2) for s in range(even)]
    odd = [swap_plane(rest[even + s], 2 * s + 1) for s in range(even + 1)]
    (mine,) = cut([(0, every, every, True)], own_half)
    held = [*firsts, *lasts, mine, *odd]
    weights = (query_weight, key_weight, value_weight)
    half_cost = cost(owners * rows * width * cols, width * cols)
    partial = pl.pallas_call(
        functools.partial(project_kernel, True, wide, plane),
        out_shape=jax.ShapeDtypeStruct((owners * rows, cols), jnp.float32),
        in_specs=[IN_VMEM] * 4,
        out_specs=IN_VMEM,
        compiler_params=params(8),
        cost_estimate=half_cost,
    )(own_half, *weights)
    partial = pl.pallas_call(
        functools.partial(project_kernel, False, wide, plane),
        out_shape=[jax.ShapeDtypeStruct((plane, rows, cols), jnp.float32)] * wide,
        in_specs=[IN_VMEM] * 6,
        out_specs=[IN_VMEM] * wide,
        scratch_shapes=[pltpu.VMEM((owners, rows, cols), jnp.float32)],
        compiler_params=params(8),
        cost_estimate=half_cost,
    )(other_half, *weights, odd[0], partial)
    partial = swap_wide(partial)

    half_dim = HD // 2
    frequency = 500000.0 ** (-np.arange(half_dim, dtype=np.float64) / half_dim)
    frequency = np.tile(frequency.astype(np.float32), 2).reshape(1, HD)
    attended = []
    for members in (range(2), range(2, plane)):
        used = held if members[0] else held[2 * even : 2 * even + 2]
        attended.append(
            pl.pallas_call(
                functools.partial(attend_kernel, wide, plane, members, rows, early, query_cols),
                out_shape=jax.ShapeDtypeStruct((len(members), rows, query_cols), jnp.bfloat16),
                in_specs=[IN_VMEM] * (1 + wide + len(used)),
                out_specs=IN_VMEM,
                compiler_params=params(8),
                cost_estimate=cost(10**10, 4 * MIB) if members[0] else cost(1, 1),
            )(jnp.asarray(frequency), *partial[::-1], *used)
        )
    attended = pl.pallas_call(
        join_kernel,
        out_shape=jax.ShapeDtypeStruct((plane, rows, query_cols), jnp.bfloat16),
        in_specs=[IN_VMEM, IN_VMEM],
        out_specs=IN_VMEM,
        compiler_params=params(8),
    )(*attended)
    head_rows = swap_wide([attended] * wide)
    parts = 2
    order = [0, *range(wide - 2, 0, -1), wide - 1]
    part_cols = out_cols // parts
    sums = []
    for p in range(parts):
        count = owners // 2
        shape = jax.ShapeDtypeStruct((count, rows, part_cols), jnp.float32)
        keep, give = pl.pallas_call(
            functools.partial(output_kernel, p * part_cols, part_cols, order),
            out_shape=(shape, shape),
            in_specs=[IN_VMEM] * (1 + wide),
            out_specs=(IN_VMEM, IN_VMEM),
            compiler_params=params(8),
            cost_estimate=cost(2 * owners * rows * depth * part_cols, 2 * depth * part_cols),
        )(out_weight, *[head_rows[k] for k in order])
        give = swap_plane(give, 1)
        step = 2
        while step < plane:
            count //= 2
            shape = jax.ShapeDtypeStruct((count, rows, part_cols), jnp.float32)
            keep, give = pl.pallas_call(
                halve_kernel,
                out_shape=(shape, shape),
                in_specs=[IN_VMEM, IN_VMEM],
                out_specs=(IN_VMEM, IN_VMEM),
                compiler_params=params(8),
            )(keep, give)
            give = swap_plane(give, step)
            step *= 2
        sums += [keep, give]
    blocks = pl.pallas_call(
        functools.partial(total_kernel, parts),
        out_shape=[jax.ShapeDtypeStruct((rows, out_cols), jnp.bfloat16)] * wide,
        in_specs=[IN_VMEM] * len(sums),
        out_specs=[IN_VMEM] * wide,
        compiler_params=params(8),
    )(*sums)
    blocks = swap_wide(blocks)
    return pl.pallas_call(
        finish_kernel,
        out_shape=jax.ShapeDtypeStruct((rows, wide * out_cols), jnp.bfloat16),
        in_specs=[IN_VMEM] * wide,
        out_specs=IN_VMEM,
        compiler_params=params(8),
    )(*blocks[::-1])


def solution(mesh):
    placed = (
        P(("groups", "gx", "gy", "gz"), None),
        P(),
        P("gx", ("gy", "gz")),
        P("gx", ("gy", "gz")),
        P("gx", ("gy", "gz")),
        P(("gy", "gz"), "gx"),
        P(("groups", "gx", "gy", "gz"), None, None),
        P(("groups", "gx", "gy", "gz"), None, None),
        P(("groups", "gx", "gy", "gz")),
    )
    return jax.shard_map(
        shards,
        mesh=mesh,
        in_specs=placed,
        out_specs=P(("groups", "gx", "gy", "gz"), None),
        check_vma=False,
    )
```

```python
import functools

import jax
import jax.numpy as jnp
import numpy as np
from jax import lax
from jax.experimental import pallas as pl
from jax.experimental.pallas import tpu as pltpu
from jax.sharding import PartitionSpec as P

HD = 128
ROW_AXES = ("gx", "gy", "gz")
PLANE = ("gy", "gz")
MIB = 1024 * 1024
IN_VMEM = pl.BlockSpec(memory_space=pltpu.VMEM)
ANYWHERE = pl.BlockSpec(memory_space=pl.ANY)


def scale_kernel(tokens_ref, scaled_ref):
    tokens = tokens_ref[...].astype(jnp.float32)
    mean_square = jnp.mean(tokens * tokens, -1, keepdims=True)
    scaled_ref[...] = tokens * lax.rsqrt(mean_square + 1e-05)


def gain_kernel(wide, plane, scaled_ref, gain_ref, blocks_ref):
    normed = (scaled_ref[...] * gain_ref[...]).astype(jnp.bfloat16)
    half = normed.shape[1] // wide // 2
    for i in range(wide):
        for j in range(plane):
            at = (2 * i + j % 2) * half
            blocks_ref[i * plane + j] = normed[:, at : at + half]


def project_kernel(own, wide, plane, rows_ref, query_ref, key_ref, value_ref, *refs):
    owners, rows, half = rows_ref.shape
    core = lax.axis_index("gz")
    at_row = pl.multiple_of((core if own else 1 - core) * half, half)
    normed = rows_ref[...].reshape(owners * rows, half)
    sums_ref = refs[-1]
    at = 0
    for weight in (query_ref, key_ref, value_ref):
        cols = weight.shape[1]
        step = min(cols, 256)
        for c in range(0, cols, step):
            part = jnp.dot(
                normed,
                weight[pl.ds(at_row, half), c : c + step],
                preferred_element_type=jnp.float32,
            )
            if own:
                sums_ref[:, at : at + step] = part
            else:
                part = part + refs[1][:, at : at + step]
                sums_ref[:, :, at : at + step] = part.reshape(owners, rows, step)
            at += step
    if not own:
        own_wide = lax.axis_index("gx")
        own_plane = 2 * lax.axis_index("gy") + core
        for k in range(wide):
            for l in range(plane):
                refs[2 + k][l] = sums_ref[(own_wide ^ k) * plane + (own_plane ^ l)]


def own_place():
    return 2 * lax.axis_index("gy") + lax.axis_index("gz")


def write_lengths(rows, lengths_ref, block_ref):
    at_row = lax.broadcasted_iota(jnp.int32, (16, block_ref.shape[1]), 0)
    filled = jnp.zeros(at_row.shape, jnp.float32)
    for r in range(rows):
        filled = jnp.where(at_row == r, lengths_ref[:, r : r + 1].astype(jnp.float32), filled)
    block_ref[block_ref.shape[0] - 16 :] = filled.astype(jnp.bfloat16)


def cut_kernel(plan, lengths_ref, keys_ref, values_ref, _, *blocks):
    rows, slots, _ = keys_ref.shape
    cols = blocks[0].shape[1]
    for (slot, key_rows, value_rows, with_lengths), block in zip(plan, blocks):
        at = pl.multiple_of((own_place() ^ slot) * cols, cols)
        start = 0
        for cache_ref, wanted in ((keys_ref, key_rows), (values_ref, value_rows)):
            for r in wanted:
                block[start : start + slots] = cache_ref[r, :, pl.ds(at, cols)]
                start += slots
        if with_lengths:
            write_lengths(rows, lengths_ref, block)


def pass_kernel(*refs):
    pass


def attend_kernel(wide, plane, members, rows, early, query_cols, frequency_ref, *refs):
    partials, held, attended_ref = refs[wide - 1 :: -1], refs[wide:-1], refs[-1]
    even = plane // 2 - 1 if members[0] else 0
    firsts, lasts, whole = held[:even], held[even : 2 * even], held[2 * even :]
    slots = (whole[0].shape[0] - 16) // (2 * rows)
    cols = partials[0].shape[-1]
    kv_cols = (cols - query_cols) // 2
    kv_heads, group = kv_cols // HD, query_cols // kv_cols
    pairs = len(members) * rows
    count = pairs * kv_heads
    heads = count * group
    scale = 1.0 / HD**0.5
    own = slice(members[0], members[-1] + 1)
    total = partials[0][own]
    for k in range(1, wide):
        total = total + partials[k][own]
    total = total.reshape(pairs, cols).astype(jnp.bfloat16).astype(jnp.float32)

    def cached(values):
        parts = []
        for p in range(pairs):
            l, r = members[p // rows], p % rows
            ref, at = whole[(l + 1) // 2], values * rows + r
            if l % 2 == 0 and l:
                ref = firsts[l // 2 - 1]
                if at >= rows + early:
                    ref, at = lasts[l // 2 - 1], at - rows - early
            parts.append(ref[at * slots : (at + 1) * slots])
        return jnp.concatenate(parts, 1)

    filled = []
    for l in members:
        block = lasts[l // 2 - 1] if l % 2 == 0 and l else whole[(l + 1) // 2]
        last = block[block.shape[0] - 16 :, :HD].astype(jnp.float32)
        filled += [last[r : r + 1] for r in range(rows)]
    angles = jnp.concatenate(filled, 0) * frequency_ref[...]
    cosine, sine = jnp.cos(angles), jnp.sin(angles)
    front = lax.broadcasted_iota(jnp.int32, (1, HD), 1) < HD // 2
    sine = jnp.where(front, -sine, sine)

    def rotate(vector):
        return vector * cosine + pltpu.roll(vector, HD // 2, 1) * sine

    query, key_new, value_new = [], [], []
    for h in range(kv_heads):
        turned = [
            rotate(total[:, (h * group + g) * HD : (h * group + g + 1) * HD]) for g in range(group)
        ]
        query.append(jnp.swapaxes(jnp.stack(turned, 0), 0, 1))
        at = query_cols + h * HD
        key_new.append(rotate(total[:, at : at + HD]))
        value_new.append(total[:, at + kv_cols : at + kv_cols + HD])
    query = jnp.stack(query, 1).reshape(heads, HD)
    turned_query = query.T.astype(jnp.bfloat16)
    key_new = jnp.stack(key_new, 1).reshape(count, HD).astype(jnp.bfloat16)
    value_new = jnp.stack(value_new, 1).reshape(count, HD)

    head_pair = lax.broadcasted_iota(jnp.int32, (1, heads), 1) // group
    by_pair = jnp.concatenate(
        [jnp.where(head_pair == b, turned_query, jnp.zeros_like(turned_query)) for b in range(count)],
        0,
    )
    scores = scale * jnp.dot(cached(0), by_pair, preferred_element_type=jnp.float32)
    own = scale * jnp.dot(key_new, turned_query, preferred_element_type=jnp.float32)
    of_pair = lax.broadcasted_iota(jnp.int32, (count, 1), 0) == head_pair
    own = jnp.sum(jnp.where(of_pair, own, 0.0), 0, keepdims=True)
    length = jnp.zeros((1, heads), jnp.float32)
    for p in range(pairs):
        length = jnp.where(head_pair // kv_heads == p, filled[p][:, :1], length)
    slot = lax.broadcasted_iota(jnp.int32, (slots, 1), 0).astype(jnp.float32)
    scores = jnp.where(slot < length, scores, -1e30)
    top = jnp.maximum(jnp.max(scores, 0, keepdims=True), own)
    weights = jnp.exp(scores - top)
    own_weight = jnp.exp(own - top)
    denominator = jnp.sum(weights, 0, keepdims=True) + own_weight
    probability = (weights / denominator).astype(jnp.bfloat16)
    own_prob = (own_weight / denominator).astype(jnp.bfloat16)
    contract_rows = (((0,), (0,)), ((), ()))
    mixed = lax.dot_general(
        probability, cached(1), contract_rows, preferred_element_type=jnp.float32
    )
    own_prob = jnp.where(of_pair, own_prob.astype(jnp.float32), 0.0).astype(jnp.bfloat16)
    fresh = lax.dot_general(
        own_prob, value_new.astype(jnp.bfloat16), contract_rows, preferred_element_type=jnp.float32
    )
    mixed = [
        mixed[b * group : (b + 1) * group, b * HD : (b + 1) * HD]
        + fresh[b * group : (b + 1) * group]
        for b in range(count)
    ]
    attended = []
    for h in range(kv_heads):
        by_head = jnp.swapaxes(jnp.stack(mixed[h::kv_heads], 0), 0, 1)
        attended += [by_head[g] for g in range(group)]
    attended = jnp.concatenate(attended, 1)
    attended_ref[...] = attended.reshape(len(members), rows, query_cols).astype(jnp.bfloat16)


def join_kernel(*refs):
    at = 0
    for block in refs[:-1]:
        refs[-1][at : at + block.shape[0]] = block[...]
        at += block.shape[0]


def output_kernel(at, cols, order, weight_ref, *refs):
    blocks, keep_ref, give_ref = [refs[n] for n in order], refs[-2], refs[-1]
    wide = len(blocks)
    plane, rows, depth = blocks[0].shape
    attended = jnp.concatenate(
        [block[...].reshape(plane * rows, depth) for block in blocks], 0
    )
    step = min(cols, 512)
    for c in range(0, cols, step):
        part = jnp.dot(
            attended, weight_ref[:, at + c : at + c + step], preferred_element_type=jnp.float32
        )
        part = part.reshape(wide * plane // 2, 2 * rows, step)
        keep_ref[:, :, c : c + step] = part[:, :rows]
        give_ref[:, :, c : c + step] = part[:, rows:]


def halve_kernel(a_ref, b_ref, keep_ref, give_ref):
    for n in range(keep_ref.shape[0]):
        keep_ref[n] = a_ref[2 * n] + b_ref[2 * n]
        give_ref[n] = a_ref[2 * n + 1] + b_ref[2 * n + 1]


def total_kernel(parts, *refs):
    sums, blocks = refs[: 2 * parts], refs[2 * parts :]
    cols = sums[0].shape[-1]
    for p in range(parts):
        for k, block in enumerate(blocks):
            total = sums[2 * p][k] + sums[2 * p + 1][k]
            block[:, p * cols : (p + 1) * cols] = total.astype(jnp.bfloat16)


def finish_kernel(*refs):
    blocks, result_ref = refs[-2::-1], refs[-1]
    own = lax.axis_index("gx")
    cols = blocks[0].shape[-1]
    for k, block in enumerate(blocks):
        at = pl.multiple_of((own ^ k) * cols, cols)
        result_ref[:, pl.ds(at, cols)] = block[...]


def swap_blocks(blocks, axes):
    return lax.all_to_all(blocks, axes, split_axis=0, concat_axis=0, tiled=True)


def swap_pairs(value, axis, step):
    return lax.ppermute(value, axis, [(i, i ^ step) for i in range(lax.axis_size(axis))])


def swap_plane(value, step):
    return lax.ppermute(value, PLANE, [(i, i ^ step) for i in range(lax.axis_size(PLANE))])


def swap_wide(blocks):
    moved = [swap_pairs(blocks[k], "gx", k) for k in range(len(blocks) - 1, 0, -1)]
    return [blocks[0]] + moved[::-1]


def shards(
    tokens,
    norm_gain,
    query_weight,
    key_weight,
    value_weight,
    out_weight,
    cache_keys,
    cache_values,
    lengths,
):
    rows = tokens.shape[0]
    wide = lax.axis_size("gx")
    plane = lax.axis_size(PLANE)
    owners = wide * plane
    width, query_cols = query_weight.shape
    kv_cols = key_weight.shape[1]
    depth, out_cols = out_weight.shape
    cols = query_cols + 2 * kv_cols

    def params(mib):
        return pltpu.CompilerParams(vmem_limit_bytes=mib * MIB)

    def cost(flops, size):
        return pl.CostEstimate(flops=flops, bytes_accessed=size, transcendentals=0)

    half = width // 2
    scaled = pl.pallas_call(
        scale_kernel,
        out_shape=jax.ShapeDtypeStruct(tokens.shape, jnp.float32),
        in_specs=[IN_VMEM],
        out_specs=IN_VMEM,
        compiler_params=params(8),
        cost_estimate=cost(6 * 10**9, MIB),
    )(tokens)
    normed = pl.pallas_call(
        functools.partial(gain_kernel, wide, plane),
        out_shape=jax.ShapeDtypeStruct((owners, rows, half), jnp.bfloat16),
        in_specs=[IN_VMEM, IN_VMEM],
        out_specs=IN_VMEM,
        compiler_params=params(8),
    )(scaled, norm_gain.reshape(1, -1))
    slots = cache_keys.shape[1]
    even = plane // 2 - 1
    early = rows // 2
    every = range(rows)

    def cut(plan, after):
        return pl.pallas_call(
            functools.partial(cut_kernel, plan),
            out_shape=[
                jax.ShapeDtypeStruct(
                    ((len(key_rows) + len(value_rows)) * slots + 16 * with_lengths, kv_cols),
                    cache_keys.dtype,
                )
                for _, key_rows, value_rows, with_lengths in plan
            ],
            in_specs=[IN_VMEM] * 4,
            out_specs=[IN_VMEM] * len(plan),
            compiler_params=params(8),
            cost_estimate=cost(40 * 10**9 if plan[0][0] else 1, MIB),
        )(lengths.reshape(1, -1), cache_keys, cache_values, after)

    plan = [(l, every, every[:early], False) for l in range(2, plane, 2)]
    plan += [(l, (), every[early:], True) for l in range(2, plane, 2)]
    plan += [(l, every, every, True) for l in range(1, plane, 2)]
    blocks = cut(plan, normed)
    firsts, rest = blocks[:even], blocks[even:]
    firsts = [swap_plane(firsts[s], 2 * s + 2) for s in range(even)]
    own_half = swap_blocks(normed, ROW_AXES)
    other_half = swap_pairs(own_half, "gz", 1)
    rest = pl.pallas_call(
        pass_kernel,
        out_shape=[jax.ShapeDtypeStruct(value.shape, value.dtype) for value in rest],
        in_specs=[ANYWHERE] * (len(rest) + even + 1),
        out_specs=[ANYWHERE] * len(rest),
        input_output_aliases={n: n for n in range(len(rest))},
        compiler_params=params(1),
    )(*rest, own_half, *firsts)
    lasts = [swap_plane(rest[s], 2 * s + 2) for s in range(even)]
    odd = [swap_plane(rest[even + s], 2 * s + 1) for s in range(even + 1)]
    (mine,) = cut([(0, every, every, True)], own_half)
    held = [*firsts, *lasts, mine, *odd]
    weights = (query_weight, key_weight, value_weight)
    half_cost = cost(owners * rows * width * cols, width * cols)
    partial = pl.pallas_call(
        functools.partial(project_kernel, True, wide, plane),
        out_shape=jax.ShapeDtypeStruct((owners * rows, cols), jnp.float32),
        in_specs=[IN_VMEM] * 4,
        out_specs=IN_VMEM,
        compiler_params=params(8),
        cost_estimate=half_cost,
    )(own_half, *weights)
    partial = pl.pallas_call(
        functools.partial(project_kernel, False, wide, plane),
        out_shape=[jax.ShapeDtypeStruct((plane, rows, cols), jnp.float32)] * wide,
        in_specs=[IN_VMEM] * 6,
        out_specs=[IN_VMEM] * wide,
        scratch_shapes=[pltpu.VMEM((owners, rows, cols), jnp.float32)],
        compiler_params=params(8),
        cost_estimate=half_cost,
    )(other_half, *weights, odd[0], partial)
    partial = swap_wide(partial)

    half_dim = HD // 2
    frequency = 500000.0 ** (-np.arange(half_dim, dtype=np.float64) / half_dim)
    frequency = np.tile(frequency.astype(np.float32), 2).reshape(1, HD)
    attended = []
    for members in (range(2), range(2, plane)):
        used = held if members[0] else held[2 * even : 2 * even + 2]
        attended.append(
            pl.pallas_call(
                functools.partial(attend_kernel, wide, plane, members, rows, early, query_cols),
                out_shape=jax.ShapeDtypeStruct((len(members), rows, query_cols), jnp.bfloat16),
                in_specs=[IN_VMEM] * (1 + wide + len(used)),
                out_specs=IN_VMEM,
                compiler_params=params(8),
                cost_estimate=cost(10**10, 4 * MIB) if members[0] else cost(1, 1),
            )(jnp.asarray(frequency), *partial[::-1], *used)
        )
    attended = pl.pallas_call(
        join_kernel,
        out_shape=jax.ShapeDtypeStruct((plane, rows, query_cols), jnp.bfloat16),
        in_specs=[IN_VMEM, IN_VMEM],
        out_specs=IN_VMEM,
        compiler_params=params(8),
    )(*attended)
    head_rows = swap_wide([attended] * wide)
    parts = 2
    order = [0, *range(wide - 2, 0, -1), wide - 1]
    part_cols = out_cols // parts
    sums = []
    for p in range(parts):
        count = owners // 2
        shape = jax.ShapeDtypeStruct((count, rows, part_cols), jnp.float32)
        keep, give = pl.pallas_call(
            functools.partial(output_kernel, p * part_cols, part_cols, order),
            out_shape=(shape, shape),
            in_specs=[IN_VMEM] * (1 + wide),
            out_specs=(IN_VMEM, IN_VMEM),
            compiler_params=params(8),
            cost_estimate=cost(2 * owners * rows * depth * part_cols, 2 * depth * part_cols),
        )(out_weight, *[head_rows[k] for k in order])
        give = swap_plane(give, 1)
        step = 2
        while step < plane:
            count //= 2
            shape = jax.ShapeDtypeStruct((count, rows, part_cols), jnp.float32)
            keep, give = pl.pallas_call(
                halve_kernel,
                out_shape=(shape, shape),
                in_specs=[IN_VMEM, IN_VMEM],
                out_specs=(IN_VMEM, IN_VMEM),
                compiler_params=params(8),
            )(keep, give)
            give = swap_plane(give, step)
            step *= 2
        sums += [keep, give]
    blocks = pl.pallas_call(
        functools.partial(total_kernel, parts),
        out_shape=[jax.ShapeDtypeStruct((rows, out_cols), jnp.bfloat16)] * wide,
        in_specs=[IN_VMEM] * len(sums),
        out_specs=[IN_VMEM] * wide,
        compiler_params=params(8),
    )(*sums)
    blocks = swap_wide(blocks)
    return pl.pallas_call(
        finish_kernel,
        out_shape=jax.ShapeDtypeStruct((rows, wide * out_cols), jnp.bfloat16),
        in_specs=[IN_VMEM] * wide,
        out_specs=IN_VMEM,
        compiler_params=params(8),
    )(*blocks[::-1])


def solution(mesh):
    placed = (
        P(("groups", "gx", "gy", "gz"), None),
        P(),
        P("gx", ("gy", "gz")),
        P("gx", ("gy", "gz")),
        P("gx", ("gy", "gz")),
        P(("gy", "gz"), "gx"),
        P(("groups", "gx", "gy", "gz"), None, None),
        P(("groups", "gx", "gy", "gz"), None, None),
        P(("groups", "gx", "gy", "gz")),
    )
    return jax.shard_map(
        shards,
        mesh=mesh,
        in_specs=placed,
        out_specs=P(("groups", "gx", "gy", "gz"), None),
        check_vma=False,
    )
```

```python
import functools

import jax
import jax.numpy as jnp
import numpy as np
from jax import lax
from jax.experimental import pallas as pl
from jax.experimental.pallas import tpu as pltpu
from jax.sharding import PartitionSpec as P

HD = 128
ROW_AXES = ("gx", "gy", "gz")
PLANE = ("gy", "gz")
MIB = 1024 * 1024
IN_VMEM = pl.BlockSpec(memory_space=pltpu.VMEM)
ANYWHERE = pl.BlockSpec(memory_space=pl.ANY)


def scale_kernel(tokens_ref, scaled_ref):
    tokens = tokens_ref[...].astype(jnp.float32)
    mean_square = jnp.mean(tokens * tokens, -1, keepdims=True)
    scaled_ref[...] = tokens * lax.rsqrt(mean_square + 1e-05)


def gain_kernel(wide, plane, scaled_ref, gain_ref, blocks_ref):
    normed = (scaled_ref[...] * gain_ref[...]).astype(jnp.bfloat16)
    half = normed.shape[1] // wide // 2
    for i in range(wide):
        for j in range(plane):
            at = (2 * i + j % 2) * half
            blocks_ref[i * plane + j] = normed[:, at : at + half]


def project_kernel(own, wide, plane, rows_ref, query_ref, key_ref, value_ref, *refs):
    half = query_ref.shape[0] // 2
    core = lax.axis_index("gz")
    at_row = pl.multiple_of((core if own else 1 - core) * half, half)
    if own:
        normed = rows_ref[...].reshape(-1, half)
    else:
        count, cols = refs[0].shape[0], rows_ref.shape[1]
        normed = jnp.concatenate(
            [rows_ref[n * count : (n + 1) * count] for n in range(half // cols)], 1
        )
        owners, rows = refs[-1].shape[:2]
    sums_ref = refs[-1]
    at = 0
    for weight in (query_ref, key_ref, value_ref):
        cols = weight.shape[1]
        step = min(cols, 256)
        for c in range(0, cols, step):
            part = jnp.dot(
                normed,
                weight[pl.ds(at_row, half), c : c + step],
                preferred_element_type=jnp.float32,
            )
            if own:
                sums_ref[:, at : at + step] = part
            else:
                part = part + refs[0][:, at : at + step]
                sums_ref[:, :, at : at + step] = part.reshape(owners, rows, step)
            at += step
    if not own:
        own_wide = lax.axis_index("gx")
        own_plane = 2 * lax.axis_index("gy") + core
        for k in range(wide):
            for l in range(plane):
                refs[1 + k][l] = sums_ref[(own_wide ^ k) * plane + (own_plane ^ l)]


def own_place():
    return 2 * lax.axis_index("gy") + lax.axis_index("gz")


def write_lengths(rows, lengths_ref, block_ref):
    at_row = lax.broadcasted_iota(jnp.int32, (16, block_ref.shape[1]), 0)
    filled = jnp.zeros(at_row.shape, jnp.float32)
    for r in range(rows):
        filled = jnp.where(at_row == r, lengths_ref[:, r : r + 1].astype(jnp.float32), filled)
    block_ref[block_ref.shape[0] - 16 :] = filled.astype(jnp.bfloat16)


def cut_kernel(plan, lengths_ref, keys_ref, values_ref, _, *blocks):
    rows, slots, _ = keys_ref.shape
    cols = blocks[0].shape[1]
    for (slot, key_rows, value_rows, with_lengths), block in zip(plan, blocks):
        at = pl.multiple_of((own_place() ^ slot) * cols, cols)
        start = 0
        for cache_ref, wanted in ((keys_ref, key_rows), (values_ref, value_rows)):
            for r in wanted:
                block[start : start + slots] = cache_ref[r, :, pl.ds(at, cols)]
                start += slots
        if with_lengths:
            write_lengths(rows, lengths_ref, block)


def mate_kernel(lengths_ref, keys_ref, values_ref, rows_ref, mate_ref):
    rows, slots, _ = keys_ref.shape
    cols = mate_ref.shape[1]
    half = rows_ref.shape[-1]
    normed = rows_ref[...].reshape(-1, half)
    count = normed.shape[0]
    start = 0
    for c in range(0, half, cols):
        mate_ref[start : start + count] = normed[:, c : c + cols]
        start += count
    at = pl.multiple_of((own_place() ^ 1) * cols, cols)
    for cache_ref in (keys_ref, values_ref):
        for r in range(rows):
            mate_ref[start : start + slots] = cache_ref[r, :, pl.ds(at, cols)]
            start += slots
    write_lengths(rows, lengths_ref, mate_ref)


def pass_kernel(*refs):
    pass


def attend_kernel(wide, plane, members, rows, early, query_cols, frequency_ref, *refs):
    partials, held, attended_ref = refs[wide - 1 :: -1], refs[wide:-1], refs[-1]
    even = plane // 2 - 1 if members[0] else 0
    firsts, lasts, whole = held[:even], held[even : 2 * even], held[2 * even :]
    slots = (whole[0].shape[0] - 16) // (2 * rows)
    cols = partials[0].shape[-1]
    kv_cols = (cols - query_cols) // 2
    kv_heads, group = kv_cols // HD, query_cols // kv_cols
    pairs = len(members) * rows
    count = pairs * kv_heads
    heads = count * group
    scale = 1.0 / HD**0.5
    own = slice(members[0], members[-1] + 1)
    total = partials[0][own]
    for k in range(1, wide):
        total = total + partials[k][own]
    total = total.reshape(pairs, cols).astype(jnp.bfloat16).astype(jnp.float32)

    def cached(values):
        parts = []
        for p in range(pairs):
            l, r = members[p // rows], p % rows
            ref, at = whole[(l + 1) // 2], values * rows + r
            shift = ref.shape[0] - whole[0].shape[0] if l == 1 else 0
            if l % 2 == 0 and l:
                ref = firsts[l // 2 - 1]
                if at >= rows + early:
                    ref, at = lasts[l // 2 - 1], at - rows - early
            parts.append(ref[shift + at * slots : shift + (at + 1) * slots])
        return jnp.concatenate(parts, 1)

    filled = []
    for l in members:
        block = lasts[l // 2 - 1] if l % 2 == 0 and l else whole[(l + 1) // 2]
        last = block[block.shape[0] - 16 :, :HD].astype(jnp.float32)
        filled += [last[r : r + 1] for r in range(rows)]
    angles = jnp.concatenate(filled, 0) * frequency_ref[...]
    cosine, sine = jnp.cos(angles), jnp.sin(angles)
    front = lax.broadcasted_iota(jnp.int32, (1, HD), 1) < HD // 2
    sine = jnp.where(front, -sine, sine)

    def rotate(vector):
        return vector * cosine + pltpu.roll(vector, HD // 2, 1) * sine

    query, key_new, value_new = [], [], []
    for h in range(kv_heads):
        turned = [
            rotate(total[:, (h * group + g) * HD : (h * group + g + 1) * HD]) for g in range(group)
        ]
        query.append(jnp.swapaxes(jnp.stack(turned, 0), 0, 1))
        at = query_cols + h * HD
        key_new.append(rotate(total[:, at : at + HD]))
        value_new.append(total[:, at + kv_cols : at + kv_cols + HD])
    query = jnp.stack(query, 1).reshape(heads, HD)
    turned_query = query.T.astype(jnp.bfloat16)
    key_new = jnp.stack(key_new, 1).reshape(count, HD).astype(jnp.bfloat16)
    value_new = jnp.stack(value_new, 1).reshape(count, HD)

    head_pair = lax.broadcasted_iota(jnp.int32, (1, heads), 1) // group
    by_pair = jnp.concatenate(
        [jnp.where(head_pair == b, turned_query, jnp.zeros_like(turned_query)) for b in range(count)],
        0,
    )
    scores = scale * jnp.dot(cached(0), by_pair, preferred_element_type=jnp.float32)
    own = scale * jnp.dot(key_new, turned_query, preferred_element_type=jnp.float32)
    of_pair = lax.broadcasted_iota(jnp.int32, (count, 1), 0) == head_pair
    own = jnp.sum(jnp.where(of_pair, own, 0.0), 0, keepdims=True)
    length = jnp.zeros((1, heads), jnp.float32)
    for p in range(pairs):
        length = jnp.where(head_pair // kv_heads == p, filled[p][:, :1], length)
    slot = lax.broadcasted_iota(jnp.int32, (slots, 1), 0).astype(jnp.float32)
    scores = jnp.where(slot < length, scores, -1e30)
    top = jnp.maximum(jnp.max(scores, 0, keepdims=True), own)
    weights = jnp.exp(scores - top)
    own_weight = jnp.exp(own - top)
    denominator = jnp.sum(weights, 0, keepdims=True) + own_weight
    probability = (weights / denominator).astype(jnp.bfloat16)
    own_prob = (own_weight / denominator).astype(jnp.bfloat16)
    contract_rows = (((0,), (0,)), ((), ()))
    mixed = lax.dot_general(
        probability, cached(1), contract_rows, preferred_element_type=jnp.float32
    )
    own_prob = jnp.where(of_pair, own_prob.astype(jnp.float32), 0.0).astype(jnp.bfloat16)
    fresh = lax.dot_general(
        own_prob, value_new.astype(jnp.bfloat16), contract_rows, preferred_element_type=jnp.float32
    )
    mixed = [
        mixed[b * group : (b + 1) * group, b * HD : (b + 1) * HD]
        + fresh[b * group : (b + 1) * group]
        for b in range(count)
    ]
    attended = []
    for h in range(kv_heads):
        by_head = jnp.swapaxes(jnp.stack(mixed[h::kv_heads], 0), 0, 1)
        attended += [by_head[g] for g in range(group)]
    attended = jnp.concatenate(attended, 1)
    attended_ref[...] = attended.reshape(len(members), rows, query_cols).astype(jnp.bfloat16)


def join_kernel(*refs):
    at = 0
    for block in refs[:-1]:
        refs[-1][at : at + block.shape[0]] = block[...]
        at += block.shape[0]


def output_kernel(at, cols, order, weight_ref, *refs):
    blocks, keep_ref, give_ref = [refs[n] for n in order], refs[-2], refs[-1]
    wide = len(blocks)
    plane, rows, depth = blocks[0].shape
    attended = jnp.concatenate(
        [block[...].reshape(plane * rows, depth) for block in blocks], 0
    )
    step = min(cols, 512)
    for c in range(0, cols, step):
        part = jnp.dot(
            attended, weight_ref[:, at + c : at + c + step], preferred_element_type=jnp.float32
        )
        part = part.reshape(wide * plane // 2, 2 * rows, step)
        keep_ref[:, :, c : c + step] = part[:, :rows]
        give_ref[:, :, c : c + step] = part[:, rows:]


def halve_kernel(a_ref, b_ref, keep_ref, give_ref):
    for n in range(keep_ref.shape[0]):
        keep_ref[n] = a_ref[2 * n] + b_ref[2 * n]
        give_ref[n] = a_ref[2 * n + 1] + b_ref[2 * n + 1]


def total_kernel(parts, *refs):
    sums, blocks = refs[: 2 * parts], refs[2 * parts :]
    cols = sums[0].shape[-1]
    for p in range(parts):
        for k, block in enumerate(blocks):
            total = sums[2 * p][k] + sums[2 * p + 1][k]
            block[:, p * cols : (p + 1) * cols] = total.astype(jnp.bfloat16)


def finish_kernel(*refs):
    blocks, result_ref = refs[-2::-1], refs[-1]
    own = lax.axis_index("gx")
    cols = blocks[0].shape[-1]
    for k, block in enumerate(blocks):
        at = pl.multiple_of((own ^ k) * cols, cols)
        result_ref[:, pl.ds(at, cols)] = block[...]


def swap_blocks(blocks, axes):
    return lax.all_to_all(blocks, axes, split_axis=0, concat_axis=0, tiled=True)


def swap_pairs(value, axis, step):
    return lax.ppermute(value, axis, [(i, i ^ step) for i in range(lax.axis_size(axis))])


def swap_plane(value, step):
    return lax.ppermute(value, PLANE, [(i, i ^ step) for i in range(lax.axis_size(PLANE))])


def swap_wide(blocks):
    moved = [swap_pairs(blocks[k], "gx", k) for k in range(len(blocks) - 1, 0, -1)]
    return [blocks[0]] + moved[::-1]


def shards(
    tokens,
    norm_gain,
    query_weight,
    key_weight,
    value_weight,
    out_weight,
    cache_keys,
    cache_values,
    lengths,
):
    rows = tokens.shape[0]
    wide = lax.axis_size("gx")
    plane = lax.axis_size(PLANE)
    owners = wide * plane
    width, query_cols = query_weight.shape
    kv_cols = key_weight.shape[1]
    depth, out_cols = out_weight.shape
    cols = query_cols + 2 * kv_cols

    def params(mib):
        return pltpu.CompilerParams(vmem_limit_bytes=mib * MIB)

    def cost(flops, size):
        return pl.CostEstimate(flops=flops, bytes_accessed=size, transcendentals=0)

    half = width // 2
    scaled = pl.pallas_call(
        scale_kernel,
        out_shape=jax.ShapeDtypeStruct(tokens.shape, jnp.float32),
        in_specs=[IN_VMEM],
        out_specs=IN_VMEM,
        compiler_params=params(8),
        cost_estimate=cost(40 * 10**9, MIB),
    )(tokens)
    normed = pl.pallas_call(
        functools.partial(gain_kernel, wide, plane),
        out_shape=jax.ShapeDtypeStruct((owners, rows, half), jnp.bfloat16),
        in_specs=[IN_VMEM, IN_VMEM],
        out_specs=IN_VMEM,
        compiler_params=params(8),
    )(scaled, norm_gain.reshape(1, -1))
    slots = cache_keys.shape[1]
    even = plane // 2 - 1
    early = rows // 2
    every = range(rows)

    def cut(plan, after):
        return pl.pallas_call(
            functools.partial(cut_kernel, plan),
            out_shape=[
                jax.ShapeDtypeStruct(
                    ((len(key_rows) + len(value_rows)) * slots + 16 * with_lengths, kv_cols),
                    cache_keys.dtype,
                )
                for _, key_rows, value_rows, with_lengths in plan
            ],
            in_specs=[IN_VMEM] * 4,
            out_specs=[IN_VMEM] * len(plan),
            compiler_params=params(8),
        )(lengths.reshape(1, -1), cache_keys, cache_values, after)

    plan = [(l, every, every[:early], False) for l in range(2, plane, 2)]
    plan += [(l, (), every[early:], True) for l in range(2, plane, 2)]
    plan += [(l, every, every, True) for l in range(3, plane, 2)]
    blocks = cut(plan, normed)
    firsts, rest = blocks[:even], blocks[even:]
    firsts = [swap_plane(firsts[s], 2 * s + 2) for s in range(even)]
    own_half = swap_blocks(normed, ROW_AXES)
    pieces = half // kv_cols
    mate = pl.pallas_call(
        mate_kernel,
        out_shape=jax.ShapeDtypeStruct(
            (pieces * owners * rows + 2 * rows * slots + 16, kv_cols), cache_keys.dtype
        ),
        in_specs=[IN_VMEM] * 4,
        out_specs=IN_VMEM,
        compiler_params=params(8),
    )(lengths.reshape(1, -1), cache_keys, cache_values, own_half)
    mate = swap_plane(mate, 1)
    rest = pl.pallas_call(
        pass_kernel,
        out_shape=[jax.ShapeDtypeStruct(value.shape, value.dtype) for value in rest],
        in_specs=[ANYWHERE] * (len(rest) + even + 1),
        out_specs=[ANYWHERE] * len(rest),
        input_output_aliases={n: n for n in range(len(rest))},
        compiler_params=params(1),
    )(*rest, own_half, *firsts)
    lasts = [swap_plane(rest[s], 2 * s + 2) for s in range(even)]
    odd = [mate, *[swap_plane(rest[even + s], 2 * s + 3) for s in range(even)]]
    (mine,) = cut([(0, every, every, True)], own_half)
    held = [*firsts, *lasts, mine, *odd]
    weights = (query_weight, key_weight, value_weight)
    half_cost = cost(owners * rows * width * cols, width * cols)
    partial = pl.pallas_call(
        functools.partial(project_kernel, True, wide, plane),
        out_shape=jax.ShapeDtypeStruct((owners * rows, cols), jnp.float32),
        in_specs=[IN_VMEM] * 4,
        out_specs=IN_VMEM,
        compiler_params=params(8),
        cost_estimate=half_cost,
    )(own_half, *weights)
    partial = pl.pallas_call(
        functools.partial(project_kernel, False, wide, plane),
        out_shape=[jax.ShapeDtypeStruct((plane, rows, cols), jnp.float32)] * wide,
        in_specs=[IN_VMEM] * 5,
        out_specs=[IN_VMEM] * wide,
        scratch_shapes=[pltpu.VMEM((owners, rows, cols), jnp.float32)],
        compiler_params=params(8),
        cost_estimate=half_cost,
    )(mate, *weights, partial)
    partial = swap_wide(partial)

    half_dim = HD // 2
    frequency = 500000.0 ** (-np.arange(half_dim, dtype=np.float64) / half_dim)
    frequency = np.tile(frequency.astype(np.float32), 2).reshape(1, HD)
    attended = []
    for members in (range(2), range(2, plane)):
        used = held if members[0] else held[2 * even : 2 * even + 2]
        attended.append(
            pl.pallas_call(
                functools.partial(attend_kernel, wide, plane, members, rows, early, query_cols),
                out_shape=jax.ShapeDtypeStruct((len(members), rows, query_cols), jnp.bfloat16),
                in_specs=[IN_VMEM] * (1 + wide + len(used)),
                out_specs=IN_VMEM,
                compiler_params=params(8),
                cost_estimate=cost(10**10, 4 * MIB) if members[0] else cost(1, 1),
            )(jnp.asarray(frequency), *partial[::-1], *used)
        )
    attended = pl.pallas_call(
        join_kernel,
        out_shape=jax.ShapeDtypeStruct((plane, rows, query_cols), jnp.bfloat16),
        in_specs=[IN_VMEM, IN_VMEM],
        out_specs=IN_VMEM,
        compiler_params=params(8),
    )(*attended)
    head_rows = swap_wide([attended] * wide)
    parts = 2
    order = [0, *range(wide - 2, 0, -1), wide - 1]
    part_cols = out_cols // parts
    sums = []
    for p in range(parts):
        count = owners // 2
        shape = jax.ShapeDtypeStruct((count, rows, part_cols), jnp.float32)
        keep, give = pl.pallas_call(
            functools.partial(output_kernel, p * part_cols, part_cols, order),
            out_shape=(shape, shape),
            in_specs=[IN_VMEM] * (1 + wide),
            out_specs=(IN_VMEM, IN_VMEM),
            compiler_params=params(8),
            cost_estimate=cost(2 * owners * rows * depth * part_cols, 2 * depth * part_cols),
        )(out_weight, *[head_rows[k] for k in order])
        give = swap_plane(give, 1)
        step = 2
        while step < plane:
            count //= 2
            shape = jax.ShapeDtypeStruct((count, rows, part_cols), jnp.float32)
            keep, give = pl.pallas_call(
                halve_kernel,
                out_shape=(shape, shape),
                in_specs=[IN_VMEM, IN_VMEM],
                out_specs=(IN_VMEM, IN_VMEM),
                compiler_params=params(8),
            )(keep, give)
            give = swap_plane(give, step)
            step *= 2
        sums += [keep, give]
    blocks = pl.pallas_call(
        functools.partial(total_kernel, parts),
        out_shape=[jax.ShapeDtypeStruct((rows, out_cols), jnp.bfloat16)] * wide,
        in_specs=[IN_VMEM] * len(sums),
        out_specs=[IN_VMEM] * wide,
        compiler_params=params(8),
    )(*sums)
    blocks = swap_wide(blocks)
    return pl.pallas_call(
        finish_kernel,
        out_shape=jax.ShapeDtypeStruct((rows, wide * out_cols), jnp.bfloat16),
        in_specs=[IN_VMEM] * wide,
        out_specs=IN_VMEM,
        compiler_params=params(8),
    )(*blocks[::-1])


def solution(mesh):
    placed = (
        P(("groups", "gx", "gy", "gz"), None),
        P(),
        P("gx", ("gy", "gz")),
        P("gx", ("gy", "gz")),
        P("gx", ("gy", "gz")),
        P(("gy", "gz"), "gx"),
        P(("groups", "gx", "gy", "gz"), None, None),
        P(("groups", "gx", "gy", "gz"), None, None),
        P(("groups", "gx", "gy", "gz")),
    )
    return jax.shard_map(
        shards,
        mesh=mesh,
        in_specs=placed,
        out_specs=P(("groups", "gx", "gy", "gz"), None),
        check_vma=False,
    )
```

```python
import functools

import jax
import jax.numpy as jnp
import numpy as np
from jax import lax
from jax.experimental import pallas as pl
from jax.experimental.pallas import tpu as pltpu
from jax.sharding import PartitionSpec as P

HD = 128
ROW_AXES = ("gx", "gy", "gz")
PLANE = ("gy", "gz")
MIB = 1024 * 1024
IN_VMEM = pl.BlockSpec(memory_space=pltpu.VMEM)
ANYWHERE = pl.BlockSpec(memory_space=pl.ANY)


def scale_kernel(tokens_ref, scaled_ref):
    tokens = tokens_ref[...].astype(jnp.float32)
    mean_square = jnp.mean(tokens * tokens, -1, keepdims=True)
    scaled_ref[...] = tokens * lax.rsqrt(mean_square + 1e-05)


def gain_kernel(wide, plane, scaled_ref, gain_ref, _, blocks_ref):
    normed = (scaled_ref[...] * gain_ref[...]).astype(jnp.bfloat16)
    half = normed.shape[1] // wide // 2
    for i in range(wide):
        for j in range(plane):
            at = (2 * i + j % 2) * half
            blocks_ref[i * plane + j] = normed[:, at : at + half]


def project_kernel(own, wide, plane, rows_ref, query_ref, key_ref, value_ref, *refs):
    half = query_ref.shape[0] // 2
    core = lax.axis_index("gz")
    at_row = pl.multiple_of((core if own else 1 - core) * half, half)
    if own:
        normed = rows_ref[...].reshape(-1, half)
    else:
        count, cols = refs[0].shape[0], rows_ref.shape[1]
        normed = jnp.concatenate(
            [rows_ref[n * count : (n + 1) * count] for n in range(half // cols)], 1
        )
        owners, rows = refs[-1].shape[:2]
    sums_ref = refs[-1]
    at = 0
    for weight in (query_ref, key_ref, value_ref):
        cols = weight.shape[1]
        step = min(cols, 256)
        for c in range(0, cols, step):
            part = jnp.dot(
                normed,
                weight[pl.ds(at_row, half), c : c + step],
                preferred_element_type=jnp.float32,
            )
            if own:
                sums_ref[:, at : at + step] = part
            else:
                part = part + refs[0][:, at : at + step]
                sums_ref[:, :, at : at + step] = part.reshape(owners, rows, step)
            at += step
    if not own:
        own_wide = lax.axis_index("gx")
        own_plane = 2 * lax.axis_index("gy") + core
        for k in range(wide):
            for l in range(plane):
                refs[1 + k][l] = sums_ref[(own_wide ^ k) * plane + (own_plane ^ l)]


def own_place():
    return 2 * lax.axis_index("gy") + lax.axis_index("gz")


def write_lengths(rows, lengths_ref, block_ref):
    at_row = lax.broadcasted_iota(jnp.int32, (16, block_ref.shape[1]), 0)
    filled = jnp.zeros(at_row.shape, jnp.float32)
    for r in range(rows):
        filled = jnp.where(at_row == r, lengths_ref[:, r : r + 1].astype(jnp.float32), filled)
    block_ref[block_ref.shape[0] - 16 :] = filled.astype(jnp.bfloat16)


def cut_kernel(plan, lengths_ref, keys_ref, values_ref, _, *blocks):
    rows, slots, _ = keys_ref.shape
    cols = blocks[0].shape[1]
    for (slot, key_rows, value_rows, with_lengths), block in zip(plan, blocks):
        at = pl.multiple_of((own_place() ^ slot) * cols, cols)
        start = 0
        for cache_ref, wanted in ((keys_ref, key_rows), (values_ref, value_rows)):
            for r in wanted:
                block[start : start + slots] = cache_ref[r, :, pl.ds(at, cols)]
                start += slots
        if with_lengths:
            write_lengths(rows, lengths_ref, block)


def mate_kernel(lengths_ref, keys_ref, values_ref, rows_ref, mate_ref):
    rows, slots, _ = keys_ref.shape
    cols = mate_ref.shape[1]
    half = rows_ref.shape[-1]
    normed = rows_ref[...].reshape(-1, half)
    count = normed.shape[0]
    start = 0
    for c in range(0, half, cols):
        mate_ref[start : start + count] = normed[:, c : c + cols]
        start += count
    at = pl.multiple_of((own_place() ^ 1) * cols, cols)
    for cache_ref in (keys_ref, values_ref):
        for r in range(rows):
            mate_ref[start : start + slots] = cache_ref[r, :, pl.ds(at, cols)]
            start += slots
    write_lengths(rows, lengths_ref, mate_ref)


def pass_kernel(*refs):
    pass


def attend_kernel(wide, plane, members, rows, early, query_cols, frequency_ref, *refs):
    partials, held, attended_ref = refs[wide - 1 :: -1], refs[wide:-1], refs[-1]
    even = plane // 2 - 1 if members[0] else 0
    firsts, lasts, whole = held[:even], held[even : 2 * even], held[2 * even :]
    slots = (whole[0].shape[0] - 16) // (2 * rows)
    cols = partials[0].shape[-1]
    kv_cols = (cols - query_cols) // 2
    kv_heads, group = kv_cols // HD, query_cols // kv_cols
    pairs = len(members) * rows
    count = pairs * kv_heads
    heads = count * group
    scale = 1.0 / HD**0.5
    own = slice(members[0], members[-1] + 1)
    total = partials[0][own]
    for k in range(1, wide):
        total = total + partials[k][own]
    total = total.reshape(pairs, cols).astype(jnp.bfloat16).astype(jnp.float32)

    def cached(values):
        parts = []
        for p in range(pairs):
            l, r = members[p // rows], p % rows
            ref, at = whole[(l + 1) // 2], values * rows + r
            shift = ref.shape[0] - whole[0].shape[0] if l == 1 else 0
            if l % 2 == 0 and l:
                ref = firsts[l // 2 - 1]
                if at >= rows + early:
                    ref, at = lasts[l // 2 - 1], at - rows - early
            parts.append(ref[shift + at * slots : shift + (at + 1) * slots])
        return jnp.concatenate(parts, 1)

    filled = []
    for l in members:
        block = lasts[l // 2 - 1] if l % 2 == 0 and l else whole[(l + 1) // 2]
        last = block[block.shape[0] - 16 :, :HD].astype(jnp.float32)
        filled += [last[r : r + 1] for r in range(rows)]
    angles = jnp.concatenate(filled, 0) * frequency_ref[...]
    cosine, sine = jnp.cos(angles), jnp.sin(angles)
    front = lax.broadcasted_iota(jnp.int32, (1, HD), 1) < HD // 2
    sine = jnp.where(front, -sine, sine)

    def rotate(vector):
        return vector * cosine + pltpu.roll(vector, HD // 2, 1) * sine

    query, key_new, value_new = [], [], []
    for h in range(kv_heads):
        turned = [
            rotate(total[:, (h * group + g) * HD : (h * group + g + 1) * HD]) for g in range(group)
        ]
        query.append(jnp.swapaxes(jnp.stack(turned, 0), 0, 1))
        at = query_cols + h * HD
        key_new.append(rotate(total[:, at : at + HD]))
        value_new.append(total[:, at + kv_cols : at + kv_cols + HD])
    query = jnp.stack(query, 1).reshape(heads, HD)
    turned_query = query.T.astype(jnp.bfloat16)
    key_new = jnp.stack(key_new, 1).reshape(count, HD).astype(jnp.bfloat16)
    value_new = jnp.stack(value_new, 1).reshape(count, HD)

    head_pair = lax.broadcasted_iota(jnp.int32, (1, heads), 1) // group
    by_pair = jnp.concatenate(
        [jnp.where(head_pair == b, turned_query, jnp.zeros_like(turned_query)) for b in range(count)],
        0,
    )
    scores = scale * jnp.dot(cached(0), by_pair, preferred_element_type=jnp.float32)
    own = scale * jnp.dot(key_new, turned_query, preferred_element_type=jnp.float32)
    of_pair = lax.broadcasted_iota(jnp.int32, (count, 1), 0) == head_pair
    own = jnp.sum(jnp.where(of_pair, own, 0.0), 0, keepdims=True)
    length = jnp.zeros((1, heads), jnp.float32)
    for p in range(pairs):
        length = jnp.where(head_pair // kv_heads == p, filled[p][:, :1], length)
    slot = lax.broadcasted_iota(jnp.int32, (slots, 1), 0).astype(jnp.float32)
    scores = jnp.where(slot < length, scores, -1e30)
    top = jnp.maximum(jnp.max(scores, 0, keepdims=True), own)
    weights = jnp.exp(scores - top)
    own_weight = jnp.exp(own - top)
    denominator = jnp.sum(weights, 0, keepdims=True) + own_weight
    probability = (weights / denominator).astype(jnp.bfloat16)
    own_prob = (own_weight / denominator).astype(jnp.bfloat16)
    contract_rows = (((0,), (0,)), ((), ()))
    mixed = lax.dot_general(
        probability, cached(1), contract_rows, preferred_element_type=jnp.float32
    )
    own_prob = jnp.where(of_pair, own_prob.astype(jnp.float32), 0.0).astype(jnp.bfloat16)
    fresh = lax.dot_general(
        own_prob, value_new.astype(jnp.bfloat16), contract_rows, preferred_element_type=jnp.float32
    )
    mixed = [
        mixed[b * group : (b + 1) * group, b * HD : (b + 1) * HD]
        + fresh[b * group : (b + 1) * group]
        for b in range(count)
    ]
    attended = []
    for h in range(kv_heads):
        by_head = jnp.swapaxes(jnp.stack(mixed[h::kv_heads], 0), 0, 1)
        attended += [by_head[g] for g in range(group)]
    attended = jnp.concatenate(attended, 1)
    attended_ref[...] = attended.reshape(len(members), rows, query_cols).astype(jnp.bfloat16)


def join_kernel(*refs):
    at = 0
    for block in refs[:-1]:
        refs[-1][at : at + block.shape[0]] = block[...]
        at += block.shape[0]


def output_kernel(at, cols, order, weight_ref, *refs):
    blocks, keep_ref, give_ref = [refs[n] for n in order], refs[-2], refs[-1]
    wide = len(blocks)
    plane, rows, depth = blocks[0].shape
    attended = jnp.concatenate(
        [block[...].reshape(plane * rows, depth) for block in blocks], 0
    )
    step = min(cols, 512)
    for c in range(0, cols, step):
        part = jnp.dot(
            attended, weight_ref[:, at + c : at + c + step], preferred_element_type=jnp.float32
        )
        part = part.reshape(wide * plane // 2, 2 * rows, step)
        keep_ref[:, :, c : c + step] = part[:, :rows]
        give_ref[:, :, c : c + step] = part[:, rows:]


def halve_kernel(a_ref, b_ref, keep_ref, give_ref):
    for n in range(keep_ref.shape[0]):
        keep_ref[n] = a_ref[2 * n] + b_ref[2 * n]
        give_ref[n] = a_ref[2 * n + 1] + b_ref[2 * n + 1]


def total_kernel(parts, *refs):
    sums, blocks = refs[: 2 * parts], refs[2 * parts :]
    cols = sums[0].shape[-1]
    for p in range(parts):
        for k, block in enumerate(blocks):
            total = sums[2 * p][k] + sums[2 * p + 1][k]
            block[:, p * cols : (p + 1) * cols] = total.astype(jnp.bfloat16)


def finish_kernel(*refs):
    blocks, result_ref = refs[-2::-1], refs[-1]
    own = lax.axis_index("gx")
    cols = blocks[0].shape[-1]
    for k, block in enumerate(blocks):
        at = pl.multiple_of((own ^ k) * cols, cols)
        result_ref[:, pl.ds(at, cols)] = block[...]


def swap_blocks(blocks, axes):
    return lax.all_to_all(blocks, axes, split_axis=0, concat_axis=0, tiled=True)


def swap_pairs(value, axis, step):
    return lax.ppermute(value, axis, [(i, i ^ step) for i in range(lax.axis_size(axis))])


def swap_plane(value, step):
    return lax.ppermute(value, PLANE, [(i, i ^ step) for i in range(lax.axis_size(PLANE))])


def swap_wide(blocks):
    moved = [swap_pairs(blocks[k], "gx", k) for k in range(len(blocks) - 1, 0, -1)]
    return [blocks[0]] + moved[::-1]


def shards(
    tokens,
    norm_gain,
    query_weight,
    key_weight,
    value_weight,
    out_weight,
    cache_keys,
    cache_values,
    lengths,
):
    rows = tokens.shape[0]
    wide = lax.axis_size("gx")
    plane = lax.axis_size(PLANE)
    owners = wide * plane
    width, query_cols = query_weight.shape
    kv_cols = key_weight.shape[1]
    depth, out_cols = out_weight.shape
    cols = query_cols + 2 * kv_cols

    def params(mib):
        return pltpu.CompilerParams(vmem_limit_bytes=mib * MIB)

    def cost(flops, size):
        return pl.CostEstimate(flops=flops, bytes_accessed=size, transcendentals=0)

    half = width // 2
    scaled = pl.pallas_call(
        scale_kernel,
        out_shape=jax.ShapeDtypeStruct(tokens.shape, jnp.float32),
        in_specs=[IN_VMEM],
        out_specs=IN_VMEM,
        compiler_params=params(8),
        cost_estimate=cost(40 * 10**9, MIB),
    )(tokens)
    slots = cache_keys.shape[1]
    even = plane // 2 - 1
    early = rows // 2
    every = range(rows)

    def cut(plan, after):
        return pl.pallas_call(
            functools.partial(cut_kernel, plan),
            out_shape=[
                jax.ShapeDtypeStruct(
                    ((len(key_rows) + len(value_rows)) * slots + 16 * with_lengths, kv_cols),
                    cache_keys.dtype,
                )
                for _, key_rows, value_rows, with_lengths in plan
            ],
            in_specs=[IN_VMEM] * 4,
            out_specs=[IN_VMEM] * len(plan),
            compiler_params=params(8),
        )(lengths.reshape(1, -1), cache_keys, cache_values, after)

    plan = [(l, every, every[:early], False) for l in range(2, plane, 2)]
    plan += [(l, (), every[early:], True) for l in range(2, plane, 2)]
    plan += [(l, every, every, True) for l in range(3, plane, 2)]
    blocks = cut(plan, scaled)
    firsts, rest = blocks[:even], blocks[even:]
    firsts = [swap_plane(firsts[s], 2 * s + 2) for s in range(even)]
    normed = pl.pallas_call(
        functools.partial(gain_kernel, wide, plane),
        out_shape=jax.ShapeDtypeStruct((owners, rows, half), jnp.bfloat16),
        in_specs=[IN_VMEM] * 3,
        out_specs=IN_VMEM,
        compiler_params=params(8),
    )(scaled, norm_gain.reshape(1, -1), rest[0])
    own_half = swap_blocks(normed, ROW_AXES)
    pieces = half // kv_cols
    mate = pl.pallas_call(
        mate_kernel,
        out_shape=jax.ShapeDtypeStruct(
            (pieces * owners * rows + 2 * rows * slots + 16, kv_cols), cache_keys.dtype
        ),
        in_specs=[IN_VMEM] * 4,
        out_specs=IN_VMEM,
        compiler_params=params(8),
    )(lengths.reshape(1, -1), cache_keys, cache_values, own_half)
    mate = swap_plane(mate, 1)
    rest = pl.pallas_call(
        pass_kernel,
        out_shape=[jax.ShapeDtypeStruct(value.shape, value.dtype) for value in rest],
        in_specs=[ANYWHERE] * (len(rest) + even + 1),
        out_specs=[ANYWHERE] * len(rest),
        input_output_aliases={n: n for n in range(len(rest))},
        compiler_params=params(1),
    )(*rest, own_half, *firsts)
    lasts = [swap_plane(rest[s], 2 * s + 2) for s in range(even)]
    odd = [mate, *[swap_plane(rest[even + s], 2 * s + 3) for s in range(even)]]
    (mine,) = cut([(0, every, every, True)], own_half)
    held = [*firsts, *lasts, mine, *odd]
    weights = (query_weight, key_weight, value_weight)
    half_cost = cost(owners * rows * width * cols, width * cols)
    partial = pl.pallas_call(
        functools.partial(project_kernel, True, wide, plane),
        out_shape=jax.ShapeDtypeStruct((owners * rows, cols), jnp.float32),
        in_specs=[IN_VMEM] * 4,
        out_specs=IN_VMEM,
        compiler_params=params(8),
        cost_estimate=half_cost,
    )(own_half, *weights)
    partial = pl.pallas_call(
        functools.partial(project_kernel, False, wide, plane),
        out_shape=[jax.ShapeDtypeStruct((plane, rows, cols), jnp.float32)] * wide,
        in_specs=[IN_VMEM] * 5,
        out_specs=[IN_VMEM] * wide,
        scratch_shapes=[pltpu.VMEM((owners, rows, cols), jnp.float32)],
        compiler_params=params(8),
        cost_estimate=half_cost,
    )(mate, *weights, partial)
    partial = swap_wide(partial)

    half_dim = HD // 2
    frequency = 500000.0 ** (-np.arange(half_dim, dtype=np.float64) / half_dim)
    frequency = np.tile(frequency.astype(np.float32), 2).reshape(1, HD)
    attended = []
    for members in (range(2), range(2, plane)):
        used = held if members[0] else held[2 * even : 2 * even + 2]
        attended.append(
            pl.pallas_call(
                functools.partial(attend_kernel, wide, plane, members, rows, early, query_cols),
                out_shape=jax.ShapeDtypeStruct((len(members), rows, query_cols), jnp.bfloat16),
                in_specs=[IN_VMEM] * (1 + wide + len(used)),
                out_specs=IN_VMEM,
                compiler_params=params(8),
                cost_estimate=cost(10**10, 4 * MIB) if members[0] else cost(1, 1),
            )(jnp.asarray(frequency), *partial[::-1], *used)
        )
    attended = pl.pallas_call(
        join_kernel,
        out_shape=jax.ShapeDtypeStruct((plane, rows, query_cols), jnp.bfloat16),
        in_specs=[IN_VMEM, IN_VMEM],
        out_specs=IN_VMEM,
        compiler_params=params(8),
    )(*attended)
    head_rows = swap_wide([attended] * wide)
    parts = 2
    order = [0, *range(wide - 2, 0, -1), wide - 1]
    part_cols = out_cols // parts
    sums = []
    for p in range(parts):
        count = owners // 2
        shape = jax.ShapeDtypeStruct((count, rows, part_cols), jnp.float32)
        keep, give = pl.pallas_call(
            functools.partial(output_kernel, p * part_cols, part_cols, order),
            out_shape=(shape, shape),
            in_specs=[IN_VMEM] * (1 + wide),
            out_specs=(IN_VMEM, IN_VMEM),
            compiler_params=params(8),
            cost_estimate=cost(2 * owners * rows * depth * part_cols, 2 * depth * part_cols),
        )(out_weight, *[head_rows[k] for k in order])
        give = swap_plane(give, 1)
        step = 2
        while step < plane:
            count //= 2
            shape = jax.ShapeDtypeStruct((count, rows, part_cols), jnp.float32)
            keep, give = pl.pallas_call(
                halve_kernel,
                out_shape=(shape, shape),
                in_specs=[IN_VMEM, IN_VMEM],
                out_specs=(IN_VMEM, IN_VMEM),
                compiler_params=params(8),
            )(keep, give)
            give = swap_plane(give, step)
            step *= 2
        sums += [keep, give]
    blocks = pl.pallas_call(
        functools.partial(total_kernel, parts),
        out_shape=[jax.ShapeDtypeStruct((rows, out_cols), jnp.bfloat16)] * wide,
        in_specs=[IN_VMEM] * len(sums),
        out_specs=[IN_VMEM] * wide,
        compiler_params=params(8),
    )(*sums)
    blocks = swap_wide(blocks)
    return pl.pallas_call(
        finish_kernel,
        out_shape=jax.ShapeDtypeStruct((rows, wide * out_cols), jnp.bfloat16),
        in_specs=[IN_VMEM] * wide,
        out_specs=IN_VMEM,
        compiler_params=params(8),
    )(*blocks[::-1])


def solution(mesh):
    placed = (
        P(("groups", "gx", "gy", "gz"), None),
        P(),
        P("gx", ("gy", "gz")),
        P("gx", ("gy", "gz")),
        P("gx", ("gy", "gz")),
        P(("gy", "gz"), "gx"),
        P(("groups", "gx", "gy", "gz"), None, None),
        P(("groups", "gx", "gy", "gz"), None, None),
        P(("groups", "gx", "gy", "gz")),
    )
    return jax.shard_map(
        shards,
        mesh=mesh,
        in_specs=placed,
        out_specs=P(("groups", "gx", "gy", "gz"), None),
        check_vma=False,
    )
```

```python
import functools

import jax
import jax.numpy as jnp
import numpy as np
from jax import lax
from jax.experimental import pallas as pl
from jax.experimental.pallas import tpu as pltpu
from jax.sharding import PartitionSpec as P

HD = 128
ROW_AXES = ("gx", "gy", "gz")
PLANE = ("gy", "gz")
MIB = 1024 * 1024
IN_VMEM = pl.BlockSpec(memory_space=pltpu.VMEM)
ANYWHERE = pl.BlockSpec(memory_space=pl.ANY)


def sequence(wide):
    return sorted(range(1, wide), key=lambda k: (k != wide // 2, -k))


def scale_kernel(tokens_ref, scaled_ref):
    tokens = tokens_ref[...].astype(jnp.float32)
    mean_square = jnp.mean(tokens * tokens, -1, keepdims=True)
    scaled_ref[...] = tokens * lax.rsqrt(mean_square + 1e-05)


def gain_kernel(wide, plane, scaled_ref, gain_ref, blocks_ref):
    normed = (scaled_ref[...] * gain_ref[...]).astype(jnp.bfloat16)
    half = normed.shape[1] // wide // 2
    for i in range(wide):
        for j in range(plane):
            at = (2 * i + j % 2) * half
            blocks_ref[i * plane + j] = normed[:, at : at + half]


def project_kernel(own, wide, plane, rows_ref, query_ref, key_ref, value_ref, *refs):
    owners, rows, half = rows_ref.shape
    core = lax.axis_index("gz")
    at_row = pl.multiple_of((core if own else 1 - core) * half, half)
    normed = rows_ref[...].reshape(owners * rows, half)
    sums_ref = refs[-1]
    at = 0
    for weight in (query_ref, key_ref, value_ref):
        cols = weight.shape[1]
        step = min(cols, 256)
        for c in range(0, cols, step):
            part = jnp.dot(
                normed,
                weight[pl.ds(at_row, half), c : c + step],
                preferred_element_type=jnp.float32,
            )
            if own:
                sums_ref[:, at : at + step] = part
            else:
                part = part + refs[1][:, at : at + step]
                sums_ref[:, :, at : at + step] = part.reshape(owners, rows, step)
            at += step
    if not own:
        own_wide = lax.axis_index("gx")
        own_plane = 2 * lax.axis_index("gy") + core
        for k in range(wide):
            for l in range(plane):
                refs[2 + k][l] = sums_ref[(own_wide ^ k) * plane + (own_plane ^ l)]


def own_place():
    return 2 * lax.axis_index("gy") + lax.axis_index("gz")


def write_lengths(rows, lengths_ref, block_ref):
    at_row = lax.broadcasted_iota(jnp.int32, (16, block_ref.shape[1]), 0)
    filled = jnp.zeros(at_row.shape, jnp.float32)
    for r in range(rows):
        filled = jnp.where(at_row == r, lengths_ref[:, r : r + 1].astype(jnp.float32), filled)
    block_ref[block_ref.shape[0] - 16 :] = filled.astype(jnp.bfloat16)


def cut_kernel(plan, lengths_ref, keys_ref, values_ref, _, *blocks):
    rows, slots, _ = keys_ref.shape
    cols = blocks[0].shape[1]
    for (slot, key_rows, value_rows, with_lengths), block in zip(plan, blocks):
        at = pl.multiple_of((own_place() ^ slot) * cols, cols)
        start = 0
        for cache_ref, wanted in ((keys_ref, key_rows), (values_ref, value_rows)):
            for r in wanted:
                block[start : start + slots] = cache_ref[r, :, pl.ds(at, cols)]
                start += slots
        if with_lengths:
            write_lengths(rows, lengths_ref, block)


def pass_kernel(*refs):
    pass


def attend_kernel(wide, plane, members, rows, early, query_cols, frequency_ref, *refs):
    partials, held, attended_ref = refs[wide - 1 :: -1], refs[wide:-1], refs[-1]
    even = plane // 2 - 1 if members[0] else 0
    firsts, lasts, whole = held[:even], held[even : 2 * even], held[2 * even :]
    slots = (whole[0].shape[0] - 16) // (2 * rows)
    cols = partials[0].shape[-1]
    kv_cols = (cols - query_cols) // 2
    kv_heads, group = kv_cols // HD, query_cols // kv_cols
    pairs = len(members) * rows
    count = pairs * kv_heads
    heads = count * group
    scale = 1.0 / HD**0.5
    own = slice(members[0], members[-1] + 1)
    total = partials[0][own]
    for k in range(1, wide):
        total = total + partials[k][own]
    total = total.reshape(pairs, cols).astype(jnp.bfloat16).astype(jnp.float32)

    def cached(values):
        parts = []
        for p in range(pairs):
            l, r = members[p // rows], p % rows
            ref, at = whole[(l + 1) // 2], values * rows + r
            if l % 2 == 0 and l:
                ref = firsts[l // 2 - 1]
                if at >= rows + early:
                    ref, at = lasts[l // 2 - 1], at - rows - early
            parts.append(ref[at * slots : (at + 1) * slots])
        return jnp.concatenate(parts, 1)

    filled = []
    for l in members:
        block = lasts[l // 2 - 1] if l % 2 == 0 and l else whole[(l + 1) // 2]
        last = block[block.shape[0] - 16 :, :HD].astype(jnp.float32)
        filled += [last[r : r + 1] for r in range(rows)]
    angles = jnp.concatenate(filled, 0) * frequency_ref[...]
    cosine, sine = jnp.cos(angles), jnp.sin(angles)
    front = lax.broadcasted_iota(jnp.int32, (1, HD), 1) < HD // 2
    sine = jnp.where(front, -sine, sine)

    def rotate(vector):
        return vector * cosine + pltpu.roll(vector, HD // 2, 1) * sine

    query, key_new, value_new = [], [], []
    for h in range(kv_heads):
        turned = [
            rotate(total[:, (h * group + g) * HD : (h * group + g + 1) * HD]) for g in range(group)
        ]
        query.append(jnp.swapaxes(jnp.stack(turned, 0), 0, 1))
        at = query_cols + h * HD
        key_new.append(rotate(total[:, at : at + HD]))
        value_new.append(total[:, at + kv_cols : at + kv_cols + HD])
    query = jnp.stack(query, 1).reshape(heads, HD)
    turned_query = query.T.astype(jnp.bfloat16)
    key_new = jnp.stack(key_new, 1).reshape(count, HD).astype(jnp.bfloat16)
    value_new = jnp.stack(value_new, 1).reshape(count, HD)

    head_pair = lax.broadcasted_iota(jnp.int32, (1, heads), 1) // group
    by_pair = jnp.concatenate(
        [jnp.where(head_pair == b, turned_query, jnp.zeros_like(turned_query)) for b in range(count)],
        0,
    )
    scores = scale * jnp.dot(cached(0), by_pair, preferred_element_type=jnp.float32)
    own = scale * jnp.dot(key_new, turned_query, preferred_element_type=jnp.float32)
    of_pair = lax.broadcasted_iota(jnp.int32, (count, 1), 0) == head_pair
    own = jnp.sum(jnp.where(of_pair, own, 0.0), 0, keepdims=True)
    length = jnp.zeros((1, heads), jnp.float32)
    for p in range(pairs):
        length = jnp.where(head_pair // kv_heads == p, filled[p][:, :1], length)
    slot = lax.broadcasted_iota(jnp.int32, (slots, 1), 0).astype(jnp.float32)
    scores = jnp.where(slot < length, scores, -1e30)
    top = jnp.maximum(jnp.max(scores, 0, keepdims=True), own)
    weights = jnp.exp(scores - top)
    own_weight = jnp.exp(own - top)
    denominator = jnp.sum(weights, 0, keepdims=True) + own_weight
    probability = (weights / denominator).astype(jnp.bfloat16)
    own_prob = (own_weight / denominator).astype(jnp.bfloat16)
    contract_rows = (((0,), (0,)), ((), ()))
    mixed = lax.dot_general(
        probability, cached(1), contract_rows, preferred_element_type=jnp.float32
    )
    own_prob = jnp.where(of_pair, own_prob.astype(jnp.float32), 0.0).astype(jnp.bfloat16)
    fresh = lax.dot_general(
        own_prob, value_new.astype(jnp.bfloat16), contract_rows, preferred_element_type=jnp.float32
    )
    mixed = [
        mixed[b * group : (b + 1) * group, b * HD : (b + 1) * HD]
        + fresh[b * group : (b + 1) * group]
        for b in range(count)
    ]
    attended = []
    for h in range(kv_heads):
        by_head = jnp.swapaxes(jnp.stack(mixed[h::kv_heads], 0), 0, 1)
        attended += [by_head[g] for g in range(group)]
    attended = jnp.concatenate(attended, 1)
    attended_ref[...] = attended.reshape(len(members), rows, query_cols).astype(jnp.bfloat16)


def join_kernel(*refs):
    at = 0
    for block in refs[:-1]:
        refs[-1][at : at + block.shape[0]] = block[...]
        at += block.shape[0]


def output_kernel(at, cols, order, weight_ref, *refs):
    keep_ref, give_ref = refs[-2:]
    blocks = [refs[order.index(k)] for k in range(len(order))]
    wide = len(blocks)
    plane, rows, depth = blocks[0].shape
    attended = jnp.concatenate(
        [block[...].reshape(plane * rows, depth) for block in blocks], 0
    )
    step = min(cols, 512)
    for c in range(0, cols, step):
        part = jnp.dot(
            attended, weight_ref[:, at + c : at + c + step], preferred_element_type=jnp.float32
        )
        part = part.reshape(wide * plane // 2, 2 * rows, step)
        keep_ref[:, :, c : c + step] = part[:, :rows]
        give_ref[:, :, c : c + step] = part[:, rows:]


def halve_kernel(a_ref, b_ref, keep_ref, give_ref):
    for n in range(keep_ref.shape[0]):
        keep_ref[n] = a_ref[2 * n] + b_ref[2 * n]
        give_ref[n] = a_ref[2 * n + 1] + b_ref[2 * n + 1]


def total_kernel(parts, *refs):
    sums, blocks = refs[: 2 * parts], refs[2 * parts :]
    cols = sums[0].shape[-1]
    for p in range(parts):
        for k, block in enumerate(blocks):
            total = sums[2 * p][k] + sums[2 * p + 1][k]
            block[:, p * cols : (p + 1) * cols] = total.astype(jnp.bfloat16)


def finish_kernel(*refs):
    result_ref = refs[-1]
    order = [*sequence(len(refs) - 1), 0]
    blocks = [refs[order.index(k)] for k in range(len(order))]
    own = lax.axis_index("gx")
    cols = blocks[0].shape[-1]
    for k, block in enumerate(blocks):
        at = pl.multiple_of((own ^ k) * cols, cols)
        result_ref[:, pl.ds(at, cols)] = block[...]


def swap_blocks(blocks, axes):
    return lax.all_to_all(blocks, axes, split_axis=0, concat_axis=0, tiled=True)


def swap_pairs(value, axis, step):
    return lax.ppermute(value, axis, [(i, i ^ step) for i in range(lax.axis_size(axis))])


def swap_plane(value, step):
    return lax.ppermute(value, PLANE, [(i, i ^ step) for i in range(lax.axis_size(PLANE))])


def swap_wide(blocks):
    moved = [swap_pairs(blocks[k], "gx", k) for k in range(len(blocks) - 1, 0, -1)]
    return [blocks[0]] + moved[::-1]


def shards(
    tokens,
    norm_gain,
    query_weight,
    key_weight,
    value_weight,
    out_weight,
    cache_keys,
    cache_values,
    lengths,
):
    rows = tokens.shape[0]
    wide = lax.axis_size("gx")
    plane = lax.axis_size(PLANE)
    owners = wide * plane
    width, query_cols = query_weight.shape
    kv_cols = key_weight.shape[1]
    depth, out_cols = out_weight.shape
    cols = query_cols + 2 * kv_cols

    def params(mib):
        return pltpu.CompilerParams(vmem_limit_bytes=mib * MIB)

    def cost(flops, size):
        return pl.CostEstimate(flops=flops, bytes_accessed=size, transcendentals=0)

    half = width // 2
    scaled = pl.pallas_call(
        scale_kernel,
        out_shape=jax.ShapeDtypeStruct(tokens.shape, jnp.float32),
        in_specs=[IN_VMEM],
        out_specs=IN_VMEM,
        compiler_params=params(8),
        cost_estimate=cost(40 * 10**9, MIB),
    )(tokens)
    normed = pl.pallas_call(
        functools.partial(gain_kernel, wide, plane),
        out_shape=jax.ShapeDtypeStruct((owners, rows, half), jnp.bfloat16),
        in_specs=[IN_VMEM, IN_VMEM],
        out_specs=IN_VMEM,
        compiler_params=params(8),
    )(scaled, norm_gain.reshape(1, -1))
    slots = cache_keys.shape[1]
    even = plane // 2 - 1
    early = rows // 2
    every = range(rows)

    def cut(plan, after):
        return pl.pallas_call(
            functools.partial(cut_kernel, plan),
            out_shape=[
                jax.ShapeDtypeStruct(
                    ((len(key_rows) + len(value_rows)) * slots + 16 * with_lengths, kv_cols),
                    cache_keys.dtype,
                )
                for _, key_rows, value_rows, with_lengths in plan
            ],
            in_specs=[IN_VMEM] * 4,
            out_specs=[IN_VMEM] * len(plan),
            compiler_params=params(8),
        )(lengths.reshape(1, -1), cache_keys, cache_values, after)

    plan = [(l, every, every[:early], False) for l in range(2, plane, 2)]
    plan += [(l, (), every[early:], True) for l in range(2, plane, 2)]
    plan += [(l, every, every, True) for l in range(1, plane, 2)]
    blocks = cut(plan, normed)
    firsts, rest = blocks[:even], blocks[even:]
    firsts = [swap_plane(firsts[s], 2 * s + 2) for s in range(even)]
    own_half = swap_blocks(normed, ROW_AXES)
    other_half = swap_pairs(own_half, "gz", 1)
    rest = pl.pallas_call(
        pass_kernel,
        out_shape=[jax.ShapeDtypeStruct(value.shape, value.dtype) for value in rest],
        in_specs=[ANYWHERE] * (len(rest) + even + 1),
        out_specs=[ANYWHERE] * len(rest),
        input_output_aliases={n: n for n in range(len(rest))},
        compiler_params=params(1),
    )(*rest, own_half, *firsts)
    lasts = [swap_plane(rest[s], 2 * s + 2) for s in range(even)]
    odd = [swap_plane(rest[even + s], 2 * s + 1) for s in range(even + 1)]
    (mine,) = cut([(0, every, every, True)], own_half)
    held = [*firsts, *lasts, mine, *odd]
    weights = (query_weight, key_weight, value_weight)
    half_cost = cost(owners * rows * width * cols, width * cols)
    partial = pl.pallas_call(
        functools.partial(project_kernel, True, wide, plane),
        out_shape=jax.ShapeDtypeStruct((owners * rows, cols), jnp.float32),
        in_specs=[IN_VMEM] * 4,
        out_specs=IN_VMEM,
        compiler_params=params(8),
        cost_estimate=half_cost,
    )(own_half, *weights)
    partial = pl.pallas_call(
        functools.partial(project_kernel, False, wide, plane),
        out_shape=[jax.ShapeDtypeStruct((plane, rows, cols), jnp.float32)] * wide,
        in_specs=[IN_VMEM] * 6,
        out_specs=[IN_VMEM] * wide,
        scratch_shapes=[pltpu.VMEM((owners, rows, cols), jnp.float32)],
        compiler_params=params(8),
        cost_estimate=half_cost,
    )(other_half, *weights, odd[0], partial)
    partial = swap_wide(partial)

    half_dim = HD // 2
    frequency = 500000.0 ** (-np.arange(half_dim, dtype=np.float64) / half_dim)
    frequency = np.tile(frequency.astype(np.float32), 2).reshape(1, HD)
    attended = []
    for members in (range(2), range(2, plane)):
        used = held if members[0] else held[2 * even : 2 * even + 2]
        attended.append(
            pl.pallas_call(
                functools.partial(attend_kernel, wide, plane, members, rows, early, query_cols),
                out_shape=jax.ShapeDtypeStruct((len(members), rows, query_cols), jnp.bfloat16),
                in_specs=[IN_VMEM] * (1 + wide + len(used)),
                out_specs=IN_VMEM,
                compiler_params=params(8),
                cost_estimate=cost(10**10, 4 * MIB) if members[0] else cost(1, 1),
            )(jnp.asarray(frequency), *partial[::-1], *used)
        )
    attended = pl.pallas_call(
        join_kernel,
        out_shape=jax.ShapeDtypeStruct((plane, rows, query_cols), jnp.bfloat16),
        in_specs=[IN_VMEM, IN_VMEM],
        out_specs=IN_VMEM,
        compiler_params=params(8),
    )(*attended)
    head_rows = swap_wide([attended] * wide)
    parts = 2
    order = [0, *sequence(wide)[1:], sequence(wide)[0]]
    part_cols = out_cols // parts
    sums = []
    for p in range(parts):
        count = owners // 2
        shape = jax.ShapeDtypeStruct((count, rows, part_cols), jnp.float32)
        keep, give = pl.pallas_call(
            functools.partial(output_kernel, p * part_cols, part_cols, order),
            out_shape=(shape, shape),
            in_specs=[IN_VMEM] * (1 + wide),
            out_specs=(IN_VMEM, IN_VMEM),
            compiler_params=params(8),
            cost_estimate=cost(2 * owners * rows * depth * part_cols, 2 * depth * part_cols),
        )(out_weight, *[head_rows[k] for k in order])
        give = swap_plane(give, 1)
        step = 2
        while step < plane:
            count //= 2
            shape = jax.ShapeDtypeStruct((count, rows, part_cols), jnp.float32)
            keep, give = pl.pallas_call(
                halve_kernel,
                out_shape=(shape, shape),
                in_specs=[IN_VMEM, IN_VMEM],
                out_specs=(IN_VMEM, IN_VMEM),
                compiler_params=params(8),
            )(keep, give)
            give = swap_plane(give, step)
            step *= 2
        sums += [keep, give]
    blocks = pl.pallas_call(
        functools.partial(total_kernel, parts),
        out_shape=[jax.ShapeDtypeStruct((rows, out_cols), jnp.bfloat16)] * wide,
        in_specs=[IN_VMEM] * len(sums),
        out_specs=[IN_VMEM] * wide,
        compiler_params=params(8),
    )(*sums)
    blocks = swap_wide(blocks)
    return pl.pallas_call(
        finish_kernel,
        out_shape=jax.ShapeDtypeStruct((rows, wide * out_cols), jnp.bfloat16),
        in_specs=[IN_VMEM] * wide,
        out_specs=IN_VMEM,
        compiler_params=params(8),
    )(*[blocks[k] for k in [*sequence(wide), 0]])


def solution(mesh):
    placed = (
        P(("groups", "gx", "gy", "gz"), None),
        P(),
        P("gx", ("gy", "gz")),
        P("gx", ("gy", "gz")),
        P("gx", ("gy", "gz")),
        P(("gy", "gz"), "gx"),
        P(("groups", "gx", "gy", "gz"), None, None),
        P(("groups", "gx", "gy", "gz"), None, None),
        P(("groups", "gx", "gy", "gz")),
    )
    return jax.shard_map(
        shards,
        mesh=mesh,
        in_specs=placed,
        out_specs=P(("groups", "gx", "gy", "gz"), None),
        check_vma=False,
    )
```

```python
import functools

import jax
import jax.numpy as jnp
import numpy as np
from jax import lax
from jax.experimental import pallas as pl
from jax.experimental.pallas import tpu as pltpu
from jax.sharding import PartitionSpec as P

HD = 128
ROW_AXES = ("gx", "gy", "gz")
PLANE = ("gy", "gz")
MIB = 1024 * 1024
IN_VMEM = pl.BlockSpec(memory_space=pltpu.VMEM)
ANYWHERE = pl.BlockSpec(memory_space=pl.ANY)


def sequence(wide):
    return sorted(range(1, wide), key=lambda k: (k != wide // 2, -k))


def scale_kernel(tokens_ref, scaled_ref):
    tokens = tokens_ref[...].astype(jnp.float32)
    mean_square = jnp.mean(tokens * tokens, -1, keepdims=True)
    scaled_ref[...] = tokens * lax.rsqrt(mean_square + 1e-05)


def gain_kernel(wide, plane, scaled_ref, gain_ref, blocks_ref):
    normed = (scaled_ref[...] * gain_ref[...]).astype(jnp.bfloat16)
    half = normed.shape[1] // wide // 2
    for i in range(wide):
        for j in range(plane):
            at = (2 * i + j % 2) * half
            blocks_ref[i * plane + j] = normed[:, at : at + half]


def project_kernel(own, wide, plane, rows_ref, query_ref, key_ref, value_ref, *refs):
    owners, rows, half = rows_ref.shape
    core = lax.axis_index("gz")
    at_row = pl.multiple_of((core if own else 1 - core) * half, half)
    normed = rows_ref[...].reshape(owners * rows, half)
    sums_ref = refs[-1]
    at = 0
    for weight in (query_ref, key_ref, value_ref):
        cols = weight.shape[1]
        step = min(cols, 256)
        for c in range(0, cols, step):
            part = jnp.dot(
                normed,
                weight[pl.ds(at_row, half), c : c + step],
                preferred_element_type=jnp.float32,
            )
            if own:
                sums_ref[:, at : at + step] = part
            else:
                part = part + refs[1][:, at : at + step]
                sums_ref[:, :, at : at + step] = part.reshape(owners, rows, step)
            at += step
    if not own:
        own_wide = lax.axis_index("gx")
        own_plane = 2 * lax.axis_index("gy") + core
        for k in range(wide):
            for l in range(plane):
                refs[2 + k][l] = sums_ref[(own_wide ^ k) * plane + (own_plane ^ l)]


def own_place():
    return 2 * lax.axis_index("gy") + lax.axis_index("gz")


def write_lengths(rows, lengths_ref, block_ref):
    at_row = lax.broadcasted_iota(jnp.int32, (16, block_ref.shape[1]), 0)
    filled = jnp.zeros(at_row.shape, jnp.float32)
    for r in range(rows):
        filled = jnp.where(at_row == r, lengths_ref[:, r : r + 1].astype(jnp.float32), filled)
    block_ref[block_ref.shape[0] - 16 :] = filled.astype(jnp.bfloat16)


def cut_kernel(plan, lengths_ref, keys_ref, values_ref, _, *blocks):
    rows, slots, _ = keys_ref.shape
    cols = blocks[0].shape[1]
    for (slot, key_rows, value_rows, with_lengths), block in zip(plan, blocks):
        at = pl.multiple_of((own_place() ^ slot) * cols, cols)
        start = 0
        for cache_ref, wanted in ((keys_ref, key_rows), (values_ref, value_rows)):
            for r in wanted:
                block[start : start + slots] = cache_ref[r, :, pl.ds(at, cols)]
                start += slots
        if with_lengths:
            write_lengths(rows, lengths_ref, block)


def pass_kernel(*refs):
    pass


def attend_kernel(wide, plane, members, rows, early, query_cols, frequency_ref, *refs):
    partials, held, attended_ref = refs[wide - 1 :: -1], refs[wide:-1], refs[-1]
    even = plane // 2 - 1 if members[0] else 0
    firsts, lasts, whole = held[:even], held[even : 2 * even], held[2 * even :]
    slots = (whole[0].shape[0] - 16) // (2 * rows)
    cols = partials[0].shape[-1]
    kv_cols = (cols - query_cols) // 2
    kv_heads, group = kv_cols // HD, query_cols // kv_cols
    pairs = len(members) * rows
    count = pairs * kv_heads
    heads = count * group
    scale = 1.0 / HD**0.5
    own = slice(members[0], members[-1] + 1)
    total = partials[0][own]
    for k in range(1, wide):
        total = total + partials[k][own]
    total = total.reshape(pairs, cols).astype(jnp.bfloat16).astype(jnp.float32)

    def cached(values):
        parts = []
        for p in range(pairs):
            l, r = members[p // rows], p % rows
            ref, at = whole[(l + 1) // 2], values * rows + r
            if l % 2 == 0 and l:
                ref = firsts[l // 2 - 1]
                if at >= rows + early:
                    ref, at = lasts[l // 2 - 1], at - rows - early
            parts.append(ref[at * slots : (at + 1) * slots])
        return jnp.concatenate(parts, 1)

    filled = []
    for l in members:
        block = lasts[l // 2 - 1] if l % 2 == 0 and l else whole[(l + 1) // 2]
        last = block[block.shape[0] - 16 :, :HD].astype(jnp.float32)
        filled += [last[r : r + 1] for r in range(rows)]
    angles = jnp.concatenate(filled, 0) * frequency_ref[...]
    cosine, sine = jnp.cos(angles), jnp.sin(angles)
    front = lax.broadcasted_iota(jnp.int32, (1, HD), 1) < HD // 2
    sine = jnp.where(front, -sine, sine)

    def rotate(vector):
        return vector * cosine + pltpu.roll(vector, HD // 2, 1) * sine

    query, key_new, value_new = [], [], []
    for h in range(kv_heads):
        turned = [
            rotate(total[:, (h * group + g) * HD : (h * group + g + 1) * HD]) for g in range(group)
        ]
        query.append(jnp.swapaxes(jnp.stack(turned, 0), 0, 1))
        at = query_cols + h * HD
        key_new.append(rotate(total[:, at : at + HD]))
        value_new.append(total[:, at + kv_cols : at + kv_cols + HD])
    query = jnp.stack(query, 1).reshape(heads, HD)
    turned_query = query.T.astype(jnp.bfloat16)
    key_new = jnp.stack(key_new, 1).reshape(count, HD).astype(jnp.bfloat16)
    value_new = jnp.stack(value_new, 1).reshape(count, HD)

    head_pair = lax.broadcasted_iota(jnp.int32, (1, heads), 1) // group
    by_pair = jnp.concatenate(
        [jnp.where(head_pair == b, turned_query, jnp.zeros_like(turned_query)) for b in range(count)],
        0,
    )
    scores = scale * jnp.dot(cached(0), by_pair, preferred_element_type=jnp.float32)
    own = scale * jnp.dot(key_new, turned_query, preferred_element_type=jnp.float32)
    of_pair = lax.broadcasted_iota(jnp.int32, (count, 1), 0) == head_pair
    own = jnp.sum(jnp.where(of_pair, own, 0.0), 0, keepdims=True)
    length = jnp.zeros((1, heads), jnp.float32)
    for p in range(pairs):
        length = jnp.where(head_pair // kv_heads == p, filled[p][:, :1], length)
    slot = lax.broadcasted_iota(jnp.int32, (slots, 1), 0).astype(jnp.float32)
    scores = jnp.where(slot < length, scores, -1e30)
    top = jnp.maximum(jnp.max(scores, 0, keepdims=True), own)
    weights = jnp.exp(scores - top)
    own_weight = jnp.exp(own - top)
    denominator = jnp.sum(weights, 0, keepdims=True) + own_weight
    probability = (weights / denominator).astype(jnp.bfloat16)
    own_prob = (own_weight / denominator).astype(jnp.bfloat16)
    contract_rows = (((0,), (0,)), ((), ()))
    mixed = lax.dot_general(
        probability, cached(1), contract_rows, preferred_element_type=jnp.float32
    )
    own_prob = jnp.where(of_pair, own_prob.astype(jnp.float32), 0.0).astype(jnp.bfloat16)
    fresh = lax.dot_general(
        own_prob, value_new.astype(jnp.bfloat16), contract_rows, preferred_element_type=jnp.float32
    )
    mixed = [
        mixed[b * group : (b + 1) * group, b * HD : (b + 1) * HD]
        + fresh[b * group : (b + 1) * group]
        for b in range(count)
    ]
    attended = []
    for h in range(kv_heads):
        by_head = jnp.swapaxes(jnp.stack(mixed[h::kv_heads], 0), 0, 1)
        attended += [by_head[g] for g in range(group)]
    attended = jnp.concatenate(attended, 1)
    attended_ref[...] = attended.reshape(len(members), rows, query_cols).astype(jnp.bfloat16)


def join_kernel(*refs):
    at = 0
    for block in refs[:-1]:
        refs[-1][at : at + block.shape[0]] = block[...]
        at += block.shape[0]


def output_kernel(at, cols, order, weight_ref, *refs):
    keep_ref, give_ref = refs[-2:]
    blocks = [refs[order.index(k)] for k in range(len(order))]
    wide = len(blocks)
    plane, rows, depth = blocks[0].shape
    attended = jnp.concatenate(
        [block[...].reshape(plane * rows, depth) for block in blocks], 0
    )
    step = min(cols, 512)
    for c in range(0, cols, step):
        part = jnp.dot(
            attended, weight_ref[:, at + c : at + c + step], preferred_element_type=jnp.float32
        )
        part = part.reshape(wide * plane // 2, 2 * rows, step)
        keep_ref[:, :, c : c + step] = part[:, :rows]
        give_ref[:, :, c : c + step] = part[:, rows:]


def halve_kernel(a_ref, b_ref, keep_ref, give_ref):
    for n in range(keep_ref.shape[0]):
        keep_ref[n] = a_ref[2 * n] + b_ref[2 * n]
        give_ref[n] = a_ref[2 * n + 1] + b_ref[2 * n + 1]


def total_kernel(parts, *refs):
    sums, blocks = refs[: 2 * parts], refs[2 * parts :]
    at = 0
    for p in range(parts):
        cols = sums[2 * p].shape[-1]
        for k, block in enumerate(blocks):
            total = sums[2 * p][k] + sums[2 * p + 1][k]
            block[:, at : at + cols] = total.astype(jnp.bfloat16)
        at += cols


def finish_kernel(*refs):
    result_ref = refs[-1]
    order = [*sequence(len(refs) - 1), 0]
    blocks = [refs[order.index(k)] for k in range(len(order))]
    own = lax.axis_index("gx")
    cols = blocks[0].shape[-1]
    for k, block in enumerate(blocks):
        at = pl.multiple_of((own ^ k) * cols, cols)
        result_ref[:, pl.ds(at, cols)] = block[...]


def swap_blocks(blocks, axes):
    return lax.all_to_all(blocks, axes, split_axis=0, concat_axis=0, tiled=True)


def swap_pairs(value, axis, step):
    return lax.ppermute(value, axis, [(i, i ^ step) for i in range(lax.axis_size(axis))])


def swap_plane(value, step):
    return lax.ppermute(value, PLANE, [(i, i ^ step) for i in range(lax.axis_size(PLANE))])


def swap_wide(blocks):
    moved = [swap_pairs(blocks[k], "gx", k) for k in range(len(blocks) - 1, 0, -1)]
    return [blocks[0]] + moved[::-1]


def shards(
    tokens,
    norm_gain,
    query_weight,
    key_weight,
    value_weight,
    out_weight,
    cache_keys,
    cache_values,
    lengths,
):
    rows = tokens.shape[0]
    wide = lax.axis_size("gx")
    plane = lax.axis_size(PLANE)
    owners = wide * plane
    width, query_cols = query_weight.shape
    kv_cols = key_weight.shape[1]
    depth, out_cols = out_weight.shape
    cols = query_cols + 2 * kv_cols

    def params(mib):
        return pltpu.CompilerParams(vmem_limit_bytes=mib * MIB)

    def cost(flops, size):
        return pl.CostEstimate(flops=flops, bytes_accessed=size, transcendentals=0)

    half = width // 2
    scaled = pl.pallas_call(
        scale_kernel,
        out_shape=jax.ShapeDtypeStruct(tokens.shape, jnp.float32),
        in_specs=[IN_VMEM],
        out_specs=IN_VMEM,
        compiler_params=params(8),
        cost_estimate=cost(40 * 10**9, MIB),
    )(tokens)
    normed = pl.pallas_call(
        functools.partial(gain_kernel, wide, plane),
        out_shape=jax.ShapeDtypeStruct((owners, rows, half), jnp.bfloat16),
        in_specs=[IN_VMEM, IN_VMEM],
        out_specs=IN_VMEM,
        compiler_params=params(8),
    )(scaled, norm_gain.reshape(1, -1))
    slots = cache_keys.shape[1]
    even = plane // 2 - 1
    early = rows // 2
    every = range(rows)

    def cut(plan, after):
        return pl.pallas_call(
            functools.partial(cut_kernel, plan),
            out_shape=[
                jax.ShapeDtypeStruct(
                    ((len(key_rows) + len(value_rows)) * slots + 16 * with_lengths, kv_cols),
                    cache_keys.dtype,
                )
                for _, key_rows, value_rows, with_lengths in plan
            ],
            in_specs=[IN_VMEM] * 4,
            out_specs=[IN_VMEM] * len(plan),
            compiler_params=params(8),
        )(lengths.reshape(1, -1), cache_keys, cache_values, after)

    plan = [(l, every, every[:early], False) for l in range(2, plane, 2)]
    plan += [(l, (), every[early:], True) for l in range(2, plane, 2)]
    plan += [(l, every, every, True) for l in range(1, plane, 2)]
    blocks = cut(plan, normed)
    firsts, rest = blocks[:even], blocks[even:]
    firsts = [swap_plane(firsts[s], 2 * s + 2) for s in range(even)]
    own_half = swap_blocks(normed, ROW_AXES)
    other_half = swap_pairs(own_half, "gz", 1)
    rest = pl.pallas_call(
        pass_kernel,
        out_shape=[jax.ShapeDtypeStruct(value.shape, value.dtype) for value in rest],
        in_specs=[ANYWHERE] * (len(rest) + even + 1),
        out_specs=[ANYWHERE] * len(rest),
        input_output_aliases={n: n for n in range(len(rest))},
        compiler_params=params(1),
    )(*rest, own_half, *firsts)
    lasts = [swap_plane(rest[s], 2 * s + 2) for s in range(even)]
    odd = [swap_plane(rest[even + s], 2 * s + 1) for s in range(even + 1)]
    (mine,) = cut([(0, every, every, True)], own_half)
    held = [*firsts, *lasts, mine, *odd]
    weights = (query_weight, key_weight, value_weight)
    half_cost = cost(owners * rows * width * cols, width * cols)
    partial = pl.pallas_call(
        functools.partial(project_kernel, True, wide, plane),
        out_shape=jax.ShapeDtypeStruct((owners * rows, cols), jnp.float32),
        in_specs=[IN_VMEM] * 4,
        out_specs=IN_VMEM,
        compiler_params=params(8),
        cost_estimate=half_cost,
    )(own_half, *weights)
    partial = pl.pallas_call(
        functools.partial(project_kernel, False, wide, plane),
        out_shape=[jax.ShapeDtypeStruct((plane, rows, cols), jnp.float32)] * wide,
        in_specs=[IN_VMEM] * 6,
        out_specs=[IN_VMEM] * wide,
        scratch_shapes=[pltpu.VMEM((owners, rows, cols), jnp.float32)],
        compiler_params=params(8),
        cost_estimate=half_cost,
    )(other_half, *weights, odd[0], partial)
    partial = swap_wide(partial)

    half_dim = HD // 2
    frequency = 500000.0 ** (-np.arange(half_dim, dtype=np.float64) / half_dim)
    frequency = np.tile(frequency.astype(np.float32), 2).reshape(1, HD)
    attended = []
    for members in (range(2), range(2, plane)):
        used = held if members[0] else held[2 * even : 2 * even + 2]
        attended.append(
            pl.pallas_call(
                functools.partial(attend_kernel, wide, plane, members, rows, early, query_cols),
                out_shape=jax.ShapeDtypeStruct((len(members), rows, query_cols), jnp.bfloat16),
                in_specs=[IN_VMEM] * (1 + wide + len(used)),
                out_specs=IN_VMEM,
                compiler_params=params(8),
                cost_estimate=cost(10**10, 4 * MIB) if members[0] else cost(1, 1),
            )(jnp.asarray(frequency), *partial[::-1], *used)
        )
    attended = pl.pallas_call(
        join_kernel,
        out_shape=jax.ShapeDtypeStruct((plane, rows, query_cols), jnp.bfloat16),
        in_specs=[IN_VMEM, IN_VMEM],
        out_specs=IN_VMEM,
        compiler_params=params(8),
    )(*attended)
    head_rows = swap_wide([attended] * wide)
    widths = (out_cols // 2, out_cols // 4, out_cols // 4)
    order = [0, *sequence(wide)[1:], sequence(wide)[0]]
    sums = []
    for p, part_cols in enumerate(widths):
        count = owners // 2
        behind = sums[:1] if p == len(widths) - 1 else []
        shape = jax.ShapeDtypeStruct((count, rows, part_cols), jnp.float32)
        keep, give = pl.pallas_call(
            functools.partial(output_kernel, sum(widths[:p]), part_cols, order),
            out_shape=(shape, shape),
            in_specs=[IN_VMEM] * (1 + wide) + [ANYWHERE] * len(behind),
            out_specs=(IN_VMEM, IN_VMEM),
            compiler_params=params(8),
            cost_estimate=cost(2 * owners * rows * depth * part_cols, 2 * depth * part_cols),
        )(out_weight, *[head_rows[k] for k in order], *behind)
        give = swap_plane(give, 1)
        step = 2
        while step < plane:
            count //= 2
            shape = jax.ShapeDtypeStruct((count, rows, part_cols), jnp.float32)
            keep, give = pl.pallas_call(
                halve_kernel,
                out_shape=(shape, shape),
                in_specs=[IN_VMEM, IN_VMEM],
                out_specs=(IN_VMEM, IN_VMEM),
                compiler_params=params(8),
            )(keep, give)
            give = swap_plane(give, step)
            step *= 2
        sums += [keep, give]
    blocks = pl.pallas_call(
        functools.partial(total_kernel, len(widths)),
        out_shape=[jax.ShapeDtypeStruct((rows, out_cols), jnp.bfloat16)] * wide,
        in_specs=[IN_VMEM] * len(sums),
        out_specs=[IN_VMEM] * wide,
        compiler_params=params(8),
    )(*sums)
    blocks = swap_wide(blocks)
    return pl.pallas_call(
        finish_kernel,
        out_shape=jax.ShapeDtypeStruct((rows, wide * out_cols), jnp.bfloat16),
        in_specs=[IN_VMEM] * wide,
        out_specs=IN_VMEM,
        compiler_params=params(8),
    )(*[blocks[k] for k in [*sequence(wide), 0]])


def solution(mesh):
    placed = (
        P(("groups", "gx", "gy", "gz"), None),
        P(),
        P("gx", ("gy", "gz")),
        P("gx", ("gy", "gz")),
        P("gx", ("gy", "gz")),
        P(("gy", "gz"), "gx"),
        P(("groups", "gx", "gy", "gz"), None, None),
        P(("groups", "gx", "gy", "gz"), None, None),
        P(("groups", "gx", "gy", "gz")),
    )
    return jax.shard_map(
        shards,
        mesh=mesh,
        in_specs=placed,
        out_specs=P(("groups", "gx", "gy", "gz"), None),
        check_vma=False,
    )
```

```python
import functools

import jax
import jax.numpy as jnp
import numpy as np
from jax import lax
from jax.experimental import pallas as pl
from jax.experimental.pallas import tpu as pltpu
from jax.sharding import PartitionSpec as P

HD = 128
ROW_AXES = ("gx", "gy", "gz")
PLANE = ("gy", "gz")
MIB = 1024 * 1024
IN_VMEM = pl.BlockSpec(memory_space=pltpu.VMEM)
ANYWHERE = pl.BlockSpec(memory_space=pl.ANY)


def sequence(wide):
    return sorted(range(1, wide), key=lambda k: (k != wide // 2, -k))


def scale_kernel(tokens_ref, scaled_ref):
    tokens = tokens_ref[...].astype(jnp.float32)
    mean_square = jnp.mean(tokens * tokens, -1, keepdims=True)
    scaled_ref[...] = tokens * lax.rsqrt(mean_square + 1e-05)


def gain_kernel(wide, plane, scaled_ref, gain_ref, blocks_ref):
    normed = (scaled_ref[...] * gain_ref[...]).astype(jnp.bfloat16)
    half = normed.shape[1] // wide // 2
    for i in range(wide):
        for j in range(plane):
            at = (2 * i + j % 2) * half
            blocks_ref[i * plane + j] = normed[:, at : at + half]


def project_kernel(own, wide, plane, rows_ref, query_ref, key_ref, value_ref, *refs):
    owners, rows, half = rows_ref.shape
    core = lax.axis_index("gz")
    at_row = pl.multiple_of((core if own else 1 - core) * half, half)
    normed = rows_ref[...].reshape(owners * rows, half)
    sums_ref = refs[-1]
    at = 0
    for weight in (query_ref, key_ref, value_ref):
        cols = weight.shape[1]
        step = min(cols, 256)
        for c in range(0, cols, step):
            part = jnp.dot(
                normed,
                weight[pl.ds(at_row, half), c : c + step],
                preferred_element_type=jnp.float32,
            )
            if own:
                sums_ref[:, at : at + step] = part
            else:
                part = part + refs[1][:, at : at + step]
                sums_ref[:, :, at : at + step] = part.reshape(owners, rows, step)
            at += step
    if not own:
        own_wide = lax.axis_index("gx")
        own_plane = 2 * lax.axis_index("gy") + core
        for k in range(wide):
            for l in range(plane):
                refs[2 + k][l] = sums_ref[(own_wide ^ k) * plane + (own_plane ^ l)]


def own_place():
    return 2 * lax.axis_index("gy") + lax.axis_index("gz")


def write_lengths(rows, lengths_ref, block_ref):
    at_row = lax.broadcasted_iota(jnp.int32, (16, block_ref.shape[1]), 0)
    filled = jnp.zeros(at_row.shape, jnp.float32)
    for r in range(rows):
        filled = jnp.where(at_row == r, lengths_ref[:, r : r + 1].astype(jnp.float32), filled)
    block_ref[block_ref.shape[0] - 16 :] = filled.astype(jnp.bfloat16)


def cut_kernel(plan, lengths_ref, keys_ref, values_ref, _, *blocks):
    cols = blocks[0].shape[1]
    for (slot, keys, values, with_lengths), block in zip(plan, blocks):
        at = pl.multiple_of((own_place() ^ slot) * cols, cols)
        start = 0
        for cache_ref, wanted in ((keys_ref, keys), (values_ref, values)):
            for r, low, high in wanted:
                block[start : start + high - low] = cache_ref[r, low:high, pl.ds(at, cols)]
                start += high - low
        if with_lengths:
            write_lengths(keys_ref.shape[0], lengths_ref, block)


def pass_kernel(*refs):
    pass


def attend_kernel(wide, plane, members, rows, early, query_cols, frequency_ref, *refs):
    partials, held, attended_ref = refs[wide - 1 :: -1], refs[wide:-1], refs[-1]
    even = plane // 2 - 1 if members[0] else 0
    firsts, lasts, whole = held[:even], held[even : 2 * even], held[2 * even :]
    slots = (whole[0].shape[0] - 16) // (2 * rows)
    cols = partials[0].shape[-1]
    kv_cols = (cols - query_cols) // 2
    kv_heads, group = kv_cols // HD, query_cols // kv_cols
    pairs = len(members) * rows
    count = pairs * kv_heads
    heads = count * group
    scale = 1.0 / HD**0.5
    own = slice(members[0], members[-1] + 1)
    total = partials[0][own]
    for k in range(1, wide):
        total = total + partials[k][own]
    total = total.reshape(pairs, cols).astype(jnp.bfloat16).astype(jnp.float32)

    def cached(values):
        parts = []
        for p in range(pairs):
            l, r = members[p // rows], p % rows
            if l % 2 or l == 0:
                at = (values * rows + r) * slots
                parts.append(whole[(l + 1) // 2][at : at + slots])
                continue
            first, last = firsts[l // 2 - 1], lasts[l // 2 - 1]
            at = (values * rows + r) * slots
            end = (rows + early) * slots + slots // 4
            if at + slots <= end:
                parts.append(first[at : at + slots])
            elif at < end:
                rest = last[: at + slots - end]
                parts.append(jnp.concatenate([first[at:end], rest], 0))
            else:
                parts.append(last[at - end : at - end + slots])
        return jnp.concatenate(parts, 1)

    filled = []
    for l in members:
        block = lasts[l // 2 - 1] if l % 2 == 0 and l else whole[(l + 1) // 2]
        last = block[block.shape[0] - 16 :, :HD].astype(jnp.float32)
        filled += [last[r : r + 1] for r in range(rows)]
    angles = jnp.concatenate(filled, 0) * frequency_ref[...]
    cosine, sine = jnp.cos(angles), jnp.sin(angles)
    front = lax.broadcasted_iota(jnp.int32, (1, HD), 1) < HD // 2
    sine = jnp.where(front, -sine, sine)

    def rotate(vector):
        return vector * cosine + pltpu.roll(vector, HD // 2, 1) * sine

    query, key_new, value_new = [], [], []
    for h in range(kv_heads):
        turned = [
            rotate(total[:, (h * group + g) * HD : (h * group + g + 1) * HD]) for g in range(group)
        ]
        query.append(jnp.swapaxes(jnp.stack(turned, 0), 0, 1))
        at = query_cols + h * HD
        key_new.append(rotate(total[:, at : at + HD]))
        value_new.append(total[:, at + kv_cols : at + kv_cols + HD])
    query = jnp.stack(query, 1).reshape(heads, HD)
    turned_query = query.T.astype(jnp.bfloat16)
    key_new = jnp.stack(key_new, 1).reshape(count, HD).astype(jnp.bfloat16)
    value_new = jnp.stack(value_new, 1).reshape(count, HD)

    head_pair = lax.broadcasted_iota(jnp.int32, (1, heads), 1) // group
    by_pair = jnp.concatenate(
        [jnp.where(head_pair == b, turned_query, jnp.zeros_like(turned_query)) for b in range(count)],
        0,
    )
    scores = scale * jnp.dot(cached(0), by_pair, preferred_element_type=jnp.float32)
    own = scale * jnp.dot(key_new, turned_query, preferred_element_type=jnp.float32)
    of_pair = lax.broadcasted_iota(jnp.int32, (count, 1), 0) == head_pair
    own = jnp.sum(jnp.where(of_pair, own, 0.0), 0, keepdims=True)
    length = jnp.zeros((1, heads), jnp.float32)
    for p in range(pairs):
        length = jnp.where(head_pair // kv_heads == p, filled[p][:, :1], length)
    slot = lax.broadcasted_iota(jnp.int32, (slots, 1), 0).astype(jnp.float32)
    scores = jnp.where(slot < length, scores, -1e30)
    top = jnp.maximum(jnp.max(scores, 0, keepdims=True), own)
    weights = jnp.exp(scores - top)
    own_weight = jnp.exp(own - top)
    denominator = jnp.sum(weights, 0, keepdims=True) + own_weight
    probability = (weights / denominator).astype(jnp.bfloat16)
    own_prob = (own_weight / denominator).astype(jnp.bfloat16)
    contract_rows = (((0,), (0,)), ((), ()))
    mixed = lax.dot_general(
        probability, cached(1), contract_rows, preferred_element_type=jnp.float32
    )
    own_prob = jnp.where(of_pair, own_prob.astype(jnp.float32), 0.0).astype(jnp.bfloat16)
    fresh = lax.dot_general(
        own_prob, value_new.astype(jnp.bfloat16), contract_rows, preferred_element_type=jnp.float32
    )
    mixed = [
        mixed[b * group : (b + 1) * group, b * HD : (b + 1) * HD]
        + fresh[b * group : (b + 1) * group]
        for b in range(count)
    ]
    attended = []
    for h in range(kv_heads):
        by_head = jnp.swapaxes(jnp.stack(mixed[h::kv_heads], 0), 0, 1)
        attended += [by_head[g] for g in range(group)]
    attended = jnp.concatenate(attended, 1)
    attended_ref[...] = attended.reshape(len(members), rows, query_cols).astype(jnp.bfloat16)


def join_kernel(*refs):
    at = 0
    for block in refs[:-1]:
        refs[-1][at : at + block.shape[0]] = block[...]
        at += block.shape[0]


def output_kernel(at, cols, order, weight_ref, *refs):
    keep_ref, give_ref = refs[-2:]
    blocks = [refs[order.index(k)] for k in range(len(order))]
    wide = len(blocks)
    plane, rows, depth = blocks[0].shape
    attended = jnp.concatenate(
        [block[...].reshape(plane * rows, depth) for block in blocks], 0
    )
    step = min(cols, 512)
    for c in range(0, cols, step):
        part = jnp.dot(
            attended, weight_ref[:, at + c : at + c + step], preferred_element_type=jnp.float32
        )
        part = part.reshape(wide * plane // 2, 2 * rows, step)
        keep_ref[:, :, c : c + step] = part[:, :rows]
        give_ref[:, :, c : c + step] = part[:, rows:]


def halve_kernel(a_ref, b_ref, keep_ref, give_ref):
    for n in range(keep_ref.shape[0]):
        keep_ref[n] = a_ref[2 * n] + b_ref[2 * n]
        give_ref[n] = a_ref[2 * n + 1] + b_ref[2 * n + 1]


def total_kernel(parts, *refs):
    sums, blocks = refs[: 2 * parts], refs[2 * parts :]
    cols = sums[0].shape[-1]
    for p in range(parts):
        for k, block in enumerate(blocks):
            total = sums[2 * p][k] + sums[2 * p + 1][k]
            block[:, p * cols : (p + 1) * cols] = total.astype(jnp.bfloat16)


def finish_kernel(*refs):
    result_ref = refs[-1]
    order = [*sequence(len(refs) - 1), 0]
    blocks = [refs[order.index(k)] for k in range(len(order))]
    own = lax.axis_index("gx")
    cols = blocks[0].shape[-1]
    for k, block in enumerate(blocks):
        at = pl.multiple_of((own ^ k) * cols, cols)
        result_ref[:, pl.ds(at, cols)] = block[...]


def swap_blocks(blocks, axes):
    return lax.all_to_all(blocks, axes, split_axis=0, concat_axis=0, tiled=True)


def swap_pairs(value, axis, step):
    return lax.ppermute(value, axis, [(i, i ^ step) for i in range(lax.axis_size(axis))])


def swap_plane(value, step):
    return lax.ppermute(value, PLANE, [(i, i ^ step) for i in range(lax.axis_size(PLANE))])


def swap_wide(blocks):
    moved = [swap_pairs(blocks[k], "gx", k) for k in range(len(blocks) - 1, 0, -1)]
    return [blocks[0]] + moved[::-1]


def shards(
    tokens,
    norm_gain,
    query_weight,
    key_weight,
    value_weight,
    out_weight,
    cache_keys,
    cache_values,
    lengths,
):
    rows = tokens.shape[0]
    wide = lax.axis_size("gx")
    plane = lax.axis_size(PLANE)
    owners = wide * plane
    width, query_cols = query_weight.shape
    kv_cols = key_weight.shape[1]
    depth, out_cols = out_weight.shape
    cols = query_cols + 2 * kv_cols

    def params(mib):
        return pltpu.CompilerParams(vmem_limit_bytes=mib * MIB)

    def cost(flops, size):
        return pl.CostEstimate(flops=flops, bytes_accessed=size, transcendentals=0)

    half = width // 2
    scaled = pl.pallas_call(
        scale_kernel,
        out_shape=jax.ShapeDtypeStruct(tokens.shape, jnp.float32),
        in_specs=[IN_VMEM],
        out_specs=IN_VMEM,
        compiler_params=params(8),
        cost_estimate=cost(40 * 10**9, MIB),
    )(tokens)
    normed = pl.pallas_call(
        functools.partial(gain_kernel, wide, plane),
        out_shape=jax.ShapeDtypeStruct((owners, rows, half), jnp.bfloat16),
        in_specs=[IN_VMEM, IN_VMEM],
        out_specs=IN_VMEM,
        compiler_params=params(8),
    )(scaled, norm_gain.reshape(1, -1))
    slots = cache_keys.shape[1]
    even = plane // 2 - 1
    early = rows // 2
    every = [(r, 0, slots) for r in range(rows)]
    cut_at = slots // 4

    def cut(plan, after):
        return pl.pallas_call(
            functools.partial(cut_kernel, plan),
            out_shape=[
                jax.ShapeDtypeStruct(
                    (sum(h - g for _, g, h in (*keys, *values)) + 16 * with_lengths, kv_cols),
                    cache_keys.dtype,
                )
                for _, keys, values, with_lengths in plan
            ],
            in_specs=[IN_VMEM] * 4,
            out_specs=[IN_VMEM] * len(plan),
            compiler_params=params(8),
        )(lengths.reshape(1, -1), cache_keys, cache_values, after)

    early_values = [*every[:early], (early, 0, cut_at)]
    late_values = [(early, cut_at, slots), *every[early + 1 :]]
    plan = [(l, every, early_values, False) for l in range(2, plane, 2)]
    plan += [(l, (), late_values, True) for l in range(2, plane, 2)]
    plan += [(l, every, every, True) for l in range(1, plane, 2)]
    blocks = cut(plan, normed)
    firsts, rest = blocks[:even], blocks[even:]
    firsts = [swap_plane(firsts[s], 2 * s + 2) for s in range(even)]
    own_half = swap_blocks(normed, ROW_AXES)
    other_half = swap_pairs(own_half, "gz", 1)
    rest = pl.pallas_call(
        pass_kernel,
        out_shape=[jax.ShapeDtypeStruct(value.shape, value.dtype) for value in rest],
        in_specs=[ANYWHERE] * (len(rest) + even + 1),
        out_specs=[ANYWHERE] * len(rest),
        input_output_aliases={n: n for n in range(len(rest))},
        compiler_params=params(1),
    )(*rest, own_half, *firsts)
    lasts = [swap_plane(rest[s], 2 * s + 2) for s in range(even)]
    odd = [swap_plane(rest[even + s], 2 * s + 1) for s in range(even + 1)]
    (mine,) = cut([(0, every, every, True)], own_half)
    held = [*firsts, *lasts, mine, *odd]
    weights = (query_weight, key_weight, value_weight)
    half_cost = cost(owners * rows * width * cols, width * cols)
    partial = pl.pallas_call(
        functools.partial(project_kernel, True, wide, plane),
        out_shape=jax.ShapeDtypeStruct((owners * rows, cols), jnp.float32),
        in_specs=[IN_VMEM] * 4,
        out_specs=IN_VMEM,
        compiler_params=params(8),
        cost_estimate=half_cost,
    )(own_half, *weights)
    partial = pl.pallas_call(
        functools.partial(project_kernel, False, wide, plane),
        out_shape=[jax.ShapeDtypeStruct((plane, rows, cols), jnp.float32)] * wide,
        in_specs=[IN_VMEM] * 6,
        out_specs=[IN_VMEM] * wide,
        scratch_shapes=[pltpu.VMEM((owners, rows, cols), jnp.float32)],
        compiler_params=params(8),
        cost_estimate=half_cost,
    )(other_half, *weights, odd[0], partial)
    partial = swap_wide(partial)

    half_dim = HD // 2
    frequency = 500000.0 ** (-np.arange(half_dim, dtype=np.float64) / half_dim)
    frequency = np.tile(frequency.astype(np.float32), 2).reshape(1, HD)
    attended = []
    for members in (range(2), range(2, plane)):
        used = held if members[0] else held[2 * even : 2 * even + 2]
        attended.append(
            pl.pallas_call(
                functools.partial(attend_kernel, wide, plane, members, rows, early, query_cols),
                out_shape=jax.ShapeDtypeStruct((len(members), rows, query_cols), jnp.bfloat16),
                in_specs=[IN_VMEM] * (1 + wide + len(used)),
                out_specs=IN_VMEM,
                compiler_params=params(8),
                cost_estimate=cost(10**10, 4 * MIB) if members[0] else cost(1, 1),
            )(jnp.asarray(frequency), *partial[::-1], *used)
        )
    attended = pl.pallas_call(
        join_kernel,
        out_shape=jax.ShapeDtypeStruct((plane, rows, query_cols), jnp.bfloat16),
        in_specs=[IN_VMEM, IN_VMEM],
        out_specs=IN_VMEM,
        compiler_params=params(8),
    )(*attended)
    head_rows = swap_wide([attended] * wide)
    parts = 2
    order = [0, *sequence(wide)[1:], sequence(wide)[0]]
    part_cols = out_cols // parts
    sums = []
    for p in range(parts):
        count = owners // 2
        shape = jax.ShapeDtypeStruct((count, rows, part_cols), jnp.float32)
        keep, give = pl.pallas_call(
            functools.partial(output_kernel, p * part_cols, part_cols, order),
            out_shape=(shape, shape),
            in_specs=[IN_VMEM] * (1 + wide),
            out_specs=(IN_VMEM, IN_VMEM),
            compiler_params=params(8),
            cost_estimate=cost(2 * owners * rows * depth * part_cols, 2 * depth * part_cols),
        )(out_weight, *[head_rows[k] for k in order])
        give = swap_plane(give, 1)
        step = 2
        while step < plane:
            count //= 2
            shape = jax.ShapeDtypeStruct((count, rows, part_cols), jnp.float32)
            keep, give = pl.pallas_call(
                halve_kernel,
                out_shape=(shape, shape),
                in_specs=[IN_VMEM, IN_VMEM],
                out_specs=(IN_VMEM, IN_VMEM),
                compiler_params=params(8),
            )(keep, give)
            give = swap_plane(give, step)
            step *= 2
        sums += [keep, give]
    blocks = pl.pallas_call(
        functools.partial(total_kernel, parts),
        out_shape=[jax.ShapeDtypeStruct((rows, out_cols), jnp.bfloat16)] * wide,
        in_specs=[IN_VMEM] * len(sums),
        out_specs=[IN_VMEM] * wide,
        compiler_params=params(8),
    )(*sums)
    blocks = swap_wide(blocks)
    return pl.pallas_call(
        finish_kernel,
        out_shape=jax.ShapeDtypeStruct((rows, wide * out_cols), jnp.bfloat16),
        in_specs=[IN_VMEM] * wide,
        out_specs=IN_VMEM,
        compiler_params=params(8),
    )(*[blocks[k] for k in [*sequence(wide), 0]])


def solution(mesh):
    placed = (
        P(("groups", "gx", "gy", "gz"), None),
        P(),
        P("gx", ("gy", "gz")),
        P("gx", ("gy", "gz")),
        P("gx", ("gy", "gz")),
        P(("gy", "gz"), "gx"),
        P(("groups", "gx", "gy", "gz"), None, None),
        P(("groups", "gx", "gy", "gz"), None, None),
        P(("groups", "gx", "gy", "gz")),
    )
    return jax.shard_map(
        shards,
        mesh=mesh,
        in_specs=placed,
        out_specs=P(("groups", "gx", "gy", "gz"), None),
        check_vma=False,
    )
```

```python
import functools

import jax
import jax.numpy as jnp
import numpy as np
from jax import lax
from jax.experimental import pallas as pl
from jax.experimental.pallas import tpu as pltpu
from jax.sharding import PartitionSpec as P

HD = 128
ROW_AXES = ("gx", "gy", "gz")
PLANE = ("gy", "gz")
MIB = 1024 * 1024
IN_VMEM = pl.BlockSpec(memory_space=pltpu.VMEM)
ANYWHERE = pl.BlockSpec(memory_space=pl.ANY)


def sequence(wide):
    return sorted(range(1, wide), key=lambda k: (k != wide // 2, -k))


def scale_kernel(tokens_ref, scaled_ref):
    tokens = tokens_ref[...].astype(jnp.float32)
    mean_square = jnp.mean(tokens * tokens, -1, keepdims=True)
    scaled_ref[...] = tokens * lax.rsqrt(mean_square + 1e-05)


def gain_kernel(wide, plane, scaled_ref, gain_ref, blocks_ref):
    normed = (scaled_ref[...] * gain_ref[...]).astype(jnp.bfloat16)
    half = normed.shape[1] // wide // 2
    for i in range(wide):
        for j in range(plane):
            at = (2 * i + j % 2) * half
            blocks_ref[i * plane + j] = normed[:, at : at + half]


def project_kernel(own, wide, plane, rows_ref, query_ref, key_ref, value_ref, *refs):
    owners, rows, half = rows_ref.shape
    core = lax.axis_index("gz")
    at_row = pl.multiple_of((core if own else 1 - core) * half, half)
    normed = rows_ref[...].reshape(owners * rows, half)
    sums_ref = refs[-1]
    at = 0
    for weight in (query_ref, key_ref, value_ref):
        cols = weight.shape[1]
        step = min(cols, 256)
        for c in range(0, cols, step):
            part = jnp.dot(
                normed,
                weight[pl.ds(at_row, half), c : c + step],
                preferred_element_type=jnp.float32,
            )
            if own:
                sums_ref[:, at : at + step] = part
            else:
                part = part + refs[1][:, at : at + step]
                sums_ref[:, :, at : at + step] = part.reshape(owners, rows, step)
            at += step
    if not own:
        own_wide = lax.axis_index("gx")
        own_plane = 2 * lax.axis_index("gy") + core
        for k in range(wide):
            for l in range(plane):
                refs[2 + k][l] = sums_ref[(own_wide ^ k) * plane + (own_plane ^ l)]


def own_place():
    return 2 * lax.axis_index("gy") + lax.axis_index("gz")


def write_lengths(rows, lengths_ref, block_ref):
    at_row = lax.broadcasted_iota(jnp.int32, (16, block_ref.shape[1]), 0)
    filled = jnp.zeros(at_row.shape, jnp.float32)
    for r in range(rows):
        filled = jnp.where(at_row == r, lengths_ref[:, r : r + 1].astype(jnp.float32), filled)
    block_ref[block_ref.shape[0] - 16 :] = filled.astype(jnp.bfloat16)


def cut_kernel(plan, lengths_ref, keys_ref, values_ref, _, *blocks):
    cols = blocks[0].shape[1]
    for (slot, keys, values, with_lengths), block in zip(plan, blocks):
        at = pl.multiple_of((own_place() ^ slot) * cols, cols)
        start = 0
        for cache_ref, wanted in ((keys_ref, keys), (values_ref, values)):
            for r, low, high in wanted:
                block[start : start + high - low] = cache_ref[r, low:high, pl.ds(at, cols)]
                start += high - low
        if with_lengths:
            write_lengths(keys_ref.shape[0], lengths_ref, block)


def pass_kernel(*refs):
    pass


def attend_kernel(wide, plane, members, rows, early, query_cols, frequency_ref, *refs):
    partials, held, attended_ref = refs[wide - 1 :: -1], refs[wide:-1], refs[-1]
    even = plane // 2 - 1 if members[0] else 0
    firsts, lasts, whole = held[:even], held[even : 2 * even], held[2 * even :]
    slots = (whole[0].shape[0] - 16) // (2 * rows)
    cols = partials[0].shape[-1]
    kv_cols = (cols - query_cols) // 2
    kv_heads, group = kv_cols // HD, query_cols // kv_cols
    pairs = len(members) * rows
    count = pairs * kv_heads
    heads = count * group
    scale = 1.0 / HD**0.5
    own = slice(members[0], members[-1] + 1)
    total = partials[0][own]
    for k in range(1, wide):
        total = total + partials[k][own]
    total = total.reshape(pairs, cols).astype(jnp.bfloat16).astype(jnp.float32)

    def cached(values):
        parts = []
        for p in range(pairs):
            l, r = members[p // rows], p % rows
            if l % 2 or l == 0:
                at = (values * rows + r) * slots
                parts.append(whole[(l + 1) // 2][at : at + slots])
                continue
            first, last = firsts[l // 2 - 1], lasts[l // 2 - 1]
            at = (values * rows + r) * slots
            end = (rows + early) * slots + slots // 8
            if at + slots <= end:
                parts.append(first[at : at + slots])
            elif at < end:
                rest = last[: at + slots - end]
                parts.append(jnp.concatenate([first[at:end], rest], 0))
            else:
                parts.append(last[at - end : at - end + slots])
        return jnp.concatenate(parts, 1)

    filled = []
    for l in members:
        block = lasts[l // 2 - 1] if l % 2 == 0 and l else whole[(l + 1) // 2]
        last = block[block.shape[0] - 16 :, :HD].astype(jnp.float32)
        filled += [last[r : r + 1] for r in range(rows)]
    angles = jnp.concatenate(filled, 0) * frequency_ref[...]
    cosine, sine = jnp.cos(angles), jnp.sin(angles)
    front = lax.broadcasted_iota(jnp.int32, (1, HD), 1) < HD // 2
    sine = jnp.where(front, -sine, sine)

    def rotate(vector):
        return vector * cosine + pltpu.roll(vector, HD // 2, 1) * sine

    query, key_new, value_new = [], [], []
    for h in range(kv_heads):
        turned = [
            rotate(total[:, (h * group + g) * HD : (h * group + g + 1) * HD]) for g in range(group)
        ]
        query.append(jnp.swapaxes(jnp.stack(turned, 0), 0, 1))
        at = query_cols + h * HD
        key_new.append(rotate(total[:, at : at + HD]))
        value_new.append(total[:, at + kv_cols : at + kv_cols + HD])
    query = jnp.stack(query, 1).reshape(heads, HD)
    turned_query = query.T.astype(jnp.bfloat16)
    key_new = jnp.stack(key_new, 1).reshape(count, HD).astype(jnp.bfloat16)
    value_new = jnp.stack(value_new, 1).reshape(count, HD)

    head_pair = lax.broadcasted_iota(jnp.int32, (1, heads), 1) // group
    by_pair = jnp.concatenate(
        [jnp.where(head_pair == b, turned_query, jnp.zeros_like(turned_query)) for b in range(count)],
        0,
    )
    scores = scale * jnp.dot(cached(0), by_pair, preferred_element_type=jnp.float32)
    own = scale * jnp.dot(key_new, turned_query, preferred_element_type=jnp.float32)
    of_pair = lax.broadcasted_iota(jnp.int32, (count, 1), 0) == head_pair
    own = jnp.sum(jnp.where(of_pair, own, 0.0), 0, keepdims=True)
    length = jnp.zeros((1, heads), jnp.float32)
    for p in range(pairs):
        length = jnp.where(head_pair // kv_heads == p, filled[p][:, :1], length)
    slot = lax.broadcasted_iota(jnp.int32, (slots, 1), 0).astype(jnp.float32)
    scores = jnp.where(slot < length, scores, -1e30)
    top = jnp.maximum(jnp.max(scores, 0, keepdims=True), own)
    weights = jnp.exp(scores - top)
    own_weight = jnp.exp(own - top)
    denominator = jnp.sum(weights, 0, keepdims=True) + own_weight
    probability = (weights / denominator).astype(jnp.bfloat16)
    own_prob = (own_weight / denominator).astype(jnp.bfloat16)
    contract_rows = (((0,), (0,)), ((), ()))
    mixed = lax.dot_general(
        probability, cached(1), contract_rows, preferred_element_type=jnp.float32
    )
    own_prob = jnp.where(of_pair, own_prob.astype(jnp.float32), 0.0).astype(jnp.bfloat16)
    fresh = lax.dot_general(
        own_prob, value_new.astype(jnp.bfloat16), contract_rows, preferred_element_type=jnp.float32
    )
    mixed = [
        mixed[b * group : (b + 1) * group, b * HD : (b + 1) * HD]
        + fresh[b * group : (b + 1) * group]
        for b in range(count)
    ]
    attended = []
    for h in range(kv_heads):
        by_head = jnp.swapaxes(jnp.stack(mixed[h::kv_heads], 0), 0, 1)
        attended += [by_head[g] for g in range(group)]
    attended = jnp.concatenate(attended, 1)
    attended_ref[...] = attended.reshape(len(members), rows, query_cols).astype(jnp.bfloat16)


def join_kernel(*refs):
    at = 0
    for block in refs[:-1]:
        refs[-1][at : at + block.shape[0]] = block[...]
        at += block.shape[0]


def output_kernel(at, cols, order, weight_ref, *refs):
    keep_ref, give_ref = refs[-2:]
    blocks = [refs[order.index(k)] for k in range(len(order))]
    wide = len(blocks)
    plane, rows, depth = blocks[0].shape
    attended = jnp.concatenate(
        [block[...].reshape(plane * rows, depth) for block in blocks], 0
    )
    step = min(cols, 512)
    for c in range(0, cols, step):
        part = jnp.dot(
            attended, weight_ref[:, at + c : at + c + step], preferred_element_type=jnp.float32
        )
        part = part.reshape(wide * plane // 2, 2 * rows, step)
        keep_ref[:, :, c : c + step] = part[:, :rows]
        give_ref[:, :, c : c + step] = part[:, rows:]


def halve_kernel(a_ref, b_ref, keep_ref, give_ref):
    for n in range(keep_ref.shape[0]):
        keep_ref[n] = a_ref[2 * n] + b_ref[2 * n]
        give_ref[n] = a_ref[2 * n + 1] + b_ref[2 * n + 1]


def total_kernel(parts, *refs):
    sums, blocks = refs[: 2 * parts], refs[2 * parts :]
    cols = sums[0].shape[-1]
    for p in range(parts):
        for k, block in enumerate(blocks):
            total = sums[2 * p][k] + sums[2 * p + 1][k]
            block[:, p * cols : (p + 1) * cols] = total.astype(jnp.bfloat16)


def finish_kernel(*refs):
    result_ref = refs[-1]
    order = [*sequence(len(refs) - 1), 0]
    blocks = [refs[order.index(k)] for k in range(len(order))]
    own = lax.axis_index("gx")
    cols = blocks[0].shape[-1]
    for k, block in enumerate(blocks):
        at = pl.multiple_of((own ^ k) * cols, cols)
        result_ref[:, pl.ds(at, cols)] = block[...]


def swap_blocks(blocks, axes):
    return lax.all_to_all(blocks, axes, split_axis=0, concat_axis=0, tiled=True)


def swap_pairs(value, axis, step):
    return lax.ppermute(value, axis, [(i, i ^ step) for i in range(lax.axis_size(axis))])


def swap_plane(value, step):
    return lax.ppermute(value, PLANE, [(i, i ^ step) for i in range(lax.axis_size(PLANE))])


def swap_wide(blocks):
    moved = [swap_pairs(blocks[k], "gx", k) for k in range(len(blocks) - 1, 0, -1)]
    return [blocks[0]] + moved[::-1]


def shards(
    tokens,
    norm_gain,
    query_weight,
    key_weight,
    value_weight,
    out_weight,
    cache_keys,
    cache_values,
    lengths,
):
    rows = tokens.shape[0]
    wide = lax.axis_size("gx")
    plane = lax.axis_size(PLANE)
    owners = wide * plane
    width, query_cols = query_weight.shape
    kv_cols = key_weight.shape[1]
    depth, out_cols = out_weight.shape
    cols = query_cols + 2 * kv_cols

    def params(mib):
        return pltpu.CompilerParams(vmem_limit_bytes=mib * MIB)

    def cost(flops, size):
        return pl.CostEstimate(flops=flops, bytes_accessed=size, transcendentals=0)

    half = width // 2
    scaled = pl.pallas_call(
        scale_kernel,
        out_shape=jax.ShapeDtypeStruct(tokens.shape, jnp.float32),
        in_specs=[IN_VMEM],
        out_specs=IN_VMEM,
        compiler_params=params(8),
        cost_estimate=cost(40 * 10**9, MIB),
    )(tokens)
    normed = pl.pallas_call(
        functools.partial(gain_kernel, wide, plane),
        out_shape=jax.ShapeDtypeStruct((owners, rows, half), jnp.bfloat16),
        in_specs=[IN_VMEM, IN_VMEM],
        out_specs=IN_VMEM,
        compiler_params=params(8),
    )(scaled, norm_gain.reshape(1, -1))
    slots = cache_keys.shape[1]
    even = plane // 2 - 1
    early = rows // 2
    every = [(r, 0, slots) for r in range(rows)]
    cut_at = slots // 8

    def cut(plan, after):
        return pl.pallas_call(
            functools.partial(cut_kernel, plan),
            out_shape=[
                jax.ShapeDtypeStruct(
                    (sum(h - g for _, g, h in (*keys, *values)) + 16 * with_lengths, kv_cols),
                    cache_keys.dtype,
                )
                for _, keys, values, with_lengths in plan
            ],
            in_specs=[IN_VMEM] * 4,
            out_specs=[IN_VMEM] * len(plan),
            compiler_params=params(8),
        )(lengths.reshape(1, -1), cache_keys, cache_values, after)

    early_values = [*every[:early], (early, 0, cut_at)]
    late_values = [(early, cut_at, slots), *every[early + 1 :]]
    plan = [(l, every, early_values, False) for l in range(2, plane, 2)]
    plan += [(l, (), late_values, True) for l in range(2, plane, 2)]
    plan += [(l, every, every, True) for l in range(1, plane, 2)]
    blocks = cut(plan, normed)
    firsts, rest = blocks[:even], blocks[even:]
    firsts = [swap_plane(firsts[s], 2 * s + 2) for s in range(even)]
    own_half = swap_blocks(normed, ROW_AXES)
    other_half = swap_pairs(own_half, "gz", 1)
    rest = pl.pallas_call(
        pass_kernel,
        out_shape=[jax.ShapeDtypeStruct(value.shape, value.dtype) for value in rest],
        in_specs=[ANYWHERE] * (len(rest) + even + 1),
        out_specs=[ANYWHERE] * len(rest),
        input_output_aliases={n: n for n in range(len(rest))},
        compiler_params=params(1),
    )(*rest, own_half, *firsts)
    lasts = [swap_plane(rest[s], 2 * s + 2) for s in range(even)]
    odd = [swap_plane(rest[even + s], 2 * s + 1) for s in range(even + 1)]
    (mine,) = cut([(0, every, every, True)], own_half)
    held = [*firsts, *lasts, mine, *odd]
    weights = (query_weight, key_weight, value_weight)
    half_cost = cost(owners * rows * width * cols, width * cols)
    partial = pl.pallas_call(
        functools.partial(project_kernel, True, wide, plane),
        out_shape=jax.ShapeDtypeStruct((owners * rows, cols), jnp.float32),
        in_specs=[IN_VMEM] * 4,
        out_specs=IN_VMEM,
        compiler_params=params(8),
        cost_estimate=half_cost,
    )(own_half, *weights)
    partial = pl.pallas_call(
        functools.partial(project_kernel, False, wide, plane),
        out_shape=[jax.ShapeDtypeStruct((plane, rows, cols), jnp.float32)] * wide,
        in_specs=[IN_VMEM] * 6,
        out_specs=[IN_VMEM] * wide,
        scratch_shapes=[pltpu.VMEM((owners, rows, cols), jnp.float32)],
        compiler_params=params(8),
        cost_estimate=half_cost,
    )(other_half, *weights, odd[0], partial)
    partial = swap_wide(partial)

    half_dim = HD // 2
    frequency = 500000.0 ** (-np.arange(half_dim, dtype=np.float64) / half_dim)
    frequency = np.tile(frequency.astype(np.float32), 2).reshape(1, HD)
    attended = []
    for members in (range(2), range(2, plane)):
        used = held if members[0] else held[2 * even : 2 * even + 2]
        attended.append(
            pl.pallas_call(
                functools.partial(attend_kernel, wide, plane, members, rows, early, query_cols),
                out_shape=jax.ShapeDtypeStruct((len(members), rows, query_cols), jnp.bfloat16),
                in_specs=[IN_VMEM] * (1 + wide + len(used)),
                out_specs=IN_VMEM,
                compiler_params=params(8),
                cost_estimate=cost(10**10, 4 * MIB) if members[0] else cost(1, 1),
            )(jnp.asarray(frequency), *partial[::-1], *used)
        )
    attended = pl.pallas_call(
        join_kernel,
        out_shape=jax.ShapeDtypeStruct((plane, rows, query_cols), jnp.bfloat16),
        in_specs=[IN_VMEM, IN_VMEM],
        out_specs=IN_VMEM,
        compiler_params=params(8),
    )(*attended)
    head_rows = swap_wide([attended] * wide)
    parts = 2
    order = [0, *sequence(wide)[1:], sequence(wide)[0]]
    part_cols = out_cols // parts
    sums = []
    for p in range(parts):
        count = owners // 2
        shape = jax.ShapeDtypeStruct((count, rows, part_cols), jnp.float32)
        keep, give = pl.pallas_call(
            functools.partial(output_kernel, p * part_cols, part_cols, order),
            out_shape=(shape, shape),
            in_specs=[IN_VMEM] * (1 + wide),
            out_specs=(IN_VMEM, IN_VMEM),
            compiler_params=params(8),
            cost_estimate=cost(2 * owners * rows * depth * part_cols, 2 * depth * part_cols),
        )(out_weight, *[head_rows[k] for k in order])
        give = swap_plane(give, 1)
        step = 2
        while step < plane:
            count //= 2
            shape = jax.ShapeDtypeStruct((count, rows, part_cols), jnp.float32)
            keep, give = pl.pallas_call(
                halve_kernel,
                out_shape=(shape, shape),
                in_specs=[IN_VMEM, IN_VMEM],
                out_specs=(IN_VMEM, IN_VMEM),
                compiler_params=params(8),
            )(keep, give)
            give = swap_plane(give, step)
            step *= 2
        sums += [keep, give]
    blocks = pl.pallas_call(
        functools.partial(total_kernel, parts),
        out_shape=[jax.ShapeDtypeStruct((rows, out_cols), jnp.bfloat16)] * wide,
        in_specs=[IN_VMEM] * len(sums),
        out_specs=[IN_VMEM] * wide,
        compiler_params=params(8),
    )(*sums)
    blocks = swap_wide(blocks)
    return pl.pallas_call(
        finish_kernel,
        out_shape=jax.ShapeDtypeStruct((rows, wide * out_cols), jnp.bfloat16),
        in_specs=[IN_VMEM] * wide,
        out_specs=IN_VMEM,
        compiler_params=params(8),
    )(*[blocks[k] for k in [*sequence(wide), 0]])


def solution(mesh):
    placed = (
        P(("groups", "gx", "gy", "gz"), None),
        P(),
        P("gx", ("gy", "gz")),
        P("gx", ("gy", "gz")),
        P("gx", ("gy", "gz")),
        P(("gy", "gz"), "gx"),
        P(("groups", "gx", "gy", "gz"), None, None),
        P(("groups", "gx", "gy", "gz"), None, None),
        P(("groups", "gx", "gy", "gz")),
    )
    return jax.shard_map(
        shards,
        mesh=mesh,
        in_specs=placed,
        out_specs=P(("groups", "gx", "gy", "gz"), None),
        check_vma=False,
    )
```

```python
import functools

import jax
import jax.numpy as jnp
import numpy as np
from jax import lax
from jax.experimental import pallas as pl
from jax.experimental.pallas import tpu as pltpu
from jax.sharding import PartitionSpec as P

HD = 128
ROW_AXES = ("gx", "gy", "gz")
PLANE = ("gy", "gz")
MIB = 1024 * 1024
IN_VMEM = pl.BlockSpec(memory_space=pltpu.VMEM)
ANYWHERE = pl.BlockSpec(memory_space=pl.ANY)


def sequence(wide):
    return sorted(range(1, wide), key=lambda k: (k != wide // 2, -k))


def scale_kernel(tokens_ref, scaled_ref):
    tokens = tokens_ref[...].astype(jnp.float32)
    mean_square = jnp.mean(tokens * tokens, -1, keepdims=True)
    scaled_ref[...] = tokens * lax.rsqrt(mean_square + 1e-05)


def gain_kernel(wide, plane, scaled_ref, gain_ref, blocks_ref):
    normed = (scaled_ref[...] * gain_ref[...]).astype(jnp.bfloat16)
    half = normed.shape[1] // wide // 2
    for i in range(wide):
        for j in range(plane):
            at = (2 * i + j % 2) * half
            blocks_ref[i * plane + j] = normed[:, at : at + half]


def project_kernel(own, wide, plane, rows_ref, query_ref, key_ref, value_ref, *refs):
    owners, rows, half = rows_ref.shape
    core = lax.axis_index("gz")
    at_row = pl.multiple_of((core if own else 1 - core) * half, half)
    normed = rows_ref[...].reshape(owners * rows, half)
    sums_ref = refs[-1]
    at = 0
    for weight in (query_ref, key_ref, value_ref):
        cols = weight.shape[1]
        step = min(cols, 256)
        for c in range(0, cols, step):
            part = jnp.dot(
                normed,
                weight[pl.ds(at_row, half), c : c + step],
                preferred_element_type=jnp.float32,
            )
            if own:
                sums_ref[:, at : at + step] = part
            else:
                part = part + refs[1][:, at : at + step]
                sums_ref[:, :, at : at + step] = part.reshape(owners, rows, step)
            at += step
    if not own:
        own_wide = lax.axis_index("gx")
        own_plane = 2 * lax.axis_index("gy") + core
        for k in range(wide):
            for l in range(plane):
                refs[2 + k][l] = sums_ref[(own_wide ^ k) * plane + (own_plane ^ l)]


def own_place():
    return 2 * lax.axis_index("gy") + lax.axis_index("gz")


def write_lengths(rows, lengths_ref, block_ref):
    at_row = lax.broadcasted_iota(jnp.int32, (16, block_ref.shape[1]), 0)
    filled = jnp.zeros(at_row.shape, jnp.float32)
    for r in range(rows):
        filled = jnp.where(at_row == r, lengths_ref[:, r : r + 1].astype(jnp.float32), filled)
    block_ref[block_ref.shape[0] - 16 :] = filled.astype(jnp.bfloat16)


def cut_kernel(plan, lengths_ref, keys_ref, values_ref, _, *blocks):
    cols = blocks[0].shape[1]
    for (slot, keys, values, with_lengths), block in zip(plan, blocks):
        at = pl.multiple_of((own_place() ^ slot) * cols, cols)
        start = 0
        for cache_ref, wanted in ((keys_ref, keys), (values_ref, values)):
            for r, low, high in wanted:
                block[start : start + high - low] = cache_ref[r, low:high, pl.ds(at, cols)]
                start += high - low
        if with_lengths:
            write_lengths(keys_ref.shape[0], lengths_ref, block)


def pass_kernel(*refs):
    pass


def attend_kernel(wide, plane, members, rows, early, query_cols, frequency_ref, *refs):
    partials, held, attended_ref = refs[wide - 1 :: -1], refs[wide:-1], refs[-1]
    even = plane // 2 - 1 if members[0] else 0
    firsts, lasts, whole = held[:even], held[even : 2 * even], held[2 * even :]
    slots = (whole[0].shape[0] - 16) // (2 * rows)
    cols = partials[0].shape[-1]
    kv_cols = (cols - query_cols) // 2
    kv_heads, group = kv_cols // HD, query_cols // kv_cols
    pairs = len(members) * rows
    count = pairs * kv_heads
    heads = count * group
    scale = 1.0 / HD**0.5
    own = slice(members[0], members[-1] + 1)
    total = partials[0][own]
    for k in range(1, wide):
        total = total + partials[k][own]
    total = total.reshape(pairs, cols).astype(jnp.bfloat16).astype(jnp.float32)

    def cached(values):
        parts = []
        for p in range(pairs):
            l, r = members[p // rows], p % rows
            if l % 2 or l == 0:
                at = (values * rows + r) * slots
                parts.append(whole[(l + 1) // 2][at : at + slots])
                continue
            first, last = firsts[l // 2 - 1], lasts[l // 2 - 1]
            at = (values * rows + r) * slots
            end = (rows + early) * slots + slots // 8
            if at + slots <= end:
                parts.append(first[at : at + slots])
            elif at < end:
                rest = last[: at + slots - end]
                parts.append(jnp.concatenate([first[at:end], rest], 0))
            else:
                parts.append(last[at - end : at - end + slots])
        return jnp.concatenate(parts, 1)

    filled = []
    for l in members:
        block = lasts[l // 2 - 1] if l % 2 == 0 and l else whole[(l + 1) // 2]
        last = block[block.shape[0] - 16 :, :HD].astype(jnp.float32)
        filled += [last[r : r + 1] for r in range(rows)]
    angles = jnp.concatenate(filled, 0) * frequency_ref[...]
    cosine, sine = jnp.cos(angles), jnp.sin(angles)
    front = lax.broadcasted_iota(jnp.int32, (1, HD), 1) < HD // 2
    sine = jnp.where(front, -sine, sine)

    def rotate(vector):
        return vector * cosine + pltpu.roll(vector, HD // 2, 1) * sine

    query, key_new, value_new = [], [], []
    for h in range(kv_heads):
        turned = [
            rotate(total[:, (h * group + g) * HD : (h * group + g + 1) * HD]) for g in range(group)
        ]
        query.append(jnp.swapaxes(jnp.stack(turned, 0), 0, 1))
        at = query_cols + h * HD
        key_new.append(rotate(total[:, at : at + HD]))
        value_new.append(total[:, at + kv_cols : at + kv_cols + HD])
    query = jnp.stack(query, 1).reshape(heads, HD)
    turned_query = query.T.astype(jnp.bfloat16)
    key_new = jnp.stack(key_new, 1).reshape(count, HD).astype(jnp.bfloat16)
    value_new = jnp.stack(value_new, 1).reshape(count, HD)

    head_pair = lax.broadcasted_iota(jnp.int32, (1, heads), 1) // group
    by_pair = jnp.concatenate(
        [jnp.where(head_pair == b, turned_query, jnp.zeros_like(turned_query)) for b in range(count)],
        0,
    )
    scores = scale * jnp.dot(cached(0), by_pair, preferred_element_type=jnp.float32)
    own = scale * jnp.dot(key_new, turned_query, preferred_element_type=jnp.float32)
    of_pair = lax.broadcasted_iota(jnp.int32, (count, 1), 0) == head_pair
    own = jnp.sum(jnp.where(of_pair, own, 0.0), 0, keepdims=True)
    length = jnp.zeros((1, heads), jnp.float32)
    for p in range(pairs):
        length = jnp.where(head_pair // kv_heads == p, filled[p][:, :1], length)
    slot = lax.broadcasted_iota(jnp.int32, (slots, 1), 0).astype(jnp.float32)
    scores = jnp.where(slot < length, scores, -1e30)
    top = jnp.maximum(jnp.max(scores, 0, keepdims=True), own)
    weights = jnp.exp(scores - top)
    own_weight = jnp.exp(own - top)
    denominator = jnp.sum(weights, 0, keepdims=True) + own_weight
    probability = (weights / denominator).astype(jnp.bfloat16)
    own_prob = (own_weight / denominator).astype(jnp.bfloat16)
    contract_rows = (((0,), (0,)), ((), ()))
    mixed = lax.dot_general(
        probability, cached(1), contract_rows, preferred_element_type=jnp.float32
    )
    own_prob = jnp.where(of_pair, own_prob.astype(jnp.float32), 0.0).astype(jnp.bfloat16)
    fresh = lax.dot_general(
        own_prob, value_new.astype(jnp.bfloat16), contract_rows, preferred_element_type=jnp.float32
    )
    mixed = [
        mixed[b * group : (b + 1) * group, b * HD : (b + 1) * HD]
        + fresh[b * group : (b + 1) * group]
        for b in range(count)
    ]
    attended = []
    for h in range(kv_heads):
        by_head = jnp.swapaxes(jnp.stack(mixed[h::kv_heads], 0), 0, 1)
        attended += [by_head[g] for g in range(group)]
    attended = jnp.concatenate(attended, 1)
    attended_ref[...] = attended.reshape(len(members), rows, query_cols).astype(jnp.bfloat16)


def join_kernel(*refs):
    at = 0
    for block in refs[:-1]:
        refs[-1][at : at + block.shape[0]] = block[...]
        at += block.shape[0]


def output_kernel(at, cols, order, weight_ref, *refs):
    keep_ref, give_ref = refs[-2:]
    blocks = [refs[order.index(k)] for k in range(len(order))]
    wide = len(blocks)
    plane, rows, depth = blocks[0].shape
    attended = jnp.concatenate(
        [block[...].reshape(plane * rows, depth) for block in blocks], 0
    )
    step = min(cols, 512)
    for c in range(0, cols, step):
        part = jnp.dot(
            attended, weight_ref[:, at + c : at + c + step], preferred_element_type=jnp.float32
        )
        part = part.reshape(wide * plane // 2, 2 * rows, step)
        keep_ref[:, :, c : c + step] = part[:, :rows]
        give_ref[:, :, c : c + step] = part[:, rows:]


def halve_kernel(a_ref, b_ref, keep_ref, give_ref):
    for n in range(keep_ref.shape[0]):
        keep_ref[n] = a_ref[2 * n] + b_ref[2 * n]
        give_ref[n] = a_ref[2 * n + 1] + b_ref[2 * n + 1]


def total_kernel(parts, *refs):
    sums, blocks = refs[: 2 * parts], refs[2 * parts :]
    cols = sums[0].shape[-1]
    for p in range(parts):
        for k, block in enumerate(blocks):
            total = sums[2 * p][k] + sums[2 * p + 1][k]
            block[:, p * cols : (p + 1) * cols] = total.astype(jnp.bfloat16)


def finish_kernel(*refs):
    result_ref = refs[-1]
    order = range(len(refs) - 2, -1, -1)
    blocks = [refs[order.index(k)] for k in range(len(order))]
    own = lax.axis_index("gx")
    cols = blocks[0].shape[-1]
    for k, block in enumerate(blocks):
        at = pl.multiple_of((own ^ k) * cols, cols)
        result_ref[:, pl.ds(at, cols)] = block[...]


def swap_blocks(blocks, axes):
    return lax.all_to_all(blocks, axes, split_axis=0, concat_axis=0, tiled=True)


def swap_pairs(value, axis, step):
    return lax.ppermute(value, axis, [(i, i ^ step) for i in range(lax.axis_size(axis))])


def swap_plane(value, step):
    return lax.ppermute(value, PLANE, [(i, i ^ step) for i in range(lax.axis_size(PLANE))])


def swap_wide(blocks):
    moved = [swap_pairs(blocks[k], "gx", k) for k in range(len(blocks) - 1, 0, -1)]
    return [blocks[0]] + moved[::-1]


def shards(
    tokens,
    norm_gain,
    query_weight,
    key_weight,
    value_weight,
    out_weight,
    cache_keys,
    cache_values,
    lengths,
):
    rows = tokens.shape[0]
    wide = lax.axis_size("gx")
    plane = lax.axis_size(PLANE)
    owners = wide * plane
    width, query_cols = query_weight.shape
    kv_cols = key_weight.shape[1]
    depth, out_cols = out_weight.shape
    cols = query_cols + 2 * kv_cols

    def params(mib):
        return pltpu.CompilerParams(vmem_limit_bytes=mib * MIB)

    def cost(flops, size):
        return pl.CostEstimate(flops=flops, bytes_accessed=size, transcendentals=0)

    half = width // 2
    scaled = pl.pallas_call(
        scale_kernel,
        out_shape=jax.ShapeDtypeStruct(tokens.shape, jnp.float32),
        in_specs=[IN_VMEM],
        out_specs=IN_VMEM,
        compiler_params=params(8),
        cost_estimate=cost(40 * 10**9, MIB),
    )(tokens)
    normed = pl.pallas_call(
        functools.partial(gain_kernel, wide, plane),
        out_shape=jax.ShapeDtypeStruct((owners, rows, half), jnp.bfloat16),
        in_specs=[IN_VMEM, IN_VMEM],
        out_specs=IN_VMEM,
        compiler_params=params(8),
    )(scaled, norm_gain.reshape(1, -1))
    slots = cache_keys.shape[1]
    even = plane // 2 - 1
    early = rows // 2
    every = [(r, 0, slots) for r in range(rows)]
    cut_at = slots // 8

    def cut(plan, after):
        return pl.pallas_call(
            functools.partial(cut_kernel, plan),
            out_shape=[
                jax.ShapeDtypeStruct(
                    (sum(h - g for _, g, h in (*keys, *values)) + 16 * with_lengths, kv_cols),
                    cache_keys.dtype,
                )
                for _, keys, values, with_lengths in plan
            ],
            in_specs=[IN_VMEM] * 4,
            out_specs=[IN_VMEM] * len(plan),
            compiler_params=params(8),
        )(lengths.reshape(1, -1), cache_keys, cache_values, after)

    early_values = [*every[:early], (early, 0, cut_at)]
    late_values = [(early, cut_at, slots), *every[early + 1 :]]
    plan = [(l, every, early_values, False) for l in range(2, plane, 2)]
    plan += [(l, (), late_values, True) for l in range(2, plane, 2)]
    plan += [(l, every, every, True) for l in range(1, plane, 2)]
    blocks = cut(plan, normed)
    firsts, rest = blocks[:even], blocks[even:]
    firsts = [swap_plane(firsts[s], 2 * s + 2) for s in range(even)]
    own_half = swap_blocks(normed, ROW_AXES)
    other_half = swap_pairs(own_half, "gz", 1)
    rest = pl.pallas_call(
        pass_kernel,
        out_shape=[jax.ShapeDtypeStruct(value.shape, value.dtype) for value in rest],
        in_specs=[ANYWHERE] * (len(rest) + even + 1),
        out_specs=[ANYWHERE] * len(rest),
        input_output_aliases={n: n for n in range(len(rest))},
        compiler_params=params(1),
    )(*rest, own_half, *firsts)
    lasts = [swap_plane(rest[s], 2 * s + 2) for s in range(even)]
    odd = [swap_plane(rest[even + s], 2 * s + 1) for s in range(even + 1)]
    (mine,) = cut([(0, every, every, True)], own_half)
    held = [*firsts, *lasts, mine, *odd]
    weights = (query_weight, key_weight, value_weight)
    half_cost = cost(owners * rows * width * cols, width * cols)
    partial = pl.pallas_call(
        functools.partial(project_kernel, True, wide, plane),
        out_shape=jax.ShapeDtypeStruct((owners * rows, cols), jnp.float32),
        in_specs=[IN_VMEM] * 4,
        out_specs=IN_VMEM,
        compiler_params=params(8),
        cost_estimate=half_cost,
    )(own_half, *weights)
    partial = pl.pallas_call(
        functools.partial(project_kernel, False, wide, plane),
        out_shape=[jax.ShapeDtypeStruct((plane, rows, cols), jnp.float32)] * wide,
        in_specs=[IN_VMEM] * 6,
        out_specs=[IN_VMEM] * wide,
        scratch_shapes=[pltpu.VMEM((owners, rows, cols), jnp.float32)],
        compiler_params=params(8),
        cost_estimate=half_cost,
    )(other_half, *weights, odd[0], partial)
    partial = swap_wide(partial)

    half_dim = HD // 2
    frequency = 500000.0 ** (-np.arange(half_dim, dtype=np.float64) / half_dim)
    frequency = np.tile(frequency.astype(np.float32), 2).reshape(1, HD)
    attended = []
    for members in (range(2), range(2, plane)):
        used = held if members[0] else held[2 * even : 2 * even + 2]
        attended.append(
            pl.pallas_call(
                functools.partial(attend_kernel, wide, plane, members, rows, early, query_cols),
                out_shape=jax.ShapeDtypeStruct((len(members), rows, query_cols), jnp.bfloat16),
                in_specs=[IN_VMEM] * (1 + wide + len(used)),
                out_specs=IN_VMEM,
                compiler_params=params(8),
                cost_estimate=cost(10**10, 4 * MIB) if members[0] else cost(1, 1),
            )(jnp.asarray(frequency), *partial[::-1], *used)
        )
    attended = pl.pallas_call(
        join_kernel,
        out_shape=jax.ShapeDtypeStruct((plane, rows, query_cols), jnp.bfloat16),
        in_specs=[IN_VMEM, IN_VMEM],
        out_specs=IN_VMEM,
        compiler_params=params(8),
    )(*attended)
    head_rows = swap_wide([attended] * wide)
    parts = 2
    order = [0, *sequence(wide)[1:], sequence(wide)[0]]
    part_cols = out_cols // parts
    sums = []
    for p in range(parts):
        count = owners // 2
        shape = jax.ShapeDtypeStruct((count, rows, part_cols), jnp.float32)
        keep, give = pl.pallas_call(
            functools.partial(output_kernel, p * part_cols, part_cols, order),
            out_shape=(shape, shape),
            in_specs=[IN_VMEM] * (1 + wide),
            out_specs=(IN_VMEM, IN_VMEM),
            compiler_params=params(8),
            cost_estimate=cost(2 * owners * rows * depth * part_cols, 2 * depth * part_cols),
        )(out_weight, *[head_rows[k] for k in order])
        give = swap_plane(give, 1)
        step = 2
        while step < plane:
            count //= 2
            shape = jax.ShapeDtypeStruct((count, rows, part_cols), jnp.float32)
            keep, give = pl.pallas_call(
                halve_kernel,
                out_shape=(shape, shape),
                in_specs=[IN_VMEM, IN_VMEM],
                out_specs=(IN_VMEM, IN_VMEM),
                compiler_params=params(8),
            )(keep, give)
            give = swap_plane(give, step)
            step *= 2
        sums += [keep, give]
    blocks = pl.pallas_call(
        functools.partial(total_kernel, parts),
        out_shape=[jax.ShapeDtypeStruct((rows, out_cols), jnp.bfloat16)] * wide,
        in_specs=[IN_VMEM] * len(sums),
        out_specs=[IN_VMEM] * wide,
        compiler_params=params(8),
    )(*sums)
    blocks = swap_wide(blocks)
    return pl.pallas_call(
        finish_kernel,
        out_shape=jax.ShapeDtypeStruct((rows, wide * out_cols), jnp.bfloat16),
        in_specs=[IN_VMEM] * wide,
        out_specs=IN_VMEM,
        compiler_params=params(8),
    )(*blocks[::-1])


def solution(mesh):
    placed = (
        P(("groups", "gx", "gy", "gz"), None),
        P(),
        P("gx", ("gy", "gz")),
        P("gx", ("gy", "gz")),
        P("gx", ("gy", "gz")),
        P(("gy", "gz"), "gx"),
        P(("groups", "gx", "gy", "gz"), None, None),
        P(("groups", "gx", "gy", "gz"), None, None),
        P(("groups", "gx", "gy", "gz")),
    )
    return jax.shard_map(
        shards,
        mesh=mesh,
        in_specs=placed,
        out_specs=P(("groups", "gx", "gy", "gz"), None),
        check_vma=False,
    )
```

```python
import functools

import jax
import jax.numpy as jnp
import numpy as np
from jax import lax
from jax.experimental import pallas as pl
from jax.experimental.pallas import tpu as pltpu
from jax.sharding import PartitionSpec as P

HD = 128
ROW_AXES = ("gx", "gy", "gz")
PLANE = ("gy", "gz")
MIB = 1024 * 1024
IN_VMEM = pl.BlockSpec(memory_space=pltpu.VMEM)
ANYWHERE = pl.BlockSpec(memory_space=pl.ANY)


def sequence(wide):
    return list(range(wide - 1, 0, -1))


def scale_kernel(tokens_ref, scaled_ref):
    tokens = tokens_ref[...].astype(jnp.float32)
    mean_square = jnp.mean(tokens * tokens, -1, keepdims=True)
    scaled_ref[...] = tokens * lax.rsqrt(mean_square + 1e-05)


def gain_kernel(wide, plane, scaled_ref, gain_ref, blocks_ref):
    normed = (scaled_ref[...] * gain_ref[...]).astype(jnp.bfloat16)
    half = normed.shape[1] // wide // 2
    for i in range(wide):
        for j in range(plane):
            at = (2 * i + j % 2) * half
            blocks_ref[i * plane + j] = normed[:, at : at + half]


def project_kernel(own, wide, plane, rows_ref, query_ref, key_ref, value_ref, *refs):
    owners, rows, half = rows_ref.shape
    core = lax.axis_index("gz")
    at_row = pl.multiple_of((core if own else 1 - core) * half, half)
    normed = rows_ref[...].reshape(owners * rows, half)
    sums_ref = refs[-1]
    at = 0
    for weight in (query_ref, key_ref, value_ref):
        cols = weight.shape[1]
        step = min(cols, 256)
        for c in range(0, cols, step):
            part = jnp.dot(
                normed,
                weight[pl.ds(at_row, half), c : c + step],
                preferred_element_type=jnp.float32,
            )
            if own:
                sums_ref[:, at : at + step] = part
            else:
                part = part + refs[1][:, at : at + step]
                sums_ref[:, :, at : at + step] = part.reshape(owners, rows, step)
            at += step
    if not own:
        own_wide = lax.axis_index("gx")
        own_plane = 2 * lax.axis_index("gy") + core
        for k in range(wide):
            for l in range(plane):
                refs[2 + k][l] = sums_ref[(own_wide ^ k) * plane + (own_plane ^ l)]


def own_place():
    return 2 * lax.axis_index("gy") + lax.axis_index("gz")


def write_lengths(rows, lengths_ref, block_ref):
    at_row = lax.broadcasted_iota(jnp.int32, (16, block_ref.shape[1]), 0)
    filled = jnp.zeros(at_row.shape, jnp.float32)
    for r in range(rows):
        filled = jnp.where(at_row == r, lengths_ref[:, r : r + 1].astype(jnp.float32), filled)
    block_ref[block_ref.shape[0] - 16 :] = filled.astype(jnp.bfloat16)


def cut_kernel(plan, lengths_ref, keys_ref, values_ref, _, *blocks):
    cols = blocks[0].shape[1]
    for (slot, keys, values, with_lengths), block in zip(plan, blocks):
        at = pl.multiple_of((own_place() ^ slot) * cols, cols)
        start = 0
        for cache_ref, wanted in ((keys_ref, keys), (values_ref, values)):
            for r, low, high in wanted:
                block[start : start + high - low] = cache_ref[r, low:high, pl.ds(at, cols)]
                start += high - low
        if with_lengths:
            write_lengths(keys_ref.shape[0], lengths_ref, block)


def pass_kernel(*refs):
    pass


def attend_kernel(wide, plane, members, rows, early, query_cols, frequency_ref, *refs):
    partials, held, attended_ref = refs[wide - 1 :: -1], refs[wide:-1], refs[-1]
    even = plane // 2 - 1 if members[0] else 0
    firsts, lasts, whole = held[:even], held[even : 2 * even], held[2 * even :]
    slots = (whole[0].shape[0] - 16) // (2 * rows)
    cols = partials[0].shape[-1]
    kv_cols = (cols - query_cols) // 2
    kv_heads, group = kv_cols // HD, query_cols // kv_cols
    pairs = len(members) * rows
    count = pairs * kv_heads
    heads = count * group
    scale = 1.0 / HD**0.5
    own = slice(members[0], members[-1] + 1)
    total = partials[0][own]
    for k in range(1, wide):
        total = total + partials[k][own]
    total = total.reshape(pairs, cols).astype(jnp.bfloat16).astype(jnp.float32)

    def cached(values):
        parts = []
        for p in range(pairs):
            l, r = members[p // rows], p % rows
            if l % 2 or l == 0:
                at = (values * rows + r) * slots
                parts.append(whole[(l + 1) // 2][at : at + slots])
                continue
            first, last = firsts[l // 2 - 1], lasts[l // 2 - 1]
            at = (values * rows + r) * slots
            end = (rows + early) * slots + slots // 8
            if at + slots <= end:
                parts.append(first[at : at + slots])
            elif at < end:
                rest = last[: at + slots - end]
                parts.append(jnp.concatenate([first[at:end], rest], 0))
            else:
                parts.append(last[at - end : at - end + slots])
        return jnp.concatenate(parts, 1)

    filled = []
    for l in members:
        block = lasts[l // 2 - 1] if l % 2 == 0 and l else whole[(l + 1) // 2]
        last = block[block.shape[0] - 16 :, :HD].astype(jnp.float32)
        filled += [last[r : r + 1] for r in range(rows)]
    angles = jnp.concatenate(filled, 0) * frequency_ref[...]
    cosine, sine = jnp.cos(angles), jnp.sin(angles)
    front = lax.broadcasted_iota(jnp.int32, (1, HD), 1) < HD // 2
    sine = jnp.where(front, -sine, sine)

    def rotate(vector):
        return vector * cosine + pltpu.roll(vector, HD // 2, 1) * sine

    query, key_new, value_new = [], [], []
    for h in range(kv_heads):
        turned = [
            rotate(total[:, (h * group + g) * HD : (h * group + g + 1) * HD]) for g in range(group)
        ]
        query.append(jnp.swapaxes(jnp.stack(turned, 0), 0, 1))
        at = query_cols + h * HD
        key_new.append(rotate(total[:, at : at + HD]))
        value_new.append(total[:, at + kv_cols : at + kv_cols + HD])
    query = jnp.stack(query, 1).reshape(heads, HD)
    turned_query = query.T.astype(jnp.bfloat16)
    key_new = jnp.stack(key_new, 1).reshape(count, HD).astype(jnp.bfloat16)
    value_new = jnp.stack(value_new, 1).reshape(count, HD)

    head_pair = lax.broadcasted_iota(jnp.int32, (1, heads), 1) // group
    by_pair = jnp.concatenate(
        [jnp.where(head_pair == b, turned_query, jnp.zeros_like(turned_query)) for b in range(count)],
        0,
    )
    scores = scale * jnp.dot(cached(0), by_pair, preferred_element_type=jnp.float32)
    own = scale * jnp.dot(key_new, turned_query, preferred_element_type=jnp.float32)
    of_pair = lax.broadcasted_iota(jnp.int32, (count, 1), 0) == head_pair
    own = jnp.sum(jnp.where(of_pair, own, 0.0), 0, keepdims=True)
    length = jnp.zeros((1, heads), jnp.float32)
    for p in range(pairs):
        length = jnp.where(head_pair // kv_heads == p, filled[p][:, :1], length)
    slot = lax.broadcasted_iota(jnp.int32, (slots, 1), 0).astype(jnp.float32)
    scores = jnp.where(slot < length, scores, -1e30)
    top = jnp.maximum(jnp.max(scores, 0, keepdims=True), own)
    weights = jnp.exp(scores - top)
    own_weight = jnp.exp(own - top)
    denominator = jnp.sum(weights, 0, keepdims=True) + own_weight
    probability = (weights / denominator).astype(jnp.bfloat16)
    own_prob = (own_weight / denominator).astype(jnp.bfloat16)
    contract_rows = (((0,), (0,)), ((), ()))
    mixed = lax.dot_general(
        probability, cached(1), contract_rows, preferred_element_type=jnp.float32
    )
    own_prob = jnp.where(of_pair, own_prob.astype(jnp.float32), 0.0).astype(jnp.bfloat16)
    fresh = lax.dot_general(
        own_prob, value_new.astype(jnp.bfloat16), contract_rows, preferred_element_type=jnp.float32
    )
    mixed = [
        mixed[b * group : (b + 1) * group, b * HD : (b + 1) * HD]
        + fresh[b * group : (b + 1) * group]
        for b in range(count)
    ]
    attended = []
    for h in range(kv_heads):
        by_head = jnp.swapaxes(jnp.stack(mixed[h::kv_heads], 0), 0, 1)
        attended += [by_head[g] for g in range(group)]
    attended = jnp.concatenate(attended, 1)
    attended_ref[...] = attended.reshape(len(members), rows, query_cols).astype(jnp.bfloat16)


def join_kernel(*refs):
    at = 0
    for block in refs[:-1]:
        refs[-1][at : at + block.shape[0]] = block[...]
        at += block.shape[0]


def output_kernel(at, cols, order, weight_ref, *refs):
    keep_ref, give_ref = refs[-2:]
    blocks = [refs[order.index(k)] for k in range(len(order))]
    wide = len(blocks)
    plane, rows, depth = blocks[0].shape
    attended = jnp.concatenate(
        [block[...].reshape(plane * rows, depth) for block in blocks], 0
    )
    step = min(cols, 512)
    for c in range(0, cols, step):
        part = jnp.dot(
            attended, weight_ref[:, at + c : at + c + step], preferred_element_type=jnp.float32
        )
        part = part.reshape(wide * plane // 2, 2 * rows, step)
        keep_ref[:, :, c : c + step] = part[:, :rows]
        give_ref[:, :, c : c + step] = part[:, rows:]


def halve_kernel(a_ref, b_ref, keep_ref, give_ref):
    for n in range(keep_ref.shape[0]):
        keep_ref[n] = a_ref[2 * n] + b_ref[2 * n]
        give_ref[n] = a_ref[2 * n + 1] + b_ref[2 * n + 1]


def total_kernel(parts, *refs):
    sums, blocks = refs[: 2 * parts], refs[2 * parts :]
    cols = sums[0].shape[-1]
    for p in range(parts):
        for k, block in enumerate(blocks):
            total = sums[2 * p][k] + sums[2 * p + 1][k]
            block[:, p * cols : (p + 1) * cols] = total.astype(jnp.bfloat16)


def finish_kernel(*refs):
    result_ref = refs[-1]
    order = range(len(refs) - 2, -1, -1)
    blocks = [refs[order.index(k)] for k in range(len(order))]
    own = lax.axis_index("gx")
    cols = blocks[0].shape[-1]
    for k, block in enumerate(blocks):
        at = pl.multiple_of((own ^ k) * cols, cols)
        result_ref[:, pl.ds(at, cols)] = block[...]


def swap_blocks(blocks, axes):
    return lax.all_to_all(blocks, axes, split_axis=0, concat_axis=0, tiled=True)


def swap_pairs(value, axis, step):
    return lax.ppermute(value, axis, [(i, i ^ step) for i in range(lax.axis_size(axis))])


def swap_plane(value, step):
    return lax.ppermute(value, PLANE, [(i, i ^ step) for i in range(lax.axis_size(PLANE))])


def swap_wide(blocks):
    moved = [swap_pairs(blocks[k], "gx", k) for k in range(len(blocks) - 1, 0, -1)]
    return [blocks[0]] + moved[::-1]


def shards(
    tokens,
    norm_gain,
    query_weight,
    key_weight,
    value_weight,
    out_weight,
    cache_keys,
    cache_values,
    lengths,
):
    rows = tokens.shape[0]
    wide = lax.axis_size("gx")
    plane = lax.axis_size(PLANE)
    owners = wide * plane
    width, query_cols = query_weight.shape
    kv_cols = key_weight.shape[1]
    depth, out_cols = out_weight.shape
    cols = query_cols + 2 * kv_cols

    def params(mib):
        return pltpu.CompilerParams(vmem_limit_bytes=mib * MIB)

    def cost(flops, size):
        return pl.CostEstimate(flops=flops, bytes_accessed=size, transcendentals=0)

    half = width // 2
    scaled = pl.pallas_call(
        scale_kernel,
        out_shape=jax.ShapeDtypeStruct(tokens.shape, jnp.float32),
        in_specs=[IN_VMEM],
        out_specs=IN_VMEM,
        compiler_params=params(8),
        cost_estimate=cost(40 * 10**9, MIB),
    )(tokens)
    normed = pl.pallas_call(
        functools.partial(gain_kernel, wide, plane),
        out_shape=jax.ShapeDtypeStruct((owners, rows, half), jnp.bfloat16),
        in_specs=[IN_VMEM, IN_VMEM],
        out_specs=IN_VMEM,
        compiler_params=params(8),
    )(scaled, norm_gain.reshape(1, -1))
    slots = cache_keys.shape[1]
    even = plane // 2 - 1
    early = rows // 2
    every = [(r, 0, slots) for r in range(rows)]
    cut_at = slots // 8

    def cut(plan, after):
        return pl.pallas_call(
            functools.partial(cut_kernel, plan),
            out_shape=[
                jax.ShapeDtypeStruct(
                    (sum(h - g for _, g, h in (*keys, *values)) + 16 * with_lengths, kv_cols),
                    cache_keys.dtype,
                )
                for _, keys, values, with_lengths in plan
            ],
            in_specs=[IN_VMEM] * 4,
            out_specs=[IN_VMEM] * len(plan),
            compiler_params=params(8),
        )(lengths.reshape(1, -1), cache_keys, cache_values, after)

    early_values = [*every[:early], (early, 0, cut_at)]
    late_values = [(early, cut_at, slots), *every[early + 1 :]]
    plan = [(l, every, early_values, False) for l in range(2, plane, 2)]
    plan += [(l, (), late_values, True) for l in range(2, plane, 2)]
    plan += [(l, every, every, True) for l in range(1, plane, 2)]
    blocks = cut(plan, normed)
    firsts, rest = blocks[:even], blocks[even:]
    firsts = [swap_plane(firsts[s], 2 * s + 2) for s in range(even)]
    own_half = swap_blocks(normed, ROW_AXES)
    other_half = swap_pairs(own_half, "gz", 1)
    rest = pl.pallas_call(
        pass_kernel,
        out_shape=[jax.ShapeDtypeStruct(value.shape, value.dtype) for value in rest],
        in_specs=[ANYWHERE] * (len(rest) + even + 1),
        out_specs=[ANYWHERE] * len(rest),
        input_output_aliases={n: n for n in range(len(rest))},
        compiler_params=params(1),
    )(*rest, own_half, *firsts)
    lasts = [swap_plane(rest[s], 2 * s + 2) for s in range(even)]
    odd = [swap_plane(rest[even + s], 2 * s + 1) for s in range(even + 1)]
    (mine,) = cut([(0, every, every, True)], own_half)
    held = [*firsts, *lasts, mine, *odd]
    weights = (query_weight, key_weight, value_weight)
    half_cost = cost(owners * rows * width * cols, width * cols)
    partial = pl.pallas_call(
        functools.partial(project_kernel, True, wide, plane),
        out_shape=jax.ShapeDtypeStruct((owners * rows, cols), jnp.float32),
        in_specs=[IN_VMEM] * 4,
        out_specs=IN_VMEM,
        compiler_params=params(8),
        cost_estimate=half_cost,
    )(own_half, *weights)
    partial = pl.pallas_call(
        functools.partial(project_kernel, False, wide, plane),
        out_shape=[jax.ShapeDtypeStruct((plane, rows, cols), jnp.float32)] * wide,
        in_specs=[IN_VMEM] * 6,
        out_specs=[IN_VMEM] * wide,
        scratch_shapes=[pltpu.VMEM((owners, rows, cols), jnp.float32)],
        compiler_params=params(8),
        cost_estimate=half_cost,
    )(other_half, *weights, odd[0], partial)
    partial = swap_wide(partial)

    half_dim = HD // 2
    frequency = 500000.0 ** (-np.arange(half_dim, dtype=np.float64) / half_dim)
    frequency = np.tile(frequency.astype(np.float32), 2).reshape(1, HD)
    attended = []
    for members in (range(2), range(2, plane)):
        used = held if members[0] else held[2 * even : 2 * even + 2]
        attended.append(
            pl.pallas_call(
                functools.partial(attend_kernel, wide, plane, members, rows, early, query_cols),
                out_shape=jax.ShapeDtypeStruct((len(members), rows, query_cols), jnp.bfloat16),
                in_specs=[IN_VMEM] * (1 + wide + len(used)),
                out_specs=IN_VMEM,
                compiler_params=params(8),
                cost_estimate=cost(10**10, 4 * MIB) if members[0] else cost(1, 1),
            )(jnp.asarray(frequency), *partial[::-1], *used)
        )
    attended = pl.pallas_call(
        join_kernel,
        out_shape=jax.ShapeDtypeStruct((plane, rows, query_cols), jnp.bfloat16),
        in_specs=[IN_VMEM, IN_VMEM],
        out_specs=IN_VMEM,
        compiler_params=params(8),
    )(*attended)
    head_rows = swap_wide([attended] * wide)
    parts = 2
    order = [0, *sequence(wide)[1:], sequence(wide)[0]]
    part_cols = out_cols // parts
    sums = []
    for p in range(parts):
        count = owners // 2
        shape = jax.ShapeDtypeStruct((count, rows, part_cols), jnp.float32)
        keep, give = pl.pallas_call(
            functools.partial(output_kernel, p * part_cols, part_cols, order),
            out_shape=(shape, shape),
            in_specs=[IN_VMEM] * (1 + wide),
            out_specs=(IN_VMEM, IN_VMEM),
            compiler_params=params(8),
            cost_estimate=cost(2 * owners * rows * depth * part_cols, 2 * depth * part_cols),
        )(out_weight, *[head_rows[k] for k in order])
        give = swap_plane(give, 1)
        step = 2
        while step < plane:
            count //= 2
            shape = jax.ShapeDtypeStruct((count, rows, part_cols), jnp.float32)
            keep, give = pl.pallas_call(
                halve_kernel,
                out_shape=(shape, shape),
                in_specs=[IN_VMEM, IN_VMEM],
                out_specs=(IN_VMEM, IN_VMEM),
                compiler_params=params(8),
            )(keep, give)
            give = swap_plane(give, step)
            step *= 2
        sums += [keep, give]
    blocks = pl.pallas_call(
        functools.partial(total_kernel, parts),
        out_shape=[jax.ShapeDtypeStruct((rows, out_cols), jnp.bfloat16)] * wide,
        in_specs=[IN_VMEM] * len(sums),
        out_specs=[IN_VMEM] * wide,
        compiler_params=params(8),
    )(*sums)
    blocks = swap_wide(blocks)
    return pl.pallas_call(
        finish_kernel,
        out_shape=jax.ShapeDtypeStruct((rows, wide * out_cols), jnp.bfloat16),
        in_specs=[IN_VMEM] * wide,
        out_specs=IN_VMEM,
        compiler_params=params(8),
    )(*blocks[::-1])


def solution(mesh):
    placed = (
        P(("groups", "gx", "gy", "gz"), None),
        P(),
        P("gx", ("gy", "gz")),
        P("gx", ("gy", "gz")),
        P("gx", ("gy", "gz")),
        P(("gy", "gz"), "gx"),
        P(("groups", "gx", "gy", "gz"), None, None),
        P(("groups", "gx", "gy", "gz"), None, None),
        P(("groups", "gx", "gy", "gz")),
    )
    return jax.shard_map(
        shards,
        mesh=mesh,
        in_specs=placed,
        out_specs=P(("groups", "gx", "gy", "gz"), None),
        check_vma=False,
    )
```
